32 devices in a mesh: fsdp: 16 (over z, x, core), tp: 2 (over y).
Axes of the slice: x: 2, y: 2, z: 4, core: 2. Of those that a mesh axis runs over, the one named last changes fastest.
Arguments:
- tokens: bfloat16 [8192, 2048], P(('fsdp', 'tp')), may hold values from -6 to 6
- cotangent: bfloat16 [8192, 2048], P(('fsdp', 'tp')), may hold values from -6 to 6
- valid_len: int32 [16], replicated, may hold values from 256 to 512, as said below
- pic_start: int32 [16], replicated, may hold values from 0 to 256, as said below
- norm_gains: float32 [2, 2048], replicated, may hold values from 0.5 to 1.5
- norm_moment: float32 [2, 2048], replicated, may hold values from -96 to 96
- norm_square: float32 [2, 2048], replicated, may hold values from 18.0224 to 73.728
- head_gains: float32 [2, 128], replicated, may hold values from 0.5 to 1.5
- head_moment: float32 [2, 128], replicated, may hold values from -448 to 448
- head_square: float32 [2, 128], replicated, may hold values from 409.6 to 1638.4
- query_weight: float32 [2048, 2048], P('fsdp', 'tp'), may hold values from -0.125 to 0.125
- query_moment: float32 [2048, 2048], P('fsdp', 'tp'), may hold values from -112 to 112
- query_square: float32 [2048, 2048], P('fsdp', 'tp'), may hold values from 24.576 to 106.496
- keyvalue_matrix: float32 [2, 2048, 1024], P(None, 'fsdp', 'tp'), may hold values from -0.125 to 0.125
- keyvalue_first_moment: float32 [2, 2048, 1024], P(None, 'fsdp', 'tp'), may hold values from -96 to 96
- keyvalue_second_moment: float32 [2, 2048, 1024], P(None, 'fsdp', 'tp'), may hold values from 20.48 to 81.92
- headgate_weight: float32 [2048, 16], P('fsdp', 'tp'), may hold values from -0.125 to 0.125
- headgate_moment: float32 [2048, 16], P('fsdp', 'tp'), may hold values from -256 to 256
- headgate_square: float32 [2048, 16], P('fsdp', 'tp'), may hold values from 163.84 to 696.32
- output_weight: float32 [2048, 2048], P('tp', 'fsdp'), may hold values from -1.5 to 1.5
- output_moment: float32 [2048, 2048], P('tp', 'fsdp'), may hold values from -6 to 6
- output_square: float32 [2048, 2048], P('tp', 'fsdp'), may hold values from 0.08192 to 0.32768
- gateup_weight: float32 [2, 2048, 6144], P(None, 'fsdp', 'tp'), may hold values from -0.125 to 0.125
- gateup_moment: float32 [2, 2048, 6144], P(None, 'fsdp', 'tp'), may hold values from -20 to 20
- gateup_square: float32 [2, 2048, 6144], P(None, 'fsdp', 'tp'), may hold values from 0.8192 to 3.2768
- down_weight: float32 [6144, 2048], P('tp', 'fsdp'), may hold values from -0.078125 to 0.078125
- down_moment: float32 [6144, 2048], P('tp', 'fsdp'), may hold values from -32 to 32
- down_square: float32 [6144, 2048], P('tp', 'fsdp'), may hold values from 2.94912 to 11.4688
Outputs:
- block_output: bfloat16 [8192, 2048], P(('fsdp', 'tp'))
- tokens_grad: float32 [8192, 2048], P(('fsdp', 'tp'))
- branch_scales: float32 [3], replicated
- updated_norms: float32 [2, 2048], replicated
- momentum_norms: float32 [2, 2048], replicated
- variance_norms: float32 [2, 2048], replicated
- updated_heads: float32 [2, 128], replicated
- momentum_heads: float32 [2, 128], replicated
- variance_heads: float32 [2, 128], replicated
- updated_query: float32 [2048, 2048], P('fsdp', 'tp')
- momentum_query: float32 [2048, 2048], P('fsdp', 'tp')
- variance_query: float32 [2048, 2048], P('fsdp', 'tp')
- updated_keyvalue: float32 [2, 2048, 1024], P(None, 'fsdp', 'tp')
- momentum_keyvalue: float32 [2, 2048, 1024], P(None, 'fsdp', 'tp')
- variance_keyvalue: float32 [2, 2048, 1024], P(None, 'fsdp', 'tp')
- updated_headgate: float32 [2048, 16], P('fsdp', 'tp')
- momentum_headgate: float32 [2048, 16], P('fsdp', 'tp')
- variance_headgate: float32 [2048, 16], P('fsdp', 'tp')
- updated_output: float32 [2048, 2048], P('tp', 'fsdp')
- momentum_output: float32 [2048, 2048], P('tp', 'fsdp')
- variance_output: float32 [2048, 2048], P('tp', 'fsdp')
- updated_gateup: float32 [2, 2048, 6144], P(None, 'fsdp', 'tp')
- momentum_gateup: float32 [2, 2048, 6144], P(None, 'fsdp', 'tp')
- variance_gateup: float32 [2, 2048, 6144], P(None, 'fsdp', 'tp')
- updated_down: float32 [6144, 2048], P('tp', 'fsdp')
- momentum_down: float32 [6144, 2048], P('tp', 'fsdp')
- variance_down: float32 [6144, 2048], P('tp', 'fsdp')
The draws below stay inside these ranges and needn't reach their ends.
Inputs may be any that keep to these rules, and one draw needn't show every extreme that they name: The first valid_len[s] tokens of sequence s are valid, the rest are padding; some sequence has all 512 tokens valid. Sequence s holds one picture piece of 256 tokens from pic_start[s], with pic_start[s] + 256 <= valid_len[s].
All inputs are finite; a program needn't handle non-finite values.
Results may differ from the reference program's by a relative error of at most 0.012.
Values may be sent and summed in bfloat16 or wider, within the bound.
A program may use at most 384 MiB of HBM per device.

```python
import math
import jax
import jax.numpy as jnp
from jax import lax

MODEL_WIDTH = 2048
QUERY_HEADS = 16
KEYVALUE_HEADS = 8
HEAD_WIDTH = 128
FF = 6144
SEQUENCE_TOKENS = 512
PIC = 256
STEP = 10
TOTAL_TOKENS = 8192


def draw_tables(key):
    number = TOTAL_TOKENS // SEQUENCE_TOKENS
    ordinal = jnp.arange(number, dtype=jnp.int32)
    floor_len = SEQUENCE_TOKENS // 3 + (SEQUENCE_TOKENS - SEQUENCE_TOKENS // 3) * ordinal // number
    jitter = jax.random.randint(jax.random.fold_in(key, 11), (number,), 0, SEQUENCE_TOKENS // 8 + 2)
    lengths = jnp.clip(floor_len + jitter, PIC, SEQUENCE_TOKENS)
    longest = jax.random.randint(jax.random.fold_in(key, 12), (), 0, number)
    lengths = jnp.where(ordinal == longest, SEQUENCE_TOKENS, lengths).astype(jnp.int32)
    starts = jax.random.randint(jax.random.fold_in(key, 13), (number,), 0, lengths - PIC + 1)
    starts = jnp.where(ordinal == longest, SEQUENCE_TOKENS - PIC, starts)
    starts = jnp.where(ordinal == (longest + 1) % number, 0, starts)
    return (lengths, starts.astype(jnp.int32))


def draw_valid_len(key, part):
    tables = draw_tables(key)
    return tables[0]


def draw_pic_start(key, part):
    tables = draw_tables(key)
    return tables[1]


def shard_levels(stream_key, shape, split, low, largest):
    gain = 1.0
    for axis_at, blocks in split:
        heights = jax.random.uniform(jax.random.fold_in(jax.random.fold_in(stream_key, 6), axis_at), (blocks,), jnp.float32, low / len(split), largest / len(split))
        gain = gain * jnp.repeat(jnp.exp(heights), shape[axis_at] // blocks).reshape((-1,) + (1,) * (len(shape) - 1 - axis_at))
    return gain


def gaussian(rng, shape, spread, most, pieces=(), kind=jnp.bfloat16):
    array = spread * jax.random.normal(rng, shape, jnp.float32)
    if pieces:
        array = array * shard_levels(rng, shape, pieces, -0.22, 0.18)
    return jnp.clip(array, -most, most).astype(kind)


def setup_inputs(seed: int = 0) -> dict:
    splits = jax.random.split(jax.random.key(seed), 29)
    return {
        "tokens": gaussian(splits[0], (TOTAL_TOKENS, MODEL_WIDTH), 1.0, 6.0, ((0, 32),)),
        "cotangent": gaussian(splits[1], (TOTAL_TOKENS, MODEL_WIDTH), 1.0, 6.0, ((0, 32),)),
        "valid_len": draw_valid_len(jax.random.fold_in(splits[28], 71), 0),
        "pic_start": draw_pic_start(jax.random.fold_in(splits[28], 71), 0),
        "norm_gains": jnp.clip(1.0 + 0.1 * jax.random.normal(splits[4], (2, MODEL_WIDTH), jnp.float32), 0.5, 1.5),
        "norm_moment": gaussian(splits[5], (2, MODEL_WIDTH), (0.17 * TOTAL_TOKENS ** 0.5), 96.0, (), jnp.float32),
        "norm_square": jnp.clip(jnp.exp(jax.random.uniform(splits[6], (2, MODEL_WIDTH), jnp.float32, math.log(18.0224), math.log(73.728))), 18.0224, 73.728),
        "head_gains": jnp.clip(1.0 + 0.1 * jax.random.normal(splits[7], (2, HEAD_WIDTH), jnp.float32), 0.5, 1.5),
        "head_moment": gaussian(splits[8], (2, HEAD_WIDTH), (0.78 * TOTAL_TOKENS ** 0.5), 448.0, (), jnp.float32),
        "head_square": jnp.clip(jnp.exp(jax.random.uniform(splits[9], (2, HEAD_WIDTH), jnp.float32, math.log(409.6), math.log(1638.4))), 409.6, 1638.4),
        "query_weight": gaussian(splits[10], (MODEL_WIDTH, QUERY_HEADS * HEAD_WIDTH), MODEL_WIDTH ** -0.5, 0.125, ((0, 16), (1, 2)), jnp.float32),
        "query_moment": gaussian(splits[11], (MODEL_WIDTH, QUERY_HEADS * HEAD_WIDTH), (0.2 * TOTAL_TOKENS ** 0.5), 112.0, ((0, 16), (1, 2)), jnp.float32),
        "query_square": jnp.clip(jnp.exp(math.log(106.496) - 1.4663371 * jax.random.uniform(splits[12], (MODEL_WIDTH, QUERY_HEADS * HEAD_WIDTH), jnp.float32) ** shard_levels(splits[12], (MODEL_WIDTH, QUERY_HEADS * HEAD_WIDTH), ((0, 16), (1, 2)), -0.2, 0.2)), 24.576, 106.496),
        "keyvalue_matrix": gaussian(splits[13], (2, MODEL_WIDTH, KEYVALUE_HEADS * HEAD_WIDTH), MODEL_WIDTH ** -0.5, 0.125, ((1, 16), (2, 2)), jnp.float32),
        "keyvalue_first_moment": gaussian(splits[14], (2, MODEL_WIDTH, KEYVALUE_HEADS * HEAD_WIDTH), (0.18 * TOTAL_TOKENS ** 0.5), 96.0, ((1, 16), (2, 2)), jnp.float32),
        "keyvalue_second_moment": jnp.clip(jnp.exp(math.log(81.92) - 1.3862944 * jax.random.uniform(splits[15], (2, MODEL_WIDTH, KEYVALUE_HEADS * HEAD_WIDTH), jnp.float32) ** shard_levels(splits[15], (2, MODEL_WIDTH, KEYVALUE_HEADS * HEAD_WIDTH), ((1, 16), (2, 2)), -0.2, 0.2)), 20.48, 81.92),
        "headgate_weight": gaussian(splits[16], (MODEL_WIDTH, QUERY_HEADS), MODEL_WIDTH ** -0.5, 0.125, ((0, 16), (1, 2)), jnp.float32),
        "headgate_moment": gaussian(splits[17], (MODEL_WIDTH, QUERY_HEADS), (0.5 * TOTAL_TOKENS ** 0.5), 256.0, ((0, 16), (1, 2)), jnp.float32),
        "headgate_square": jnp.clip(jnp.exp(math.log(696.32) - 1.446919 * jax.random.uniform(splits[18], (MODEL_WIDTH, QUERY_HEADS), jnp.float32) ** shard_levels(splits[18], (MODEL_WIDTH, QUERY_HEADS), ((0, 16), (1, 2)), -0.2, 0.2)), 163.84, 696.32),
        "output_weight": gaussian(splits[19], (QUERY_HEADS * HEAD_WIDTH, MODEL_WIDTH), (max(QUERY_HEADS * HEAD_WIDTH // 128, 4)) ** -0.5, 1.5, ((0, 2), (1, 16)), jnp.float32),
        "output_moment": gaussian(splits[20], (QUERY_HEADS * HEAD_WIDTH, MODEL_WIDTH), (0.011 * TOTAL_TOKENS ** 0.5), 6.0, ((0, 2), (1, 16)), jnp.float32),
        "output_square": jnp.clip(jnp.exp(math.log(0.32768) - 1.3862944 * jax.random.uniform(splits[21], (QUERY_HEADS * HEAD_WIDTH, MODEL_WIDTH), jnp.float32) ** shard_levels(splits[21], (QUERY_HEADS * HEAD_WIDTH, MODEL_WIDTH), ((0, 2), (1, 16)), -0.2, 0.2)), 0.08192, 0.32768),
        "gateup_weight": gaussian(splits[22], (2, MODEL_WIDTH, FF), MODEL_WIDTH ** -0.5, 0.125, ((1, 16), (2, 2)), jnp.float32),
        "gateup_moment": gaussian(splits[23], (2, MODEL_WIDTH, FF), (0.037 * TOTAL_TOKENS ** 0.5), 20.0, ((1, 16), (2, 2)), jnp.float32),
        "gateup_square": jnp.clip(jnp.exp(math.log(3.2768) - 1.3862944 * jax.random.uniform(splits[24], (2, MODEL_WIDTH, FF), jnp.float32) ** shard_levels(splits[24], (2, MODEL_WIDTH, FF), ((1, 16), (2, 2)), -0.2, 0.2)), 0.8192, 3.2768),
        "down_weight": gaussian(splits[25], (FF, MODEL_WIDTH), FF ** -0.5, 0.078125, ((0, 2), (1, 16)), jnp.float32),
        "down_moment": gaussian(splits[26], (FF, MODEL_WIDTH), (0.067 * TOTAL_TOKENS ** 0.5), 32.0, ((0, 2), (1, 16)), jnp.float32),
        "down_square": jnp.clip(jnp.exp(math.log(11.4688) - 1.3581234 * jax.random.uniform(splits[27], (FF, MODEL_WIDTH), jnp.float32) ** shard_levels(splits[27], (FF, MODEL_WIDTH), ((0, 2), (1, 16)), -0.2, 0.2)), 2.94912, 11.4688),
    }


norm_epsilon = 1e-06
rope_base = 1000000.0
beta_first = 0.9
beta_second = 0.999
adam_epsilon = 1e-08
weight_decay = 0.1
masked_score = -1e+30
highest = lax.Precision.HIGHEST

@jax.custom_vjp
def low_precision(v):
    return lax.optimization_barrier(v.astype(jnp.bfloat16)).astype(jnp.float32)

@jax.custom_vjp
def low_precision_backward(v):
    return v

def low_keep(v):
    return (low_precision(v), None)

def low_pass(kept, grad):
    return (grad,)

def back_keep(v):
    return (v, None)

def back_low(kept, grad):
    return (low_precision(grad),)
low_precision.defvjp(low_keep, low_pass)
low_precision_backward.defvjp(back_keep, back_low)

def normalize(values, scaling):
    return values * lax.rsqrt(lax.optimization_barrier(jnp.mean(values * values, axis=-1, keepdims=True)) + norm_epsilon) * scaling

def rotary_tables(length_value, head_width):
    halves = head_width // 2
    frequency = rope_base ** (-(jnp.arange(halves, dtype=jnp.float32) * 2.0 / head_width))
    angles = jnp.arange(length_value, dtype=jnp.float32)[:, None] * frequency[None, :]
    return (jnp.cos(angles), jnp.sin(angles))

def rotate(values, cosine, sine_table):
    halves = values.shape[-1] // 2
    former = values[..., :halves]
    latter = values[..., halves:]
    cosine = cosine[:, None, :]
    sine_table = sine_table[:, None, :]
    return jnp.concatenate([former * cosine - latter * sine_table, latter * cosine + former * sine_table], axis=-1)

def visible(length_value, valid_count, piece_start, piece_size):
    places = jnp.arange(length_value, dtype=jnp.int32)
    inside = (places >= piece_start) & (places < piece_start + piece_size)
    causal = places[None, :] <= places[:, None]
    return (places[None, :] < valid_count) & (causal | inside[:, None] & inside[None, :])

def attend(query_rows, key_rows, value_rows, allowed):
    length_value = query_rows.shape[0]
    grouped_heads = query_rows.reshape(length_value, KEYVALUE_HEADS, QUERY_HEADS // KEYVALUE_HEADS, HEAD_WIDTH)
    scores = jnp.einsum('qhgd,khd->hgqk', grouped_heads, key_rows, precision=highest) * HEAD_WIDTH ** (-0.5)
    scores = jnp.where(allowed, low_precision_backward(scores), masked_score)
    highest_score = lax.optimization_barrier(jnp.max(scores, axis=-1, keepdims=True))
    expos = jnp.exp(scores - highest_score)
    probs_low = low_precision(expos / lax.optimization_barrier(jnp.sum(expos, axis=-1, keepdims=True)))
    mixed = jnp.einsum('hgqk,khd->qhgd', probs_low, value_rows, precision=highest)
    return mixed.reshape(length_value, QUERY_HEADS, HEAD_WIDTH)

def layer(block_rows, lengths, starts, gains, matrices):
    norm_gains, head_gains = gains
    query_weight, keyvalue_matrix, headgate_weight, output_weight, gateup_weight, down_weight = matrices
    row_count = block_rows.shape[0]
    sequence_count = row_count // SEQUENCE_TOKENS
    first_low = low_precision(normalize(block_rows, norm_gains[0]))
    query_rows = low_precision_backward(jnp.dot(first_low, query_weight, precision=highest)).reshape(sequence_count, SEQUENCE_TOKENS, QUERY_HEADS, HEAD_WIDTH)
    keyvalue_rows = jnp.einsum('td,sde->ste', first_low, keyvalue_matrix, precision=highest)
    key_rows = low_precision_backward(keyvalue_rows[0]).reshape(sequence_count, SEQUENCE_TOKENS, KEYVALUE_HEADS, HEAD_WIDTH)
    value_rows = low_precision_backward(low_precision(keyvalue_rows[1])).reshape(sequence_count, SEQUENCE_TOKENS, KEYVALUE_HEADS, HEAD_WIDTH)
    gate_logit = low_precision_backward(jnp.dot(first_low, headgate_weight, precision=highest))
    cosine, sine_table = rotary_tables(SEQUENCE_TOKENS, HEAD_WIDTH)
    query_rows = low_precision(rotate(normalize(query_rows, head_gains[0]), cosine, sine_table))
    key_rows = low_precision(rotate(normalize(key_rows, head_gains[1]), cosine, sine_table))

    def one_sequence(item):
        seq_queries, seq_keys, seq_values, seq_length, seq_start = item
        return attend(seq_queries, seq_keys, seq_values, visible(SEQUENCE_TOKENS, seq_length, seq_start, PIC))
    mixed = lax.map(jax.checkpoint(one_sequence), (query_rows, key_rows, value_rows, lengths, starts))
    mixed = low_precision_backward(mixed.reshape(row_count, QUERY_HEADS, HEAD_WIDTH))
    gate_value = jax.nn.sigmoid(gate_logit)
    gated = low_precision((mixed * gate_value[:, :, None]).reshape(row_count, QUERY_HEADS * HEAD_WIDTH))
    attention_out = low_precision_backward(jnp.dot(gated, output_weight, precision=highest))
    middle = block_rows + attention_out
    second_low = low_precision(normalize(middle, norm_gains[1]))
    gateup = jnp.einsum('td,sdf->stf', second_low, gateup_weight, precision=highest)
    hidden = low_precision(jax.nn.silu(low_precision_backward(gateup[0])) * low_precision_backward(gateup[1]))
    feedforward_out = low_precision_backward(jnp.dot(hidden, down_weight, precision=highest))
    places = jnp.arange(SEQUENCE_TOKENS, dtype=jnp.int32)
    counted = (places[None, :] < lengths[:, None]).astype(jnp.float32).reshape(row_count, 1)
    branch_sums = jnp.stack([jnp.sum(counted * attention_out * attention_out), jnp.sum(counted * feedforward_out * feedforward_out)])
    return (middle + feedforward_out, branch_sums)

def forward(inputs, gains, matrices, valid_len, pic_start):
    matrices = tuple((low_precision(matrix) for matrix in matrices))
    number = valid_len.shape[0]
    per_group = math.gcd(number, max(1, 4096 // SEQUENCE_TOKENS))
    group_count = number // per_group
    blocks = inputs.reshape(group_count, per_group * SEQUENCE_TOKENS, MODEL_WIDTH)

    def one_group(carry, item):
        block_rows, lengths, starts = item
        result, branch_sums = jax.checkpoint(layer)(block_rows, lengths, starts, gains, matrices)
        return (carry + branch_sums, result)
    sums_total, results = lax.scan(one_group, jnp.zeros((2,), jnp.float32), (blocks, valid_len.reshape(group_count, per_group), pic_start.reshape(group_count, per_group)))
    return (results.reshape(number * SEQUENCE_TOKENS, MODEL_WIDTH), sums_total)

def adam_update(weight, moment, square, gradient, step_rate, decay_rate):
    moment_new = beta_first * moment + (1.0 - beta_first) * gradient
    square_new = beta_second * square + (1.0 - beta_second) * gradient * gradient
    bias_first = 1.0 - beta_first ** STEP
    bias_second = 1.0 - beta_second ** STEP
    update = moment_new / bias_first / (jnp.sqrt(square_new / bias_second) + adam_epsilon)
    return (weight - step_rate * (update + decay_rate * weight), moment_new, square_new)

def reference(tokens, cotangent, valid_len, pic_start, norm_gains, norm_moment, norm_square, head_gains, head_moment, head_square, query_weight, query_moment, query_square, keyvalue_matrix, keyvalue_first_moment, keyvalue_second_moment, headgate_weight, headgate_moment, headgate_square, output_weight, output_moment, output_square, gateup_weight, gateup_moment, gateup_square, down_weight, down_moment, down_square):
    inputs = tokens.astype(jnp.float32)
    gains = (norm_gains, head_gains)
    matrices = (query_weight, keyvalue_matrix, headgate_weight, output_weight, gateup_weight, down_weight)

    def forward_only(input_rows, gain_arrays, matrix_arrays):
        return forward(input_rows, gain_arrays, matrix_arrays, valid_len, pic_start)
    (result, branch_sums), pullback = jax.vjp(forward_only, inputs, gains, matrices)
    tokens_grad, gain_grads, matrix_grads = pullback((cotangent.astype(jnp.float32), jnp.zeros((2,), jnp.float32)))
    places = jnp.arange(SEQUENCE_TOKENS, dtype=jnp.int32)
    counted = (places[None, :] < valid_len[:, None]).astype(jnp.float32).reshape(-1, 1)
    input_sum = jnp.sum(counted * inputs * inputs)
    denominator = jnp.sum(valid_len).astype(jnp.float32) * MODEL_WIDTH
    branch_scales = jnp.sqrt(jnp.stack([input_sum, branch_sums[0], branch_sums[1]]) / denominator)
    input_rate = MODEL_WIDTH ** (-0.5)
    down_rate = FF ** (-0.5)
    output_rate = max(QUERY_HEADS * HEAD_WIDTH // 128, 4) ** (-0.5)
    gain_rate = 0.5
    norms_new = adam_update(norm_gains, norm_moment, norm_square, gain_grads[0], gain_rate, 0.0)
    heads_new = adam_update(head_gains, head_moment, head_square, gain_grads[1], gain_rate, 0.0)
    query_new = adam_update(query_weight, query_moment, query_square, matrix_grads[0], input_rate, weight_decay)
    keyvalue_new = adam_update(keyvalue_matrix, keyvalue_first_moment, keyvalue_second_moment, matrix_grads[1], input_rate, weight_decay)
    headgate_new = adam_update(headgate_weight, headgate_moment, headgate_square, matrix_grads[2], input_rate, weight_decay)
    output_new = adam_update(output_weight, output_moment, output_square, matrix_grads[3], output_rate, weight_decay)
    gateup_new = adam_update(gateup_weight, gateup_moment, gateup_square, matrix_grads[4], input_rate, weight_decay)
    down_new = adam_update(down_weight, down_moment, down_square, matrix_grads[5], down_rate, weight_decay)
    return (result.astype(jnp.bfloat16), tokens_grad, branch_scales, norms_new[0], norms_new[1], norms_new[2], heads_new[0], heads_new[1], heads_new[2], query_new[0], query_new[1], query_new[2], keyvalue_new[0], keyvalue_new[1], keyvalue_new[2], headgate_new[0], headgate_new[1], headgate_new[2], output_new[0], output_new[1], output_new[2], gateup_new[0], gateup_new[1], gateup_new[2], down_new[0], down_new[1], down_new[2])
```

```python
import jax
import jax.numpy as jnp
from jax import lax
from jax.sharding import Mesh
from jax.sharding import PartitionSpec as P

MODEL_WIDTH = 2048
QUERY_HEADS = 16
HEAD_WIDTH = 128
FF = 6144
PIC = 256
STEP = 10

norm_epsilon = 1e-06
rope_base = 1000000.0
beta_first = 0.9
beta_second = 0.999
adam_epsilon = 1e-08
weight_decay = 0.1
masked_score = -1e30
low = jnp.bfloat16
wide = jnp.float32


def normalize(values, scaling):
    return (
        values
        * lax.rsqrt(jnp.mean(values * values, axis=-1, keepdims=True) + norm_epsilon)
        * scaling
    )


def norm_back(values, scaling, upstream):
    factor = lax.rsqrt(jnp.mean(values * values, axis=-1, keepdims=True) + norm_epsilon)
    weighted = upstream * scaling
    projected = jnp.mean(weighted * values, axis=-1, keepdims=True)
    result = factor * weighted - values * (factor * factor * factor) * projected
    return (result, jnp.sum(upstream * values * factor, axis=tuple(range(values.ndim - 1))))


def rotary_tables(length_value, head_width):
    halves = head_width // 2
    frequency = rope_base ** (-(jnp.arange(halves, dtype=wide) * 2.0 / head_width))
    angles = jnp.arange(length_value, dtype=wide)[:, None] * frequency[None, :]
    return (jnp.cos(angles), jnp.sin(angles))


def rotate(values, cosine, sine_table):
    halves = values.shape[-1] // 2
    former = values[..., :halves]
    latter = values[..., halves:]
    cosine = cosine[:, None, :]
    sine_table = sine_table[:, None, :]
    return jnp.concatenate(
        [former * cosine - latter * sine_table, latter * cosine + former * sine_table], axis=-1
    )


def visible(length_value, valid_count, piece_start, piece_size):
    places = jnp.arange(length_value, dtype=jnp.int32)
    inside = (places >= piece_start) & (places < piece_start + piece_size)
    causal = places[None, :] <= places[:, None]
    return (places[None, :] < valid_count) & (causal | inside[:, None] & inside[None, :])


def adam_update(weight, moment, square, gradient, step_rate, decay_rate):
    moment_new = beta_first * moment + (1.0 - beta_first) * gradient
    square_new = beta_second * square + (1.0 - beta_second) * gradient * gradient
    bias_first = 1.0 - beta_first**STEP
    bias_second = 1.0 - beta_second**STEP
    update = moment_new / bias_first / (jnp.sqrt(square_new / bias_second) + adam_epsilon)
    return (weight - step_rate * (update + decay_rate * weight), moment_new, square_new)


def dot(left, right, left_dim, right_dim):
    return lax.dot_general(
        left, right, (((left_dim,), (right_dim,)), ((), ())), preferred_element_type=wide
    )


SWAP = [(0, 1), (1, 0)]


def swap(values, axis):
    return lax.ppermute(values, axis, SWAP)


def joined(mine, other, axis):
    index = lax.axis_index(axis)
    return jnp.concatenate(
        [jnp.where(index == 0, mine, other), jnp.where(index == 0, other, mine)], axis=0
    )


def halves_of(values, axis, dim):
    index = lax.axis_index(axis)
    size = values.shape[dim] // 2
    mine = lax.dynamic_slice_in_dim(values, index * size, size, dim)
    other = lax.dynamic_slice_in_dim(values, (1 - index) * size, size, dim)
    return mine, other


def spread_rows(values):
    pair = joined(values, swap(values, "t"), "t")
    return joined(pair, swap(pair, "c"), "c")


def collect_rows(values):
    mine, other = halves_of(values, "c", 0)
    pair = mine + swap(other.astype(low), "c").astype(wide)
    mine, other = halves_of(pair, "t", 0)
    return mine + swap(other.astype(low), "t").astype(wide)


def fetch(parts):
    mine, other = [], []
    for part in parts:
        keep, give = halves_of(part.astype(low), "c", 1)
        mine.append(keep)
        other.append(give)
    mine = jnp.concatenate(mine, axis=1)
    other = jnp.concatenate(other, axis=1)
    return lax.all_gather(joined(mine, swap(other, "c"), "c"), "w", axis=0, tiled=True)


def deliver(full):
    owned = lax.psum_scatter(full, "w", scatter_dimension=0, tiled=True)
    mine, other = halves_of(owned, "c", 0)
    return mine, swap(other, "c")


def delivered(pair, start, size):
    index = lax.axis_index("c")
    mine = pair[0][:, start : start + size].astype(wide)
    other = pair[1][:, start : start + size].astype(wide)
    return jnp.concatenate(
        [jnp.where(index == 0, mine, other), jnp.where(index == 0, other, mine)], axis=1
    )


def local(
    tokens,
    cotangent,
    valid_len,
    pic_start,
    norm_gains,
    norm_moment,
    norm_square,
    head_gains,
    head_moment,
    head_square,
    query_weight,
    query_moment,
    query_square,
    keyvalue_matrix,
    keyvalue_first_moment,
    keyvalue_second_moment,
    headgate_weight,
    headgate_moment,
    headgate_square,
    output_weight,
    output_moment,
    output_square,
    gateup_weight,
    gateup_moment,
    gateup_square,
    down_weight,
    down_moment,
    down_square,
):
    local_rows = tokens.shape[0]
    length_value = local_rows * 2
    rows = length_value * 2
    group = lax.axis_index("w")
    core = lax.axis_index("c")
    place = lax.axis_index("t")
    heads_here = query_weight.shape[1] // HEAD_WIDTH // 2
    groups_here = keyvalue_matrix.shape[2] // HEAD_WIDTH // 2
    share = heads_here // groups_here
    score_scale = HEAD_WIDTH ** (-0.5)
    head_cols = heads_here * HEAD_WIDTH
    group_cols = groups_here * HEAD_WIDTH
    hidden_here = gateup_weight.shape[2] // 2

    attention_full = fetch(
        [query_weight, keyvalue_matrix[0], keyvalue_matrix[1], output_weight.T, headgate_weight]
    )
    feedforward_full = fetch([gateup_weight[0], gateup_weight[1], down_weight.T])
    bounds = [0, head_cols, group_cols, group_cols, head_cols, heads_here]
    edges = [sum(bounds[: i + 1]) for i in range(6)]
    query_full, key_full, value_full, output_full, headgate_full = (
        attention_full[:, edges[i] : edges[i + 1]] for i in range(5)
    )
    gate_full, up_full, down_full = (
        feedforward_full[:, i * hidden_here : (i + 1) * hidden_here] for i in range(3)
    )

    residual = tokens.astype(wide)
    first_full = spread_rows(normalize(residual, norm_gains[0]).astype(low))
    output_grad_full = spread_rows(cotangent)

    query_pre = dot(first_full, query_full, 1, 0).reshape(2, length_value, heads_here, HEAD_WIDTH)
    key_pre = dot(first_full, key_full, 1, 0).reshape(2, length_value, groups_here, HEAD_WIDTH)
    value_low = (
        dot(first_full, value_full, 1, 0)
        .astype(low)
        .reshape(2, length_value, groups_here, HEAD_WIDTH)
    )
    gate_logit = dot(first_full, headgate_full, 1, 0).reshape(2, length_value, heads_here)
    cosine, sine_table = rotary_tables(length_value, HEAD_WIDTH)
    query_low = rotate(normalize(query_pre, head_gains[0]), cosine, sine_table).astype(low)
    key_low = rotate(normalize(key_pre, head_gains[1]), cosine, sine_table).astype(low)
    valid_pair = lax.dynamic_slice_in_dim(valid_len, 2 * group, 2)
    start_pair = lax.dynamic_slice_in_dim(pic_start, 2 * group, 2)
    allowed = jax.vmap(lambda a, b: visible(length_value, a, b, PIC))(valid_pair, start_pair)
    allowed = allowed[:, None, None]
    grouped = query_low.reshape(2, length_value, groups_here, share, HEAD_WIDTH)

    def score_block():
        raw = (
            jnp.einsum("sqhgd,skhd->shgqk", grouped, key_low, preferred_element_type=wide)
            * score_scale
        )
        return jnp.where(allowed, raw, masked_score)

    scores = score_block()
    highest_score = jnp.max(scores, axis=-1, keepdims=True)
    expos = jnp.exp(scores - highest_score)
    row_total = jnp.sum(expos, axis=-1, keepdims=True)
    log_total = highest_score + jnp.log(row_total)
    probs_low = (expos / row_total).astype(low)
    mixed = jnp.einsum(
        "shgqk,skhd->sqhgd", probs_low, value_low, preferred_element_type=wide
    ).reshape(2, length_value, heads_here, HEAD_WIDTH)
    gate_value = jax.nn.sigmoid(gate_logit)
    gated_low = (mixed * gate_value[..., None]).reshape(rows, head_cols).astype(low)
    attention_local = collect_rows(dot(gated_low, output_full, 1, 1))
    middle = residual + attention_local
    second_full = spread_rows(normalize(middle, norm_gains[1]).astype(low))

    gate_part = dot(second_full, gate_full, 1, 0)
    up_part = dot(second_full, up_full, 1, 0)
    sigmoid_gate = jax.nn.sigmoid(gate_part)
    silu_gate = gate_part * sigmoid_gate
    hidden_low = (silu_gate * up_part).astype(low)
    hidden_grad = dot(output_grad_full, down_full, 1, 0)
    gate_grad = (
        hidden_grad * up_part * sigmoid_gate * (1.0 + gate_part * (1.0 - sigmoid_gate))
    ).astype(low)
    up_grad = (hidden_grad * silu_gate).astype(low)
    second_partial = dot(gate_grad, gate_full, 1, 1) + dot(up_grad, up_full, 1, 1)
    feedforward_partial = dot(hidden_low, down_full, 1, 1)
    feedforward_wgrad = jnp.concatenate(
        [
            dot(second_full, gate_grad, 0, 0).astype(low),
            dot(second_full, up_grad, 0, 0).astype(low),
            dot(output_grad_full, hidden_low, 0, 0).astype(low),
        ],
        axis=1,
    )
    feedforward_sum = deliver(feedforward_wgrad)

    second_grad = collect_rows(second_partial)
    middle_grad, second_gain_grad = norm_back(middle, norm_gains[1], second_grad)
    middle_grad = middle_grad + cotangent.astype(wide)
    attention_grad = spread_rows(middle_grad.astype(low))
    feedforward_local = collect_rows(feedforward_partial)
    block_output = (middle + feedforward_local).astype(low)
    own_places = place * local_rows + jnp.arange(local_rows, dtype=jnp.int32)
    counted = (own_places < valid_pair[core]).astype(wide)[:, None]
    squares = jnp.stack(
        [
            jnp.sum(counted * residual * residual),
            jnp.sum(counted * attention_local * attention_local),
            jnp.sum(counted * feedforward_local * feedforward_local),
        ]
    )

    output_wgrad = dot(attention_grad, gated_low, 0, 0).astype(low)
    gated_grad = dot(attention_grad, output_full, 1, 0).reshape(
        2, length_value, heads_here, HEAD_WIDTH
    )
    mixed_grad = (
        (gated_grad * gate_value[..., None])
        .astype(low)
        .reshape(2, length_value, groups_here, share, HEAD_WIDTH)
    )
    logit_grad = (
        (jnp.sum(gated_grad * mixed, axis=-1) * gate_value * (1.0 - gate_value))
        .astype(low)
        .reshape(rows, heads_here)
    )
    probs_again = jnp.exp(score_block() - log_total)
    value_grad = jnp.einsum(
        "shgqk,sqhgd->skhd", probs_again.astype(low), mixed_grad, preferred_element_type=wide
    ).astype(low)
    prob_grad = jnp.einsum("sqhgd,skhd->shgqk", mixed_grad, value_low, preferred_element_type=wide)
    score_grad = (
        probs_again * (prob_grad - jnp.sum(prob_grad * probs_again, axis=-1, keepdims=True))
    ).astype(low)
    query_rot_grad = (
        jnp.einsum("shgqk,skhd->sqhgd", score_grad, key_low, preferred_element_type=wide).reshape(
            2, length_value, heads_here, HEAD_WIDTH
        )
        * score_scale
    )
    key_rot_grad = (
        jnp.einsum("shgqk,sqhgd->skhd", score_grad, grouped, preferred_element_type=wide)
        * score_scale
    )
    query_pre_grad, query_gain_grad = norm_back(
        query_pre, head_gains[0], rotate(query_rot_grad, cosine, -sine_table)
    )
    key_pre_grad, key_gain_grad = norm_back(
        key_pre, head_gains[1], rotate(key_rot_grad, cosine, -sine_table)
    )
    projection_grad = jnp.concatenate(
        [
            query_pre_grad.reshape(rows, head_cols).astype(low),
            key_pre_grad.reshape(rows, group_cols).astype(low),
            value_grad.reshape(rows, group_cols),
        ],
        axis=1,
    )
    first_partial = dot(projection_grad, attention_full[:, : edges[3]], 1, 1) + dot(
        logit_grad, headgate_full, 1, 1
    )
    attention_wgrad = jnp.concatenate(
        [
            dot(first_full, projection_grad, 0, 0).astype(low),
            output_wgrad,
            dot(first_full, logit_grad, 0, 0).astype(low),
        ],
        axis=1,
    )
    attention_sum = deliver(attention_wgrad)
    first_grad = collect_rows(first_partial)
    tokens_partial, first_gain_grad = norm_back(residual, norm_gains[0], first_grad)
    tokens_grad = tokens_partial + middle_grad
    norms_total, heads_total, squares_total = lax.psum(
        (
            jnp.stack([first_gain_grad, second_gain_grad]),
            jnp.stack([query_gain_grad, key_gain_grad]),
            squares,
        ),
        ("w", "c", "t"),
    )
    denominator = jnp.sum(valid_len).astype(wide) * MODEL_WIDTH
    branch_scales = jnp.sqrt(squares_total / denominator)
    input_rate = MODEL_WIDTH ** (-0.5)
    down_rate = FF ** (-0.5)
    output_rate = max(QUERY_HEADS * HEAD_WIDTH // 128, 4) ** (-0.5)
    gain_rate = 0.5
    norms_new = adam_update(norm_gains, norm_moment, norm_square, norms_total, gain_rate, 0.0)
    heads_new = adam_update(head_gains, head_moment, head_square, heads_total, gain_rate, 0.0)
    gateup_sum = jnp.stack(
        [delivered(feedforward_sum, i * hidden_here, hidden_here) for i in range(2)]
    )
    down_sum = delivered(feedforward_sum, 2 * hidden_here, hidden_here).T
    query_sum, key_sum, value_sum, output_sum, headgate_sum = (
        delivered(attention_sum, edges[i], edges[i + 1] - edges[i]) for i in range(5)
    )
    query_new = adam_update(
        query_weight, query_moment, query_square, query_sum, input_rate, weight_decay
    )
    keyvalue_new = adam_update(
        keyvalue_matrix,
        keyvalue_first_moment,
        keyvalue_second_moment,
        jnp.stack([key_sum, value_sum]),
        input_rate,
        weight_decay,
    )
    headgate_new = adam_update(
        headgate_weight, headgate_moment, headgate_square, headgate_sum, input_rate, weight_decay
    )
    output_new = adam_update(
        output_weight, output_moment, output_square, output_sum.T, output_rate, weight_decay
    )
    gateup_new = adam_update(
        gateup_weight, gateup_moment, gateup_square, gateup_sum, input_rate, weight_decay
    )
    down_new = adam_update(down_weight, down_moment, down_square, down_sum, down_rate, weight_decay)
    return (
        block_output,
        tokens_grad,
        branch_scales,
        *norms_new,
        *heads_new,
        *query_new,
        *keyvalue_new,
        *headgate_new,
        *output_new,
        *gateup_new,
        *down_new,
    )


def solution(mesh):
    fsdp, tp = mesh.devices.shape
    fine = Mesh(mesh.devices.reshape(fsdp // 2, 2, tp), ("w", "c", "t"))
    whole = ("w", "c")
    rows = P(("w", "c", "t"), None)
    first = P(whole, "t")
    second = P(None, whole, "t")
    last = P("t", whole)
    matrices = (first,) * 3 + (second,) * 3 + (first,) * 3 + (last,) * 3 + (second,) * 3 + (last,) * 3
    return jax.shard_map(
        local,
        mesh=fine,
        in_specs=(rows, rows, P(), P()) + (P(),) * 6 + matrices,
        out_specs=(rows, rows, P()) + (P(),) * 6 + matrices,
        check_vma=False,
    )
```

```python
import jax
import jax.numpy as jnp
from jax import lax
from jax.sharding import Mesh
from jax.sharding import PartitionSpec as P

MODEL_WIDTH = 2048
QUERY_HEADS = 16
HEAD_WIDTH = 128
FF = 6144
PIC = 256
STEP = 10

norm_epsilon = 1e-06
rope_base = 1000000.0
beta_first = 0.9
beta_second = 0.999
adam_epsilon = 1e-08
weight_decay = 0.1
masked_score = -1e30
low = jnp.bfloat16
wide = jnp.float32


def normalize(values, scaling):
    return (
        values
        * lax.rsqrt(jnp.mean(values * values, axis=-1, keepdims=True) + norm_epsilon)
        * scaling
    )


def norm_back(values, scaling, upstream):
    factor = lax.rsqrt(jnp.mean(values * values, axis=-1, keepdims=True) + norm_epsilon)
    weighted = upstream * scaling
    projected = jnp.mean(weighted * values, axis=-1, keepdims=True)
    result = factor * weighted - values * (factor * factor * factor) * projected
    return (result, jnp.sum(upstream * values * factor, axis=tuple(range(values.ndim - 1))))


def rotary_tables(length_value, head_width):
    halves = head_width // 2
    frequency = rope_base ** (-(jnp.arange(halves, dtype=wide) * 2.0 / head_width))
    angles = jnp.arange(length_value, dtype=wide)[:, None] * frequency[None, :]
    return (jnp.cos(angles), jnp.sin(angles))


def rotate(values, cosine, sine_table):
    halves = values.shape[-1] // 2
    former = values[..., :halves]
    latter = values[..., halves:]
    cosine = cosine[:, None, :]
    sine_table = sine_table[:, None, :]
    return jnp.concatenate(
        [former * cosine - latter * sine_table, latter * cosine + former * sine_table], axis=-1
    )


def visible(length_value, valid_count, piece_start, piece_size):
    places = jnp.arange(length_value, dtype=jnp.int32)
    inside = (places >= piece_start) & (places < piece_start + piece_size)
    causal = places[None, :] <= places[:, None]
    return (places[None, :] < valid_count) & (causal | inside[:, None] & inside[None, :])


def adam_update(weight, moment, square, gradient, step_rate, decay_rate):
    moment_new = beta_first * moment + (1.0 - beta_first) * gradient
    square_new = beta_second * square + (1.0 - beta_second) * gradient * gradient
    bias_first = 1.0 - beta_first**STEP
    bias_second = 1.0 - beta_second**STEP
    update = moment_new / bias_first / (jnp.sqrt(square_new / bias_second) + adam_epsilon)
    return (weight - step_rate * (update + decay_rate * weight), moment_new, square_new)


def dot(left, right, left_dim, right_dim):
    return lax.dot_general(
        left, right, (((left_dim,), (right_dim,)), ((), ())), preferred_element_type=wide
    )


SWAP = [(0, 1), (1, 0)]


def swap(values, axis):
    return lax.ppermute(values, axis, SWAP)


def joined(mine, other, axis):
    index = lax.axis_index(axis)
    return jnp.concatenate(
        [jnp.where(index == 0, mine, other), jnp.where(index == 0, other, mine)], axis=0
    )


def halves_of(values, axis, dim):
    index = lax.axis_index(axis)
    size = values.shape[dim] // 2
    mine = lax.dynamic_slice_in_dim(values, index * size, size, dim)
    other = lax.dynamic_slice_in_dim(values, (1 - index) * size, size, dim)
    return mine, other


def spread_rows(values):
    pair = joined(values, swap(values, "t"), "t")
    return joined(pair, swap(pair, "c"), "c")


def collect_rows(values):
    mine, other = halves_of(values, "c", 0)
    pair = mine + swap(other.astype(low), "c").astype(wide)
    mine, other = halves_of(pair, "t", 0)
    return mine + swap(other.astype(low), "t").astype(wide)


def fetch(parts):
    pieces = []
    for core in range(2):
        for part in parts:
            size = part.shape[1] // 2
            pieces.append(part[:, core * size : (core + 1) * size].astype(low))
    count = len(parts)
    local_block = jnp.stack(
        [jnp.concatenate(pieces[core * count : (core + 1) * count], axis=1) for core in range(2)]
    )
    both = lax.all_gather(local_block, ("w", "c"), axis=1, tiled=True)
    return lax.dynamic_index_in_dim(both, lax.axis_index("c"), 0, keepdims=False)


def ring_order(count):
    width = 2 if count <= 8 else 4
    rows = count // width
    if rows < 2 or rows % 2:
        return list(range(count))
    order = [0]
    for row in range(rows):
        columns = list(range(1, width))
        if row % 2:
            columns.reverse()
        order += [row * width + column for column in columns]
    return order + [row * width for row in range(rows - 1, 0, -1)]


def ring_sum(own, direction):
    count = lax.axis_size("w")
    order = ring_order(count)
    position = [0] * count
    for spot, index in enumerate(order):
        position[index] = spot
    order_table = jnp.array(order, jnp.int32)
    here = jnp.array(position, jnp.int32)[lax.axis_index("w")]
    links = [(order[spot], order[(spot + direction) % count]) for spot in range(count)]
    running = own(order_table[(here - direction) % count]).astype(low)
    for step in range(count - 1):
        arrived = lax.ppermute(running, "w", links)
        owner = order_table[(here - direction * (2 + step)) % count]
        total = arrived.astype(wide) + own(owner)
        running = total.astype(low)
    return total


def deliver(total):
    mine, other = halves_of(total, "c", 0)
    other = swap(other.astype(low), "c").astype(wide)
    core = lax.axis_index("c")
    return jnp.concatenate(
        [jnp.where(core == 0, mine, other), jnp.where(core == 0, other, mine)], axis=1
    )


def local(
    tokens,
    cotangent,
    valid_len,
    pic_start,
    norm_gains,
    norm_moment,
    norm_square,
    head_gains,
    head_moment,
    head_square,
    query_weight,
    query_moment,
    query_square,
    keyvalue_matrix,
    keyvalue_first_moment,
    keyvalue_second_moment,
    headgate_weight,
    headgate_moment,
    headgate_square,
    output_weight,
    output_moment,
    output_square,
    gateup_weight,
    gateup_moment,
    gateup_square,
    down_weight,
    down_moment,
    down_square,
):
    local_rows = tokens.shape[0]
    length_value = local_rows * 2
    rows = length_value * 2
    group = lax.axis_index("w")
    core = lax.axis_index("c")
    place = lax.axis_index("t")
    heads_here = query_weight.shape[1] // HEAD_WIDTH // 2
    groups_here = keyvalue_matrix.shape[2] // HEAD_WIDTH // 2
    share = heads_here // groups_here
    score_scale = HEAD_WIDTH ** (-0.5)
    head_cols = heads_here * HEAD_WIDTH
    group_cols = groups_here * HEAD_WIDTH
    hidden_here = gateup_weight.shape[2] // 2

    attention_full = fetch(
        [query_weight, keyvalue_matrix[0], keyvalue_matrix[1], output_weight.T, headgate_weight]
    )
    feedforward_full = fetch([gateup_weight[0], gateup_weight[1], down_weight.T])
    bounds = [0, head_cols, group_cols, group_cols, head_cols, heads_here]
    edges = [sum(bounds[: i + 1]) for i in range(6)]
    query_full, key_full, value_full, output_full, headgate_full = (
        attention_full[:, edges[i] : edges[i + 1]] for i in range(5)
    )
    gate_full, up_full, down_full = (
        feedforward_full[:, i * hidden_here : (i + 1) * hidden_here] for i in range(3)
    )

    residual = tokens.astype(wide)
    first_full = spread_rows(normalize(residual, norm_gains[0]).astype(low))
    output_grad_full = spread_rows(cotangent)

    query_pre = dot(first_full, query_full, 1, 0).reshape(2, length_value, heads_here, HEAD_WIDTH)
    key_pre = dot(first_full, key_full, 1, 0).reshape(2, length_value, groups_here, HEAD_WIDTH)
    value_low = (
        dot(first_full, value_full, 1, 0)
        .astype(low)
        .reshape(2, length_value, groups_here, HEAD_WIDTH)
    )
    gate_logit = dot(first_full, headgate_full, 1, 0).reshape(2, length_value, heads_here)
    cosine, sine_table = rotary_tables(length_value, HEAD_WIDTH)
    query_low = rotate(normalize(query_pre, head_gains[0]), cosine, sine_table).astype(low)
    key_low = rotate(normalize(key_pre, head_gains[1]), cosine, sine_table).astype(low)
    valid_pair = lax.dynamic_slice_in_dim(valid_len, 2 * group, 2)
    start_pair = lax.dynamic_slice_in_dim(pic_start, 2 * group, 2)
    allowed = jax.vmap(lambda a, b: visible(length_value, a, b, PIC))(valid_pair, start_pair)
    allowed = allowed[:, None, None]
    grouped = query_low.reshape(2, length_value, groups_here, share, HEAD_WIDTH)

    def score_block():
        raw = (
            jnp.einsum("sqhgd,skhd->shgqk", grouped, key_low, preferred_element_type=wide)
            * score_scale
        )
        return jnp.where(allowed, raw, masked_score)

    scores = score_block()
    highest_score = jnp.max(scores, axis=-1, keepdims=True)
    expos = jnp.exp(scores - highest_score)
    row_total = jnp.sum(expos, axis=-1, keepdims=True)
    log_total = highest_score + jnp.log(row_total)
    probs_low = (expos / row_total).astype(low)
    mixed = jnp.einsum(
        "shgqk,skhd->sqhgd", probs_low, value_low, preferred_element_type=wide
    ).reshape(2, length_value, heads_here, HEAD_WIDTH)
    gate_value = jax.nn.sigmoid(gate_logit)
    gated_low = (mixed * gate_value[..., None]).reshape(rows, head_cols).astype(low)
    attention_local = collect_rows(dot(gated_low, output_full, 1, 1))
    middle = residual + attention_local
    second_full = spread_rows(normalize(middle, norm_gains[1]).astype(low))

    gate_part = dot(second_full, gate_full, 1, 0)
    up_part = dot(second_full, up_full, 1, 0)
    sigmoid_gate = jax.nn.sigmoid(gate_part)
    silu_gate = gate_part * sigmoid_gate
    hidden_low = (silu_gate * up_part).astype(low)
    hidden_grad = dot(output_grad_full, down_full, 1, 0)
    gate_grad = (
        hidden_grad * up_part * sigmoid_gate * (1.0 + gate_part * (1.0 - sigmoid_gate))
    ).astype(low)
    up_grad = (hidden_grad * silu_gate).astype(low)
    second_partial = dot(gate_grad, gate_full, 1, 1) + dot(up_grad, up_full, 1, 1)
    feedforward_partial = dot(hidden_low, down_full, 1, 1)
    block = MODEL_WIDTH // lax.axis_size("w")

    def product(left, right):
        def own(owner):
            return dot(lax.dynamic_slice_in_dim(left, owner * block, block, 1), right, 0, 0)

        return own

    half_hidden = hidden_here // 2
    gate_sum = ring_sum(product(second_full, gate_grad), 1)
    up_first = ring_sum(product(second_full, up_grad[:, :half_hidden]), 1)
    down_sum = ring_sum(product(output_grad_full, hidden_low), -1)
    up_last = ring_sum(product(second_full, up_grad[:, half_hidden:]), -1)

    second_grad = collect_rows(second_partial)
    middle_grad, second_gain_grad = norm_back(middle, norm_gains[1], second_grad)
    middle_grad = middle_grad + cotangent.astype(wide)
    attention_grad = spread_rows(middle_grad.astype(low))
    feedforward_local = collect_rows(feedforward_partial)
    block_output = (middle + feedforward_local).astype(low)
    own_places = place * local_rows + jnp.arange(local_rows, dtype=jnp.int32)
    counted = (own_places < valid_pair[core]).astype(wide)[:, None]
    squares = jnp.stack(
        [
            jnp.sum(counted * residual * residual),
            jnp.sum(counted * attention_local * attention_local),
            jnp.sum(counted * feedforward_local * feedforward_local),
        ]
    )

    output_sum = ring_sum(product(attention_grad, gated_low), -1)
    gated_grad = dot(attention_grad, output_full, 1, 0).reshape(
        2, length_value, heads_here, HEAD_WIDTH
    )
    mixed_grad = (
        (gated_grad * gate_value[..., None])
        .astype(low)
        .reshape(2, length_value, groups_here, share, HEAD_WIDTH)
    )
    logit_grad = (
        (jnp.sum(gated_grad * mixed, axis=-1) * gate_value * (1.0 - gate_value))
        .astype(low)
        .reshape(rows, heads_here)
    )
    probs_again = jnp.exp(score_block() - log_total)
    value_grad = jnp.einsum(
        "shgqk,sqhgd->skhd", probs_again.astype(low), mixed_grad, preferred_element_type=wide
    ).astype(low)
    prob_grad = jnp.einsum("sqhgd,skhd->shgqk", mixed_grad, value_low, preferred_element_type=wide)
    score_grad = (
        probs_again * (prob_grad - jnp.sum(prob_grad * probs_again, axis=-1, keepdims=True))
    ).astype(low)
    query_rot_grad = (
        jnp.einsum("shgqk,skhd->sqhgd", score_grad, key_low, preferred_element_type=wide).reshape(
            2, length_value, heads_here, HEAD_WIDTH
        )
        * score_scale
    )
    key_rot_grad = (
        jnp.einsum("shgqk,sqhgd->skhd", score_grad, grouped, preferred_element_type=wide)
        * score_scale
    )
    query_pre_grad, query_gain_grad = norm_back(
        query_pre, head_gains[0], rotate(query_rot_grad, cosine, -sine_table)
    )
    key_pre_grad, key_gain_grad = norm_back(
        key_pre, head_gains[1], rotate(key_rot_grad, cosine, -sine_table)
    )
    query_key_grad = jnp.concatenate(
        [
            query_pre_grad.reshape(rows, head_cols).astype(low),
            key_pre_grad.reshape(rows, group_cols).astype(low),
        ],
        axis=1,
    )
    value_grad = value_grad.reshape(rows, group_cols)
    first_partial = (
        dot(query_key_grad, attention_full[:, : edges[2]], 1, 1)
        + dot(value_grad, value_full, 1, 1)
        + dot(logit_grad, headgate_full, 1, 1)
    )
    query_key_sum = ring_sum(product(first_full, query_key_grad), 1)
    value_sum = ring_sum(product(first_full, value_grad), -1)
    headgate_sum = lax.psum_scatter(
        dot(logit_grad, first_full, 0, 0), "w", scatter_dimension=1, tiled=True
    )
    first_grad = collect_rows(first_partial)
    tokens_partial, first_gain_grad = norm_back(residual, norm_gains[0], first_grad)
    tokens_grad = tokens_partial + middle_grad
    small = jnp.concatenate([query_gain_grad, key_gain_grad, squares])
    stats = jnp.stack(
        [
            first_gain_grad,
            second_gain_grad,
            jnp.pad(small, (0, MODEL_WIDTH - small.shape[0])),
        ]
    )
    stats = jnp.sum(lax.all_gather(stats, ("w", "c", "t"), axis=0), axis=0)
    norms_total = stats[:2]
    heads_total = stats[2, : 2 * HEAD_WIDTH].reshape(2, HEAD_WIDTH)
    squares_total = stats[2, 2 * HEAD_WIDTH : 2 * HEAD_WIDTH + 3]
    denominator = jnp.sum(valid_len).astype(wide) * MODEL_WIDTH
    branch_scales = jnp.sqrt(squares_total / denominator)
    input_rate = MODEL_WIDTH ** (-0.5)
    down_rate = FF ** (-0.5)
    output_rate = max(QUERY_HEADS * HEAD_WIDTH // 128, 4) ** (-0.5)
    gain_rate = 0.5
    norms_new = adam_update(norm_gains, norm_moment, norm_square, norms_total, gain_rate, 0.0)
    heads_new = adam_update(head_gains, head_moment, head_square, heads_total, gain_rate, 0.0)
    gateup_sum = jnp.stack(
        [deliver(gate_sum), deliver(jnp.concatenate([up_first, up_last], axis=1))]
    )
    down_sum = deliver(down_sum).T
    query_sum = deliver(query_key_sum[:, :head_cols])
    key_sum = deliver(query_key_sum[:, head_cols:])
    value_sum = deliver(value_sum)
    output_sum = deliver(output_sum)
    headgate_sum = deliver(headgate_sum.T)
    query_new = adam_update(
        query_weight, query_moment, query_square, query_sum, input_rate, weight_decay
    )
    keyvalue_new = adam_update(
        keyvalue_matrix,
        keyvalue_first_moment,
        keyvalue_second_moment,
        jnp.stack([key_sum, value_sum]),
        input_rate,
        weight_decay,
    )
    headgate_new = adam_update(
        headgate_weight, headgate_moment, headgate_square, headgate_sum, input_rate, weight_decay
    )
    output_new = adam_update(
        output_weight, output_moment, output_square, output_sum.T, output_rate, weight_decay
    )
    gateup_new = adam_update(
        gateup_weight, gateup_moment, gateup_square, gateup_sum, input_rate, weight_decay
    )
    down_new = adam_update(down_weight, down_moment, down_square, down_sum, down_rate, weight_decay)
    return (
        block_output,
        tokens_grad,
        branch_scales,
        *norms_new,
        *heads_new,
        *query_new,
        *keyvalue_new,
        *headgate_new,
        *output_new,
        *gateup_new,
        *down_new,
    )


def solution(mesh):
    fsdp, tp = mesh.devices.shape
    fine = Mesh(mesh.devices.reshape(fsdp // 2, 2, tp), ("w", "c", "t"))
    whole = ("w", "c")
    rows = P(("w", "c", "t"), None)
    first = P(whole, "t")
    second = P(None, whole, "t")
    last = P("t", whole)
    matrices = (first,) * 3 + (second,) * 3 + (first,) * 3 + (last,) * 3 + (second,) * 3 + (last,) * 3
    return jax.shard_map(
        local,
        mesh=fine,
        in_specs=(rows, rows, P(), P()) + (P(),) * 6 + matrices,
        out_specs=(rows, rows, P()) + (P(),) * 6 + matrices,
        check_vma=False,
    )
```

```python
import jax
import jax.numpy as jnp
from jax import lax
from jax.sharding import Mesh
from jax.sharding import PartitionSpec as P

MODEL_WIDTH = 2048
QUERY_HEADS = 16
HEAD_WIDTH = 128
FF = 6144
PIC = 256
STEP = 10

norm_epsilon = 1e-06
rope_base = 1000000.0
beta_first = 0.9
beta_second = 0.999
adam_epsilon = 1e-08
weight_decay = 0.1
masked_score = -1e30
low = jnp.bfloat16
wide = jnp.float32


def normalize(values, scaling):
    return (
        values
        * lax.rsqrt(jnp.mean(values * values, axis=-1, keepdims=True) + norm_epsilon)
        * scaling
    )


def norm_back(values, scaling, upstream):
    factor = lax.rsqrt(jnp.mean(values * values, axis=-1, keepdims=True) + norm_epsilon)
    weighted = upstream * scaling
    projected = jnp.mean(weighted * values, axis=-1, keepdims=True)
    result = factor * weighted - values * (factor * factor * factor) * projected
    return (result, jnp.sum(upstream * values * factor, axis=tuple(range(values.ndim - 1))))


def rotary_tables(length_value, head_width):
    halves = head_width // 2
    frequency = rope_base ** (-(jnp.arange(halves, dtype=wide) * 2.0 / head_width))
    angles = jnp.arange(length_value, dtype=wide)[:, None] * frequency[None, :]
    return (jnp.cos(angles), jnp.sin(angles))


def rotate(values, cosine, sine_table):
    halves = values.shape[-1] // 2
    former = values[..., :halves]
    latter = values[..., halves:]
    cosine = cosine[:, None, :]
    sine_table = sine_table[:, None, :]
    return jnp.concatenate(
        [former * cosine - latter * sine_table, latter * cosine + former * sine_table], axis=-1
    )


def visible(length_value, valid_count, piece_start, piece_size):
    places = jnp.arange(length_value, dtype=jnp.int32)
    inside = (places >= piece_start) & (places < piece_start + piece_size)
    causal = places[None, :] <= places[:, None]
    return (places[None, :] < valid_count) & (causal | inside[:, None] & inside[None, :])


def adam_update(weight, moment, square, gradient, step_rate, decay_rate):
    moment_new = beta_first * moment + (1.0 - beta_first) * gradient
    square_new = beta_second * square + (1.0 - beta_second) * gradient * gradient
    bias_first = 1.0 - beta_first**STEP
    bias_second = 1.0 - beta_second**STEP
    update = moment_new / bias_first / (jnp.sqrt(square_new / bias_second) + adam_epsilon)
    return (weight - step_rate * (update + decay_rate * weight), moment_new, square_new)


def dot(left, right, left_dim, right_dim):
    return lax.dot_general(
        left, right, (((left_dim,), (right_dim,)), ((), ())), preferred_element_type=wide
    )


SWAP = [(0, 1), (1, 0)]


def swap(values, axis):
    return lax.ppermute(values, axis, SWAP)


def joined(mine, other, axis):
    index = lax.axis_index(axis)
    return jnp.concatenate(
        [jnp.where(index == 0, mine, other), jnp.where(index == 0, other, mine)], axis=0
    )


def halves_of(values, axis, dim):
    index = lax.axis_index(axis)
    size = values.shape[dim] // 2
    mine = lax.dynamic_slice_in_dim(values, index * size, size, dim)
    other = lax.dynamic_slice_in_dim(values, (1 - index) * size, size, dim)
    return mine, other


def spread_rows(values):
    pair = joined(values, swap(values, "t"), "t")
    return joined(pair, swap(pair, "c"), "c")


def collect_rows(values):
    mine, other = halves_of(values, "c", 0)
    pair = mine + swap(other.astype(low), "c").astype(wide)
    mine, other = halves_of(pair, "t", 0)
    return mine + swap(other.astype(low), "t").astype(wide)


def fetch(parts):
    pieces = []
    for core in range(2):
        for part in parts:
            size = part.shape[1] // 2
            piece = part[:, core * size : (core + 1) * size].astype(low)
            pieces.append(jnp.pad(piece, ((0, 0), (0, -size % 128))))
    count = len(parts)
    local_block = jnp.stack(
        [jnp.concatenate(pieces[core * count : (core + 1) * count], axis=1) for core in range(2)]
    )
    return lax.all_gather(local_block, ("w", "c"), axis=1, tiled=True)


def columns_of(both, start, size):
    return lax.dynamic_slice(
        both, (lax.axis_index("c"), 0, start), (1, both.shape[1], size)
    ).reshape(both.shape[1], size)


def ring_order(count):
    width = 2 if count <= 8 else 4
    rows = count // width
    if rows < 2 or rows % 2:
        return list(range(count))
    order = [0]
    for row in range(rows):
        columns = list(range(1, width))
        if row % 2:
            columns.reverse()
        order += [row * width + column for column in columns]
    return order + [row * width for row in range(rows - 1, 0, -1)]


class Ring:
    def __init__(self, own, direction):
        self.count = lax.axis_size("w")
        order = ring_order(self.count)
        position = [0] * self.count
        for spot, index in enumerate(order):
            position[index] = spot
        self.order = jnp.array(order, jnp.int32)
        self.here = jnp.array(position, jnp.int32)[lax.axis_index("w")]
        self.links = [
            (order[spot], order[(spot + direction) % self.count]) for spot in range(self.count)
        ]
        self.own = own
        self.direction = direction
        self.step = 0
        self.total = None
        self.running = self.partial(1).astype(low)

    def partial(self, distance):
        return self.own(self.order[(self.here - self.direction * distance) % self.count])

    def send(self):
        if self.total is None:
            self.arrived = lax.ppermute(self.running, "w", self.links)

    def add(self, arrived):
        total = arrived.astype(wide) + self.partial(2 + self.step)
        self.step += 1
        if self.step == self.count - 1:
            self.total = total
        self.running = total.astype(low)


class Schedule:
    def __init__(self):
        self.sets = []

    def begin(self, rings):
        for ring in rings:
            ring.send()
        self.sets.append(rings)

    def move(self, anchor, count=1):
        for _ in range(count):
            if not self.sets:
                return anchor
            rings = self.sets.pop(0)
            anchor, arrived = lax.optimization_barrier((anchor, [ring.arrived for ring in rings]))
            for ring, value in zip(rings, arrived):
                ring.add(value)
            if rings[0].total is None:
                anchor, running = lax.optimization_barrier(
                    (anchor, [ring.running for ring in rings])
                )
                for ring, value in zip(rings, running):
                    ring.running = value
                    ring.send()
                self.sets.append(rings)
        return anchor

    def swap(self, values, axis, count):
        received = swap(values, axis)
        if count and self.sets:
            values = self.move(values, count)
            received, values = lax.optimization_barrier((received, values))
        return received

    def spread(self, values, counts):
        pair = joined(values, self.swap(values, "t", counts[0]), "t")
        return joined(pair, self.swap(pair, "c", counts[1]), "c")

    def collect(self, values, counts):
        mine, other = halves_of(values, "c", 0)
        pair = mine + self.swap(other.astype(low), "c", counts[0]).astype(wide)
        mine, other = halves_of(pair, "t", 0)
        return mine + self.swap(other.astype(low), "t", counts[1]).astype(wide)

    def finish(self, rings):
        while any(ring.total is None for ring in rings):
            self.move(jnp.zeros((), wide), 1)


def total_sum(values):
    for axis in ("c", "t", "w"):
        count = lax.axis_size(axis)
        if count & (count - 1):
            values = lax.psum(values, axis)
            continue
        distance = 1
        while distance < count:
            values = values + lax.ppermute(
                values, axis, [(index, index ^ distance) for index in range(count)]
            )
            distance *= 2
    return values


def deliver(total):
    mine, other = halves_of(total, "c", 0)
    other = swap(other.astype(low), "c").astype(wide)
    core = lax.axis_index("c")
    return jnp.concatenate(
        [jnp.where(core == 0, mine, other), jnp.where(core == 0, other, mine)], axis=1
    )


def local(
    tokens,
    cotangent,
    valid_len,
    pic_start,
    norm_gains,
    norm_moment,
    norm_square,
    head_gains,
    head_moment,
    head_square,
    query_weight,
    query_moment,
    query_square,
    keyvalue_matrix,
    keyvalue_first_moment,
    keyvalue_second_moment,
    headgate_weight,
    headgate_moment,
    headgate_square,
    output_weight,
    output_moment,
    output_square,
    gateup_weight,
    gateup_moment,
    gateup_square,
    down_weight,
    down_moment,
    down_square,
):
    local_rows = tokens.shape[0]
    length_value = local_rows * 2
    rows = length_value * 2
    group = lax.axis_index("w")
    core = lax.axis_index("c")
    place = lax.axis_index("t")
    heads_here = query_weight.shape[1] // HEAD_WIDTH // 2
    groups_here = keyvalue_matrix.shape[2] // HEAD_WIDTH // 2
    share = heads_here // groups_here
    score_scale = HEAD_WIDTH ** (-0.5)
    head_cols = heads_here * HEAD_WIDTH
    group_cols = groups_here * HEAD_WIDTH
    hidden_here = gateup_weight.shape[2] // 2

    chunks = 2
    chunk = hidden_here // chunks

    def chunk_columns(values, index):
        return jnp.concatenate(
            [
                values[:, (core * chunks + index) * chunk : (core * chunks + index + 1) * chunk]
                for core in range(2)
            ],
            axis=1,
        )

    attention_both = fetch(
        [query_weight, keyvalue_matrix[0], keyvalue_matrix[1], output_weight.T, headgate_weight]
    )
    down_turned = down_weight.T
    feedforward_both = [
        fetch(
            [
                chunk_columns(values, index)
                for values in (gateup_weight[0], gateup_weight[1], down_turned)
            ]
        )
        for index in range(chunks)
    ]
    bounds = [0, head_cols, group_cols, group_cols, head_cols, 128]
    edges = [sum(bounds[: i + 1]) for i in range(6)]
    query_full, key_full, value_full, output_full, headgate_full = (
        columns_of(attention_both, edges[i], edges[i + 1] - edges[i]) for i in range(5)
    )
    schedule = Schedule()

    residual = tokens.astype(wide)
    first_full = spread_rows(normalize(residual, norm_gains[0]).astype(low))
    output_grad_full = spread_rows(cotangent)

    query_pre = dot(first_full, query_full, 1, 0).reshape(2, length_value, heads_here, HEAD_WIDTH)
    key_pre = dot(first_full, key_full, 1, 0).reshape(2, length_value, groups_here, HEAD_WIDTH)
    value_low = (
        dot(first_full, value_full, 1, 0)
        .astype(low)
        .reshape(2, length_value, groups_here, HEAD_WIDTH)
    )
    gate_logit = dot(first_full, headgate_full, 1, 0)[:, :heads_here].reshape(
        2, length_value, heads_here
    )
    cosine, sine_table = rotary_tables(length_value, HEAD_WIDTH)
    query_low = rotate(normalize(query_pre, head_gains[0]), cosine, sine_table).astype(low)
    key_low = rotate(normalize(key_pre, head_gains[1]), cosine, sine_table).astype(low)
    valid_pair = lax.dynamic_slice_in_dim(valid_len, 2 * group, 2)
    start_pair = lax.dynamic_slice_in_dim(pic_start, 2 * group, 2)
    allowed = jax.vmap(lambda a, b: visible(length_value, a, b, PIC))(valid_pair, start_pair)
    allowed = allowed[:, None, None]
    grouped = query_low.reshape(2, length_value, groups_here, share, HEAD_WIDTH)

    def score_block():
        raw = (
            jnp.einsum("sqhgd,skhd->shgqk", grouped, key_low, preferred_element_type=wide)
            * score_scale
        )
        return jnp.where(allowed, raw, masked_score)

    scores = score_block()
    highest_score = jnp.max(scores, axis=-1, keepdims=True)
    expos = jnp.exp(scores - highest_score)
    row_total = jnp.sum(expos, axis=-1, keepdims=True)
    log_total = highest_score + jnp.log(row_total)
    probs_low = (expos / row_total).astype(low)
    mixed = jnp.einsum(
        "shgqk,skhd->sqhgd", probs_low, value_low, preferred_element_type=wide
    ).reshape(2, length_value, heads_here, HEAD_WIDTH)
    gate_value = jax.nn.sigmoid(gate_logit)
    gated_low = (mixed * gate_value[..., None]).reshape(rows, head_cols).astype(low)
    attention_local = collect_rows(dot(gated_low, output_full, 1, 1))
    middle = residual + attention_local
    second_full = spread_rows(normalize(middle, norm_gains[1]).astype(low))

    block = MODEL_WIDTH // lax.axis_size("w")

    def product(left, right):
        def own(owner):
            return dot(lax.dynamic_slice_in_dim(left, owner * block, block, 1), right, 0, 0)

        return own

    half = chunk // 2
    second_partial = None
    feedforward_partial = None
    ring_sets = []
    for index in range(chunks):
        gate_full, up_full, down_full = (
            columns_of(feedforward_both[index], i * chunk, chunk) for i in range(3)
        )
        gate_part = schedule.move(dot(second_full, gate_full, 1, 0))
        up_part = schedule.move(dot(second_full, up_full, 1, 0))
        sigmoid_gate = jax.nn.sigmoid(gate_part)
        silu_gate = gate_part * sigmoid_gate
        hidden_low = (silu_gate * up_part).astype(low)
        hidden_grad = dot(output_grad_full, down_full, 1, 0)
        gate_grad = (
            hidden_grad * up_part * sigmoid_gate * (1.0 + gate_part * (1.0 - sigmoid_gate))
        ).astype(low)
        up_grad = (hidden_grad * silu_gate).astype(low)
        gate_grad, up_grad, hidden_low = schedule.move((gate_grad, up_grad, hidden_low))
        partial = dot(gate_grad, gate_full, 1, 1) + dot(up_grad, up_full, 1, 1)
        second_partial = partial if second_partial is None else second_partial + partial
        long_set = [
            Ring(product(second_full, gate_grad), 1),
            Ring(product(output_grad_full, hidden_low), -1),
        ]
        short_set = [
            Ring(product(second_full, up_grad[:, :half]), 1),
            Ring(product(second_full, up_grad[:, half:]), -1),
        ]
        schedule.begin(long_set)
        schedule.begin(short_set)
        ring_sets.append(long_set + short_set)
        second_partial = schedule.move(second_partial)
        partial = dot(hidden_low, down_full, 1, 1)
        feedforward_partial = (
            partial if feedforward_partial is None else feedforward_partial + partial
        )
        if index < chunks - 1:
            feedforward_partial, second_partial = schedule.move(
                (feedforward_partial, second_partial)
            )

    second_grad = schedule.collect(second_partial, (1, 4))
    middle_grad, second_gain_grad = norm_back(middle, norm_gains[1], second_grad)
    middle_grad = middle_grad + cotangent.astype(wide)
    attention_grad = schedule.spread(middle_grad.astype(low), (4, 1))

    output_set = [Ring(product(attention_grad, gated_low), 1)]
    gated_grad = dot(attention_grad, output_full, 1, 0).reshape(
        2, length_value, heads_here, HEAD_WIDTH
    )
    gated_grad = schedule.move(gated_grad, 1)
    mixed_grad = (
        (gated_grad * gate_value[..., None])
        .astype(low)
        .reshape(2, length_value, groups_here, share, HEAD_WIDTH)
    )
    logit_grad = (
        (jnp.sum(gated_grad * mixed, axis=-1) * gate_value * (1.0 - gate_value))
        .astype(low)
        .reshape(rows, heads_here)
    )
    mixed_grad, logit_grad = schedule.move((mixed_grad, logit_grad), 1)
    schedule.begin(output_set)
    probs_again = jnp.exp(score_block() - log_total)
    probs_again = schedule.move(probs_again, 1)
    value_grad = jnp.einsum(
        "shgqk,sqhgd->skhd", probs_again.astype(low), mixed_grad, preferred_element_type=wide
    ).astype(low)
    prob_grad = jnp.einsum("sqhgd,skhd->shgqk", mixed_grad, value_low, preferred_element_type=wide)
    prob_grad, value_grad = schedule.move((prob_grad, value_grad), 1)
    score_grad = (
        probs_again * (prob_grad - jnp.sum(prob_grad * probs_again, axis=-1, keepdims=True))
    ).astype(low)
    score_grad = schedule.move(score_grad, 1)
    query_rot_grad = (
        jnp.einsum("shgqk,skhd->sqhgd", score_grad, key_low, preferred_element_type=wide).reshape(
            2, length_value, heads_here, HEAD_WIDTH
        )
        * score_scale
    )
    key_rot_grad = (
        jnp.einsum("shgqk,sqhgd->skhd", score_grad, grouped, preferred_element_type=wide)
        * score_scale
    )
    query_rot_grad, key_rot_grad = schedule.move((query_rot_grad, key_rot_grad), 1)
    query_pre_grad, query_gain_grad = norm_back(
        query_pre, head_gains[0], rotate(query_rot_grad, cosine, -sine_table)
    )
    query_grad_low = query_pre_grad.reshape(rows, head_cols).astype(low)
    query_grad_low = schedule.move(query_grad_low, 1)
    key_pre_grad, key_gain_grad = norm_back(
        key_pre, head_gains[1], rotate(key_rot_grad, cosine, -sine_table)
    )
    mixed_columns = jnp.concatenate(
        [
            key_pre_grad.reshape(rows, group_cols).astype(low),
            value_grad.reshape(rows, group_cols),
            jnp.pad(logit_grad, ((0, 0), (0, 128 - heads_here))),
        ],
        axis=1,
    )
    mixed_columns, query_grad_low = schedule.move((mixed_columns, query_grad_low), 1)
    last_set = [
        Ring(product(first_full, query_grad_low), 1),
        Ring(product(first_full, mixed_columns), -1),
    ]
    schedule.begin(last_set)
    first_partial = dot(query_grad_low, query_full, 1, 1) + dot(
        mixed_columns[:, : 2 * group_cols], columns_of(attention_both, edges[1], 2 * group_cols), 1, 1
    )
    first_partial = first_partial + dot(
        mixed_columns[:, 2 * group_cols :], headgate_full, 1, 1
    )
    first_partial = schedule.move(first_partial, 1)
    first_grad = schedule.collect(first_partial, (1, 2))
    tokens_partial, first_gain_grad = norm_back(residual, norm_gains[0], first_grad)
    tokens_grad = tokens_partial + middle_grad

    feedforward_local = schedule.collect(feedforward_partial, (1, 1))
    block_output = (middle + feedforward_local).astype(low)
    own_places = place * local_rows + jnp.arange(local_rows, dtype=jnp.int32)
    counted = (own_places < valid_pair[core]).astype(wide)[:, None]
    squares = jnp.stack(
        [
            jnp.sum(counted * residual * residual),
            jnp.sum(counted * attention_local * attention_local),
            jnp.sum(counted * feedforward_local * feedforward_local),
        ]
    )

    small = jnp.concatenate([query_gain_grad, key_gain_grad, squares])
    stats = jnp.stack(
        [
            first_gain_grad,
            second_gain_grad,
            jnp.pad(small, (0, MODEL_WIDTH - small.shape[0])),
        ]
    )
    stats = total_sum(stats)
    schedule.finish(last_set)
    for rings in ring_sets:
        schedule.finish(rings)
    schedule.finish(output_set)
    norms_total = stats[:2]
    heads_total = stats[2, : 2 * HEAD_WIDTH].reshape(2, HEAD_WIDTH)
    squares_total = stats[2, 2 * HEAD_WIDTH : 2 * HEAD_WIDTH + 3]
    denominator = jnp.sum(valid_len).astype(wide) * MODEL_WIDTH
    branch_scales = jnp.sqrt(squares_total / denominator)
    input_rate = MODEL_WIDTH ** (-0.5)
    down_rate = FF ** (-0.5)
    output_rate = max(QUERY_HEADS * HEAD_WIDTH // 128, 4) ** (-0.5)
    gain_rate = 0.5
    norms_new = adam_update(norm_gains, norm_moment, norm_square, norms_total, gain_rate, 0.0)
    heads_new = adam_update(head_gains, head_moment, head_square, heads_total, gain_rate, 0.0)
    def gathered(parts):
        return deliver(jnp.concatenate([value for part in parts for value in part], axis=1))

    gateup_sum = jnp.stack(
        [
            gathered([[rings[0].total] for rings in ring_sets]),
            gathered([[rings[2].total, rings[3].total] for rings in ring_sets]),
        ]
    )
    down_sum = gathered([[rings[1].total] for rings in ring_sets]).T
    query_sum = deliver(last_set[0].total)
    key_sum = deliver(last_set[1].total[:, :group_cols])
    value_sum = deliver(last_set[1].total[:, group_cols : 2 * group_cols])
    headgate_sum = deliver(last_set[1].total[:, 2 * group_cols : 2 * group_cols + heads_here])
    output_sum = deliver(output_set[0].total)
    query_new = adam_update(
        query_weight, query_moment, query_square, query_sum, input_rate, weight_decay
    )
    keyvalue_new = adam_update(
        keyvalue_matrix,
        keyvalue_first_moment,
        keyvalue_second_moment,
        jnp.stack([key_sum, value_sum]),
        input_rate,
        weight_decay,
    )
    headgate_new = adam_update(
        headgate_weight, headgate_moment, headgate_square, headgate_sum, input_rate, weight_decay
    )
    output_new = adam_update(
        output_weight, output_moment, output_square, output_sum.T, output_rate, weight_decay
    )
    gateup_new = adam_update(
        gateup_weight, gateup_moment, gateup_square, gateup_sum, input_rate, weight_decay
    )
    down_new = adam_update(down_weight, down_moment, down_square, down_sum, down_rate, weight_decay)
    return (
        block_output,
        tokens_grad,
        branch_scales,
        *norms_new,
        *heads_new,
        *query_new,
        *keyvalue_new,
        *headgate_new,
        *output_new,
        *gateup_new,
        *down_new,
    )


def solution(mesh):
    fsdp, tp = mesh.devices.shape
    fine = Mesh(mesh.devices.reshape(fsdp // 2, 2, tp), ("w", "c", "t"))
    whole = ("w", "c")
    rows = P(("w", "c", "t"), None)
    first = P(whole, "t")
    second = P(None, whole, "t")
    last = P("t", whole)
    matrices = (first,) * 3 + (second,) * 3 + (first,) * 3 + (last,) * 3 + (second,) * 3 + (last,) * 3
    return jax.shard_map(
        local,
        mesh=fine,
        in_specs=(rows, rows, P(), P()) + (P(),) * 6 + matrices,
        out_specs=(rows, rows, P()) + (P(),) * 6 + matrices,
        check_vma=False,
    )
```

```python
import jax
import jax.numpy as jnp
from jax import lax
from jax.experimental import pallas as pl
from jax.experimental.pallas import tpu as pltpu
from jax.sharding import Mesh
from jax.sharding import PartitionSpec as P

MODEL_WIDTH = 2048
QUERY_HEADS = 16
HEAD_WIDTH = 128
FF = 6144
PIC = 256
STEP = 10

norm_epsilon = 1e-06
rope_base = 1000000.0
beta_first = 0.9
beta_second = 0.999
adam_epsilon = 1e-08
weight_decay = 0.1
masked_score = -1e30
low = jnp.bfloat16
wide = jnp.float32


def normalize(values, scaling):
    return (
        values
        * lax.rsqrt(jnp.mean(values * values, axis=-1, keepdims=True) + norm_epsilon)
        * scaling
    )


def norm_back(values, scaling, upstream):
    factor = lax.rsqrt(jnp.mean(values * values, axis=-1, keepdims=True) + norm_epsilon)
    weighted = upstream * scaling
    projected = jnp.mean(weighted * values, axis=-1, keepdims=True)
    result = factor * weighted - values * (factor * factor * factor) * projected
    return (result, jnp.sum(upstream * values * factor, axis=tuple(range(values.ndim - 1))))


def rotary_tables(length_value, head_width):
    halves = head_width // 2
    frequency = rope_base ** (-(jnp.arange(halves, dtype=wide) * 2.0 / head_width))
    angles = jnp.arange(length_value, dtype=wide)[:, None] * frequency[None, :]
    return (jnp.cos(angles), jnp.sin(angles))


def rotate(values, cosine, sine_table):
    halves = values.shape[-1] // 2
    former = values[..., :halves]
    latter = values[..., halves:]
    cosine = cosine[:, None, :]
    sine_table = sine_table[:, None, :]
    return jnp.concatenate(
        [former * cosine - latter * sine_table, latter * cosine + former * sine_table], axis=-1
    )


def visible(length_value, valid_count, piece_start, piece_size):
    places = jnp.arange(length_value, dtype=jnp.int32)
    inside = (places >= piece_start) & (places < piece_start + piece_size)
    causal = places[None, :] <= places[:, None]
    return (places[None, :] < valid_count) & (causal | inside[:, None] & inside[None, :])


def adam_update(weight, moment, square, gradient, step_rate, decay_rate):
    moment_new = beta_first * moment + (1.0 - beta_first) * gradient
    square_new = beta_second * square + (1.0 - beta_second) * gradient * gradient
    bias_first = 1.0 - beta_first**STEP
    bias_second = 1.0 - beta_second**STEP
    update = moment_new / bias_first / (jnp.sqrt(square_new / bias_second) + adam_epsilon)
    return (weight - step_rate * (update + decay_rate * weight), moment_new, square_new)


def dot(left, right, left_dim, right_dim):
    return lax.dot_general(
        left, right, (((left_dim,), (right_dim,)), ((), ())), preferred_element_type=wide
    )


def fetch(parts):
    pieces = []
    for core in range(2):
        for part in parts:
            size = part.shape[1] // 2
            pieces.append(part[:, core * size : (core + 1) * size].astype(low))
    count = len(parts)
    local_block = jnp.stack(
        [jnp.concatenate(pieces[core * count : (core + 1) * count], axis=1) for core in range(2)]
    )
    return lax.all_gather(local_block, ("w", "c"), axis=1, tiled=True)


def columns_of(both, start, size):
    return lax.dynamic_slice(
        both, (lax.axis_index("c"), 0, start), (1, both.shape[1], size)
    ).reshape(both.shape[1], size)


MESH = pl.DeviceIdType.MESH
BLOCKS = 4
STRIP = 16
ANY = pl.BlockSpec(memory_space=pl.ANY)
VMEM = pl.BlockSpec(memory_space=pltpu.VMEM)


def ring_place(index, count):
    odd = lax.rem(index, 2)
    pair = lax.div(index, 2)
    return (1 - odd) * pair + odd * (count - 1 - pair)


def ring_index(place, count):
    late = lax.div(place, count // 2)
    return (1 - late) * 2 * place + late * (2 * (count - 1 - place) + 1)


class Device:
    def __init__(self, semaphores):
        self.w, self.c, self.t = (lax.axis_index(axis) for axis in ("w", "c", "t"))
        self.count = lax.axis_size("w")
        self.place = ring_place(self.w, self.count)
        self.semaphores = semaphores
        self.used = 0
        self.other_core = {"c": 1 - self.c}
        self.other_row = {"t": 1 - self.t}

    def owner(self, distance):
        return ring_index(lax.rem(self.place + distance + self.count, self.count), self.count)

    def meet(self, partners):
        barrier = pltpu.get_barrier_semaphore()
        for partner in partners:
            pl.semaphore_signal(barrier, inc=1, device_id=partner, device_id_type=MESH)
        pl.semaphore_wait(barrier, len(partners))

    def remote(self, source, target, device):
        slot = self.used
        self.used += 1
        return pltpu.make_async_remote_copy(
            src_ref=source,
            dst_ref=target,
            send_sem=self.semaphores.at[0, slot],
            recv_sem=self.semaphores.at[1, slot],
            device_id=device,
            device_id_type=MESH,
        )

    def inside(self, source, target):
        slot = self.used
        self.used += 1
        return pltpu.make_async_copy(source, target, self.semaphores.at[0, slot])


def rows_at(start, size):
    return pl.ds(pl.multiple_of(start, STRIP), size)


class Spread:
    def __init__(self, device, full):
        self.device, self.full = device, full
        self.size = full.shape[0] // 4
        self.block = self.size // BLOCKS
        self.rows, self.core, self.passed, self.kept = {}, {}, {}, {}

    def where(self, core, row, index):
        return self.full.at[
            rows_at((core * 2 + row) * self.size + index * self.block, self.block)
        ]

    def put(self, index, source):
        device = self.device
        target = self.where(device.c, device.t, index)
        self.rows[index] = device.remote(source, target, device.other_row)
        self.core[index] = device.remote(source, target, device.other_core)
        self.kept[index] = device.inside(source, target)
        for copy in (self.rows[index], self.core[index], self.kept[index]):
            copy.start()

    def forward(self, index):
        device = self.device
        self.rows[index].wait_recv()
        place = self.where(device.c, 1 - device.t, index)
        self.passed[index] = device.remote(place, place, device.other_core)
        self.passed[index].start()

    def finish(self):
        for index in range(BLOCKS):
            self.rows[index].wait_send()
            self.core[index].wait()
            self.passed[index].wait()
            self.kept[index].wait()


class Collect:
    def __init__(self, device, partial, near, far, sent, came):
        self.device = device
        self.partial, self.near, self.far, self.sent, self.came = partial, near, far, sent, came
        self.size = partial.shape[0] // 4
        self.block = self.size // BLOCKS
        self.core, self.rows = {}, {}

    def start(self):
        device = self.device
        self.load = device.inside(
            self.partial.at[rows_at(device.c * 2 * self.size, 2 * self.size)], self.near
        )
        for part, row in enumerate((1 - device.t, device.t)):
            for index in range(BLOCKS):
                start = row * self.size + index * self.block
                copy = device.remote(
                    self.partial.at[rows_at((1 - device.c) * 2 * self.size + start, self.block)],
                    self.far.at[rows_at(start, self.block)],
                    device.other_core,
                )
                copy.start()
                self.core[part, index] = copy
        self.load.start()

    def pass_on(self, index):
        device = self.device
        if index == 0:
            self.load.wait()
        self.core[0, index].wait_recv()

        @pl.loop(0, self.block // STRIP)
        def _(strip):
            at = index * self.block + strip * STRIP
            rows = rows_at((1 - device.t) * self.size + at, STRIP)
            total = self.near[rows, :].astype(wide) + self.far[rows, :].astype(wide)
            self.sent[rows_at(at, STRIP), :] = total.astype(low)

        place = rows_at(index * self.block, self.block)
        self.rows[index] = device.remote(
            self.sent.at[place], self.came.at[place], device.other_row
        )
        self.rows[index].start()

    def take(self, index, use):
        device = self.device
        self.core[1, index].wait_recv()
        self.rows[index].wait_recv()

        @pl.loop(0, self.block // STRIP)
        def _(strip):
            at = index * self.block + strip * STRIP
            rows = rows_at(device.t * self.size + at, STRIP)
            mine = rows_at(at, STRIP)
            total = (
                self.near[rows, :].astype(wide)
                + self.far[rows, :].astype(wide)
                + self.came[mine, :].astype(wide)
            )
            use(mine, total)

    def finish(self):
        for index in range(BLOCKS):
            self.core[0, index].wait_send()
            self.core[1, index].wait_send()
            self.rows[index].wait_send()


class RingSum:
    def __init__(self, device, grads, slots, totals, sums):
        self.device, self.grads, self.slots = device, grads, slots
        self.totals, self.sums = totals, sums
        self.half = grads.shape[0] // device.count // 2
        self.parts = 2
        self.part = self.half // self.parts
        self.copies = {}
        self.ticks = [
            (step, part) for step in range(device.count) for part in range(self.parts)
        ]

    def own(self, way, distance, part):
        direction = 1 - 2 * way
        owner = self.device.owner(-direction * distance)
        return rows_at((owner * 2 + way) * self.half + part * self.part, self.part)

    def slot(self, way, step, part):
        return self.slots.at[
            way * (self.device.count - 1) + step, pl.ds(part * self.part, self.part)
        ]

    def send(self, way, step, part):
        device = self.device
        if step == 0:
            source = self.grads.at[self.own(way, 1, part)]
        else:
            source = self.slot(way, step - 1, part)
        copy = device.remote(
            source, self.slot(way, step, part), {"w": device.owner(1 - 2 * way)}
        )
        copy.start()
        self.copies[way, step, part] = copy

    def tick(self, count=1):
        device = self.device
        for _ in range(count):
            if not self.ticks:
                return
            step, part = self.ticks.pop(0)
            for way in range(2):
                if step > 0:
                    self.copies[way, step - 1, part].wait_recv()
                    own = self.own(way, step + 1, part)
                    slot = self.slot(way, step - 1, part)
                    total = (slot[...].astype(wide) + self.grads[own, :].astype(wide)).astype(low)
                    if step < device.count - 1:
                        slot[...] = total
                    else:
                        self.totals[way, pl.ds(part * self.part, self.part), :] = total
                if step < device.count - 1:
                    self.send(way, step, part)

    def finish(self):
        device = self.device
        self.tick(len(self.ticks))
        away = device.remote(
            self.totals.at[1 - device.c], self.sums.at[device.c], device.other_core
        )
        kept = device.inside(self.totals.at[device.c], self.sums.at[device.c])
        away.start()
        kept.start()
        for copy in self.copies.values():
            copy.wait_send()
        away.wait()
        kept.wait()


def ring_shapes(columns, count):
    half = MODEL_WIDTH // count // 2
    return [
        pltpu.VMEM((2 * (count - 1), half, columns), low),
        pltpu.VMEM((2, half, columns), low),
    ]


def collect_shapes(size):
    return [
        pltpu.VMEM((2 * size, MODEL_WIDTH), low),
        pltpu.VMEM((2 * size, MODEL_WIDTH), low),
        pltpu.VMEM((size, MODEL_WIDTH), low),
        pltpu.VMEM((size, MODEL_WIDTH), low),
    ]


def semaphores_for(count):
    return pltpu.SemaphoreType.DMA((2, count))


def settings(collective):
    return pltpu.CompilerParams(
        collective_id=collective, has_side_effects=True, vmem_limit_bytes=48 * 2**20
    )


def neighbours(device):
    return [
        device.other_core,
        device.other_row,
        {"w": device.owner(1)},
        {"w": device.owner(-1)},
    ]


def gather_kernel(mine, other, first, second, full, first_full, second_full, semaphores):
    device = Device(semaphores)
    device.meet(neighbours(device))
    size = mine.shape[0]
    here = rows_at((device.w * 2 + device.c) * size, size)
    kept = device.inside(mine, full.at[here])
    crossed = device.remote(other, full.at[here], device.other_core)
    kept.start()
    crossed.start()
    spreads = []
    for rows, target in ((first, first_full), (second, second_full)):
        spread = Spread(device, target)
        block = spread.block
        for index in range(BLOCKS):
            spread.put(index, rows.at[pl.ds(index * block, block)])
        spreads.append(spread)
    kept.wait()
    crossed.wait()
    parts = 2
    part_rows = size // parts
    copies = {}
    waiting = [(spread, index) for spread in spreads for index in range(BLOCKS)]

    def piece(way, distance, part):
        owner = device.owner(-(1 - 2 * way) * distance)
        return full.at[rows_at((owner * 2 + way) * size + part * part_rows, part_rows)]

    for step in range(device.count - 1):
        for part in range(parts):
            for way in range(2):
                if step > 0:
                    copies[way, step - 1, part].wait_recv()
                block = piece(way, step, part)
                copy = device.remote(block, block, {"w": device.owner(1 - 2 * way)})
                copy.start()
                copies[way, step, part] = copy
        if waiting:
            spread, index = waiting.pop(0)
            spread.forward(index)
    for spread, index in waiting:
        spread.forward(index)
    for part in range(parts):
        for way in range(2):
            copies[way, device.count - 2, part].wait_recv()
    for copy in copies.values():
        copy.wait_send()
    for spread in spreads:
        spread.finish()


def gather_attention(mine, other, first, second):
    count = lax.axis_size("w")
    rows = first.shape[0] * 4
    return pl.pallas_call(
        gather_kernel,
        out_shape=[
            jax.ShapeDtypeStruct((MODEL_WIDTH, mine.shape[1]), low),
            jax.ShapeDtypeStruct((rows, MODEL_WIDTH), low),
            jax.ShapeDtypeStruct((rows, MODEL_WIDTH), low),
        ],
        in_specs=[ANY] * 4,
        out_specs=[ANY] * 3,
        scratch_shapes=[semaphores_for(4 * (count - 1) + 8 * BLOCKS + 2)],
        compiler_params=settings(1),
        cost_estimate=pl.CostEstimate(flops=0, bytes_accessed=64 * 2**20, transcendentals=0),
        name="gather_attention",
    )(mine, other, first, second)


def forward_kernel(partial, rows, gain, total, full, near, far, sent, came, normed, semaphores):
    device = Device(semaphores)
    device.meet([device.other_core, device.other_row])
    collect = Collect(device, partial, near, far, sent, came)
    spread = Spread(device, full)
    collect.start()
    for index in range(BLOCKS):
        collect.pass_on(index)

    def use(at, value):
        total[at, :] = value
        middle = rows[at, :].astype(wide) + value
        normed[at, :] = normalize(middle, gain[...]).astype(low)

    for index in range(BLOCKS):
        collect.take(index, use)
        spread.put(index, normed.at[pl.ds(index * spread.block, spread.block)])
        if index > 0:
            spread.forward(index - 1)
    spread.forward(BLOCKS - 1)
    spread.finish()
    collect.finish()


def exchange_forward(partial, rows, gain):
    size = rows.shape[0]
    return pl.pallas_call(
        forward_kernel,
        out_shape=[
            jax.ShapeDtypeStruct((size, MODEL_WIDTH), wide),
            jax.ShapeDtypeStruct((4 * size, MODEL_WIDTH), low),
        ],
        in_specs=[ANY, VMEM, VMEM],
        out_specs=[VMEM, ANY],
        scratch_shapes=collect_shapes(size)
        + [pltpu.VMEM((size, MODEL_WIDTH), low), semaphores_for(16 * BLOCKS)],
        compiler_params=settings(2),
        cost_estimate=pl.CostEstimate(flops=0, bytes_accessed=64 * 2**20, transcendentals=0),
        name="exchange_forward",
    )(partial, rows, gain)


def backward_kernel(
    partial, middle, rows, gain, grads, grad, gain_grad, full, sums,
    near, far, sent, came, rounded, slots, totals, semaphores,
):
    device = Device(semaphores)
    device.meet(neighbours(device))
    collect = Collect(device, partial, near, far, sent, came)
    spread = Spread(device, full)
    ring = RingSum(device, grads, slots, totals, sums)
    collect.start()
    ring.tick(2)
    gain_grad[...] = jnp.zeros_like(gain_grad)
    for index in range(BLOCKS):
        collect.pass_on(index)
    ring.tick(1)

    def use(at, upstream):
        values = middle[at, :]
        factor = lax.rsqrt(jnp.mean(values * values, axis=-1, keepdims=True) + norm_epsilon)
        weighted = upstream * gain[...]
        projected = jnp.mean(weighted * values, axis=-1, keepdims=True)
        result = factor * weighted - values * (factor * factor * factor) * projected
        result = result + rows[at, :].astype(wide)
        grad[at, :] = result
        rounded[at, :] = result.astype(low)
        gain_grad[...] += jnp.sum(upstream * values * factor, axis=0, keepdims=True)

    for index in range(BLOCKS):
        collect.take(index, use)
        spread.put(index, rounded.at[pl.ds(index * spread.block, spread.block)])
        ring.tick(1)
        if index > 0:
            spread.forward(index - 1)
    ring.tick(1)
    spread.forward(BLOCKS - 1)
    ring.finish()
    spread.finish()
    collect.finish()


def exchange_backward(partial, middle, rows, gain, grads):
    size = rows.shape[0]
    count = lax.axis_size("w")
    half = MODEL_WIDTH // count // 2
    return pl.pallas_call(
        backward_kernel,
        out_shape=[
            jax.ShapeDtypeStruct((size, MODEL_WIDTH), wide),
            jax.ShapeDtypeStruct((1, MODEL_WIDTH), wide),
            jax.ShapeDtypeStruct((4 * size, MODEL_WIDTH), low),
            jax.ShapeDtypeStruct((2, half, grads.shape[1]), low),
        ],
        in_specs=[ANY] + [VMEM] * 4,
        out_specs=[VMEM, VMEM, ANY, ANY],
        scratch_shapes=collect_shapes(size)
        + [pltpu.VMEM((size, MODEL_WIDTH), low)]
        + ring_shapes(grads.shape[1], count)
        + [semaphores_for(16 * BLOCKS + 4 * count)],
        compiler_params=settings(3),
        cost_estimate=pl.CostEstimate(flops=0, bytes_accessed=128 * 2**20, transcendentals=0),
        name="exchange_backward",
    )(partial, middle, rows, gain, grads)


def last_kernel(first, second, grads, first_total, second_total, sums, *scratch):
    device = Device(scratch[-1])
    device.meet(neighbours(device))
    collects = [
        Collect(device, first, *scratch[:4]),
        Collect(device, second, *scratch[4:8]),
    ]
    ring = RingSum(device, grads, scratch[8], scratch[9], sums)
    collects[0].start()
    ring.tick(2)
    collects[1].start()
    for collect, total in zip(collects, (first_total, second_total)):
        for index in range(BLOCKS):
            collect.pass_on(index)
        ring.tick(1)

        def use(at, value):
            total[at, :] = value

        for index in range(BLOCKS):
            collect.take(index, use)
            ring.tick(1)
    ring.finish()
    for collect in collects:
        collect.finish()


def exchange_last(first, second, grads):
    size = first.shape[0] // 4
    count = lax.axis_size("w")
    half = MODEL_WIDTH // count // 2
    return pl.pallas_call(
        last_kernel,
        out_shape=[
            jax.ShapeDtypeStruct((size, MODEL_WIDTH), wide),
            jax.ShapeDtypeStruct((size, MODEL_WIDTH), wide),
            jax.ShapeDtypeStruct((2, half, grads.shape[1]), low),
        ],
        in_specs=[ANY, ANY, VMEM],
        out_specs=[VMEM, VMEM, ANY],
        scratch_shapes=collect_shapes(size) * 2
        + ring_shapes(grads.shape[1], count)
        + [semaphores_for(32 * BLOCKS + 4 * count)],
        compiler_params=settings(4),
        cost_estimate=pl.CostEstimate(flops=0, bytes_accessed=128 * 2**20, transcendentals=0),
        name="exchange_last",
    )(first, second, grads)


def deliver(total):
    core = lax.axis_index("c")
    size = total.shape[0] // 2
    mine = lax.dynamic_slice_in_dim(total, core * size, size, 0)
    other = lax.dynamic_slice_in_dim(total, (1 - core) * size, size, 0)
    other = lax.ppermute(other, "c", [(0, 1), (1, 0)])
    return jnp.stack(
        [jnp.where(core == 0, mine, other), jnp.where(core == 0, other, mine)], axis=0
    )


def take_columns(sums, start, size):
    part = sums[:, :, start : start + size].astype(wide)
    return jnp.concatenate([part[0], part[1]], axis=1)


def total_sum(values):
    for axis in ("c", "t", "w"):
        count = lax.axis_size(axis)
        if count & (count - 1):
            values = lax.psum(values, axis)
            continue
        distance = 1
        while distance < count:
            values = values + lax.ppermute(
                values, axis, [(index, index ^ distance) for index in range(count)]
            )
            distance *= 2
    return values


def local(
    tokens,
    cotangent,
    valid_len,
    pic_start,
    norm_gains,
    norm_moment,
    norm_square,
    head_gains,
    head_moment,
    head_square,
    query_weight,
    query_moment,
    query_square,
    keyvalue_matrix,
    keyvalue_first_moment,
    keyvalue_second_moment,
    headgate_weight,
    headgate_moment,
    headgate_square,
    output_weight,
    output_moment,
    output_square,
    gateup_weight,
    gateup_moment,
    gateup_square,
    down_weight,
    down_moment,
    down_square,
):
    local_rows = tokens.shape[0]
    length_value = local_rows * 2
    rows = length_value * 2
    group = lax.axis_index("w")
    core = lax.axis_index("c")
    place = lax.axis_index("t")
    heads_here = query_weight.shape[1] // HEAD_WIDTH // 2
    groups_here = keyvalue_matrix.shape[2] // HEAD_WIDTH // 2
    share = heads_here // groups_here
    score_scale = HEAD_WIDTH ** (-0.5)
    head_cols = heads_here * HEAD_WIDTH
    group_cols = groups_here * HEAD_WIDTH
    hidden_here = gateup_weight.shape[2] // 2

    chunks = 2
    chunk = hidden_here // chunks

    def chunk_columns(values, index):
        return jnp.concatenate(
            [
                values[:, (core * chunks + index) * chunk : (core * chunks + index + 1) * chunk]
                for core in range(2)
            ],
            axis=1,
        )

    bounds = [0, head_cols, group_cols, group_cols, head_cols, 128]
    edges = [sum(bounds[: i + 1]) for i in range(6)]
    quarters = []
    for index in range(2):
        pieces = []
        for matrix in (
            query_weight, keyvalue_matrix[0], keyvalue_matrix[1], output_weight.T, headgate_weight
        ):
            size = matrix.shape[1] // 2
            piece = matrix[:, index * size : (index + 1) * size].astype(low)
            pieces.append(jnp.pad(piece, ((0, 0), (0, -size % 128))))
        quarters.append(jnp.concatenate(pieces, axis=1))
    residual = tokens.astype(wide)
    attention_full, first_full, output_grad_full = gather_attention(
        jnp.where(core == 0, quarters[0], quarters[1]),
        jnp.where(core == 0, quarters[1], quarters[0]),
        normalize(residual, norm_gains[0]).astype(low),
        cotangent,
    )
    down_turned = down_weight.T
    feedforward_both = [
        fetch(
            [
                chunk_columns(values, index)
                for values in (gateup_weight[0], gateup_weight[1], down_turned)
            ]
        )
        for index in range(chunks)
    ]
    query_full, key_full, value_full, output_full, headgate_full = (
        attention_full[:, edges[i] : edges[i + 1]] for i in range(5)
    )
    query_pre = dot(first_full, query_full, 1, 0).reshape(2, length_value, heads_here, HEAD_WIDTH)
    key_pre = dot(first_full, key_full, 1, 0).reshape(2, length_value, groups_here, HEAD_WIDTH)
    value_low = (
        dot(first_full, value_full, 1, 0)
        .astype(low)
        .reshape(2, length_value, groups_here, HEAD_WIDTH)
    )
    gate_logit = dot(first_full, headgate_full, 1, 0)[:, :heads_here].reshape(
        2, length_value, heads_here
    )
    cosine, sine_table = rotary_tables(length_value, HEAD_WIDTH)
    query_low = rotate(normalize(query_pre, head_gains[0]), cosine, sine_table).astype(low)
    key_low = rotate(normalize(key_pre, head_gains[1]), cosine, sine_table).astype(low)
    valid_pair = lax.dynamic_slice_in_dim(valid_len, 2 * group, 2)
    start_pair = lax.dynamic_slice_in_dim(pic_start, 2 * group, 2)
    allowed = jax.vmap(lambda a, b: visible(length_value, a, b, PIC))(valid_pair, start_pair)
    allowed = allowed[:, None, None]
    grouped = query_low.reshape(2, length_value, groups_here, share, HEAD_WIDTH)

    def score_block():
        raw = (
            jnp.einsum("sqhgd,skhd->shgqk", grouped, key_low, preferred_element_type=wide)
            * score_scale
        )
        return jnp.where(allowed, raw, masked_score)

    scores = score_block()
    highest_score = jnp.max(scores, axis=-1, keepdims=True)
    expos = jnp.exp(scores - highest_score)
    row_total = jnp.sum(expos, axis=-1, keepdims=True)
    log_total = highest_score + jnp.log(row_total)
    probs_low = (expos / row_total).astype(low)
    mixed = jnp.einsum(
        "shgqk,skhd->sqhgd", probs_low, value_low, preferred_element_type=wide
    ).reshape(2, length_value, heads_here, HEAD_WIDTH)
    gate_value = jax.nn.sigmoid(gate_logit)
    gated_low = (mixed * gate_value[..., None]).reshape(rows, head_cols).astype(low)
    attention_local, second_full = exchange_forward(
        dot(gated_low, output_full, 1, 1).astype(low), tokens, norm_gains[1:2]
    )
    middle = residual + attention_local

    second_partial = None
    feedforward_partial = None
    up_wgrads = []
    chunk_sums = []
    for index in range(chunks):
        gate_full, up_full, down_full = (
            columns_of(feedforward_both[index], i * chunk, chunk) for i in range(3)
        )
        gate_part = dot(second_full, gate_full, 1, 0)
        up_part = dot(second_full, up_full, 1, 0)
        sigmoid_gate = jax.nn.sigmoid(gate_part)
        silu_gate = gate_part * sigmoid_gate
        hidden_low = (silu_gate * up_part).astype(low)
        hidden_grad = dot(output_grad_full, down_full, 1, 0)
        gate_grad = (
            hidden_grad * up_part * sigmoid_gate * (1.0 + gate_part * (1.0 - sigmoid_gate))
        ).astype(low)
        up_grad = (hidden_grad * silu_gate).astype(low)
        wgrads = jnp.concatenate(
            [
                dot(second_full, gate_grad, 0, 0).astype(low),
                dot(output_grad_full, hidden_low, 0, 0).astype(low),
            ],
            axis=1,
        )
        chunk_sums.append(
            deliver(lax.psum_scatter(wgrads, "w", scatter_dimension=0, tiled=True))
        )
        up_wgrads.append(dot(second_full, up_grad, 0, 0).astype(low))
        partial = dot(gate_grad, gate_full, 1, 1) + dot(up_grad, up_full, 1, 1)
        second_partial = partial if second_partial is None else second_partial + partial
        partial = dot(hidden_low, down_full, 1, 1)
        feedforward_partial = (
            partial if feedforward_partial is None else feedforward_partial + partial
        )

    middle_grad, second_gain_grad, attention_grad, up_sums = exchange_backward(
        second_partial.astype(low),
        middle,
        cotangent,
        norm_gains[1:2],
        jnp.concatenate(up_wgrads, axis=1),
    )
    second_gain_grad = second_gain_grad[0]

    output_wgrad = dot(attention_grad, gated_low, 0, 0).astype(low)
    gated_grad = dot(attention_grad, output_full, 1, 0).reshape(
        2, length_value, heads_here, HEAD_WIDTH
    )
    mixed_grad = (
        (gated_grad * gate_value[..., None])
        .astype(low)
        .reshape(2, length_value, groups_here, share, HEAD_WIDTH)
    )
    logit_grad = (
        (jnp.sum(gated_grad * mixed, axis=-1) * gate_value * (1.0 - gate_value))
        .astype(low)
        .reshape(rows, heads_here)
    )
    probs_again = jnp.exp(score_block() - log_total)
    value_grad = jnp.einsum(
        "shgqk,sqhgd->skhd", probs_again.astype(low), mixed_grad, preferred_element_type=wide
    ).astype(low)
    prob_grad = jnp.einsum("sqhgd,skhd->shgqk", mixed_grad, value_low, preferred_element_type=wide)
    score_grad = (
        probs_again * (prob_grad - jnp.sum(prob_grad * probs_again, axis=-1, keepdims=True))
    ).astype(low)
    query_rot_grad = (
        jnp.einsum("shgqk,skhd->sqhgd", score_grad, key_low, preferred_element_type=wide).reshape(
            2, length_value, heads_here, HEAD_WIDTH
        )
        * score_scale
    )
    key_rot_grad = (
        jnp.einsum("shgqk,sqhgd->skhd", score_grad, grouped, preferred_element_type=wide)
        * score_scale
    )
    query_pre_grad, query_gain_grad = norm_back(
        query_pre, head_gains[0], rotate(query_rot_grad, cosine, -sine_table)
    )
    key_pre_grad, key_gain_grad = norm_back(
        key_pre, head_gains[1], rotate(key_rot_grad, cosine, -sine_table)
    )
    projection_grad = jnp.concatenate(
        [
            query_pre_grad.reshape(rows, head_cols).astype(low),
            key_pre_grad.reshape(rows, group_cols).astype(low),
            value_grad.reshape(rows, group_cols),
        ],
        axis=1,
    )
    logit_columns = jnp.pad(logit_grad, ((0, 0), (0, 128 - heads_here)))
    first_partial = dot(projection_grad, attention_full[:, : edges[3]], 1, 1) + dot(
        logit_columns, headgate_full, 1, 1
    )
    attention_wgrad = jnp.concatenate(
        [
            dot(first_full, projection_grad, 0, 0).astype(low),
            output_wgrad,
            dot(first_full, logit_columns, 0, 0).astype(low),
        ],
        axis=1,
    )
    first_grad, feedforward_local, attention_sums = exchange_last(
        first_partial.astype(low), feedforward_partial.astype(low), attention_wgrad
    )
    tokens_partial, first_gain_grad = norm_back(residual, norm_gains[0], first_grad)
    tokens_grad = tokens_partial + middle_grad
    block_output = (middle + feedforward_local).astype(low)
    own_places = place * local_rows + jnp.arange(local_rows, dtype=jnp.int32)
    counted = (own_places < valid_pair[core]).astype(wide)[:, None]
    squares = jnp.stack(
        [
            jnp.sum(counted * residual * residual),
            jnp.sum(counted * attention_local * attention_local),
            jnp.sum(counted * feedforward_local * feedforward_local),
        ]
    )

    small = jnp.concatenate([query_gain_grad, key_gain_grad, squares])
    stats = jnp.stack(
        [
            first_gain_grad,
            second_gain_grad,
            jnp.pad(small, (0, MODEL_WIDTH - small.shape[0])),
        ]
    )
    stats = total_sum(stats)
    norms_total = stats[:2]
    heads_total = stats[2, : 2 * HEAD_WIDTH].reshape(2, HEAD_WIDTH)
    squares_total = stats[2, 2 * HEAD_WIDTH : 2 * HEAD_WIDTH + 3]
    denominator = jnp.sum(valid_len).astype(wide) * MODEL_WIDTH
    branch_scales = jnp.sqrt(squares_total / denominator)
    input_rate = MODEL_WIDTH ** (-0.5)
    down_rate = FF ** (-0.5)
    output_rate = max(QUERY_HEADS * HEAD_WIDTH // 128, 4) ** (-0.5)
    gain_rate = 0.5
    norms_new = adam_update(norm_gains, norm_moment, norm_square, norms_total, gain_rate, 0.0)
    heads_new = adam_update(head_gains, head_moment, head_square, heads_total, gain_rate, 0.0)
    gateup_sum = jnp.stack(
        [
            jnp.concatenate(
                [sums[core, :, :chunk] for core in range(2) for sums in chunk_sums], axis=1
            ).astype(wide),
            take_columns(up_sums, 0, hidden_here),
        ]
    )
    down_sum = (
        jnp.concatenate([sums[core, :, chunk:] for core in range(2) for sums in chunk_sums], axis=1)
        .astype(wide)
        .T
    )
    query_sum, key_sum, value_sum, output_sum = (
        take_columns(attention_sums, edges[i], edges[i + 1] - edges[i]) for i in range(4)
    )
    headgate_sum = take_columns(attention_sums, edges[4], heads_here)
    query_new = adam_update(
        query_weight, query_moment, query_square, query_sum, input_rate, weight_decay
    )
    keyvalue_new = adam_update(
        keyvalue_matrix,
        keyvalue_first_moment,
        keyvalue_second_moment,
        jnp.stack([key_sum, value_sum]),
        input_rate,
        weight_decay,
    )
    headgate_new = adam_update(
        headgate_weight, headgate_moment, headgate_square, headgate_sum, input_rate, weight_decay
    )
    output_new = adam_update(
        output_weight, output_moment, output_square, output_sum.T, output_rate, weight_decay
    )
    gateup_new = adam_update(
        gateup_weight, gateup_moment, gateup_square, gateup_sum, input_rate, weight_decay
    )
    down_new = adam_update(down_weight, down_moment, down_square, down_sum, down_rate, weight_decay)
    return (
        block_output,
        tokens_grad,
        branch_scales,
        *norms_new,
        *heads_new,
        *query_new,
        *keyvalue_new,
        *headgate_new,
        *output_new,
        *gateup_new,
        *down_new,
    )


def solution(mesh):
    fsdp, tp = mesh.devices.shape
    fine = Mesh(mesh.devices.reshape(fsdp // 2, 2, tp), ("w", "c", "t"))
    whole = ("w", "c")
    rows = P(("w", "c", "t"), None)
    first = P(whole, "t")
    second = P(None, whole, "t")
    last = P("t", whole)
    matrices = (first,) * 3 + (second,) * 3 + (first,) * 3 + (last,) * 3 + (second,) * 3 + (last,) * 3
    return jax.shard_map(
        local,
        mesh=fine,
        in_specs=(rows, rows, P(), P()) + (P(),) * 6 + matrices,
        out_specs=(rows, rows, P()) + (P(),) * 6 + matrices,
        check_vma=False,
    )
```

```python
import jax
import jax.numpy as jnp
from jax import lax
from jax.experimental import pallas as pl
from jax.experimental.pallas import tpu as pltpu
from jax.sharding import Mesh
from jax.sharding import PartitionSpec as P

MODEL_WIDTH = 2048
QUERY_HEADS = 16
HEAD_WIDTH = 128
FF = 6144
PIC = 256
STEP = 10

norm_epsilon = 1e-06
rope_base = 1000000.0
beta_first = 0.9
beta_second = 0.999
adam_epsilon = 1e-08
weight_decay = 0.1
masked_score = -1e30
low = jnp.bfloat16
wide = jnp.float32


def normalize(values, scaling):
    return (
        values
        * lax.rsqrt(jnp.mean(values * values, axis=-1, keepdims=True) + norm_epsilon)
        * scaling
    )


def norm_back(values, scaling, upstream):
    factor = lax.rsqrt(jnp.mean(values * values, axis=-1, keepdims=True) + norm_epsilon)
    weighted = upstream * scaling
    projected = jnp.mean(weighted * values, axis=-1, keepdims=True)
    result = factor * weighted - values * (factor * factor * factor) * projected
    return (result, jnp.sum(upstream * values * factor, axis=tuple(range(values.ndim - 1))))


def rotary_tables(length_value):
    halves = HEAD_WIDTH // 2
    frequency = rope_base ** (-(jnp.arange(halves, dtype=wide) * 2.0 / HEAD_WIDTH))
    angles = jnp.arange(length_value, dtype=wide)[:, None] * frequency[None, :]
    cosine, sine = jnp.cos(angles), jnp.sin(angles)
    return (
        jnp.concatenate([cosine, cosine], axis=1),
        jnp.concatenate([-sine, sine], axis=1),
    )


def adam_update(weight, moment, square, gradient, step_rate, decay_rate):
    moment_new = beta_first * moment + (1.0 - beta_first) * gradient
    square_new = beta_second * square + (1.0 - beta_second) * gradient * gradient
    bias_first = 1.0 - beta_first**STEP
    bias_second = 1.0 - beta_second**STEP
    update = moment_new / bias_first / (jnp.sqrt(square_new / bias_second) + adam_epsilon)
    return (weight - step_rate * (update + decay_rate * weight), moment_new, square_new)


def dot(left, right, left_dim, right_dim):
    return lax.dot_general(
        left, right, (((left_dim,), (right_dim,)), ((), ())), preferred_element_type=wide
    )


def fetch(parts):
    pieces = []
    for core in range(2):
        for part in parts:
            size = part.shape[1] // 2
            pieces.append(part[:, core * size : (core + 1) * size].astype(low))
    count = len(parts)
    local_block = jnp.stack(
        [jnp.concatenate(pieces[core * count : (core + 1) * count], axis=1) for core in range(2)]
    )
    return lax.all_gather(local_block, ("w", "c"), axis=1, tiled=True)


def columns_of(both, start, size):
    return lax.dynamic_slice(
        both, (lax.axis_index("c"), 0, start), (1, both.shape[1], size)
    ).reshape(both.shape[1], size)


MESH = pl.DeviceIdType.MESH
BLOCKS = 4
STRIP = 16
ANY = pl.BlockSpec(memory_space=pl.ANY)
VMEM = pl.BlockSpec(memory_space=pltpu.VMEM)


def ring_place(index, count):
    odd = lax.rem(index, 2)
    pair = lax.div(index, 2)
    return (1 - odd) * pair + odd * (count - 1 - pair)


def ring_index(place, count):
    late = lax.div(place, count // 2)
    return (1 - late) * 2 * place + late * (2 * (count - 1 - place) + 1)


class Device:
    def __init__(self, semaphores):
        self.w, self.c, self.t = (lax.axis_index(axis) for axis in ("w", "c", "t"))
        self.count = lax.axis_size("w")
        self.place = ring_place(self.w, self.count)
        self.semaphores = semaphores
        self.used = 0
        self.other_core = {"c": 1 - self.c}
        self.other_row = {"t": 1 - self.t}

    def owner(self, distance):
        return ring_index(lax.rem(self.place + distance + self.count, self.count), self.count)

    def meet(self, partners):
        barrier = pltpu.get_barrier_semaphore()
        for partner in partners:
            pl.semaphore_signal(barrier, inc=1, device_id=partner, device_id_type=MESH)
        pl.semaphore_wait(barrier, len(partners))

    def remote(self, source, target, device):
        slot = self.used
        self.used += 1
        return pltpu.make_async_remote_copy(
            src_ref=source,
            dst_ref=target,
            send_sem=self.semaphores.at[0, slot],
            recv_sem=self.semaphores.at[1, slot],
            device_id=device,
            device_id_type=MESH,
        )

    def inside(self, source, target):
        slot = self.used
        self.used += 1
        return pltpu.make_async_copy(source, target, self.semaphores.at[0, slot])


def rows_at(start, size):
    return pl.ds(pl.multiple_of(start, STRIP), size)


class Spread:
    def __init__(self, device, full):
        self.device, self.full = device, full
        self.size = full.shape[0] // 4
        self.block = self.size // BLOCKS
        self.rows, self.core, self.passed, self.kept = {}, {}, {}, {}

    def where(self, core, row, index):
        return self.full.at[
            rows_at((core * 2 + row) * self.size + index * self.block, self.block)
        ]

    def put(self, index, source):
        device = self.device
        target = self.where(device.c, device.t, index)
        self.rows[index] = device.remote(source, target, device.other_row)
        self.core[index] = device.remote(source, target, device.other_core)
        self.kept[index] = device.inside(source, target)
        for copy in (self.rows[index], self.core[index], self.kept[index]):
            copy.start()

    def forward(self, index):
        device = self.device
        self.rows[index].wait_recv()
        place = self.where(device.c, 1 - device.t, index)
        self.passed[index] = device.remote(place, place, device.other_core)
        self.passed[index].start()

    def finish(self):
        for index in range(BLOCKS):
            self.rows[index].wait_send()
            self.core[index].wait()
            self.passed[index].wait()
            self.kept[index].wait()


class Collect:
    def __init__(self, device, partial, near, far, sent, came):
        self.device = device
        self.partial, self.near, self.far, self.sent, self.came = partial, near, far, sent, came
        self.size = partial.shape[0] // 4
        self.block = self.size // BLOCKS
        self.core, self.rows = {}, {}

    def start(self):
        device = self.device
        self.load = device.inside(
            self.partial.at[rows_at(device.c * 2 * self.size, 2 * self.size)], self.near
        )
        for part, row in enumerate((1 - device.t, device.t)):
            for index in range(BLOCKS):
                start = row * self.size + index * self.block
                copy = device.remote(
                    self.partial.at[rows_at((1 - device.c) * 2 * self.size + start, self.block)],
                    self.far.at[rows_at(start, self.block)],
                    device.other_core,
                )
                copy.start()
                self.core[part, index] = copy
        self.load.start()

    def pass_on(self, index):
        device = self.device
        if index == 0:
            self.load.wait()
        self.core[0, index].wait_recv()

        @pl.loop(0, self.block // STRIP)
        def _(strip):
            at = index * self.block + strip * STRIP
            rows = rows_at((1 - device.t) * self.size + at, STRIP)
            total = self.near[rows, :].astype(wide) + self.far[rows, :].astype(wide)
            self.sent[rows_at(at, STRIP), :] = total.astype(low)

        place = rows_at(index * self.block, self.block)
        self.rows[index] = device.remote(
            self.sent.at[place], self.came.at[place], device.other_row
        )
        self.rows[index].start()

    def take(self, index, use):
        device = self.device
        self.core[1, index].wait_recv()
        self.rows[index].wait_recv()

        @pl.loop(0, self.block // STRIP)
        def _(strip):
            at = index * self.block + strip * STRIP
            rows = rows_at(device.t * self.size + at, STRIP)
            mine = rows_at(at, STRIP)
            total = (
                self.near[rows, :].astype(wide)
                + self.far[rows, :].astype(wide)
                + self.came[mine, :].astype(wide)
            )
            use(mine, total)

    def finish(self):
        for index in range(BLOCKS):
            self.core[0, index].wait_send()
            self.core[1, index].wait_send()
            self.rows[index].wait_send()


class RingSum:
    def __init__(self, device, grads, slots, totals, sums):
        self.device, self.grads, self.slots = device, grads, slots
        self.totals, self.sums = totals, sums
        self.half = grads.shape[0] // device.count // 2
        self.parts = 2
        self.part = self.half // self.parts
        self.copies = {}
        self.ticks = [
            (step, part) for step in range(device.count) for part in range(self.parts)
        ]

    def own(self, way, distance, part):
        direction = 1 - 2 * way
        owner = self.device.owner(-direction * distance)
        return rows_at((owner * 2 + way) * self.half + part * self.part, self.part)

    def slot(self, way, step, part):
        return self.slots.at[
            way * (self.device.count - 1) + step, pl.ds(part * self.part, self.part)
        ]

    def send(self, way, step, part):
        device = self.device
        if step == 0:
            source = self.grads.at[self.own(way, 1, part)]
        else:
            source = self.slot(way, step - 1, part)
        copy = device.remote(
            source, self.slot(way, step, part), {"w": device.owner(1 - 2 * way)}
        )
        copy.start()
        self.copies[way, step, part] = copy

    def tick(self, count=1):
        device = self.device
        for _ in range(count):
            if not self.ticks:
                return
            step, part = self.ticks.pop(0)
            for way in range(2):
                if step > 0:
                    self.copies[way, step - 1, part].wait_recv()
                    own = self.own(way, step + 1, part)
                    slot = self.slot(way, step - 1, part)
                    total = (slot[...].astype(wide) + self.grads[own, :].astype(wide)).astype(low)
                    if step < device.count - 1:
                        slot[...] = total
                    else:
                        self.totals[way, pl.ds(part * self.part, self.part), :] = total
                if step < device.count - 1:
                    self.send(way, step, part)

    def finish(self):
        device = self.device
        self.tick(len(self.ticks))
        away = device.remote(
            self.totals.at[1 - device.c], self.sums.at[device.c], device.other_core
        )
        kept = device.inside(self.totals.at[device.c], self.sums.at[device.c])
        away.start()
        kept.start()
        for copy in self.copies.values():
            copy.wait_send()
        away.wait()
        kept.wait()


def ring_shapes(columns, count):
    half = MODEL_WIDTH // count // 2
    return [
        pltpu.VMEM((2 * (count - 1), half, columns), low),
        pltpu.VMEM((2, half, columns), low),
    ]


def collect_shapes(size):
    return [
        pltpu.VMEM((2 * size, MODEL_WIDTH), low),
        pltpu.VMEM((2 * size, MODEL_WIDTH), low),
        pltpu.VMEM((size, MODEL_WIDTH), low),
        pltpu.VMEM((size, MODEL_WIDTH), low),
    ]


def semaphores_for(count):
    return pltpu.SemaphoreType.DMA((2, count))


def settings(collective):
    return pltpu.CompilerParams(
        collective_id=collective, has_side_effects=True, vmem_limit_bytes=48 * 2**20
    )


def neighbours(device):
    return [
        device.other_core,
        device.other_row,
        {"w": device.owner(1)},
        {"w": device.owner(-1)},
    ]


def gather_kernel(mine, other, first, second, full, first_full, second_full, semaphores):
    device = Device(semaphores)
    device.meet(neighbours(device))
    size = mine.shape[0]
    here = rows_at((device.w * 2 + device.c) * size, size)
    kept = device.inside(mine, full.at[here])
    crossed = device.remote(other, full.at[here], device.other_core)
    kept.start()
    crossed.start()
    spreads = []
    for rows, target in ((first, first_full), (second, second_full)):
        spread = Spread(device, target)
        block = spread.block
        for index in range(BLOCKS):
            spread.put(index, rows.at[pl.ds(index * block, block)])
        spreads.append(spread)
    kept.wait()
    crossed.wait()
    parts = 2
    part_rows = size // parts
    copies = {}
    waiting = [(spread, index) for spread in spreads for index in range(BLOCKS)]

    def piece(way, distance, part):
        owner = device.owner(-(1 - 2 * way) * distance)
        return full.at[rows_at((owner * 2 + way) * size + part * part_rows, part_rows)]

    for step in range(device.count - 1):
        for part in range(parts):
            for way in range(2):
                if step > 0:
                    copies[way, step - 1, part].wait_recv()
                block = piece(way, step, part)
                copy = device.remote(block, block, {"w": device.owner(1 - 2 * way)})
                copy.start()
                copies[way, step, part] = copy
        if waiting:
            spread, index = waiting.pop(0)
            spread.forward(index)
    for spread, index in waiting:
        spread.forward(index)
    for part in range(parts):
        for way in range(2):
            copies[way, device.count - 2, part].wait_recv()
    for copy in copies.values():
        copy.wait_send()
    for spread in spreads:
        spread.finish()


def gather_attention(mine, other, first, second):
    count = lax.axis_size("w")
    rows = first.shape[0] * 4
    return pl.pallas_call(
        gather_kernel,
        out_shape=[
            jax.ShapeDtypeStruct((MODEL_WIDTH, mine.shape[1]), low),
            jax.ShapeDtypeStruct((rows, MODEL_WIDTH), low),
            jax.ShapeDtypeStruct((rows, MODEL_WIDTH), low),
        ],
        in_specs=[ANY] * 4,
        out_specs=[ANY] * 3,
        scratch_shapes=[semaphores_for(4 * (count - 1) + 8 * BLOCKS + 2)],
        compiler_params=settings(1),
        cost_estimate=pl.CostEstimate(flops=0, bytes_accessed=64 * 2**20, transcendentals=0),
        name="gather_attention",
    )(mine, other, first, second)


def forward_kernel(partial, rows, gain, total, full, near, far, sent, came, normed, semaphores):
    device = Device(semaphores)
    device.meet([device.other_core, device.other_row])
    collect = Collect(device, partial, near, far, sent, came)
    spread = Spread(device, full)
    collect.start()
    for index in range(BLOCKS):
        collect.pass_on(index)

    def use(at, value):
        total[at, :] = value
        middle = rows[at, :].astype(wide) + value
        normed[at, :] = normalize(middle, gain[...]).astype(low)

    for index in range(BLOCKS):
        collect.take(index, use)
        spread.put(index, normed.at[pl.ds(index * spread.block, spread.block)])
        if index > 0:
            spread.forward(index - 1)
    spread.forward(BLOCKS - 1)
    spread.finish()
    collect.finish()


def exchange_forward(partial, rows, gain):
    size = rows.shape[0]
    return pl.pallas_call(
        forward_kernel,
        out_shape=[
            jax.ShapeDtypeStruct((size, MODEL_WIDTH), wide),
            jax.ShapeDtypeStruct((4 * size, MODEL_WIDTH), low),
        ],
        in_specs=[ANY, VMEM, VMEM],
        out_specs=[VMEM, ANY],
        scratch_shapes=collect_shapes(size)
        + [pltpu.VMEM((size, MODEL_WIDTH), low), semaphores_for(16 * BLOCKS)],
        compiler_params=settings(2),
        cost_estimate=pl.CostEstimate(flops=0, bytes_accessed=64 * 2**20, transcendentals=0),
        name="exchange_forward",
    )(partial, rows, gain)


class Rings:
    def __init__(self, rings):
        self.rings = rings
        self.next = 0

    def tick(self, count=1):
        for _ in range(count):
            self.rings[self.next].tick()
            self.next = (self.next + 1) % len(self.rings)

    def finish(self):
        while any(ring.ticks for ring in self.rings):
            self.tick()
        for ring in self.rings:
            ring.finish()


def norm_back_rows(values, gain, upstream):
    factor = lax.rsqrt(jnp.mean(values * values, axis=-1, keepdims=True) + norm_epsilon)
    weighted = upstream * gain
    projected = jnp.mean(weighted * values, axis=-1, keepdims=True)
    result = factor * weighted - values * (factor * factor * factor) * projected
    return result, jnp.sum(upstream * values * factor, axis=0, keepdims=True)


def backward_kernel(
    partial, middle, rows, gain, grads, grad, gain_grad, full, sums,
    near, far, sent, came, rounded, slots, totals, semaphores,
):
    device = Device(semaphores)
    device.meet(neighbours(device))
    collect = Collect(device, partial, near, far, sent, came)
    spread = Spread(device, full)
    ring = RingSum(device, grads, slots, totals, sums)
    collect.start()
    ring.tick(2)
    gain_grad[...] = jnp.zeros_like(gain_grad)
    for index in range(BLOCKS):
        collect.pass_on(index)
    ring.tick(1)

    def use(at, upstream):
        result, gained = norm_back_rows(middle[at, :], gain[...], upstream)
        result = result + rows[at, :].astype(wide)
        grad[at, :] = result
        rounded[at, :] = result.astype(low)
        gain_grad[...] += gained

    for index in range(BLOCKS):
        collect.take(index, use)
        spread.put(index, rounded.at[pl.ds(index * spread.block, spread.block)])
        ring.tick(2)
        if index > 0:
            spread.forward(index - 1)
    ring.tick(1)
    spread.forward(BLOCKS - 1)
    ring.finish()
    spread.finish()
    collect.finish()


def ring_outputs(grads):
    half = MODEL_WIDTH // lax.axis_size("w") // 2
    return [jax.ShapeDtypeStruct((2, half, value.shape[1]), low) for value in grads]


def exchange_backward(partial, middle, rows, gain, grads):
    size = rows.shape[0]
    count = lax.axis_size("w")
    return pl.pallas_call(
        backward_kernel,
        out_shape=[
            jax.ShapeDtypeStruct((size, MODEL_WIDTH), wide),
            jax.ShapeDtypeStruct((1, MODEL_WIDTH), wide),
            jax.ShapeDtypeStruct((4 * size, MODEL_WIDTH), low),
            *ring_outputs([grads]),
        ],
        in_specs=[ANY] + [VMEM] * 4,
        out_specs=[VMEM, VMEM, ANY, ANY],
        scratch_shapes=collect_shapes(size)
        + [pltpu.VMEM((size, MODEL_WIDTH), low)]
        + ring_shapes(grads.shape[1], count)
        + [semaphores_for(16 * BLOCKS + 4 * count)],
        compiler_params=settings(3),
        cost_estimate=pl.CostEstimate(flops=0, bytes_accessed=128 * 2**20, transcendentals=0),
        name="exchange_backward",
    )(partial, middle, rows, gain, grads)


class Total:
    def __init__(self, device, mine, crossed, gathered):
        self.device, self.mine = device, mine
        self.crossed, self.gathered = crossed, gathered
        self.copies = {}
        self.steps = [("c", 0), ("t", 0)] + [("w", step) for step in range(device.count // 2)]

    def tick(self):
        device = self.device
        if not self.steps:
            return
        axis, step = self.steps.pop(0)
        if axis != "w":
            slot = 0 if axis == "c" else 1
            partner = device.other_core if axis == "c" else device.other_row
            copy = device.remote(self.mine.at[slot], self.crossed.at[slot], partner)
            copy.start()
            copy.wait()
            total = self.mine[slot] + self.crossed[slot]
            if slot == 0:
                self.mine[1] = total
            else:
                self.gathered[device.w] = total
            return
        for way in range(2):
            if way == 1 and step == device.count // 2 - 1:
                continue
            if step > 0:
                self.copies[way, step - 1].wait_recv()
            block = self.gathered.at[device.owner(-(1 - 2 * way) * step)]
            copy = device.remote(block, block, {"w": device.owner(1 - 2 * way)})
            copy.start()
            self.copies[way, step] = copy

    def finish(self, target):
        while self.steps:
            self.tick()
        half = self.device.count // 2
        self.copies[0, half - 1].wait_recv()
        self.copies[1, half - 2].wait_recv()
        for copy in self.copies.values():
            copy.wait_send()
        target[...] = self.gathered[0]
        for index in range(1, self.device.count):
            target[...] += self.gathered[index]


def last_kernel(
    first, second, tokens, gain, middle_grad, counted, stats, *refs
):
    grads, refs = refs[:3], refs[3:]
    first_total, second_total, stats_total, refs = refs[0], refs[1], refs[2], refs[3:]
    sums, scratch = refs[:3], refs[3:]
    device = Device(scratch[-1])
    device.meet(neighbours(device))
    first_collect = Collect(device, first, *scratch[:4])
    second_collect = Collect(device, second, *scratch[4:8])
    mine, crossed, gathered = scratch[8:11]
    rings = Rings(
        [
            RingSum(device, grads[i], scratch[11 + 2 * i], scratch[12 + 2 * i], sums[i])
            for i in range(3)
        ]
    )
    total = Total(device, mine, crossed, gathered)
    mine[0] = stats[...]
    second_collect.start()
    rings.tick(3)
    first_collect.start()

    def use_second(at, value):
        second_total[at, :] = value
        mine[0, 3:4, :] += jnp.sum(counted[at, :] * value * value, axis=0, keepdims=True)

    def use_first(at, upstream):
        result, gained = norm_back_rows(tokens[at, :].astype(wide), gain[...], upstream)
        first_total[at, :] = result + middle_grad[at, :]
        mine[0, 0:1, :] += gained

    for index in range(BLOCKS):
        second_collect.pass_on(index)
    rings.tick(3)
    for index in range(BLOCKS):
        first_collect.pass_on(index)
        rings.tick(1)
    for index in range(BLOCKS):
        second_collect.take(index, use_second)
        rings.tick(2)
    for index in range(BLOCKS):
        first_collect.take(index, use_first)
        rings.tick(2)
    while total.steps:
        total.tick()
        rings.tick(1)
    rings.finish()
    total.finish(stats_total)
    second_collect.finish()
    first_collect.finish()


def exchange_last(first, second, tokens, gain, middle_grad, counted, stats, grads):
    size = tokens.shape[0]
    count = lax.axis_size("w")
    return pl.pallas_call(
        last_kernel,
        out_shape=[
            jax.ShapeDtypeStruct((size, MODEL_WIDTH), wide),
            jax.ShapeDtypeStruct((size, MODEL_WIDTH), wide),
            jax.ShapeDtypeStruct(stats.shape, wide),
            *ring_outputs(grads),
        ],
        in_specs=[ANY, ANY] + [VMEM] * (5 + len(grads)),
        out_specs=[VMEM] * 3 + [ANY] * len(grads),
        scratch_shapes=collect_shapes(size) * 2
        + [
            pltpu.VMEM((2, *stats.shape), wide),
            pltpu.VMEM((2, *stats.shape), wide),
            pltpu.VMEM((count, *stats.shape), wide),
        ]
        + [shape for value in grads for shape in ring_shapes(value.shape[1], count)]
        + [semaphores_for(32 * BLOCKS + 16 * count)],
        compiler_params=settings(4),
        cost_estimate=pl.CostEstimate(flops=0, bytes_accessed=128 * 2**20, transcendentals=0),
        name="exchange_last",
    )(first, second, tokens, gain, middle_grad, counted, stats, *grads)


def head_rows(values, gain, cosine, sine):
    factor = lax.rsqrt(jnp.mean(values * values, axis=-1, keepdims=True) + norm_epsilon)
    normed = values * factor * gain
    return (normed * cosine + pltpu.roll(normed, HEAD_WIDTH // 2, 1) * sine).astype(low)


def head_back(values, gain, cosine, sine, upstream):
    turned = upstream * cosine - pltpu.roll(upstream, HEAD_WIDTH // 2, 1) * sine
    return norm_back_rows(values, gain, turned)


def head_at(index):
    return slice(index * HEAD_WIDTH, (index + 1) * HEAD_WIDTH)


def gate_column(logits, head):
    lanes = lax.broadcasted_iota(jnp.int32, logits.shape, 1)
    logit = jnp.sum(jnp.where(lanes == head, logits, 0.0), axis=-1, keepdims=True)
    return jax.nn.sigmoid(logit)


def probabilities(queries, keys, start, valid_count, piece_start):
    raw = dot(queries, keys, 1, 1) * HEAD_WIDTH ** (-0.5)
    row = start + lax.broadcasted_iota(jnp.int32, raw.shape, 0)
    column = lax.broadcasted_iota(jnp.int32, raw.shape, 1)
    last = piece_start + PIC
    inside = (row >= piece_start) & (row < last) & (column >= piece_start) & (column < last)
    allowed = (column < valid_count) & ((column <= row) | inside)
    scores = jnp.where(allowed, raw, masked_score)
    expos = jnp.exp(scores - jnp.max(scores, axis=-1, keepdims=True))
    return expos * (1.0 / jnp.sum(expos, axis=-1, keepdims=True))


QUERY_ROWS = 256


def attention_forward_kernel(groups, share, valid, start, pre, gains, cosine, sine, gated):
    sequence = pl.program_id(0)
    heads = groups * share
    length = pre.shape[0]
    for group in range(groups):
        keys = head_rows(pre[:, head_at(heads + group)], gains[1:2, :], cosine[...], sine[...])
        values = pre[:, head_at(heads + groups + group)].astype(low)
        for head in range(group * share, (group + 1) * share):
            for at in range(0, length, QUERY_ROWS):
                rows = slice(at, at + QUERY_ROWS)
                queries = head_rows(
                    pre[rows, head_at(head)], gains[0:1, :], cosine[rows, :], sine[rows, :]
                )
                probs = probabilities(queries, keys, at, valid[sequence], start[sequence])
                mixed = dot(probs.astype(low), values, 1, 0)
                gate = gate_column(pre[rows, head_at(heads + 2 * groups)], head)
                gated[rows, head_at(head)] = (mixed * gate).astype(low)


def attention_backward_kernel(
    groups, share, valid, start, pre, upstream, gains, cosine, sine, grads, gain_grads
):
    sequence = pl.program_id(0)
    heads = groups * share
    length = pre.shape[0]
    scale = HEAD_WIDTH ** (-0.5)

    @pl.when(sequence == 0)
    def _():
        gain_grads[...] = jnp.zeros_like(gain_grads)

    logit_grads = [jnp.zeros((QUERY_ROWS, HEAD_WIDTH), wide)] * (length // QUERY_ROWS)
    for group in range(groups):
        key_pre = pre[:, head_at(heads + group)]
        keys = head_rows(key_pre, gains[1:2, :], cosine[...], sine[...])
        values = pre[:, head_at(heads + groups + group)].astype(low)
        value_grad = jnp.zeros((length, HEAD_WIDTH), wide)
        key_grad = jnp.zeros((length, HEAD_WIDTH), wide)
        for head in range(group * share, (group + 1) * share):
            for block, at in enumerate(range(0, length, QUERY_ROWS)):
                rows = slice(at, at + QUERY_ROWS)
                query_pre = pre[rows, head_at(head)]
                queries = head_rows(query_pre, gains[0:1, :], cosine[rows, :], sine[rows, :])
                probs = probabilities(queries, keys, at, valid[sequence], start[sequence])
                probs_low = probs.astype(low)
                mixed = dot(probs_low, values, 1, 0)
                gate = gate_column(pre[rows, head_at(heads + 2 * groups)], head)
                gated_grad = upstream[rows, head_at(head)]
                mixed_grad = (gated_grad * gate).astype(low)
                logit_grad = (
                    jnp.sum(gated_grad * mixed, axis=-1, keepdims=True) * gate * (1.0 - gate)
                )
                lanes = lax.broadcasted_iota(jnp.int32, (QUERY_ROWS, HEAD_WIDTH), 1)
                logit_grads[block] = logit_grads[block] + jnp.where(lanes == head, logit_grad, 0.0)
                value_grad = value_grad + dot(probs_low, mixed_grad, 0, 0)
                prob_grad = dot(mixed_grad, values, 1, 1)
                score_grad = (
                    probs * (prob_grad - jnp.sum(prob_grad * probs, axis=-1, keepdims=True))
                ).astype(low)
                key_grad = key_grad + dot(score_grad, queries, 0, 0)
                query_grad, gained = head_back(
                    query_pre,
                    gains[0:1, :],
                    cosine[rows, :],
                    sine[rows, :],
                    dot(score_grad, keys, 1, 0) * scale,
                )
                grads[rows, head_at(head)] = query_grad.astype(low)
                gain_grads[0:1, :] += gained
        key_grad, gained = head_back(
            key_pre, gains[1:2, :], cosine[...], sine[...], key_grad * scale
        )
        gain_grads[1:2, :] += gained
        grads[:, head_at(heads + group)] = key_grad.astype(low)
        grads[:, head_at(heads + groups + group)] = value_grad.astype(low)
    for block, at in enumerate(range(0, length, QUERY_ROWS)):
        grads[slice(at, at + QUERY_ROWS), head_at(heads + 2 * groups)] = logit_grads[block].astype(
            low
        )


def sequence_block(columns, length):
    return pl.BlockSpec((length, columns), lambda sequence: (sequence, 0))


def fixed_block(*shape):
    return pl.BlockSpec(shape, lambda sequence: (0, 0))


SCALARS = pl.BlockSpec(memory_space=pltpu.SMEM)


def attention_forward(groups, share, valid, start, pre, gains, cosine, sine):
    length, columns = cosine.shape[0], groups * share * HEAD_WIDTH

    def body(*refs):
        attention_forward_kernel(groups, share, *refs)

    return pl.pallas_call(
        body,
        grid=(pre.shape[0] // length,),
        out_shape=jax.ShapeDtypeStruct((pre.shape[0], columns), low),
        in_specs=[
            SCALARS,
            SCALARS,
            sequence_block(pre.shape[1], length),
            fixed_block(2, HEAD_WIDTH),
            fixed_block(length, HEAD_WIDTH),
            fixed_block(length, HEAD_WIDTH),
        ],
        out_specs=sequence_block(columns, length),
        compiler_params=pltpu.CompilerParams(vmem_limit_bytes=48 * 2**20),
        cost_estimate=pl.CostEstimate(
            flops=2**30, bytes_accessed=8 * 2**20, transcendentals=2**21
        ),
        name="attention_forward",
    )(valid, start, pre, gains, cosine, sine)


def attention_backward(groups, share, valid, start, pre, upstream, gains, cosine, sine):
    length = cosine.shape[0]

    def body(*refs):
        attention_backward_kernel(groups, share, *refs)

    return pl.pallas_call(
        body,
        grid=(pre.shape[0] // length,),
        out_shape=[
            jax.ShapeDtypeStruct(pre.shape, low),
            jax.ShapeDtypeStruct((2, HEAD_WIDTH), wide),
        ],
        in_specs=[
            SCALARS,
            SCALARS,
            sequence_block(pre.shape[1], length),
            sequence_block(upstream.shape[1], length),
            fixed_block(2, HEAD_WIDTH),
            fixed_block(length, HEAD_WIDTH),
            fixed_block(length, HEAD_WIDTH),
        ],
        out_specs=[sequence_block(pre.shape[1], length), fixed_block(2, HEAD_WIDTH)],
        compiler_params=pltpu.CompilerParams(vmem_limit_bytes=48 * 2**20),
        cost_estimate=pl.CostEstimate(
            flops=2**32, bytes_accessed=12 * 2**20, transcendentals=2**21
        ),
        name="attention_backward",
    )(valid, start, pre, upstream, gains, cosine, sine)


def deliver(total):
    core = lax.axis_index("c")
    size = total.shape[0] // 2
    mine = lax.dynamic_slice_in_dim(total, core * size, size, 0)
    other = lax.dynamic_slice_in_dim(total, (1 - core) * size, size, 0)
    other = lax.ppermute(other, "c", [(0, 1), (1, 0)])
    return jnp.stack(
        [jnp.where(core == 0, mine, other), jnp.where(core == 0, other, mine)], axis=0
    )


def take_columns(sums, start, size):
    part = sums[:, :, start : start + size].astype(wide)
    return jnp.concatenate([part[0], part[1]], axis=1)


def local(
    tokens,
    cotangent,
    valid_len,
    pic_start,
    norm_gains,
    norm_moment,
    norm_square,
    head_gains,
    head_moment,
    head_square,
    query_weight,
    query_moment,
    query_square,
    keyvalue_matrix,
    keyvalue_first_moment,
    keyvalue_second_moment,
    headgate_weight,
    headgate_moment,
    headgate_square,
    output_weight,
    output_moment,
    output_square,
    gateup_weight,
    gateup_moment,
    gateup_square,
    down_weight,
    down_moment,
    down_square,
):
    local_rows = tokens.shape[0]
    length_value = local_rows * 2
    rows = length_value * 2
    group = lax.axis_index("w")
    core = lax.axis_index("c")
    place = lax.axis_index("t")
    heads_here = query_weight.shape[1] // HEAD_WIDTH // 2
    groups_here = keyvalue_matrix.shape[2] // HEAD_WIDTH // 2
    share = heads_here // groups_here
    head_cols = heads_here * HEAD_WIDTH
    group_cols = groups_here * HEAD_WIDTH
    hidden_here = gateup_weight.shape[2] // 2

    chunks = 2
    chunk = hidden_here // chunks

    def chunk_columns(values, index):
        return jnp.concatenate(
            [
                values[:, (core * chunks + index) * chunk : (core * chunks + index + 1) * chunk]
                for core in range(2)
            ],
            axis=1,
        )

    bounds = [0, head_cols, group_cols, group_cols, 128, head_cols]
    edges = [sum(bounds[: i + 1]) for i in range(6)]
    quarters = []
    for index in range(2):
        pieces = []
        for matrix in (
            query_weight, keyvalue_matrix[0], keyvalue_matrix[1], headgate_weight, output_weight.T
        ):
            size = matrix.shape[1] // 2
            piece = matrix[:, index * size : (index + 1) * size].astype(low)
            pieces.append(jnp.pad(piece, ((0, 0), (0, -size % 128))))
        quarters.append(jnp.concatenate(pieces, axis=1))
    residual = tokens.astype(wide)
    attention_full, first_full, output_grad_full = gather_attention(
        jnp.where(core == 0, quarters[0], quarters[1]),
        jnp.where(core == 0, quarters[1], quarters[0]),
        normalize(residual, norm_gains[0]).astype(low),
        cotangent,
    )
    down_turned = down_weight.T
    feedforward_both = [
        fetch(
            [
                chunk_columns(values, index)
                for values in (gateup_weight[0], gateup_weight[1], down_turned)
            ]
        )
        for index in range(chunks)
    ]
    projection_full, output_full = attention_full[:, : edges[4]], attention_full[:, edges[4] :]
    valid_pair = lax.dynamic_slice_in_dim(valid_len, 2 * group, 2)
    start_pair = lax.dynamic_slice_in_dim(pic_start, 2 * group, 2)
    cosine, sine = rotary_tables(length_value)
    projected = dot(first_full, projection_full, 1, 0)
    gated_low = attention_forward(
        groups_here, share, valid_pair, start_pair, projected, head_gains, cosine, sine
    )
    attention_local, second_full = exchange_forward(
        dot(gated_low, output_full, 1, 1).astype(low), tokens, norm_gains[1:2]
    )
    middle = residual + attention_local

    held = []
    second_partial = None
    for index in range(chunks):
        gate_full, up_full, down_full = (
            columns_of(feedforward_both[index], i * chunk, chunk) for i in range(3)
        )
        gate_part = dot(second_full, gate_full, 1, 0)
        up_part = dot(second_full, up_full, 1, 0)
        sigmoid_gate = jax.nn.sigmoid(gate_part)
        silu_gate = gate_part * sigmoid_gate
        hidden_low = (silu_gate * up_part).astype(low)
        hidden_grad = dot(output_grad_full, down_full, 1, 0)
        gate_grad = (
            hidden_grad * up_part * sigmoid_gate * (1.0 + gate_part * (1.0 - sigmoid_gate))
        ).astype(low)
        up_grad = (hidden_grad * silu_gate).astype(low)
        partial = dot(gate_grad, gate_full, 1, 1) + dot(up_grad, up_full, 1, 1)
        second_partial = partial if second_partial is None else second_partial + partial
        held.append((gate_grad, up_grad, hidden_low, down_full))

    def product(left, right):
        return dot(left, right, 0, 0).astype(low)

    gate_grad, up_grad, hidden_low, down_full = held[0]
    early_sums = deliver(
        lax.psum_scatter(
            jnp.concatenate(
                [product(second_full, gate_grad), product(output_grad_full, hidden_low)], axis=1
            ),
            "w",
            scatter_dimension=0,
            tiled=True,
        )
    )
    feedforward_partial = dot(hidden_low, down_full, 1, 1)
    middle_grad, second_gain_grad, attention_grad, first_up_sums = exchange_backward(
        second_partial.astype(low),
        middle,
        cotangent,
        norm_gains[1:2],
        product(second_full, up_grad),
    )
    second_gain_grad = second_gain_grad[0]
    gate_grad, up_grad, hidden_low, down_full = held[1]
    attention_grad, gate_grad, up_grad, hidden_low = lax.optimization_barrier(
        (attention_grad, gate_grad, up_grad, hidden_low)
    )
    late_sums = deliver(
        lax.psum_scatter(
            product(output_grad_full, hidden_low), "w", scatter_dimension=0, tiled=True
        )
    )
    feedforward_partial = feedforward_partial + dot(hidden_low, down_full, 1, 1)

    projected_grad, head_gain_grads = attention_backward(
        groups_here,
        share,
        valid_pair,
        start_pair,
        projected,
        dot(attention_grad, output_full, 1, 0),
        head_gains,
        cosine,
        sine,
    )
    first_partial = dot(projected_grad, projection_full, 1, 1)
    attention_wgrad = jnp.concatenate(
        [product(first_full, projected_grad), product(attention_grad, gated_low)], axis=1
    )
    own_places = place * local_rows + jnp.arange(local_rows, dtype=jnp.int32)
    counted = (own_places < valid_pair[core]).astype(wide)[:, None]
    squares = jnp.stack(
        [
            jnp.sum(counted * residual * residual),
            jnp.sum(counted * attention_local * attention_local),
        ]
    )
    small = jnp.concatenate([head_gain_grads.reshape(-1), squares])
    nothing = jnp.zeros((1, MODEL_WIDTH), wide)
    stats = jnp.concatenate(
        [
            nothing,
            second_gain_grad[None],
            jnp.pad(small, (0, MODEL_WIDTH - small.shape[0]))[None],
            jnp.tile(nothing, (5, 1)),
        ]
    )
    tokens_grad, feedforward_local, stats, second_up_sums, second_gate_sums, attention_sums = (
        exchange_last(
            first_partial.astype(low),
            feedforward_partial.astype(low),
            tokens,
            norm_gains[0:1],
            middle_grad,
            counted,
            stats,
            [
                product(second_full, up_grad),
                product(second_full, gate_grad),
                attention_wgrad,
            ],
        )
    )
    block_output = (middle + feedforward_local).astype(low)
    norms_total = stats[:2]
    heads_total = stats[2, : 2 * HEAD_WIDTH].reshape(2, HEAD_WIDTH)
    squares_total = jnp.concatenate(
        [stats[2, 2 * HEAD_WIDTH : 2 * HEAD_WIDTH + 2], jnp.sum(stats[3], keepdims=True)]
    )
    denominator = jnp.sum(valid_len).astype(wide) * MODEL_WIDTH
    branch_scales = jnp.sqrt(squares_total / denominator)
    input_rate = MODEL_WIDTH ** (-0.5)
    down_rate = FF ** (-0.5)
    output_rate = max(QUERY_HEADS * HEAD_WIDTH // 128, 4) ** (-0.5)
    gain_rate = 0.5
    norms_new = adam_update(norm_gains, norm_moment, norm_square, norms_total, gain_rate, 0.0)
    heads_new = adam_update(head_gains, head_moment, head_square, heads_total, gain_rate, 0.0)
    def both_columns(first_sums, second_sums):
        return jnp.concatenate(
            [sums[index] for index in range(2) for sums in (first_sums, second_sums)], axis=1
        ).astype(wide)

    gateup_sum = jnp.stack(
        [
            both_columns(early_sums[:, :, :chunk], second_gate_sums),
            both_columns(first_up_sums, second_up_sums),
        ]
    )
    down_sum = both_columns(early_sums[:, :, chunk:], late_sums).T
    query_sum, key_sum, value_sum = (
        take_columns(attention_sums, edges[i], edges[i + 1] - edges[i]) for i in range(3)
    )
    headgate_sum = take_columns(attention_sums, edges[3], heads_here)
    output_sum = take_columns(attention_sums, edges[4], head_cols)
    query_new = adam_update(
        query_weight, query_moment, query_square, query_sum, input_rate, weight_decay
    )
    keyvalue_new = adam_update(
        keyvalue_matrix,
        keyvalue_first_moment,
        keyvalue_second_moment,
        jnp.stack([key_sum, value_sum]),
        input_rate,
        weight_decay,
    )
    headgate_new = adam_update(
        headgate_weight, headgate_moment, headgate_square, headgate_sum, input_rate, weight_decay
    )
    output_new = adam_update(
        output_weight, output_moment, output_square, output_sum.T, output_rate, weight_decay
    )
    gateup_new = adam_update(
        gateup_weight, gateup_moment, gateup_square, gateup_sum, input_rate, weight_decay
    )
    down_new = adam_update(down_weight, down_moment, down_square, down_sum, down_rate, weight_decay)
    return (
        block_output,
        tokens_grad,
        branch_scales,
        *norms_new,
        *heads_new,
        *query_new,
        *keyvalue_new,
        *headgate_new,
        *output_new,
        *gateup_new,
        *down_new,
    )


def solution(mesh):
    fsdp, tp = mesh.devices.shape
    fine = Mesh(mesh.devices.reshape(fsdp // 2, 2, tp), ("w", "c", "t"))
    whole = ("w", "c")
    rows = P(("w", "c", "t"), None)
    first = P(whole, "t")
    second = P(None, whole, "t")
    last = P("t", whole)
    matrices = (first,) * 3 + (second,) * 3 + (first,) * 3 + (last,) * 3 + (second,) * 3 + (last,) * 3
    return jax.shard_map(
        local,
        mesh=fine,
        in_specs=(rows, rows, P(), P()) + (P(),) * 6 + matrices,
        out_specs=(rows, rows, P()) + (P(),) * 6 + matrices,
        check_vma=False,
    )
```

```python
import jax
import jax.numpy as jnp
from jax import lax
from jax.experimental import pallas as pl
from jax.experimental.pallas import tpu as pltpu
from jax.sharding import Mesh
from jax.sharding import PartitionSpec as P

MODEL_WIDTH = 2048
QUERY_HEADS = 16
HEAD_WIDTH = 128
FF = 6144
PIC = 256
STEP = 10

norm_epsilon = 1e-06
rope_base = 1000000.0
beta_first = 0.9
beta_second = 0.999
adam_epsilon = 1e-08
weight_decay = 0.1
masked_score = -1e30
low = jnp.bfloat16
wide = jnp.float32


def normalize(values, scaling):
    return (
        values
        * lax.rsqrt(jnp.mean(values * values, axis=-1, keepdims=True) + norm_epsilon)
        * scaling
    )


def norm_back(values, scaling, upstream):
    factor = lax.rsqrt(jnp.mean(values * values, axis=-1, keepdims=True) + norm_epsilon)
    weighted = upstream * scaling
    projected = jnp.mean(weighted * values, axis=-1, keepdims=True)
    result = factor * weighted - values * (factor * factor * factor) * projected
    return (result, jnp.sum(upstream * values * factor, axis=tuple(range(values.ndim - 1))))


def rotary_tables(length_value):
    halves = HEAD_WIDTH // 2
    frequency = rope_base ** (-(jnp.arange(halves, dtype=wide) * 2.0 / HEAD_WIDTH))
    angles = jnp.arange(length_value, dtype=wide)[:, None] * frequency[None, :]
    cosine, sine = jnp.cos(angles), jnp.sin(angles)
    return (
        jnp.concatenate([cosine, cosine], axis=1),
        jnp.concatenate([-sine, sine], axis=1),
    )


def adam_update(weight, moment, square, gradient, step_rate, decay_rate):
    moment_new = beta_first * moment + (1.0 - beta_first) * gradient
    square_new = beta_second * square + (1.0 - beta_second) * gradient * gradient
    bias_first = 1.0 - beta_first**STEP
    bias_second = 1.0 - beta_second**STEP
    update = moment_new / bias_first / (jnp.sqrt(square_new / bias_second) + adam_epsilon)
    return (weight - step_rate * (update + decay_rate * weight), moment_new, square_new)


def dot(left, right, left_dim, right_dim):
    return lax.dot_general(
        left, right, (((left_dim,), (right_dim,)), ((), ())), preferred_element_type=wide
    )


def fetch(parts):
    pieces = []
    for core in range(2):
        for part in parts:
            size = part.shape[1] // 2
            pieces.append(part[:, core * size : (core + 1) * size].astype(low))
    count = len(parts)
    local_block = jnp.stack(
        [jnp.concatenate(pieces[core * count : (core + 1) * count], axis=1) for core in range(2)]
    )
    return lax.all_gather(local_block, ("w", "c"), axis=1, tiled=True)


def columns_of(both, start, size):
    return lax.dynamic_slice(
        both, (lax.axis_index("c"), 0, start), (1, both.shape[1], size)
    ).reshape(both.shape[1], size)


MESH = pl.DeviceIdType.MESH
BLOCKS = 4
STRIP = 16
ANY = pl.BlockSpec(memory_space=pl.ANY)
VMEM = pl.BlockSpec(memory_space=pltpu.VMEM)


def ring_place(index, count):
    odd = lax.rem(index, 2)
    pair = lax.div(index, 2)
    return (1 - odd) * pair + odd * (count - 1 - pair)


def ring_index(place, count):
    late = lax.div(place, count // 2)
    return (1 - late) * 2 * place + late * (2 * (count - 1 - place) + 1)


class Device:
    def __init__(self, semaphores):
        self.w, self.c, self.t = (lax.axis_index(axis) for axis in ("w", "c", "t"))
        self.count = lax.axis_size("w")
        self.place = ring_place(self.w, self.count)
        self.semaphores = semaphores
        self.used = 0
        self.other_core = {"c": 1 - self.c}
        self.other_row = {"t": 1 - self.t}

    def owner(self, distance):
        return ring_index(lax.rem(self.place + distance + self.count, self.count), self.count)

    def meet(self, partners):
        barrier = pltpu.get_barrier_semaphore()
        for partner in partners:
            pl.semaphore_signal(barrier, inc=1, device_id=partner, device_id_type=MESH)
        pl.semaphore_wait(barrier, len(partners))

    def remote(self, source, target, device):
        slot = self.used
        self.used += 1
        return pltpu.make_async_remote_copy(
            src_ref=source,
            dst_ref=target,
            send_sem=self.semaphores.at[0, slot],
            recv_sem=self.semaphores.at[1, slot],
            device_id=device,
            device_id_type=MESH,
        )

    def inside(self, source, target):
        slot = self.used
        self.used += 1
        return pltpu.make_async_copy(source, target, self.semaphores.at[0, slot])


def rows_at(start, size):
    return pl.ds(pl.multiple_of(start, STRIP), size)


class Spread:
    def __init__(self, device, full):
        self.device, self.full = device, full
        self.size = full.shape[0] // 4
        self.block = self.size // BLOCKS
        self.rows, self.core, self.passed, self.kept = {}, {}, {}, {}

    def where(self, core, row, index):
        return self.full.at[
            rows_at((core * 2 + row) * self.size + index * self.block, self.block)
        ]

    def put(self, index, source):
        device = self.device
        target = self.where(device.c, device.t, index)
        self.rows[index] = device.remote(source, target, device.other_row)
        self.core[index] = device.remote(source, target, device.other_core)
        self.kept[index] = device.inside(source, target)
        for copy in (self.rows[index], self.core[index], self.kept[index]):
            copy.start()

    def forward(self, index):
        device = self.device
        self.rows[index].wait_recv()
        place = self.where(device.c, 1 - device.t, index)
        self.passed[index] = device.remote(place, place, device.other_core)
        self.passed[index].start()

    def finish(self):
        for index in range(BLOCKS):
            self.rows[index].wait_send()
            self.core[index].wait()
            self.passed[index].wait()
            self.kept[index].wait()


class Collect:
    def __init__(self, device, partial, near, far, sent, came):
        self.device = device
        self.partial, self.near, self.far, self.sent, self.came = partial, near, far, sent, came
        self.size = partial.shape[0] // 4
        self.block = self.size // BLOCKS
        self.core, self.rows = {}, {}

    def start(self):
        device = self.device
        self.load = device.inside(
            self.partial.at[rows_at(device.c * 2 * self.size, 2 * self.size)], self.near
        )
        for part, row in enumerate((1 - device.t, device.t)):
            for index in range(BLOCKS):
                start = row * self.size + index * self.block
                copy = device.remote(
                    self.partial.at[rows_at((1 - device.c) * 2 * self.size + start, self.block)],
                    self.far.at[rows_at(start, self.block)],
                    device.other_core,
                )
                copy.start()
                self.core[part, index] = copy
        self.load.start()

    def pass_on(self, index):
        device = self.device
        if index == 0:
            self.load.wait()
        self.core[0, index].wait_recv()

        @pl.loop(0, self.block // STRIP)
        def _(strip):
            at = index * self.block + strip * STRIP
            rows = rows_at((1 - device.t) * self.size + at, STRIP)
            total = self.near[rows, :].astype(wide) + self.far[rows, :].astype(wide)
            self.sent[rows_at(at, STRIP), :] = total.astype(low)

        place = rows_at(index * self.block, self.block)
        self.rows[index] = device.remote(
            self.sent.at[place], self.came.at[place], device.other_row
        )
        self.rows[index].start()

    def take(self, index, use):
        device = self.device
        self.core[1, index].wait_recv()
        self.rows[index].wait_recv()

        @pl.loop(0, self.block // STRIP)
        def _(strip):
            at = index * self.block + strip * STRIP
            rows = rows_at(device.t * self.size + at, STRIP)
            mine = rows_at(at, STRIP)
            total = (
                self.near[rows, :].astype(wide)
                + self.far[rows, :].astype(wide)
                + self.came[mine, :].astype(wide)
            )
            use(mine, total)

    def finish(self):
        for index in range(BLOCKS):
            self.core[0, index].wait_send()
            self.core[1, index].wait_send()
            self.rows[index].wait_send()


class RingSum:
    def __init__(self, device, grads, slots, totals, sums):
        self.device, self.grads, self.slots = device, grads, slots
        self.totals, self.sums = totals, sums
        self.half = grads.shape[0] // device.count // 2
        self.parts = 2
        self.part = self.half // self.parts
        self.copies = {}
        self.ticks = [
            (step, part) for step in range(device.count) for part in range(self.parts)
        ]

    def own(self, way, distance, part):
        direction = 1 - 2 * way
        owner = self.device.owner(-direction * distance)
        return rows_at((owner * 2 + way) * self.half + part * self.part, self.part)

    def slot(self, way, step, part):
        return self.slots.at[
            way * (self.device.count - 1) + step, pl.ds(part * self.part, self.part)
        ]

    def send(self, way, step, part):
        device = self.device
        if step == 0:
            source = self.grads.at[self.own(way, 1, part)]
        else:
            source = self.slot(way, step - 1, part)
        copy = device.remote(
            source, self.slot(way, step, part), {"w": device.owner(1 - 2 * way)}
        )
        copy.start()
        self.copies[way, step, part] = copy

    def tick(self, count=1):
        device = self.device
        for _ in range(count):
            if not self.ticks:
                return
            step, part = self.ticks.pop(0)
            for way in range(2):
                if step > 0:
                    self.copies[way, step - 1, part].wait_recv()
                    own = self.own(way, step + 1, part)
                    slot = self.slot(way, step - 1, part)
                    total = (slot[...].astype(wide) + self.grads[own, :].astype(wide)).astype(low)
                    if step < device.count - 1:
                        slot[...] = total
                    else:
                        self.totals[way, pl.ds(part * self.part, self.part), :] = total
                if step < device.count - 1:
                    self.send(way, step, part)

    def finish(self):
        device = self.device
        self.tick(len(self.ticks))
        away = device.remote(
            self.totals.at[1 - device.c], self.sums.at[device.c], device.other_core
        )
        kept = device.inside(self.totals.at[device.c], self.sums.at[device.c])
        away.start()
        kept.start()
        for copy in self.copies.values():
            copy.wait_send()
        away.wait()
        kept.wait()


def ring_shapes(columns, count):
    half = MODEL_WIDTH // count // 2
    return [
        pltpu.VMEM((2 * (count - 1), half, columns), low),
        pltpu.VMEM((2, half, columns), low),
    ]


def collect_shapes(size):
    return [
        pltpu.VMEM((2 * size, MODEL_WIDTH), low),
        pltpu.VMEM((2 * size, MODEL_WIDTH), low),
        pltpu.VMEM((size, MODEL_WIDTH), low),
        pltpu.VMEM((size, MODEL_WIDTH), low),
    ]


def semaphores_for(count):
    return pltpu.SemaphoreType.DMA((2, count))


def settings(collective):
    return pltpu.CompilerParams(
        collective_id=collective, has_side_effects=True, vmem_limit_bytes=48 * 2**20
    )


def neighbours(device):
    return [
        device.other_core,
        device.other_row,
        {"w": device.owner(1)},
        {"w": device.owner(-1)},
    ]


class RingGather:
    def __init__(self, device, mine, other, full):
        self.device, self.full = device, full
        self.size = mine.shape[0]
        self.parts = 2
        self.part = self.size // self.parts
        here = rows_at((device.w * 2 + device.c) * self.size, self.size)
        self.kept = device.inside(mine, full.at[here])
        self.crossed = device.remote(other, full.at[here], device.other_core)
        self.copies = {}
        self.ticks = [
            (step, part) for step in range(device.count - 1) for part in range(self.parts)
        ]

    def start(self):
        self.kept.start()
        self.crossed.start()

    def ready(self):
        self.kept.wait()
        self.crossed.wait()

    def tick(self, count=1):
        device = self.device
        for _ in range(count):
            if not self.ticks:
                return
            step, part = self.ticks.pop(0)
            for way in range(2):
                if step > 0:
                    self.copies[way, step - 1, part].wait_recv()
                owner = device.owner(-(1 - 2 * way) * step)
                block = self.full.at[
                    rows_at((owner * 2 + way) * self.size + part * self.part, self.part)
                ]
                copy = device.remote(block, block, {"w": device.owner(1 - 2 * way)})
                copy.start()
                self.copies[way, step, part] = copy

    def finish(self):
        self.tick(len(self.ticks))
        for part in range(self.parts):
            for way in range(2):
                self.copies[way, self.device.count - 2, part].wait_recv()
        for copy in self.copies.values():
            copy.wait_send()


def gather_kernel(mine, other, first, second, full, first_full, second_full, semaphores):
    device = Device(semaphores)
    device.meet(neighbours(device))
    gather = RingGather(device, mine, other, full)
    gather.start()
    spreads = []
    for rows, target in ((first, first_full), (second, second_full)):
        spread = Spread(device, target)
        block = spread.block
        for index in range(BLOCKS):
            spread.put(index, rows.at[pl.ds(index * block, block)])
        spreads.append(spread)
    gather.ready()
    for spread in spreads:
        for index in range(BLOCKS):
            gather.tick(2)
            spread.forward(index)
    gather.finish()
    for spread in spreads:
        spread.finish()


def gather_attention(mine, other, first, second):
    count = lax.axis_size("w")
    rows = first.shape[0] * 4
    return pl.pallas_call(
        gather_kernel,
        out_shape=[
            jax.ShapeDtypeStruct((MODEL_WIDTH, mine.shape[1]), low),
            jax.ShapeDtypeStruct((rows, MODEL_WIDTH), low),
            jax.ShapeDtypeStruct((rows, MODEL_WIDTH), low),
        ],
        in_specs=[ANY] * 4,
        out_specs=[ANY] * 3,
        scratch_shapes=[semaphores_for(4 * (count - 1) + 8 * BLOCKS + 2)],
        compiler_params=settings(1),
        cost_estimate=pl.CostEstimate(flops=0, bytes_accessed=64 * 2**20, transcendentals=0),
        name="gather_attention",
    )(mine, other, first, second)


def forward_kernel(
    partial, rows, gain, mine, other, total, full, gathered,
    near, far, sent, came, normed, semaphores,
):
    device = Device(semaphores)
    device.meet(neighbours(device))
    collect = Collect(device, partial, near, far, sent, came)
    spread = Spread(device, full)
    gather = RingGather(device, mine, other, gathered)
    collect.start()
    gather.start()
    collect.pass_on(0)
    gather.ready()
    gather.tick(2)
    for index in range(1, BLOCKS):
        collect.pass_on(index)
    gather.tick(2)

    def use(at, value):
        total[at, :] = value
        middle = rows[at, :].astype(wide) + value
        normed[at, :] = normalize(middle, gain[...]).astype(low)

    for index in range(BLOCKS):
        collect.take(index, use)
        spread.put(index, normed.at[pl.ds(index * spread.block, spread.block)])
        gather.tick(1)
        if index > 0:
            spread.forward(index - 1)
            gather.tick(1)
    spread.forward(BLOCKS - 1)
    gather.finish()
    spread.finish()
    collect.finish()


def exchange_forward(partial, rows, gain, mine, other):
    size = rows.shape[0]
    count = lax.axis_size("w")
    return pl.pallas_call(
        forward_kernel,
        out_shape=[
            jax.ShapeDtypeStruct((size, MODEL_WIDTH), wide),
            jax.ShapeDtypeStruct((4 * size, MODEL_WIDTH), low),
            jax.ShapeDtypeStruct((MODEL_WIDTH, mine.shape[1]), low),
        ],
        in_specs=[ANY, VMEM, VMEM, ANY, ANY],
        out_specs=[VMEM, ANY, ANY],
        scratch_shapes=collect_shapes(size)
        + [
            pltpu.VMEM((size, MODEL_WIDTH), low),
            semaphores_for(16 * BLOCKS + 4 * count + 2),
        ],
        compiler_params=settings(2),
        cost_estimate=pl.CostEstimate(flops=0, bytes_accessed=64 * 2**20, transcendentals=0),
        name="exchange_forward",
    )(partial, rows, gain, mine, other)


class Rings:
    def __init__(self, rings):
        self.rings = rings
        self.next = 0

    def tick(self, count=1):
        for _ in range(count):
            self.rings[self.next].tick()
            self.next = (self.next + 1) % len(self.rings)

    def finish(self):
        while any(ring.ticks for ring in self.rings):
            self.tick()
        for ring in self.rings:
            ring.finish()


def norm_back_rows(values, gain, upstream):
    factor = lax.rsqrt(jnp.mean(values * values, axis=-1, keepdims=True) + norm_epsilon)
    weighted = upstream * gain
    projected = jnp.mean(weighted * values, axis=-1, keepdims=True)
    result = factor * weighted - values * (factor * factor * factor) * projected
    return result, jnp.sum(upstream * values * factor, axis=0, keepdims=True)


def backward_kernel(partial, middle, rows, gain, *refs):
    grads, refs = refs[:2], refs[2:]
    grad, gain_grad, full, sums, refs = refs[0], refs[1], refs[2], refs[3:5], refs[5:]
    near, far, sent, came, rounded = refs[:5]
    device = Device(refs[-1])
    device.meet(neighbours(device))
    collect = Collect(device, partial, near, far, sent, came)
    spread = Spread(device, full)
    rings = Rings(
        [RingSum(device, grads[i], refs[5 + 2 * i], refs[6 + 2 * i], sums[i]) for i in range(2)]
    )
    collect.start()
    rings.tick(4)
    gain_grad[...] = jnp.zeros_like(gain_grad)
    for index in range(BLOCKS):
        collect.pass_on(index)
    rings.tick(4)

    def use(at, upstream):
        result, gained = norm_back_rows(middle[at, :], gain[...], upstream)
        result = result + rows[at, :].astype(wide)
        grad[at, :] = result
        rounded[at, :] = result.astype(low)
        gain_grad[...] += gained

    for index in range(BLOCKS):
        collect.take(index, use)
        spread.put(index, rounded.at[pl.ds(index * spread.block, spread.block)])
        rings.tick(3)
        if index > 0:
            spread.forward(index - 1)
    rings.tick(2)
    spread.forward(BLOCKS - 1)
    rings.finish()
    spread.finish()
    collect.finish()


def ring_outputs(grads):
    half = MODEL_WIDTH // lax.axis_size("w") // 2
    return [jax.ShapeDtypeStruct((2, half, value.shape[1]), low) for value in grads]


def exchange_backward(partial, middle, rows, gain, grads):
    size = rows.shape[0]
    count = lax.axis_size("w")
    return pl.pallas_call(
        backward_kernel,
        out_shape=[
            jax.ShapeDtypeStruct((size, MODEL_WIDTH), wide),
            jax.ShapeDtypeStruct((1, MODEL_WIDTH), wide),
            jax.ShapeDtypeStruct((4 * size, MODEL_WIDTH), low),
            *ring_outputs(grads),
        ],
        in_specs=[ANY] + [VMEM] * (3 + len(grads)),
        out_specs=[VMEM, VMEM, ANY] + [ANY] * len(grads),
        scratch_shapes=collect_shapes(size)
        + [pltpu.VMEM((size, MODEL_WIDTH), low)]
        + [shape for value in grads for shape in ring_shapes(value.shape[1], count)]
        + [semaphores_for(16 * BLOCKS + 8 * count)],
        compiler_params=settings(3),
        cost_estimate=pl.CostEstimate(flops=0, bytes_accessed=128 * 2**20, transcendentals=0),
        name="exchange_backward",
    )(partial, middle, rows, gain, *grads)


class Total:
    def __init__(self, device, mine, crossed, gathered):
        self.device, self.mine = device, mine
        self.crossed, self.gathered = crossed, gathered
        self.copies = {}
        self.steps = [("c", 0), ("t", 0)] + [("w", step) for step in range(device.count // 2)]

    def tick(self):
        device = self.device
        if not self.steps:
            return
        axis, step = self.steps.pop(0)
        if axis != "w":
            slot = 0 if axis == "c" else 1
            partner = device.other_core if axis == "c" else device.other_row
            copy = device.remote(self.mine.at[slot], self.crossed.at[slot], partner)
            copy.start()
            copy.wait()
            total = self.mine[slot] + self.crossed[slot]
            if slot == 0:
                self.mine[1] = total
            else:
                self.gathered[device.w] = total
            return
        for way in range(2):
            if way == 1 and step == device.count // 2 - 1:
                continue
            if step > 0:
                self.copies[way, step - 1].wait_recv()
            block = self.gathered.at[device.owner(-(1 - 2 * way) * step)]
            copy = device.remote(block, block, {"w": device.owner(1 - 2 * way)})
            copy.start()
            self.copies[way, step] = copy

    def finish(self, target):
        while self.steps:
            self.tick()
        half = self.device.count // 2
        self.copies[0, half - 1].wait_recv()
        self.copies[1, half - 2].wait_recv()
        for copy in self.copies.values():
            copy.wait_send()
        target[...] = self.gathered[0]
        for index in range(1, self.device.count):
            target[...] += self.gathered[index]


def last_kernel(
    first, second, tokens, gain, middle_grad, counted, stats, *refs
):
    grads, refs = refs[:2], refs[2:]
    first_total, second_total, stats_total, refs = refs[0], refs[1], refs[2], refs[3:]
    sums, scratch = refs[:2], refs[2:]
    device = Device(scratch[-1])
    device.meet(neighbours(device))
    first_collect = Collect(device, first, *scratch[:4])
    second_collect = Collect(device, second, *scratch[4:8])
    mine, crossed, gathered = scratch[8:11]
    rings = Rings(
        [
            RingSum(device, grads[i], scratch[11 + 2 * i], scratch[12 + 2 * i], sums[i])
            for i in range(2)
        ]
    )
    total = Total(device, mine, crossed, gathered)
    mine[0] = stats[...]
    second_collect.start()
    rings.tick(3)
    first_collect.start()

    def use_second(at, value):
        second_total[at, :] = value
        mine[0, 3:4, :] += jnp.sum(counted[at, :] * value * value, axis=0, keepdims=True)

    def use_first(at, upstream):
        result, gained = norm_back_rows(tokens[at, :].astype(wide), gain[...], upstream)
        first_total[at, :] = result + middle_grad[at, :]
        mine[0, 0:1, :] += gained

    for index in range(BLOCKS):
        second_collect.pass_on(index)
    rings.tick(3)
    for index in range(BLOCKS):
        first_collect.pass_on(index)
        rings.tick(1)
    for index in range(BLOCKS):
        second_collect.take(index, use_second)
        rings.tick(2)
    for index in range(BLOCKS):
        first_collect.take(index, use_first)
        rings.tick(2)
    while total.steps:
        total.tick()
        rings.tick(1)
    rings.finish()
    total.finish(stats_total)
    second_collect.finish()
    first_collect.finish()


def exchange_last(first, second, tokens, gain, middle_grad, counted, stats, grads):
    size = tokens.shape[0]
    count = lax.axis_size("w")
    return pl.pallas_call(
        last_kernel,
        out_shape=[
            jax.ShapeDtypeStruct((size, MODEL_WIDTH), wide),
            jax.ShapeDtypeStruct((size, MODEL_WIDTH), wide),
            jax.ShapeDtypeStruct(stats.shape, wide),
            *ring_outputs(grads),
        ],
        in_specs=[ANY, ANY] + [VMEM] * (5 + len(grads)),
        out_specs=[VMEM] * 3 + [ANY] * len(grads),
        scratch_shapes=collect_shapes(size) * 2
        + [
            pltpu.VMEM((2, *stats.shape), wide),
            pltpu.VMEM((2, *stats.shape), wide),
            pltpu.VMEM((count, *stats.shape), wide),
        ]
        + [shape for value in grads for shape in ring_shapes(value.shape[1], count)]
        + [semaphores_for(32 * BLOCKS + 16 * count)],
        compiler_params=settings(4),
        cost_estimate=pl.CostEstimate(flops=0, bytes_accessed=128 * 2**20, transcendentals=0),
        name="exchange_last",
    )(first, second, tokens, gain, middle_grad, counted, stats, *grads)


def head_rows(values, gain, cosine, sine):
    factor = lax.rsqrt(jnp.mean(values * values, axis=-1, keepdims=True) + norm_epsilon)
    normed = values * factor * gain
    return (normed * cosine + pltpu.roll(normed, HEAD_WIDTH // 2, 1) * sine).astype(low)


def head_back(values, gain, cosine, sine, upstream):
    turned = upstream * cosine - pltpu.roll(upstream, HEAD_WIDTH // 2, 1) * sine
    return norm_back_rows(values, gain, turned)


def head_at(index):
    return slice(index * HEAD_WIDTH, (index + 1) * HEAD_WIDTH)


def gate_column(logits, head):
    lanes = lax.broadcasted_iota(jnp.int32, logits.shape, 1)
    logit = jnp.sum(jnp.where(lanes == head, logits, 0.0), axis=-1, keepdims=True)
    return jax.nn.sigmoid(logit)


def probabilities(queries, keys, start, valid_count, piece_start):
    raw = dot(queries, keys, 1, 1) * HEAD_WIDTH ** (-0.5)
    row = start + lax.broadcasted_iota(jnp.int32, raw.shape, 0)
    column = lax.broadcasted_iota(jnp.int32, raw.shape, 1)
    last = piece_start + PIC
    inside = (row >= piece_start) & (row < last) & (column >= piece_start) & (column < last)
    allowed = (column < valid_count) & ((column <= row) | inside)
    scores = jnp.where(allowed, raw, masked_score)
    expos = jnp.exp(scores - jnp.max(scores, axis=-1, keepdims=True))
    return expos * (1.0 / jnp.sum(expos, axis=-1, keepdims=True))


QUERY_ROWS = 256


def attention_forward_kernel(groups, share, valid, start, pre, gains, cosine, sine, gated):
    sequence = pl.program_id(0)
    heads = groups * share
    length = pre.shape[0]
    for group in range(groups):
        keys = head_rows(pre[:, head_at(heads + group)], gains[1:2, :], cosine[...], sine[...])
        values = pre[:, head_at(heads + groups + group)].astype(low)
        for head in range(group * share, (group + 1) * share):
            for at in range(0, length, QUERY_ROWS):
                rows = slice(at, at + QUERY_ROWS)
                queries = head_rows(
                    pre[rows, head_at(head)], gains[0:1, :], cosine[rows, :], sine[rows, :]
                )
                probs = probabilities(queries, keys, at, valid[sequence], start[sequence])
                mixed = dot(probs.astype(low), values, 1, 0)
                gate = gate_column(pre[rows, head_at(heads + 2 * groups)], head)
                gated[rows, head_at(head)] = (mixed * gate).astype(low)


def attention_backward_kernel(
    groups, share, valid, start, pre, upstream, gains, cosine, sine, grads, gain_grads
):
    sequence = pl.program_id(0)
    heads = groups * share
    length = pre.shape[0]
    scale = HEAD_WIDTH ** (-0.5)

    @pl.when(sequence == 0)
    def _():
        gain_grads[...] = jnp.zeros_like(gain_grads)

    logit_grads = [jnp.zeros((QUERY_ROWS, HEAD_WIDTH), wide)] * (length // QUERY_ROWS)
    for group in range(groups):
        key_pre = pre[:, head_at(heads + group)]
        keys = head_rows(key_pre, gains[1:2, :], cosine[...], sine[...])
        values = pre[:, head_at(heads + groups + group)].astype(low)
        value_grad = jnp.zeros((length, HEAD_WIDTH), wide)
        key_grad = jnp.zeros((length, HEAD_WIDTH), wide)
        for head in range(group * share, (group + 1) * share):
            for block, at in enumerate(range(0, length, QUERY_ROWS)):
                rows = slice(at, at + QUERY_ROWS)
                query_pre = pre[rows, head_at(head)]
                queries = head_rows(query_pre, gains[0:1, :], cosine[rows, :], sine[rows, :])
                probs = probabilities(queries, keys, at, valid[sequence], start[sequence])
                probs_low = probs.astype(low)
                mixed = dot(probs_low, values, 1, 0)
                gate = gate_column(pre[rows, head_at(heads + 2 * groups)], head)
                gated_grad = upstream[rows, head_at(head)]
                mixed_grad = (gated_grad * gate).astype(low)
                logit_grad = (
                    jnp.sum(gated_grad * mixed, axis=-1, keepdims=True) * gate * (1.0 - gate)
                )
                lanes = lax.broadcasted_iota(jnp.int32, (QUERY_ROWS, HEAD_WIDTH), 1)
                logit_grads[block] = logit_grads[block] + jnp.where(lanes == head, logit_grad, 0.0)
                value_grad = value_grad + dot(probs_low, mixed_grad, 0, 0)
                prob_grad = dot(mixed_grad, values, 1, 1)
                score_grad = (
                    probs * (prob_grad - jnp.sum(prob_grad * probs, axis=-1, keepdims=True))
                ).astype(low)
                key_grad = key_grad + dot(score_grad, queries, 0, 0)
                query_grad, gained = head_back(
                    query_pre,
                    gains[0:1, :],
                    cosine[rows, :],
                    sine[rows, :],
                    dot(score_grad, keys, 1, 0) * scale,
                )
                grads[rows, head_at(head)] = query_grad.astype(low)
                gain_grads[0:1, :] += gained
        key_grad, gained = head_back(
            key_pre, gains[1:2, :], cosine[...], sine[...], key_grad * scale
        )
        gain_grads[1:2, :] += gained
        grads[:, head_at(heads + group)] = key_grad.astype(low)
        grads[:, head_at(heads + groups + group)] = value_grad.astype(low)
    for block, at in enumerate(range(0, length, QUERY_ROWS)):
        grads[slice(at, at + QUERY_ROWS), head_at(heads + 2 * groups)] = logit_grads[block].astype(
            low
        )


def sequence_block(columns, length):
    return pl.BlockSpec((length, columns), lambda sequence: (sequence, 0))


def fixed_block(*shape):
    return pl.BlockSpec(shape, lambda sequence: (0, 0))


SCALARS = pl.BlockSpec(memory_space=pltpu.SMEM)


def attention_forward(groups, share, valid, start, pre, gains, cosine, sine):
    length, columns = cosine.shape[0], groups * share * HEAD_WIDTH

    def body(*refs):
        attention_forward_kernel(groups, share, *refs)

    return pl.pallas_call(
        body,
        grid=(pre.shape[0] // length,),
        out_shape=jax.ShapeDtypeStruct((pre.shape[0], columns), low),
        in_specs=[
            SCALARS,
            SCALARS,
            sequence_block(pre.shape[1], length),
            fixed_block(2, HEAD_WIDTH),
            fixed_block(length, HEAD_WIDTH),
            fixed_block(length, HEAD_WIDTH),
        ],
        out_specs=sequence_block(columns, length),
        compiler_params=pltpu.CompilerParams(vmem_limit_bytes=48 * 2**20),
        cost_estimate=pl.CostEstimate(
            flops=2**30, bytes_accessed=8 * 2**20, transcendentals=2**21
        ),
        name="attention_forward",
    )(valid, start, pre, gains, cosine, sine)


def attention_backward(groups, share, valid, start, pre, upstream, gains, cosine, sine):
    length = cosine.shape[0]

    def body(*refs):
        attention_backward_kernel(groups, share, *refs)

    return pl.pallas_call(
        body,
        grid=(pre.shape[0] // length,),
        out_shape=[
            jax.ShapeDtypeStruct(pre.shape, low),
            jax.ShapeDtypeStruct((2, HEAD_WIDTH), wide),
        ],
        in_specs=[
            SCALARS,
            SCALARS,
            sequence_block(pre.shape[1], length),
            sequence_block(upstream.shape[1], length),
            fixed_block(2, HEAD_WIDTH),
            fixed_block(length, HEAD_WIDTH),
            fixed_block(length, HEAD_WIDTH),
        ],
        out_specs=[sequence_block(pre.shape[1], length), fixed_block(2, HEAD_WIDTH)],
        compiler_params=pltpu.CompilerParams(vmem_limit_bytes=48 * 2**20),
        cost_estimate=pl.CostEstimate(
            flops=2**32, bytes_accessed=12 * 2**20, transcendentals=2**21
        ),
        name="attention_backward",
    )(valid, start, pre, upstream, gains, cosine, sine)


def deliver(total):
    core = lax.axis_index("c")
    size = total.shape[0] // 2
    mine = lax.dynamic_slice_in_dim(total, core * size, size, 0)
    other = lax.dynamic_slice_in_dim(total, (1 - core) * size, size, 0)
    other = lax.ppermute(other, "c", [(0, 1), (1, 0)])
    return jnp.stack(
        [jnp.where(core == 0, mine, other), jnp.where(core == 0, other, mine)], axis=0
    )


def take_columns(sums, start, size):
    part = sums[:, :, start : start + size].astype(wide)
    return jnp.concatenate([part[0], part[1]], axis=1)


def adam_kernel(layouts, names, *refs):
    sources, refs = dict(zip(names, refs)), refs[len(names) :]
    count = len(layouts)
    states, refs = refs[: 3 * count], refs[3 * count :]
    targets, refs = refs[: 3 * count], refs[3 * count :]
    buffers, semaphores = refs[: 3 * count], refs[3 * count]
    loads = [
        pltpu.make_async_copy(states[i], buffers[i], semaphores.at[0, i]) for i in range(3 * count)
    ]
    stores = [
        pltpu.make_async_copy(buffers[i], targets[i], semaphores.at[1, i])
        for i in range(3 * count)
    ]
    for load in loads:
        load.start()
    for number, (transposed, rate, leads) in enumerate(layouts):
        matrix = buffers[3 * number : 3 * number + 3]
        for load in loads[3 * number : 3 * number + 3]:
            load.wait()
        for lead, pieces in enumerate(leads):
            quarter = sum(size for _, _, size in pieces)
            for core in range(2):
                start = core * quarter
                for name, column, size in pieces:
                    step = min(size, 256)

                    @pl.loop(0, size // step)
                    def _(block):
                        columns = pl.ds(pl.multiple_of(column + block * step, 128), step)
                        gradient = sources[name][core, :, columns].astype(wide)
                        place = pl.ds(pl.multiple_of(start + block * step, 128), step)
                        if transposed:
                            gradient = gradient.T
                            at = (place, slice(None))
                        elif len(leads) > 1:
                            at = (lead, slice(None), place)
                        else:
                            at = (slice(None), place)
                        weight, moment, square = (part[at] for part in matrix)
                        for part, value in zip(
                            matrix,
                            adam_update(weight, moment, square, gradient, rate, weight_decay),
                        ):
                            part[at] = value

                    start += size
        for store in stores[3 * number : 3 * number + 3]:
            store.start()
    for store in stores:
        store.wait()


def adam_matrices(layouts, sums, states):
    def body(*refs):
        adam_kernel(layouts, list(sums), *refs)

    shapes = [jax.ShapeDtypeStruct(value.shape, value.dtype) for value in states]
    return pl.pallas_call(
        body,
        out_shape=shapes,
        in_specs=[VMEM] * len(sums) + [ANY] * len(states),
        out_specs=[ANY] * len(states),
        scratch_shapes=[pltpu.VMEM(value.shape, value.dtype) for value in states]
        + [pltpu.SemaphoreType.DMA((2, len(states)))],
        compiler_params=pltpu.CompilerParams(vmem_limit_bytes=48 * 2**20),
        cost_estimate=pl.CostEstimate(
            flops=2**25, bytes_accessed=40 * 2**20, transcendentals=2**21
        ),
        name="adam_matrices",
    )(*sums.values(), *states)


def local(
    tokens,
    cotangent,
    valid_len,
    pic_start,
    norm_gains,
    norm_moment,
    norm_square,
    head_gains,
    head_moment,
    head_square,
    query_weight,
    query_moment,
    query_square,
    keyvalue_matrix,
    keyvalue_first_moment,
    keyvalue_second_moment,
    headgate_weight,
    headgate_moment,
    headgate_square,
    output_weight,
    output_moment,
    output_square,
    gateup_weight,
    gateup_moment,
    gateup_square,
    down_weight,
    down_moment,
    down_square,
):
    local_rows = tokens.shape[0]
    length_value = local_rows * 2
    rows = length_value * 2
    group = lax.axis_index("w")
    core = lax.axis_index("c")
    place = lax.axis_index("t")
    heads_here = query_weight.shape[1] // HEAD_WIDTH // 2
    groups_here = keyvalue_matrix.shape[2] // HEAD_WIDTH // 2
    share = heads_here // groups_here
    head_cols = heads_here * HEAD_WIDTH
    group_cols = groups_here * HEAD_WIDTH
    hidden_here = gateup_weight.shape[2] // 2

    bounds = [0, head_cols, group_cols, group_cols, 128, head_cols]
    edges = [sum(bounds[: i + 1]) for i in range(6)]
    quarters = []
    for index in range(2):
        pieces = []
        for matrix in (
            query_weight, keyvalue_matrix[0], keyvalue_matrix[1], headgate_weight, output_weight.T
        ):
            size = matrix.shape[1] // 2
            piece = matrix[:, index * size : (index + 1) * size].astype(low)
            pieces.append(jnp.pad(piece, ((0, 0), (0, -size % 128))))
        quarters.append(jnp.concatenate(pieces, axis=1))
    residual = tokens.astype(wide)
    attention_full, first_full, output_grad_full = gather_attention(
        jnp.where(core == 0, quarters[0], quarters[1]),
        jnp.where(core == 0, quarters[1], quarters[0]),
        normalize(residual, norm_gains[0]).astype(low),
        cotangent,
    )
    feedforward = (gateup_weight[0], gateup_weight[1], down_weight.T)
    late_size = hidden_here // 3
    early_size = hidden_here - late_size

    def quarter_columns(index, start, size):
        return jnp.concatenate(
            [
                matrix[:, index * hidden_here + start : index * hidden_here + start + size].astype(
                    low
                )
                for matrix in feedforward
            ],
            axis=1,
        )

    large_both = lax.all_gather(
        jnp.stack([quarter_columns(index, 0, early_size) for index in range(2)]),
        ("w", "c"),
        axis=1,
        tiled=True,
    )
    small_quarters = [quarter_columns(index, early_size, late_size) for index in range(2)]
    projection_full, output_full = attention_full[:, : edges[4]], attention_full[:, edges[4] :]
    valid_pair = lax.dynamic_slice_in_dim(valid_len, 2 * group, 2)
    start_pair = lax.dynamic_slice_in_dim(pic_start, 2 * group, 2)
    cosine, sine = rotary_tables(length_value)
    projected = dot(first_full, projection_full, 1, 0)
    gated_low = attention_forward(
        groups_here, share, valid_pair, start_pair, projected, head_gains, cosine, sine
    )
    attention_local, second_full, small_full = exchange_forward(
        dot(gated_low, output_full, 1, 1).astype(low),
        tokens,
        norm_gains[1:2],
        jnp.where(core == 0, small_quarters[0], small_quarters[1]),
        jnp.where(core == 0, small_quarters[1], small_quarters[0]),
    )
    middle = residual + attention_local

    def product(left, right):
        return dot(left, right, 0, 0).astype(low)

    def feedforward_grads(rows_full, gate_full, up_full, down_full):
        gate_part = dot(rows_full, gate_full, 1, 0)
        up_part = dot(rows_full, up_full, 1, 0)
        sigmoid_gate = jax.nn.sigmoid(gate_part)
        silu_gate = gate_part * sigmoid_gate
        hidden_low = (silu_gate * up_part).astype(low)
        hidden_grad = dot(output_grad_full, down_full, 1, 0)
        gate_grad = (
            hidden_grad * up_part * sigmoid_gate * (1.0 + gate_part * (1.0 - sigmoid_gate))
        ).astype(low)
        up_grad = (hidden_grad * silu_gate).astype(low)
        partial = dot(gate_grad, gate_full, 1, 1) + dot(up_grad, up_full, 1, 1)
        return gate_grad, up_grad, hidden_low, partial

    gate_small, up_small, down_small = (
        small_full[:, i * late_size : (i + 1) * late_size] for i in range(3)
    )
    gate_large, up_large, down_large = (
        columns_of(large_both, i * early_size, early_size) for i in range(3)
    )
    small_gate_grad, small_up_grad, small_hidden, second_partial = feedforward_grads(
        second_full, gate_small, up_small, down_small
    )
    small_wgrad = jnp.concatenate(
        [product(second_full, small_gate_grad), product(output_grad_full, small_hidden)], axis=1
    )
    second_again, small_wgrad, small_up_grad, small_hidden = lax.optimization_barrier(
        (second_full, small_wgrad, small_up_grad, small_hidden)
    )
    early_sums = lax.psum_scatter(small_wgrad, "w", scatter_dimension=0, tiled=True)
    gate_grad, up_grad, hidden_low, partial = feedforward_grads(
        second_again, gate_large, up_large, down_large
    )
    second_partial = second_partial + partial
    middle_grad, second_gain_grad, attention_grad, first_up_sums, gate_sums = exchange_backward(
        second_partial.astype(low),
        middle,
        cotangent,
        norm_gains[1:2],
        [product(second_again, small_up_grad), product(second_again, gate_grad)],
    )
    second_gain_grad = second_gain_grad[0]
    attention_grad, up_grad, hidden_low, small_hidden, early_sums = lax.optimization_barrier(
        (attention_grad, up_grad, hidden_low, small_hidden, early_sums)
    )
    early_sums = deliver(early_sums)
    late_sums = lax.psum_scatter(
        product(output_grad_full, hidden_low), "w", scatter_dimension=0, tiled=True
    )
    projected_grad, head_gain_grads = attention_backward(
        groups_here,
        share,
        valid_pair,
        start_pair,
        projected,
        dot(attention_grad, output_full, 1, 0),
        head_gains,
        cosine,
        sine,
    )
    first_partial = dot(projected_grad, projection_full, 1, 1)
    attention_wgrad = jnp.concatenate(
        [product(first_full, projected_grad), product(attention_grad, gated_low)], axis=1
    )
    own_places = place * local_rows + jnp.arange(local_rows, dtype=jnp.int32)
    counted = (own_places < valid_pair[core]).astype(wide)[:, None]
    squares = jnp.stack(
        [
            jnp.sum(counted * residual * residual),
            jnp.sum(counted * attention_local * attention_local),
        ]
    )
    small = jnp.concatenate([head_gain_grads.reshape(-1), squares])
    nothing = jnp.zeros((1, MODEL_WIDTH), wide)
    stats = jnp.concatenate(
        [
            nothing,
            second_gain_grad[None],
            jnp.pad(small, (0, MODEL_WIDTH - small.shape[0]))[None],
            jnp.tile(nothing, (5, 1)),
        ]
    )
    feedforward_partial = dot(hidden_low, down_large, 1, 1) + dot(small_hidden, down_small, 1, 1)
    tokens_grad, feedforward_local, stats, up_sums, attention_sums = exchange_last(
        first_partial.astype(low),
        feedforward_partial.astype(low),
        tokens,
        norm_gains[0:1],
        middle_grad,
        counted,
        stats,
        [product(second_again, up_grad), attention_wgrad],
    )
    late_sums = deliver(late_sums)
    block_output = (middle + feedforward_local).astype(low)
    norms_total = stats[:2]
    heads_total = stats[2, : 2 * HEAD_WIDTH].reshape(2, HEAD_WIDTH)
    squares_total = jnp.concatenate(
        [stats[2, 2 * HEAD_WIDTH : 2 * HEAD_WIDTH + 2], jnp.sum(stats[3], keepdims=True)]
    )
    denominator = jnp.sum(valid_len).astype(wide) * MODEL_WIDTH
    branch_scales = jnp.sqrt(squares_total / denominator)
    input_rate = MODEL_WIDTH ** (-0.5)
    down_rate = FF ** (-0.5)
    output_rate = max(QUERY_HEADS * HEAD_WIDTH // 128, 4) ** (-0.5)
    gain_rate = 0.5
    norms_new = adam_update(norm_gains, norm_moment, norm_square, norms_total, gain_rate, 0.0)
    heads_new = adam_update(head_gains, head_moment, head_square, heads_total, gain_rate, 0.0)
    headgate_new = adam_update(
        headgate_weight,
        headgate_moment,
        headgate_square,
        take_columns(attention_sums, edges[3], heads_here),
        input_rate,
        weight_decay,
    )
    layouts = [
        (
            False,
            input_rate,
            [
                [("gate", 0, early_size), ("early", 0, late_size)],
                [("up", 0, early_size), ("first", 0, late_size)],
            ],
        ),
        (True, down_rate, [[("late", 0, early_size), ("early", late_size, late_size)]]),
        (False, input_rate, [[("attention", edges[0], head_cols)]]),
        (
            False,
            input_rate,
            [[("attention", edges[1], group_cols)], [("attention", edges[2], group_cols)]],
        ),
        (True, output_rate, [[("attention", edges[4], head_cols)]]),
    ]
    sums = {
        "gate": gate_sums,
        "up": up_sums,
        "early": early_sums,
        "first": first_up_sums,
        "late": late_sums,
        "attention": attention_sums,
    }
    updated = adam_matrices(
        layouts,
        sums,
        [
            gateup_weight,
            gateup_moment,
            gateup_square,
            down_weight,
            down_moment,
            down_square,
            query_weight,
            query_moment,
            query_square,
            keyvalue_matrix,
            keyvalue_first_moment,
            keyvalue_second_moment,
            output_weight,
            output_moment,
            output_square,
        ],
    )
    gateup_new, down_new, query_new, keyvalue_new, output_new = (
        updated[3 * i : 3 * i + 3] for i in range(5)
    )
    return (
        block_output,
        tokens_grad,
        branch_scales,
        *norms_new,
        *heads_new,
        *query_new,
        *keyvalue_new,
        *headgate_new,
        *output_new,
        *gateup_new,
        *down_new,
    )


def solution(mesh):
    fsdp, tp = mesh.devices.shape
    fine = Mesh(mesh.devices.reshape(fsdp // 2, 2, tp), ("w", "c", "t"))
    whole = ("w", "c")
    rows = P(("w", "c", "t"), None)
    first = P(whole, "t")
    second = P(None, whole, "t")
    last = P("t", whole)
    matrices = (first,) * 3 + (second,) * 3 + (first,) * 3 + (last,) * 3 + (second,) * 3 + (last,) * 3
    return jax.shard_map(
        local,
        mesh=fine,
        in_specs=(rows, rows, P(), P()) + (P(),) * 6 + matrices,
        out_specs=(rows, rows, P()) + (P(),) * 6 + matrices,
        check_vma=False,
    )
```

```python
import jax
import jax.numpy as jnp
from jax import lax
from jax.experimental import pallas as pl
from jax.experimental.pallas import tpu as pltpu
from jax.sharding import Mesh
from jax.sharding import PartitionSpec as P

MODEL_WIDTH = 2048
QUERY_HEADS = 16
HEAD_WIDTH = 128
FF = 6144
PIC = 256
STEP = 10

norm_epsilon = 1e-06
rope_base = 1000000.0
beta_first = 0.9
beta_second = 0.999
adam_epsilon = 1e-08
weight_decay = 0.1
masked_score = -1e30
low = jnp.bfloat16
wide = jnp.float32


def normalize(values, scaling):
    return (
        values
        * lax.rsqrt(jnp.mean(values * values, axis=-1, keepdims=True) + norm_epsilon)
        * scaling
    )


def norm_back(values, scaling, upstream):
    factor = lax.rsqrt(jnp.mean(values * values, axis=-1, keepdims=True) + norm_epsilon)
    weighted = upstream * scaling
    projected = jnp.mean(weighted * values, axis=-1, keepdims=True)
    result = factor * weighted - values * (factor * factor * factor) * projected
    return (result, jnp.sum(upstream * values * factor, axis=tuple(range(values.ndim - 1))))


def rotary_tables(length_value):
    halves = HEAD_WIDTH // 2
    frequency = rope_base ** (-(jnp.arange(halves, dtype=wide) * 2.0 / HEAD_WIDTH))
    angles = jnp.arange(length_value, dtype=wide)[:, None] * frequency[None, :]
    cosine, sine = jnp.cos(angles), jnp.sin(angles)
    return (
        jnp.concatenate([cosine, cosine], axis=1),
        jnp.concatenate([-sine, sine], axis=1),
    )


def adam_update(weight, moment, square, gradient, step_rate, decay_rate):
    moment_new = beta_first * moment + (1.0 - beta_first) * gradient
    square_new = beta_second * square + (1.0 - beta_second) * gradient * gradient
    bias_first = 1.0 - beta_first**STEP
    bias_second = 1.0 - beta_second**STEP
    update = moment_new / bias_first / (jnp.sqrt(square_new / bias_second) + adam_epsilon)
    return (weight - step_rate * (update + decay_rate * weight), moment_new, square_new)


def dot(left, right, left_dim, right_dim):
    return lax.dot_general(
        left, right, (((left_dim,), (right_dim,)), ((), ())), preferred_element_type=wide
    )


def fetch(parts):
    pieces = []
    for core in range(2):
        for part in parts:
            size = part.shape[1] // 2
            pieces.append(part[:, core * size : (core + 1) * size].astype(low))
    count = len(parts)
    local_block = jnp.stack(
        [jnp.concatenate(pieces[core * count : (core + 1) * count], axis=1) for core in range(2)]
    )
    return lax.all_gather(local_block, ("w", "c"), axis=1, tiled=True)


def columns_of(both, start, size):
    return lax.dynamic_slice(
        both, (lax.axis_index("c"), 0, start), (1, both.shape[1], size)
    ).reshape(both.shape[1], size)


MESH = pl.DeviceIdType.MESH
BLOCKS = 4
STRIP = 16
ANY = pl.BlockSpec(memory_space=pl.ANY)
VMEM = pl.BlockSpec(memory_space=pltpu.VMEM)


def ring_place(index, count):
    odd = lax.rem(index, 2)
    pair = lax.div(index, 2)
    return (1 - odd) * pair + odd * (count - 1 - pair)


def ring_index(place, count):
    late = lax.div(place, count // 2)
    return (1 - late) * 2 * place + late * (2 * (count - 1 - place) + 1)


class Device:
    def __init__(self, semaphores):
        self.w, self.c, self.t = (lax.axis_index(axis) for axis in ("w", "c", "t"))
        self.count = lax.axis_size("w")
        self.place = ring_place(self.w, self.count)
        self.semaphores = semaphores
        self.used = 0
        self.other_core = {"c": 1 - self.c}
        self.other_row = {"t": 1 - self.t}

    def owner(self, distance):
        return ring_index(lax.rem(self.place + distance + self.count, self.count), self.count)

    def meet(self, partners):
        barrier = pltpu.get_barrier_semaphore()
        for partner in partners:
            pl.semaphore_signal(barrier, inc=1, device_id=partner, device_id_type=MESH)
        pl.semaphore_wait(barrier, len(partners))

    def remote(self, source, target, device):
        slot = self.used
        self.used += 1
        return pltpu.make_async_remote_copy(
            src_ref=source,
            dst_ref=target,
            send_sem=self.semaphores.at[0, slot],
            recv_sem=self.semaphores.at[1, slot],
            device_id=device,
            device_id_type=MESH,
        )

    def inside(self, source, target):
        slot = self.used
        self.used += 1
        return pltpu.make_async_copy(source, target, self.semaphores.at[0, slot])


def rows_at(start, size):
    return pl.ds(pl.multiple_of(start, STRIP), size)


class Spread:
    def __init__(self, device, full):
        self.device, self.full = device, full
        self.size = full.shape[0] // 4
        self.block = self.size // BLOCKS
        self.rows, self.core, self.passed, self.kept = {}, {}, {}, {}

    def where(self, core, row, index):
        return self.full.at[
            rows_at((core * 2 + row) * self.size + index * self.block, self.block)
        ]

    def put(self, index, source):
        device = self.device
        target = self.where(device.c, device.t, index)
        self.rows[index] = device.remote(source, target, device.other_row)
        self.core[index] = device.remote(source, target, device.other_core)
        self.kept[index] = device.inside(source, target)
        for copy in (self.rows[index], self.core[index], self.kept[index]):
            copy.start()

    def forward(self, index):
        device = self.device
        self.rows[index].wait_recv()
        place = self.where(device.c, 1 - device.t, index)
        self.passed[index] = device.remote(place, place, device.other_core)
        self.passed[index].start()

    def finish(self):
        for index in range(BLOCKS):
            self.rows[index].wait_send()
            self.core[index].wait()
            self.passed[index].wait()
            self.kept[index].wait()


class Collect:
    def __init__(self, device, partial, near, far, sent, came):
        self.device = device
        self.partial, self.near, self.far, self.sent, self.came = partial, near, far, sent, came
        self.size = partial.shape[0] // 4
        self.block = self.size // BLOCKS
        self.core, self.rows = {}, {}

    def start(self):
        device = self.device
        self.load = device.inside(
            self.partial.at[rows_at(device.c * 2 * self.size, 2 * self.size)], self.near
        )
        for part, row in enumerate((1 - device.t, device.t)):
            for index in range(BLOCKS):
                start = row * self.size + index * self.block
                copy = device.remote(
                    self.partial.at[rows_at((1 - device.c) * 2 * self.size + start, self.block)],
                    self.far.at[rows_at(start, self.block)],
                    device.other_core,
                )
                copy.start()
                self.core[part, index] = copy
        self.load.start()

    def pass_on(self, index):
        device = self.device
        if index == 0:
            self.load.wait()
        self.core[0, index].wait_recv()

        @pl.loop(0, self.block // STRIP)
        def _(strip):
            at = index * self.block + strip * STRIP
            rows = rows_at((1 - device.t) * self.size + at, STRIP)
            total = self.near[rows, :].astype(wide) + self.far[rows, :].astype(wide)
            self.sent[rows_at(at, STRIP), :] = total.astype(low)

        place = rows_at(index * self.block, self.block)
        self.rows[index] = device.remote(
            self.sent.at[place], self.came.at[place], device.other_row
        )
        self.rows[index].start()

    def take(self, index, use):
        device = self.device
        self.core[1, index].wait_recv()
        self.rows[index].wait_recv()

        @pl.loop(0, self.block // STRIP)
        def _(strip):
            at = index * self.block + strip * STRIP
            rows = rows_at(device.t * self.size + at, STRIP)
            mine = rows_at(at, STRIP)
            total = (
                self.near[rows, :].astype(wide)
                + self.far[rows, :].astype(wide)
                + self.came[mine, :].astype(wide)
            )
            use(mine, total)

    def finish(self):
        for index in range(BLOCKS):
            self.core[0, index].wait_send()
            self.core[1, index].wait_send()
            self.rows[index].wait_send()


class Given:
    parts = 2

    def __init__(self, grads):
        self.rows, self.columns = grads.shape
        self.grads = grads

    def take(self, start, size):
        return self.grads[rows_at(start, size), :].astype(wide)

    def source(self, start, size, keep):
        return self.grads.at[rows_at(start, size)]


class Product:
    parts = 1

    def __init__(self, left, right, start, columns):
        self.rows, self.columns = left.shape[1], columns
        self.left, self.right, self.start = left, right, start

    def take(self, start, size):
        left = self.left[:, pl.ds(pl.multiple_of(start, 128), size)]
        return dot(left, self.right[:, self.start : self.start + self.columns], 0, 0)

    def source(self, start, size, keep):
        keep[...] = self.take(start, size).astype(low)
        return keep


class RingSum:
    def __init__(self, device, grads, scratch, sums):
        self.device, self.grads, self.sums = device, grads, sums
        self.slots, self.totals, self.first = scratch
        self.half = grads.rows // device.count // 2
        self.parts = grads.parts
        self.part = self.half // self.parts
        self.copies = {}
        self.ticks = [
            (step, part) for step in range(device.count) for part in range(self.parts)
        ]

    def own(self, way, distance, part):
        owner = self.device.owner(-(1 - 2 * way) * distance)
        return (owner * 2 + way) * self.half + part * self.part

    def slot(self, way, step, part):
        return self.slots.at[
            way * (self.device.count - 1) + step, pl.ds(part * self.part, self.part)
        ]

    def send(self, way, step, part):
        device = self.device
        if step == 0:
            source = self.grads.source(self.own(way, 1, part), self.part, self.first.at[way])
        else:
            source = self.slot(way, step - 1, part)
        copy = device.remote(
            source, self.slot(way, step, part), {"w": device.owner(1 - 2 * way)}
        )
        copy.start()
        self.copies[way, step, part] = copy

    def tick(self, count=1):
        device = self.device
        for _ in range(count):
            if not self.ticks:
                return
            step, part = self.ticks.pop(0)
            for way in range(2):
                if step > 0:
                    own = self.grads.take(self.own(way, step + 1, part), self.part)
                    self.copies[way, step - 1, part].wait_recv()
                    slot = self.slot(way, step - 1, part)
                    total = (slot[...].astype(wide) + own).astype(low)
                    if step < device.count - 1:
                        slot[...] = total
                    else:
                        self.totals[way, pl.ds(part * self.part, self.part), :] = total
                if step < device.count - 1:
                    self.send(way, step, part)

    def close(self):
        device = self.device
        self.tick(len(self.ticks))
        self.away = device.remote(
            self.totals.at[1 - device.c], self.sums.at[device.c], device.other_core
        )
        self.kept = device.inside(self.totals.at[device.c], self.sums.at[device.c])
        self.away.start()
        self.kept.start()

    def finish(self):
        for copy in self.copies.values():
            copy.wait_send()
        self.away.wait()
        self.kept.wait()


def ring_shapes(columns, count):
    half = MODEL_WIDTH // count // 2
    return [
        pltpu.VMEM((2 * (count - 1), half, columns), low),
        pltpu.VMEM((2, half, columns), low),
        pltpu.VMEM((2, half, columns), low),
    ]


class RingWork:
    def __init__(self, pairs):
        self.pairs = pairs
        self.columns = [columns for _, _, _, columns in pairs]
        self.fit = (MODEL_WIDTH // lax.axis_size("w") // 2) % 128 == 0
        self.operands, self.places = [], []
        for left, right, start, columns in pairs:
            if self.fit:
                self.places.append((self.add(left), self.add(right), start, columns))
            else:
                part = right[:, start : start + columns]
                self.places.append((self.add(dot(left, part, 0, 0).astype(low)),))

    def add(self, value):
        for index, other in enumerate(self.operands):
            if other is value:
                return index
        self.operands.append(value)
        return len(self.operands) - 1

    def sources(self, refs):
        sources = [
            Product(refs[place[0]], refs[place[1]], *place[2:]) if self.fit else Given(refs[place[0]])
            for place in self.places
        ]
        return sources, refs[len(self.operands) :]

    def outputs(self):
        half = MODEL_WIDTH // lax.axis_size("w") // 2
        return [jax.ShapeDtypeStruct((2, half, size), low) for size in self.columns]

    def scratch(self):
        count = lax.axis_size("w")
        return [shape for size in self.columns for shape in ring_shapes(size, count)]

    def semaphores(self):
        return 4 * (lax.axis_size("w") + 1) * len(self.columns)


def collect_shapes(size):
    return [
        pltpu.VMEM((2 * size, MODEL_WIDTH), low),
        pltpu.VMEM((2 * size, MODEL_WIDTH), low),
        pltpu.VMEM((size, MODEL_WIDTH), low),
        pltpu.VMEM((size, MODEL_WIDTH), low),
    ]


def semaphores_for(count):
    return pltpu.SemaphoreType.DMA((2, count))


def settings(collective):
    return pltpu.CompilerParams(
        collective_id=collective, has_side_effects=True, vmem_limit_bytes=56 * 2**20
    )


def neighbours(device):
    return [
        device.other_core,
        device.other_row,
        {"w": device.owner(1)},
        {"w": device.owner(-1)},
    ]


class RingGather:
    def __init__(self, device, mine, other, full):
        self.device, self.full = device, full
        self.size = mine.shape[0]
        self.parts = 2
        self.part = self.size // self.parts
        here = rows_at((device.w * 2 + device.c) * self.size, self.size)
        self.kept = device.inside(mine, full.at[here])
        self.crossed = device.remote(other, full.at[here], device.other_core)
        self.copies = {}
        self.ticks = [
            (step, part) for step in range(device.count - 1) for part in range(self.parts)
        ]

    def start(self):
        self.kept.start()
        self.crossed.start()

    def ready(self):
        self.kept.wait()
        self.crossed.wait()

    def tick(self, count=1):
        device = self.device
        for _ in range(count):
            if not self.ticks:
                return
            step, part = self.ticks.pop(0)
            for way in range(2):
                if step > 0:
                    self.copies[way, step - 1, part].wait_recv()
                owner = device.owner(-(1 - 2 * way) * step)
                block = self.full.at[
                    rows_at((owner * 2 + way) * self.size + part * self.part, self.part)
                ]
                copy = device.remote(block, block, {"w": device.owner(1 - 2 * way)})
                copy.start()
                self.copies[way, step, part] = copy

    def finish(self):
        self.tick(len(self.ticks))
        for part in range(self.parts):
            for way in range(2):
                self.copies[way, self.device.count - 2, part].wait_recv()
        for copy in self.copies.values():
            copy.wait_send()


def gather_kernel(mine, other, first, second, full, first_full, second_full, semaphores):
    device = Device(semaphores)
    device.meet(neighbours(device))
    gather = RingGather(device, mine, other, full)
    gather.start()
    spreads = []
    for rows, target in ((first, first_full), (second, second_full)):
        spread = Spread(device, target)
        block = spread.block
        for index in range(BLOCKS):
            spread.put(index, rows.at[pl.ds(index * block, block)])
        spreads.append(spread)
    gather.ready()
    for spread in spreads:
        for index in range(BLOCKS):
            gather.tick(2)
            spread.forward(index)
    gather.finish()
    for spread in spreads:
        spread.finish()


def gather_attention(mine, other, first, second):
    count = lax.axis_size("w")
    rows = first.shape[0] * 4
    return pl.pallas_call(
        gather_kernel,
        out_shape=[
            jax.ShapeDtypeStruct((MODEL_WIDTH, mine.shape[1]), low),
            jax.ShapeDtypeStruct((rows, MODEL_WIDTH), low),
            jax.ShapeDtypeStruct((rows, MODEL_WIDTH), low),
        ],
        in_specs=[ANY] * 4,
        out_specs=[ANY] * 3,
        scratch_shapes=[semaphores_for(4 * (count - 1) + 8 * BLOCKS + 2)],
        compiler_params=settings(1),
        cost_estimate=pl.CostEstimate(flops=0, bytes_accessed=64 * 2**20, transcendentals=0),
        name="gather_attention",
    )(mine, other, first, second)


def forward_kernel(
    partial, rows, gain, mine, other, total, full, gathered,
    near, far, sent, came, normed, semaphores,
):
    device = Device(semaphores)
    device.meet(neighbours(device))
    collect = Collect(device, partial, near, far, sent, came)
    spread = Spread(device, full)
    gather = RingGather(device, mine, other, gathered)
    collect.start()
    gather.start()
    collect.pass_on(0)
    gather.ready()
    gather.tick(2)
    for index in range(1, BLOCKS):
        collect.pass_on(index)
    gather.tick(2)

    def use(at, value):
        total[at, :] = value
        middle = rows[at, :].astype(wide) + value
        normed[at, :] = normalize(middle, gain[...]).astype(low)

    for index in range(BLOCKS):
        collect.take(index, use)
        spread.put(index, normed.at[pl.ds(index * spread.block, spread.block)])
        gather.tick(1)
        if index > 0:
            spread.forward(index - 1)
            gather.tick(1)
    spread.forward(BLOCKS - 1)
    gather.finish()
    spread.finish()
    collect.finish()


def exchange_forward(partial, rows, gain, mine, other):
    size = rows.shape[0]
    count = lax.axis_size("w")
    return pl.pallas_call(
        forward_kernel,
        out_shape=[
            jax.ShapeDtypeStruct((size, MODEL_WIDTH), wide),
            jax.ShapeDtypeStruct((4 * size, MODEL_WIDTH), low),
            jax.ShapeDtypeStruct((MODEL_WIDTH, mine.shape[1]), low),
        ],
        in_specs=[ANY, VMEM, VMEM, ANY, ANY],
        out_specs=[VMEM, ANY, ANY],
        scratch_shapes=collect_shapes(size)
        + [
            pltpu.VMEM((size, MODEL_WIDTH), low),
            semaphores_for(16 * BLOCKS + 4 * count + 2),
        ],
        compiler_params=settings(2),
        cost_estimate=pl.CostEstimate(flops=0, bytes_accessed=64 * 2**20, transcendentals=0),
        name="exchange_forward",
    )(partial, rows, gain, mine, other)


class Rings:
    def __init__(self, rings):
        self.rings = rings
        self.next = 0

    def tick(self, count=1):
        for _ in range(count):
            ring = self.rings[self.next]
            self.next = (self.next + 1) % len(self.rings)
            ring.tick()

    def finish(self):
        while any(ring.ticks for ring in self.rings):
            self.tick()
        for ring in self.rings:
            ring.close()
        for ring in self.rings:
            ring.finish()


def norm_back_rows(values, gain, upstream):
    factor = lax.rsqrt(jnp.mean(values * values, axis=-1, keepdims=True) + norm_epsilon)
    weighted = upstream * gain
    projected = jnp.mean(weighted * values, axis=-1, keepdims=True)
    result = factor * weighted - values * (factor * factor * factor) * projected
    return result, jnp.sum(upstream * values * factor, axis=0, keepdims=True)


def backward_kernel(work, partial, middle, rows, gain, *refs):
    count = len(work.columns)
    grads, refs = work.sources(refs)
    grad, gain_grad, full, refs = refs[0], refs[1], refs[2], refs[3:]
    sums, refs = refs[:count], refs[count:]
    near, far, sent, came, rounded = refs[:5]
    device = Device(refs[-1])
    device.meet(neighbours(device))
    collect = Collect(device, partial, near, far, sent, came)
    spread = Spread(device, full)
    rings = Rings(
        [RingSum(device, grads[i], refs[5 + 3 * i : 8 + 3 * i], sums[i]) for i in range(count)]
    )
    collect.start()
    rings.tick(2)
    gain_grad[...] = jnp.zeros_like(gain_grad)
    for index in range(BLOCKS):
        collect.pass_on(index)
    rings.tick(2)

    def use(at, upstream):
        result, gained = norm_back_rows(middle[at, :], gain[...], upstream)
        result = result + rows[at, :].astype(wide)
        grad[at, :] = result
        rounded[at, :] = result.astype(low)
        gain_grad[...] += gained

    for index in range(BLOCKS):
        collect.take(index, use)
        spread.put(index, rounded.at[pl.ds(index * spread.block, spread.block)])
        rings.tick(2)
        if index > 0:
            spread.forward(index - 1)
    rings.tick(1)
    spread.forward(BLOCKS - 1)
    rings.finish()
    spread.finish()
    collect.finish()


def exchange_backward(partial, middle, rows, gain, pairs):
    size = rows.shape[0]
    work = RingWork(pairs)

    def body(*refs):
        backward_kernel(work, *refs)

    return pl.pallas_call(
        body,
        out_shape=[
            jax.ShapeDtypeStruct((size, MODEL_WIDTH), wide),
            jax.ShapeDtypeStruct((1, MODEL_WIDTH), wide),
            jax.ShapeDtypeStruct((4 * size, MODEL_WIDTH), low),
            *work.outputs(),
        ],
        in_specs=[ANY] + [VMEM] * (3 + len(work.operands)),
        out_specs=[VMEM, VMEM, ANY] + [ANY] * len(work.columns),
        scratch_shapes=collect_shapes(size)
        + [pltpu.VMEM((size, MODEL_WIDTH), low)]
        + work.scratch()
        + [semaphores_for(16 * BLOCKS + work.semaphores())],
        compiler_params=settings(3),
        cost_estimate=pl.CostEstimate(flops=0, bytes_accessed=128 * 2**20, transcendentals=0),
        name="exchange_backward",
    )(partial, middle, rows, gain, *work.operands)


class Total:
    def __init__(self, device, mine, crossed, gathered):
        self.device, self.mine = device, mine
        self.crossed, self.gathered = crossed, gathered
        self.copies = {}
        self.steps = [("c", 0), ("t", 0)] + [("w", step) for step in range(device.count // 2)]

    def tick(self):
        device = self.device
        if not self.steps:
            return
        axis, step = self.steps.pop(0)
        if axis != "w":
            slot = 0 if axis == "c" else 1
            partner = device.other_core if axis == "c" else device.other_row
            copy = device.remote(self.mine.at[slot], self.crossed.at[slot], partner)
            copy.start()
            copy.wait()
            total = self.mine[slot] + self.crossed[slot]
            if slot == 0:
                self.mine[1] = total
            else:
                self.gathered[device.w] = total
            return
        for way in range(2):
            if way == 1 and step == device.count // 2 - 1:
                continue
            if step > 0:
                self.copies[way, step - 1].wait_recv()
            block = self.gathered.at[device.owner(-(1 - 2 * way) * step)]
            copy = device.remote(block, block, {"w": device.owner(1 - 2 * way)})
            copy.start()
            self.copies[way, step] = copy

    def finish(self, target):
        while self.steps:
            self.tick()
        half = self.device.count // 2
        self.copies[0, half - 1].wait_recv()
        self.copies[1, half - 2].wait_recv()
        for copy in self.copies.values():
            copy.wait_send()
        target[...] = self.gathered[0]
        for index in range(1, self.device.count):
            target[...] += self.gathered[index]


def last_kernel(work, first, second, tokens, gain, middle_grad, counted, stats, *refs):
    count = len(work.columns)
    grads, refs = work.sources(refs)
    first_total, second_total, stats_total, refs = refs[0], refs[1], refs[2], refs[3:]
    sums, scratch = refs[:count], refs[count:]
    device = Device(scratch[-1])
    device.meet(neighbours(device))
    first_collect = Collect(device, first, *scratch[:4])
    second_collect = Collect(device, second, *scratch[4:8])
    mine, crossed, gathered = scratch[8:11]
    rings = Rings(
        [
            RingSum(device, grads[i], scratch[11 + 3 * i : 14 + 3 * i], sums[i])
            for i in range(count)
        ]
    )
    total = Total(device, mine, crossed, gathered)
    mine[0] = stats[...]
    second_collect.start()
    rings.tick(count)
    first_collect.start()

    def use_second(at, value):
        second_total[at, :] = value
        mine[0, 3:4, :] += jnp.sum(counted[at, :] * value * value, axis=0, keepdims=True)

    def use_first(at, upstream):
        result, gained = norm_back_rows(tokens[at, :].astype(wide), gain[...], upstream)
        first_total[at, :] = result + middle_grad[at, :]
        mine[0, 0:1, :] += gained

    for index in range(BLOCKS):
        second_collect.pass_on(index)
    rings.tick(count)
    for index in range(BLOCKS):
        first_collect.pass_on(index)
    rings.tick(count)
    for index in range(BLOCKS):
        second_collect.take(index, use_second)
        rings.tick(1)
    for index in range(BLOCKS):
        first_collect.take(index, use_first)
        rings.tick(1)
    while total.steps:
        total.tick()
        rings.tick(1)
    rings.finish()
    total.finish(stats_total)
    second_collect.finish()
    first_collect.finish()


def exchange_last(first, second, tokens, gain, middle_grad, counted, stats, pairs):
    size = tokens.shape[0]
    count = lax.axis_size("w")
    work = RingWork(pairs)

    def body(*refs):
        last_kernel(work, *refs)

    return pl.pallas_call(
        body,
        out_shape=[
            jax.ShapeDtypeStruct((size, MODEL_WIDTH), wide),
            jax.ShapeDtypeStruct((size, MODEL_WIDTH), wide),
            jax.ShapeDtypeStruct(stats.shape, wide),
            *work.outputs(),
        ],
        in_specs=[ANY, ANY] + [VMEM] * (5 + len(work.operands)),
        out_specs=[VMEM] * 3 + [ANY] * len(work.columns),
        scratch_shapes=collect_shapes(size) * 2
        + [
            pltpu.VMEM((2, *stats.shape), wide),
            pltpu.VMEM((2, *stats.shape), wide),
            pltpu.VMEM((count, *stats.shape), wide),
        ]
        + work.scratch()
        + [semaphores_for(32 * BLOCKS + 2 * count + 4 + work.semaphores())],
        compiler_params=settings(4),
        cost_estimate=pl.CostEstimate(flops=0, bytes_accessed=128 * 2**20, transcendentals=0),
        name="exchange_last",
    )(first, second, tokens, gain, middle_grad, counted, stats, *work.operands)


FEEDFORWARD_ROWS = 256
FEEDFORWARD_COLUMNS = 512


def feedforward_kernel(
    sizes, core, rows, upstream, large, small, gate_out, up_out, hidden_out, back_out, down_out
):
    weights = [(large.at[0], 0, sizes[0]), (small, sizes[0], sizes[1])]
    for weight, base, size in weights:
        for start in range(0, size, FEEDFORWARD_COLUMNS):
            width = min(FEEDFORWARD_COLUMNS, size - start)
            columns = slice(base + start, base + start + width)
            gate_part = dot(rows[...], weight[:, start : start + width], 1, 0)
            up_part = dot(rows[...], weight[:, size + start : size + start + width], 1, 0)
            hidden_grad = dot(
                upstream[...], weight[:, 2 * size + start : 2 * size + start + width], 1, 0
            )
            sigmoid_gate = jax.nn.sigmoid(gate_part)
            silu_gate = gate_part * sigmoid_gate
            hidden_out[:, columns] = (silu_gate * up_part).astype(low)
            gate_out[:, columns] = (
                hidden_grad * up_part * sigmoid_gate * (1.0 + gate_part * (1.0 - sigmoid_gate))
            ).astype(low)
            up_out[:, columns] = (hidden_grad * silu_gate).astype(low)
    for start in range(0, MODEL_WIDTH, FEEDFORWARD_COLUMNS):
        across = slice(start, start + FEEDFORWARD_COLUMNS)
        back = 0.0
        down = 0.0
        for weight, base, size in weights:
            columns = slice(base, base + size)
            back = back + dot(gate_out[:, columns], weight[across, :size], 1, 1)
            back = back + dot(up_out[:, columns], weight[across, size : 2 * size], 1, 1)
            down = down + dot(hidden_out[:, columns], weight[across, 2 * size :], 1, 1)
        back_out[:, across] = back.astype(low)
        down_out[:, across] = down.astype(low)


def feedforward(core, rows, upstream, large, small):
    sizes = (large.shape[2] // 3, small.shape[1] // 3)
    count = rows.shape[0]
    hidden = sum(sizes)

    def body(*refs):
        feedforward_kernel(sizes, *refs)

    def block(columns):
        return pl.BlockSpec((FEEDFORWARD_ROWS, columns), lambda index, core: (index, 0))

    once = pl.Buffered(1)
    return pl.pallas_call(
        body,
        grid_spec=pltpu.PrefetchScalarGridSpec(
            num_scalar_prefetch=1,
            grid=(count // FEEDFORWARD_ROWS,),
            in_specs=[
                block(MODEL_WIDTH),
                block(MODEL_WIDTH),
                pl.BlockSpec(
                    (1, *large.shape[1:]),
                    lambda index, core: (core[0], 0, 0),
                    pipeline_mode=once,
                ),
                pl.BlockSpec(small.shape, lambda index, core: (0, 0), pipeline_mode=once),
            ],
            out_specs=[block(hidden)] * 3 + [block(MODEL_WIDTH)] * 2,
        ),
        out_shape=[jax.ShapeDtypeStruct((count, hidden), low)] * 3
        + [jax.ShapeDtypeStruct((count, MODEL_WIDTH), low)] * 2,
        compiler_params=pltpu.CompilerParams(vmem_limit_bytes=52 * 2**20),
        cost_estimate=pl.CostEstimate(
            flops=12 * count * MODEL_WIDTH * hidden,
            bytes_accessed=48 * 2**20,
            transcendentals=count * hidden,
        ),
        name="feedforward",
    )(core, rows, upstream, large, small)


def head_rows(values, gain, cosine, sine):
    factor = lax.rsqrt(jnp.mean(values * values, axis=-1, keepdims=True) + norm_epsilon)
    normed = values * factor * gain
    return (normed * cosine + pltpu.roll(normed, HEAD_WIDTH // 2, 1) * sine).astype(low)


def head_back(values, gain, cosine, sine, upstream):
    turned = upstream * cosine - pltpu.roll(upstream, HEAD_WIDTH // 2, 1) * sine
    return norm_back_rows(values, gain, turned)


def head_at(index):
    return slice(index * HEAD_WIDTH, (index + 1) * HEAD_WIDTH)


def gate_column(logits, head):
    lanes = lax.broadcasted_iota(jnp.int32, logits.shape, 1)
    logit = jnp.sum(jnp.where(lanes == head, logits, 0.0), axis=-1, keepdims=True)
    return jax.nn.sigmoid(logit)


def probabilities(queries, keys, start, valid_count, piece_start):
    raw = dot(queries, keys, 1, 1) * HEAD_WIDTH ** (-0.5)
    row = start + lax.broadcasted_iota(jnp.int32, raw.shape, 0)
    column = lax.broadcasted_iota(jnp.int32, raw.shape, 1)
    last = piece_start + PIC
    inside = (row >= piece_start) & (row < last) & (column >= piece_start) & (column < last)
    allowed = (column < valid_count) & ((column <= row) | inside)
    scores = jnp.where(allowed, raw, masked_score)
    expos = jnp.exp(scores - jnp.max(scores, axis=-1, keepdims=True))
    return expos * (1.0 / jnp.sum(expos, axis=-1, keepdims=True))


QUERY_ROWS = 256


def attention_forward_kernel(groups, share, valid, start, pre, gains, cosine, sine, gated):
    sequence = pl.program_id(0)
    heads = groups * share
    length = pre.shape[0]
    for group in range(groups):
        keys = head_rows(pre[:, head_at(heads + group)], gains[1:2, :], cosine[...], sine[...])
        values = pre[:, head_at(heads + groups + group)].astype(low)
        for head in range(group * share, (group + 1) * share):
            for at in range(0, length, QUERY_ROWS):
                rows = slice(at, at + QUERY_ROWS)
                queries = head_rows(
                    pre[rows, head_at(head)], gains[0:1, :], cosine[rows, :], sine[rows, :]
                )
                probs = probabilities(queries, keys, at, valid[sequence], start[sequence])
                mixed = dot(probs.astype(low), values, 1, 0)
                gate = gate_column(pre[rows, head_at(heads + 2 * groups)], head)
                gated[rows, head_at(head)] = (mixed * gate).astype(low)


def attention_backward_kernel(
    groups, share, valid, start, pre, upstream, gains, cosine, sine, grads, gain_grads
):
    sequence = pl.program_id(0)
    heads = groups * share
    length = pre.shape[0]
    scale = HEAD_WIDTH ** (-0.5)

    @pl.when(sequence == 0)
    def _():
        gain_grads[...] = jnp.zeros_like(gain_grads)

    logit_grads = [jnp.zeros((QUERY_ROWS, HEAD_WIDTH), wide)] * (length // QUERY_ROWS)
    for group in range(groups):
        key_pre = pre[:, head_at(heads + group)]
        keys = head_rows(key_pre, gains[1:2, :], cosine[...], sine[...])
        values = pre[:, head_at(heads + groups + group)].astype(low)
        value_grad = jnp.zeros((length, HEAD_WIDTH), wide)
        key_grad = jnp.zeros((length, HEAD_WIDTH), wide)
        for head in range(group * share, (group + 1) * share):
            for block, at in enumerate(range(0, length, QUERY_ROWS)):
                rows = slice(at, at + QUERY_ROWS)
                query_pre = pre[rows, head_at(head)]
                queries = head_rows(query_pre, gains[0:1, :], cosine[rows, :], sine[rows, :])
                probs = probabilities(queries, keys, at, valid[sequence], start[sequence])
                probs_low = probs.astype(low)
                mixed = dot(probs_low, values, 1, 0)
                gate = gate_column(pre[rows, head_at(heads + 2 * groups)], head)
                gated_grad = upstream[rows, head_at(head)]
                mixed_grad = (gated_grad * gate).astype(low)
                logit_grad = (
                    jnp.sum(gated_grad * mixed, axis=-1, keepdims=True) * gate * (1.0 - gate)
                )
                lanes = lax.broadcasted_iota(jnp.int32, (QUERY_ROWS, HEAD_WIDTH), 1)
                logit_grads[block] = logit_grads[block] + jnp.where(lanes == head, logit_grad, 0.0)
                value_grad = value_grad + dot(probs_low, mixed_grad, 0, 0)
                prob_grad = dot(mixed_grad, values, 1, 1)
                score_grad = (
                    probs * (prob_grad - jnp.sum(prob_grad * probs, axis=-1, keepdims=True))
                ).astype(low)
                key_grad = key_grad + dot(score_grad, queries, 0, 0)
                query_grad, gained = head_back(
                    query_pre,
                    gains[0:1, :],
                    cosine[rows, :],
                    sine[rows, :],
                    dot(score_grad, keys, 1, 0) * scale,
                )
                grads[rows, head_at(head)] = query_grad.astype(low)
                gain_grads[0:1, :] += gained
        key_grad, gained = head_back(
            key_pre, gains[1:2, :], cosine[...], sine[...], key_grad * scale
        )
        gain_grads[1:2, :] += gained
        grads[:, head_at(heads + group)] = key_grad.astype(low)
        grads[:, head_at(heads + groups + group)] = value_grad.astype(low)
    for block, at in enumerate(range(0, length, QUERY_ROWS)):
        grads[slice(at, at + QUERY_ROWS), head_at(heads + 2 * groups)] = logit_grads[block].astype(
            low
        )


def sequence_block(columns, length):
    return pl.BlockSpec((length, columns), lambda sequence: (sequence, 0))


def fixed_block(*shape):
    return pl.BlockSpec(shape, lambda sequence: (0, 0))


SCALARS = pl.BlockSpec(memory_space=pltpu.SMEM)


def attention_forward(groups, share, valid, start, pre, gains, cosine, sine):
    length, columns = cosine.shape[0], groups * share * HEAD_WIDTH

    def body(*refs):
        attention_forward_kernel(groups, share, *refs)

    return pl.pallas_call(
        body,
        grid=(pre.shape[0] // length,),
        out_shape=jax.ShapeDtypeStruct((pre.shape[0], columns), low),
        in_specs=[
            SCALARS,
            SCALARS,
            sequence_block(pre.shape[1], length),
            fixed_block(2, HEAD_WIDTH),
            fixed_block(length, HEAD_WIDTH),
            fixed_block(length, HEAD_WIDTH),
        ],
        out_specs=sequence_block(columns, length),
        compiler_params=pltpu.CompilerParams(vmem_limit_bytes=48 * 2**20),
        cost_estimate=pl.CostEstimate(
            flops=2**30, bytes_accessed=8 * 2**20, transcendentals=2**21
        ),
        name="attention_forward",
    )(valid, start, pre, gains, cosine, sine)


def attention_backward(groups, share, valid, start, pre, upstream, gains, cosine, sine):
    length = cosine.shape[0]

    def body(*refs):
        attention_backward_kernel(groups, share, *refs)

    return pl.pallas_call(
        body,
        grid=(pre.shape[0] // length,),
        out_shape=[
            jax.ShapeDtypeStruct(pre.shape, low),
            jax.ShapeDtypeStruct((2, HEAD_WIDTH), wide),
        ],
        in_specs=[
            SCALARS,
            SCALARS,
            sequence_block(pre.shape[1], length),
            sequence_block(upstream.shape[1], length),
            fixed_block(2, HEAD_WIDTH),
            fixed_block(length, HEAD_WIDTH),
            fixed_block(length, HEAD_WIDTH),
        ],
        out_specs=[sequence_block(pre.shape[1], length), fixed_block(2, HEAD_WIDTH)],
        compiler_params=pltpu.CompilerParams(vmem_limit_bytes=48 * 2**20),
        cost_estimate=pl.CostEstimate(
            flops=2**32, bytes_accessed=12 * 2**20, transcendentals=2**21
        ),
        name="attention_backward",
    )(valid, start, pre, upstream, gains, cosine, sine)


def deliver(total):
    core = lax.axis_index("c")
    size = total.shape[0] // 2
    mine = lax.dynamic_slice_in_dim(total, core * size, size, 0)
    other = lax.dynamic_slice_in_dim(total, (1 - core) * size, size, 0)
    other = lax.ppermute(other, "c", [(0, 1), (1, 0)])
    return jnp.stack(
        [jnp.where(core == 0, mine, other), jnp.where(core == 0, other, mine)], axis=0
    )


def take_columns(sums, start, size):
    part = sums[:, :, start : start + size].astype(wide)
    return jnp.concatenate([part[0], part[1]], axis=1)


def adam_kernel(layouts, names, *refs):
    sources, refs = dict(zip(names, refs)), refs[len(names) :]
    count = len(layouts)
    states, refs = refs[: 3 * count], refs[3 * count :]
    targets, refs = refs[: 3 * count], refs[3 * count :]
    buffers, semaphores = refs[: 3 * count], refs[3 * count]
    loads = [
        pltpu.make_async_copy(states[i], buffers[i], semaphores.at[0, i]) for i in range(3 * count)
    ]
    stores = [
        pltpu.make_async_copy(buffers[i], targets[i], semaphores.at[1, i])
        for i in range(3 * count)
    ]
    for load in loads:
        load.start()
    for number, (transposed, rate, leads) in enumerate(layouts):
        matrix = buffers[3 * number : 3 * number + 3]
        for load in loads[3 * number : 3 * number + 3]:
            load.wait()
        for lead, pieces in enumerate(leads):
            quarter = sum(size for _, _, size in pieces)
            for core in range(2):
                start = core * quarter
                for name, column, size in pieces:
                    step = min(size, 256)

                    @pl.loop(0, size // step)
                    def _(block):
                        columns = pl.ds(pl.multiple_of(column + block * step, 128), step)
                        gradient = sources[name][core, :, columns].astype(wide)
                        place = pl.ds(pl.multiple_of(start + block * step, 128), step)
                        if transposed:
                            gradient = gradient.T
                            at = (place, slice(None))
                        elif len(leads) > 1:
                            at = (lead, slice(None), place)
                        else:
                            at = (slice(None), place)
                        weight, moment, square = (part[at] for part in matrix)
                        for part, value in zip(
                            matrix,
                            adam_update(weight, moment, square, gradient, rate, weight_decay),
                        ):
                            part[at] = value

                    start += size
        for store in stores[3 * number : 3 * number + 3]:
            store.start()
    for store in stores:
        store.wait()


def adam_matrices(layouts, sums, states):
    def body(*refs):
        adam_kernel(layouts, list(sums), *refs)

    shapes = [jax.ShapeDtypeStruct(value.shape, value.dtype) for value in states]
    return pl.pallas_call(
        body,
        out_shape=shapes,
        in_specs=[VMEM] * len(sums) + [ANY] * len(states),
        out_specs=[ANY] * len(states),
        scratch_shapes=[pltpu.VMEM(value.shape, value.dtype) for value in states]
        + [pltpu.SemaphoreType.DMA((2, len(states)))],
        compiler_params=pltpu.CompilerParams(vmem_limit_bytes=48 * 2**20),
        cost_estimate=pl.CostEstimate(
            flops=2**25, bytes_accessed=40 * 2**20, transcendentals=2**21
        ),
        name="adam_matrices",
    )(*sums.values(), *states)


def local(
    tokens,
    cotangent,
    valid_len,
    pic_start,
    norm_gains,
    norm_moment,
    norm_square,
    head_gains,
    head_moment,
    head_square,
    query_weight,
    query_moment,
    query_square,
    keyvalue_matrix,
    keyvalue_first_moment,
    keyvalue_second_moment,
    headgate_weight,
    headgate_moment,
    headgate_square,
    output_weight,
    output_moment,
    output_square,
    gateup_weight,
    gateup_moment,
    gateup_square,
    down_weight,
    down_moment,
    down_square,
):
    local_rows = tokens.shape[0]
    length_value = local_rows * 2
    rows = length_value * 2
    group = lax.axis_index("w")
    core = lax.axis_index("c")
    place = lax.axis_index("t")
    heads_here = query_weight.shape[1] // HEAD_WIDTH // 2
    groups_here = keyvalue_matrix.shape[2] // HEAD_WIDTH // 2
    share = heads_here // groups_here
    head_cols = heads_here * HEAD_WIDTH
    group_cols = groups_here * HEAD_WIDTH
    hidden_here = gateup_weight.shape[2] // 2

    bounds = [0, head_cols, group_cols, group_cols, 128, head_cols]
    edges = [sum(bounds[: i + 1]) for i in range(6)]
    quarters = []
    for index in range(2):
        pieces = []
        for matrix in (
            query_weight, keyvalue_matrix[0], keyvalue_matrix[1], headgate_weight, output_weight.T
        ):
            size = matrix.shape[1] // 2
            piece = matrix[:, index * size : (index + 1) * size].astype(low)
            pieces.append(jnp.pad(piece, ((0, 0), (0, -size % 128))))
        quarters.append(jnp.concatenate(pieces, axis=1))
    residual = tokens.astype(wide)
    attention_full, first_full, output_grad_full = gather_attention(
        jnp.where(core == 0, quarters[0], quarters[1]),
        jnp.where(core == 0, quarters[1], quarters[0]),
        normalize(residual, norm_gains[0]).astype(low),
        cotangent,
    )
    matrices = (gateup_weight[0], gateup_weight[1], down_weight.T)
    late_size = hidden_here // 3
    early_size = hidden_here - late_size

    def quarter_columns(index, start, size):
        return jnp.concatenate(
            [
                matrix[:, index * hidden_here + start : index * hidden_here + start + size].astype(
                    low
                )
                for matrix in matrices
            ],
            axis=1,
        )

    large_both = lax.all_gather(
        jnp.stack([quarter_columns(index, 0, early_size) for index in range(2)]),
        ("w", "c"),
        axis=1,
        tiled=True,
    )
    small_quarters = [quarter_columns(index, early_size, late_size) for index in range(2)]
    projection_full, output_full = attention_full[:, : edges[4]], attention_full[:, edges[4] :]
    valid_pair = lax.dynamic_slice_in_dim(valid_len, 2 * group, 2)
    start_pair = lax.dynamic_slice_in_dim(pic_start, 2 * group, 2)
    cosine, sine = rotary_tables(length_value)
    projected = dot(first_full, projection_full, 1, 0)
    gated_low = attention_forward(
        groups_here, share, valid_pair, start_pair, projected, head_gains, cosine, sine
    )
    attention_local, second_full, small_full = exchange_forward(
        dot(gated_low, output_full, 1, 1).astype(low),
        tokens,
        norm_gains[1:2],
        jnp.where(core == 0, small_quarters[0], small_quarters[1]),
        jnp.where(core == 0, small_quarters[1], small_quarters[0]),
    )
    middle = residual + attention_local

    def product(left, right):
        return dot(left, right, 0, 0).astype(low)

    gate_grad, up_grad, hidden_low, second_partial, feedforward_partial = feedforward(
        core[None], second_full, output_grad_full, large_both, small_full
    )
    up_split = hidden_here // 2
    down_wgrad = product(output_grad_full, hidden_low)
    up_wgrad = product(second_full, up_grad[:, :up_split])
    second_partial, down_wgrad, up_wgrad = lax.optimization_barrier(
        (second_partial, down_wgrad, up_wgrad)
    )
    down_sums = lax.psum_scatter(down_wgrad, "w", scatter_dimension=0, tiled=True)
    first_up_sums = lax.psum_scatter(up_wgrad, "w", scatter_dimension=0, tiled=True)
    middle_grad, second_gain_grad, attention_grad, first_gate_sums, second_gate_sums = exchange_backward(
        second_partial,
        middle,
        cotangent,
        norm_gains[1:2],
        [
            (second_full, gate_grad, 0, up_split),
            (second_full, gate_grad, up_split, hidden_here - up_split),
        ],
    )
    second_gain_grad = second_gain_grad[0]
    projected_grad, head_gain_grads = attention_backward(
        groups_here,
        share,
        valid_pair,
        start_pair,
        projected,
        dot(attention_grad, output_full, 1, 0),
        head_gains,
        cosine,
        sine,
    )
    first_partial = dot(projected_grad, projection_full, 1, 1)
    own_places = place * local_rows + jnp.arange(local_rows, dtype=jnp.int32)
    counted = (own_places < valid_pair[core]).astype(wide)[:, None]
    squares = jnp.stack(
        [
            jnp.sum(counted * residual * residual),
            jnp.sum(counted * attention_local * attention_local),
        ]
    )
    small = jnp.concatenate([head_gain_grads.reshape(-1), squares])
    nothing = jnp.zeros((1, MODEL_WIDTH), wide)
    stats = jnp.concatenate(
        [
            nothing,
            second_gain_grad[None],
            jnp.pad(small, (0, MODEL_WIDTH - small.shape[0]))[None],
            jnp.tile(nothing, (5, 1)),
        ]
    )
    tokens_grad, feedforward_local, stats, projected_sums, output_sums, second_up_sums = (
        exchange_last(
            first_partial.astype(low),
            feedforward_partial,
            tokens,
            norm_gains[0:1],
            middle_grad,
            counted,
            stats,
            [
                (first_full, projected_grad, 0, edges[4]),
                (attention_grad, gated_low, 0, head_cols),
                (second_full, up_grad, up_split, hidden_here - up_split),
            ],
        )
    )
    down_sums, first_up_sums = deliver(down_sums), deliver(first_up_sums)
    block_output = (middle + feedforward_local).astype(low)
    norms_total = stats[:2]
    heads_total = stats[2, : 2 * HEAD_WIDTH].reshape(2, HEAD_WIDTH)
    squares_total = jnp.concatenate(
        [stats[2, 2 * HEAD_WIDTH : 2 * HEAD_WIDTH + 2], jnp.sum(stats[3], keepdims=True)]
    )
    denominator = jnp.sum(valid_len).astype(wide) * MODEL_WIDTH
    branch_scales = jnp.sqrt(squares_total / denominator)
    input_rate = MODEL_WIDTH ** (-0.5)
    down_rate = FF ** (-0.5)
    output_rate = max(QUERY_HEADS * HEAD_WIDTH // 128, 4) ** (-0.5)
    gain_rate = 0.5
    norms_new = adam_update(norm_gains, norm_moment, norm_square, norms_total, gain_rate, 0.0)
    heads_new = adam_update(head_gains, head_moment, head_square, heads_total, gain_rate, 0.0)
    headgate_new = adam_update(
        headgate_weight,
        headgate_moment,
        headgate_square,
        take_columns(projected_sums, edges[3], heads_here),
        input_rate,
        weight_decay,
    )
    layouts = [
        (
            False,
            input_rate,
            [
                [("gate 0", 0, up_split), ("gate 1", 0, hidden_here - up_split)],
                [("up 0", 0, up_split), ("up 1", 0, hidden_here - up_split)],
            ],
        ),
        (True, down_rate, [[("down", 0, hidden_here)]]),
        (False, input_rate, [[("projected", edges[0], head_cols)]]),
        (
            False,
            input_rate,
            [[("projected", edges[1], group_cols)], [("projected", edges[2], group_cols)]],
        ),
        (True, output_rate, [[("output", 0, head_cols)]]),
    ]
    sums = {
        "gate 0": first_gate_sums,
        "gate 1": second_gate_sums,
        "up 0": first_up_sums,
        "up 1": second_up_sums,
        "down": down_sums,
        "projected": projected_sums,
        "output": output_sums,
    }
    updated = adam_matrices(
        layouts,
        sums,
        [
            gateup_weight,
            gateup_moment,
            gateup_square,
            down_weight,
            down_moment,
            down_square,
            query_weight,
            query_moment,
            query_square,
            keyvalue_matrix,
            keyvalue_first_moment,
            keyvalue_second_moment,
            output_weight,
            output_moment,
            output_square,
        ],
    )
    gateup_new, down_new, query_new, keyvalue_new, output_new = (
        updated[3 * i : 3 * i + 3] for i in range(5)
    )
    return (
        block_output,
        tokens_grad,
        branch_scales,
        *norms_new,
        *heads_new,
        *query_new,
        *keyvalue_new,
        *headgate_new,
        *output_new,
        *gateup_new,
        *down_new,
    )


def solution(mesh):
    fsdp, tp = mesh.devices.shape
    fine = Mesh(mesh.devices.reshape(fsdp // 2, 2, tp), ("w", "c", "t"))
    whole = ("w", "c")
    rows = P(("w", "c", "t"), None)
    first = P(whole, "t")
    second = P(None, whole, "t")
    last = P("t", whole)
    matrices = (first,) * 3 + (second,) * 3 + (first,) * 3 + (last,) * 3 + (second,) * 3 + (last,) * 3
    return jax.shard_map(
        local,
        mesh=fine,
        in_specs=(rows, rows, P(), P()) + (P(),) * 6 + matrices,
        out_specs=(rows, rows, P()) + (P(),) * 6 + matrices,
        check_vma=False,
    )
```

```python
import jax
import jax.numpy as jnp
from jax import lax
from jax.experimental import pallas as pl
from jax.experimental.pallas import tpu as pltpu
from jax.sharding import Mesh
from jax.sharding import PartitionSpec as P

MODEL_WIDTH = 2048
QUERY_HEADS = 16
HEAD_WIDTH = 128
FF = 6144
PIC = 256
STEP = 10

norm_epsilon = 1e-06
rope_base = 1000000.0
beta_first = 0.9
beta_second = 0.999
adam_epsilon = 1e-08
weight_decay = 0.1
masked_score = -1e30
low = jnp.bfloat16
wide = jnp.float32


def normalize(values, scaling):
    return (
        values
        * lax.rsqrt(jnp.mean(values * values, axis=-1, keepdims=True) + norm_epsilon)
        * scaling
    )


def norm_back(values, scaling, upstream):
    factor = lax.rsqrt(jnp.mean(values * values, axis=-1, keepdims=True) + norm_epsilon)
    weighted = upstream * scaling
    projected = jnp.mean(weighted * values, axis=-1, keepdims=True)
    result = factor * weighted - values * (factor * factor * factor) * projected
    return (result, jnp.sum(upstream * values * factor, axis=tuple(range(values.ndim - 1))))


def rotary_tables(length_value):
    halves = HEAD_WIDTH // 2
    frequency = rope_base ** (-(jnp.arange(halves, dtype=wide) * 2.0 / HEAD_WIDTH))
    angles = jnp.arange(length_value, dtype=wide)[:, None] * frequency[None, :]
    cosine, sine = jnp.cos(angles), jnp.sin(angles)
    return (
        jnp.concatenate([cosine, cosine], axis=1),
        jnp.concatenate([-sine, sine], axis=1),
    )


def adam_update(weight, moment, square, gradient, step_rate, decay_rate):
    moment_new = beta_first * moment + (1.0 - beta_first) * gradient
    square_new = beta_second * square + (1.0 - beta_second) * gradient * gradient
    bias_first = 1.0 - beta_first**STEP
    bias_second = 1.0 - beta_second**STEP
    update = moment_new / bias_first / (jnp.sqrt(square_new / bias_second) + adam_epsilon)
    return (weight - step_rate * (update + decay_rate * weight), moment_new, square_new)


def dot(left, right, left_dim, right_dim):
    return lax.dot_general(
        left, right, (((left_dim,), (right_dim,)), ((), ())), preferred_element_type=wide
    )


def fetch(parts):
    pieces = []
    for core in range(2):
        for part in parts:
            size = part.shape[1] // 2
            pieces.append(part[:, core * size : (core + 1) * size].astype(low))
    count = len(parts)
    local_block = jnp.stack(
        [jnp.concatenate(pieces[core * count : (core + 1) * count], axis=1) for core in range(2)]
    )
    return lax.all_gather(local_block, ("w", "c"), axis=1, tiled=True)


def columns_of(both, start, size):
    return lax.dynamic_slice(
        both, (lax.axis_index("c"), 0, start), (1, both.shape[1], size)
    ).reshape(both.shape[1], size)


MESH = pl.DeviceIdType.MESH
BLOCKS = 4
STRIP = 16
ANY = pl.BlockSpec(memory_space=pl.ANY)
VMEM = pl.BlockSpec(memory_space=pltpu.VMEM)


def ring_place(index, count):
    odd = lax.rem(index, 2)
    pair = lax.div(index, 2)
    return (1 - odd) * pair + odd * (count - 1 - pair)


def ring_index(place, count):
    late = lax.div(place, count // 2)
    return (1 - late) * 2 * place + late * (2 * (count - 1 - place) + 1)


class Device:
    def __init__(self, semaphores):
        self.w, self.c, self.t = (lax.axis_index(axis) for axis in ("w", "c", "t"))
        self.count = lax.axis_size("w")
        self.place = ring_place(self.w, self.count)
        self.semaphores = semaphores
        self.used = 0
        self.other_core = {"c": 1 - self.c}
        self.other_row = {"t": 1 - self.t}

    def owner(self, distance):
        return ring_index(lax.rem(self.place + distance + self.count, self.count), self.count)

    def meet(self, partners):
        barrier = pltpu.get_barrier_semaphore()
        for partner in partners:
            pl.semaphore_signal(barrier, inc=1, device_id=partner, device_id_type=MESH)
        pl.semaphore_wait(barrier, len(partners))

    def remote(self, source, target, device):
        slot = self.used
        self.used += 1
        return pltpu.make_async_remote_copy(
            src_ref=source,
            dst_ref=target,
            send_sem=self.semaphores.at[0, slot],
            recv_sem=self.semaphores.at[1, slot],
            device_id=device,
            device_id_type=MESH,
        )

    def inside(self, source, target):
        slot = self.used
        self.used += 1
        return pltpu.make_async_copy(source, target, self.semaphores.at[0, slot])


def rows_at(start, size):
    return pl.ds(pl.multiple_of(start, STRIP), size)


class Spread:
    def __init__(self, device, full):
        self.device, self.full = device, full
        self.size = full.shape[0] // 4
        self.block = self.size // BLOCKS
        self.rows, self.core, self.passed, self.kept = {}, {}, {}, {}

    def where(self, core, row, index):
        return self.full.at[
            rows_at((core * 2 + row) * self.size + index * self.block, self.block)
        ]

    def put(self, index, source):
        device = self.device
        target = self.where(device.c, device.t, index)
        self.rows[index] = device.remote(source, target, device.other_row)
        self.core[index] = device.remote(source, target, device.other_core)
        self.kept[index] = device.inside(source, target)
        for copy in (self.rows[index], self.core[index], self.kept[index]):
            copy.start()

    def forward(self, index):
        device = self.device
        self.rows[index].wait_recv()
        place = self.where(device.c, 1 - device.t, index)
        self.passed[index] = device.remote(place, place, device.other_core)
        self.passed[index].start()

    def finish(self):
        for index in range(BLOCKS):
            self.rows[index].wait_send()
            self.core[index].wait()
            self.passed[index].wait()
            self.kept[index].wait()


class Collect:
    def __init__(self, device, partial, near, far, sent, came):
        self.device = device
        self.partial, self.near, self.far, self.sent, self.came = partial, near, far, sent, came
        self.size = partial.shape[0] // 4
        self.block = self.size // BLOCKS
        self.core, self.rows = {}, {}

    def start(self):
        device = self.device
        self.load = device.inside(
            self.partial.at[rows_at(device.c * 2 * self.size, 2 * self.size)], self.near
        )
        for part, row in enumerate((1 - device.t, device.t)):
            for index in range(BLOCKS):
                start = row * self.size + index * self.block
                copy = device.remote(
                    self.partial.at[rows_at((1 - device.c) * 2 * self.size + start, self.block)],
                    self.far.at[rows_at(start, self.block)],
                    device.other_core,
                )
                copy.start()
                self.core[part, index] = copy
        self.load.start()

    def pass_on(self, index):
        device = self.device
        if index == 0:
            self.load.wait()
        self.core[0, index].wait_recv()

        @pl.loop(0, self.block // STRIP)
        def _(strip):
            at = index * self.block + strip * STRIP
            rows = rows_at((1 - device.t) * self.size + at, STRIP)
            total = self.near[rows, :].astype(wide) + self.far[rows, :].astype(wide)
            self.sent[rows_at(at, STRIP), :] = total.astype(low)

        place = rows_at(index * self.block, self.block)
        self.rows[index] = device.remote(
            self.sent.at[place], self.came.at[place], device.other_row
        )
        self.rows[index].start()

    def take(self, index, use):
        device = self.device
        self.core[1, index].wait_recv()
        self.rows[index].wait_recv()

        @pl.loop(0, self.block // STRIP)
        def _(strip):
            at = index * self.block + strip * STRIP
            rows = rows_at(device.t * self.size + at, STRIP)
            mine = rows_at(at, STRIP)
            total = (
                self.near[rows, :].astype(wide)
                + self.far[rows, :].astype(wide)
                + self.came[mine, :].astype(wide)
            )
            use(mine, total)

    def finish(self):
        for index in range(BLOCKS):
            self.core[0, index].wait_send()
            self.core[1, index].wait_send()
            self.rows[index].wait_send()


class Given:
    parts = 2

    def __init__(self, grads):
        self.rows, self.columns = grads.shape
        self.grads = grads

    def take(self, start, size):
        return self.grads[rows_at(start, size), :].astype(wide)

    def source(self, start, size, keep):
        return self.grads.at[rows_at(start, size)]


class Product:
    parts = 1

    def __init__(self, left, right, start, columns):
        self.rows, self.columns = left.shape[1], columns
        self.left, self.right, self.start = left, right, start

    def take(self, start, size):
        left = self.left[:, pl.ds(pl.multiple_of(start, 128), size)]
        return dot(left, self.right[:, self.start : self.start + self.columns], 0, 0)

    def source(self, start, size, keep):
        keep[...] = self.take(start, size).astype(low)
        return keep


class RingSum:
    def __init__(self, device, grads, scratch, sums):
        self.device, self.grads, self.sums = device, grads, sums
        self.slots, self.totals, self.first = scratch
        self.half = grads.rows // device.count // 2
        self.parts = grads.parts
        self.part = self.half // self.parts
        self.copies = {}
        self.ticks = [
            (step, part) for step in range(device.count) for part in range(self.parts)
        ]

    def own(self, way, distance, part):
        owner = self.device.owner(-(1 - 2 * way) * distance)
        return (owner * 2 + way) * self.half + part * self.part

    def slot(self, way, step, part):
        return self.slots.at[
            way * (self.device.count - 1) + step, pl.ds(part * self.part, self.part)
        ]

    def send(self, way, step, part):
        device = self.device
        if step == 0:
            source = self.grads.source(self.own(way, 1, part), self.part, self.first.at[way])
        else:
            source = self.slot(way, step - 1, part)
        copy = device.remote(
            source, self.slot(way, step, part), {"w": device.owner(1 - 2 * way)}
        )
        copy.start()
        self.copies[way, step, part] = copy

    def tick(self, count=1):
        device = self.device
        for _ in range(count):
            if not self.ticks:
                return
            step, part = self.ticks.pop(0)
            for way in range(2):
                if step > 0:
                    own = self.grads.take(self.own(way, step + 1, part), self.part)
                    self.copies[way, step - 1, part].wait_recv()
                    slot = self.slot(way, step - 1, part)
                    total = (slot[...].astype(wide) + own).astype(low)
                    if step < device.count - 1:
                        slot[...] = total
                    else:
                        self.totals[way, pl.ds(part * self.part, self.part), :] = total
                if step < device.count - 1:
                    self.send(way, step, part)

    def close(self):
        device = self.device
        self.tick(len(self.ticks))
        self.away = device.remote(
            self.totals.at[1 - device.c], self.sums.at[device.c], device.other_core
        )
        self.kept = device.inside(self.totals.at[device.c], self.sums.at[device.c])
        self.away.start()
        self.kept.start()

    def finish(self):
        for copy in self.copies.values():
            copy.wait_send()
        self.away.wait()
        self.kept.wait()


def ring_shapes(columns, count):
    half = MODEL_WIDTH // count // 2
    return [
        pltpu.VMEM((2 * (count - 1), half, columns), low),
        pltpu.VMEM((2, half, columns), low),
        pltpu.VMEM((2, half, columns), low),
    ]


class RingWork:
    def __init__(self, pairs):
        self.pairs = pairs
        self.columns = [columns for _, _, _, columns in pairs]
        self.fit = (MODEL_WIDTH // lax.axis_size("w") // 2) % 128 == 0
        self.operands, self.places = [], []
        for left, right, start, columns in pairs:
            if self.fit:
                self.places.append((self.add(left), self.add(right), start, columns))
            else:
                part = right[:, start : start + columns]
                self.places.append((self.add(dot(left, part, 0, 0).astype(low)),))

    def add(self, value):
        for index, other in enumerate(self.operands):
            if other is value:
                return index
        self.operands.append(value)
        return len(self.operands) - 1

    def sources(self, refs):
        sources = [
            Product(refs[place[0]], refs[place[1]], *place[2:]) if self.fit else Given(refs[place[0]])
            for place in self.places
        ]
        return sources, refs[len(self.operands) :]

    def outputs(self):
        half = MODEL_WIDTH // lax.axis_size("w") // 2
        return [jax.ShapeDtypeStruct((2, half, size), low) for size in self.columns]

    def scratch(self):
        count = lax.axis_size("w")
        return [shape for size in self.columns for shape in ring_shapes(size, count)]

    def semaphores(self):
        return 4 * (lax.axis_size("w") + 1) * len(self.columns)


def collect_shapes(size):
    return [
        pltpu.VMEM((2 * size, MODEL_WIDTH), low),
        pltpu.VMEM((2 * size, MODEL_WIDTH), low),
        pltpu.VMEM((size, MODEL_WIDTH), low),
        pltpu.VMEM((size, MODEL_WIDTH), low),
    ]


def semaphores_for(count):
    return pltpu.SemaphoreType.DMA((2, count))


def settings(collective):
    return pltpu.CompilerParams(
        collective_id=collective, has_side_effects=True, vmem_limit_bytes=56 * 2**20
    )


def neighbours(device):
    return [
        device.other_core,
        device.other_row,
        {"w": device.owner(1)},
        {"w": device.owner(-1)},
    ]


class RingGather:
    def __init__(self, device, mine, other, full):
        self.device, self.full = device, full
        self.size = mine.shape[0]
        self.parts = 2
        self.part = self.size // self.parts
        here = rows_at((device.w * 2 + device.c) * self.size, self.size)
        self.kept = device.inside(mine, full.at[here])
        self.crossed = device.remote(other, full.at[here], device.other_core)
        self.copies = {}
        self.ticks = [
            (step, part) for step in range(device.count - 1) for part in range(self.parts)
        ]

    def start(self):
        self.kept.start()
        self.crossed.start()

    def ready(self):
        self.kept.wait()
        self.crossed.wait()

    def tick(self, count=1):
        device = self.device
        for _ in range(count):
            if not self.ticks:
                return
            step, part = self.ticks.pop(0)
            for way in range(2):
                if step > 0:
                    self.copies[way, step - 1, part].wait_recv()
                owner = device.owner(-(1 - 2 * way) * step)
                block = self.full.at[
                    rows_at((owner * 2 + way) * self.size + part * self.part, self.part)
                ]
                copy = device.remote(block, block, {"w": device.owner(1 - 2 * way)})
                copy.start()
                self.copies[way, step, part] = copy

    def finish(self):
        self.tick(len(self.ticks))
        for part in range(self.parts):
            for way in range(2):
                self.copies[way, self.device.count - 2, part].wait_recv()
        for copy in self.copies.values():
            copy.wait_send()


def gather_kernel(mine, other, first, second, full, first_full, second_full, semaphores):
    device = Device(semaphores)
    device.meet(neighbours(device))
    gather = RingGather(device, mine, other, full)
    gather.start()
    spreads = []
    for rows, target in ((first, first_full), (second, second_full)):
        spread = Spread(device, target)
        block = spread.block
        for index in range(BLOCKS):
            spread.put(index, rows.at[pl.ds(index * block, block)])
        spreads.append(spread)
    gather.ready()
    for spread in spreads:
        for index in range(BLOCKS):
            gather.tick(2)
            spread.forward(index)
    gather.finish()
    for spread in spreads:
        spread.finish()


def gather_attention(mine, other, first, second):
    count = lax.axis_size("w")
    rows = first.shape[0] * 4
    return pl.pallas_call(
        gather_kernel,
        out_shape=[
            jax.ShapeDtypeStruct((MODEL_WIDTH, mine.shape[1]), low),
            jax.ShapeDtypeStruct((rows, MODEL_WIDTH), low),
            jax.ShapeDtypeStruct((rows, MODEL_WIDTH), low),
        ],
        in_specs=[ANY] * 4,
        out_specs=[ANY] * 3,
        scratch_shapes=[semaphores_for(4 * (count - 1) + 8 * BLOCKS + 2)],
        compiler_params=settings(1),
        cost_estimate=pl.CostEstimate(flops=0, bytes_accessed=64 * 2**20, transcendentals=0),
        name="gather_attention",
    )(mine, other, first, second)


def forward_kernel(
    partial, rows, gain, mine, other, total, full, gathered,
    near, far, sent, came, normed, semaphores,
):
    device = Device(semaphores)
    device.meet(neighbours(device))
    collect = Collect(device, partial, near, far, sent, came)
    spread = Spread(device, full)
    gather = RingGather(device, mine, other, gathered)
    collect.start()
    gather.start()
    collect.pass_on(0)
    gather.ready()
    gather.tick(2)
    for index in range(1, BLOCKS):
        collect.pass_on(index)
    gather.tick(2)

    def use(at, value):
        total[at, :] = value
        middle = rows[at, :].astype(wide) + value
        normed[at, :] = normalize(middle, gain[...]).astype(low)

    for index in range(BLOCKS):
        collect.take(index, use)
        spread.put(index, normed.at[pl.ds(index * spread.block, spread.block)])
        gather.tick(1)
    gather.tick(2)
    for index in range(BLOCKS):
        spread.forward(index)
        gather.tick(1)
    gather.finish()
    spread.finish()
    collect.finish()


def exchange_forward(partial, rows, gain, mine, other):
    size = rows.shape[0]
    count = lax.axis_size("w")
    return pl.pallas_call(
        forward_kernel,
        out_shape=[
            jax.ShapeDtypeStruct((size, MODEL_WIDTH), wide),
            jax.ShapeDtypeStruct((4 * size, MODEL_WIDTH), low),
            jax.ShapeDtypeStruct((MODEL_WIDTH, mine.shape[1]), low),
        ],
        in_specs=[ANY, VMEM, VMEM, ANY, ANY],
        out_specs=[VMEM, ANY, ANY],
        scratch_shapes=collect_shapes(size)
        + [
            pltpu.VMEM((size, MODEL_WIDTH), low),
            semaphores_for(16 * BLOCKS + 4 * count + 2),
        ],
        compiler_params=settings(2),
        cost_estimate=pl.CostEstimate(flops=0, bytes_accessed=64 * 2**20, transcendentals=0),
        name="exchange_forward",
    )(partial, rows, gain, mine, other)


class Rings:
    def __init__(self, rings):
        self.rings = rings
        self.next = 0

    def tick(self, count=1):
        for _ in range(count):
            ring = self.rings[self.next]
            self.next = (self.next + 1) % len(self.rings)
            ring.tick()

    def finish(self):
        while any(ring.ticks for ring in self.rings):
            self.tick()
        for ring in self.rings:
            ring.close()
        for ring in self.rings:
            ring.finish()


def norm_back_rows(values, gain, upstream):
    factor = lax.rsqrt(jnp.mean(values * values, axis=-1, keepdims=True) + norm_epsilon)
    weighted = upstream * gain
    projected = jnp.mean(weighted * values, axis=-1, keepdims=True)
    result = factor * weighted - values * (factor * factor * factor) * projected
    return result, jnp.sum(upstream * values * factor, axis=0, keepdims=True)


def backward_kernel(work, partial, output, middle, rows, gain, counted, *refs):
    count = len(work.columns)
    grads, refs = work.sources(refs)
    grad, gain_grad, output_total, squares, full, refs = *refs[:5], refs[5:]
    sums, refs = refs[:count], refs[count:]
    rounded = refs[8]
    device = Device(refs[-1])
    device.meet(neighbours(device))
    collect = Collect(device, partial, *refs[:4])
    output_collect = Collect(device, output, *refs[4:8])
    spread = Spread(device, full)
    rings = Rings(
        [RingSum(device, grads[i], refs[9 + 3 * i : 12 + 3 * i], sums[i]) for i in range(count)]
    )
    collect.start()
    rings.tick(2)
    gain_grad[...] = jnp.zeros_like(gain_grad)
    squares[...] = jnp.zeros_like(squares)
    for index in range(BLOCKS):
        collect.pass_on(index)
    rings.tick(count - 2)
    output_collect.start()

    def use(at, upstream):
        result, gained = norm_back_rows(middle[at, :], gain[...], upstream)
        result = result + rows[at, :].astype(wide)
        grad[at, :] = result
        rounded[at, :] = result.astype(low)
        gain_grad[...] += gained

    def use_output(at, value):
        output_total[at, :] = value
        squares[...] += jnp.sum(counted[at, :] * value * value, axis=0, keepdims=True)

    for index in range(BLOCKS):
        collect.take(index, use)
        spread.put(index, rounded.at[pl.ds(index * spread.block, spread.block)])
        rings.tick(1)
    for index in range(BLOCKS):
        output_collect.pass_on(index)
    rings.tick(2)
    for index in range(BLOCKS):
        spread.forward(index)
        rings.tick(1)
    for index in range(BLOCKS):
        output_collect.take(index, use_output)
        rings.tick(1)
    rings.finish()
    spread.finish()
    collect.finish()
    output_collect.finish()


def exchange_backward(partial, output, middle, rows, gain, counted, pairs):
    size = rows.shape[0]
    work = RingWork(pairs)

    def body(*refs):
        backward_kernel(work, *refs)

    return pl.pallas_call(
        body,
        out_shape=[
            jax.ShapeDtypeStruct((size, MODEL_WIDTH), wide),
            jax.ShapeDtypeStruct((1, MODEL_WIDTH), wide),
            jax.ShapeDtypeStruct((size, MODEL_WIDTH), wide),
            jax.ShapeDtypeStruct((1, MODEL_WIDTH), wide),
            jax.ShapeDtypeStruct((4 * size, MODEL_WIDTH), low),
            *work.outputs(),
        ],
        in_specs=[ANY, ANY] + [VMEM] * (4 + len(work.operands)),
        out_specs=[VMEM] * 4 + [ANY] * (1 + len(work.columns)),
        scratch_shapes=collect_shapes(size) * 2
        + [pltpu.VMEM((size, MODEL_WIDTH), low)]
        + work.scratch()
        + [semaphores_for(32 * BLOCKS + work.semaphores())],
        compiler_params=settings(3),
        cost_estimate=pl.CostEstimate(flops=0, bytes_accessed=128 * 2**20, transcendentals=0),
        name="exchange_backward",
    )(partial, output, middle, rows, gain, counted, *work.operands)


class Total:
    def __init__(self, device, mine, crossed, gathered):
        self.device, self.mine = device, mine
        self.crossed, self.gathered = crossed, gathered
        self.copies = {}
        self.steps = [("c", 0), ("t", 0)] + [("w", step) for step in range(device.count // 2)]

    def tick(self):
        device = self.device
        if not self.steps:
            return
        axis, step = self.steps.pop(0)
        if axis != "w":
            slot = 0 if axis == "c" else 1
            partner = device.other_core if axis == "c" else device.other_row
            copy = device.remote(self.mine.at[slot], self.crossed.at[slot], partner)
            copy.start()
            copy.wait()
            total = self.mine[slot] + self.crossed[slot]
            if slot == 0:
                self.mine[1] = total
            else:
                self.gathered[device.w] = total
            return
        for way in range(2):
            if way == 1 and step == device.count // 2 - 1:
                continue
            if step > 0:
                self.copies[way, step - 1].wait_recv()
            block = self.gathered.at[device.owner(-(1 - 2 * way) * step)]
            copy = device.remote(block, block, {"w": device.owner(1 - 2 * way)})
            copy.start()
            self.copies[way, step] = copy

    def finish(self, target):
        while self.steps:
            self.tick()
        half = self.device.count // 2
        self.copies[0, half - 1].wait_recv()
        self.copies[1, half - 2].wait_recv()
        for copy in self.copies.values():
            copy.wait_send()
        target[...] = self.gathered[0]
        for index in range(1, self.device.count):
            target[...] += self.gathered[index]


def last_kernel(work, first, tokens, gain, middle_grad, stats, *refs):
    count = len(work.columns)
    grads, refs = work.sources(refs)
    first_total, stats_total, refs = refs[0], refs[1], refs[2:]
    sums, scratch = refs[:count], refs[count:]
    device = Device(scratch[-1])
    device.meet(neighbours(device))
    collect = Collect(device, first, *scratch[:4])
    mine, crossed, gathered = scratch[4:7]
    rings = Rings(
        [
            RingSum(device, grads[i], scratch[7 + 3 * i : 10 + 3 * i], sums[i])
            for i in range(count)
        ]
    )
    total = Total(device, mine, crossed, gathered)
    mine[0] = stats[...]
    collect.start()
    rings.tick(2)
    for index in range(BLOCKS):
        collect.pass_on(index)
    rings.tick(count - 2)

    def use(at, upstream):
        result, gained = norm_back_rows(tokens[at, :].astype(wide), gain[...], upstream)
        first_total[at, :] = result + middle_grad[at, :]
        mine[0, 0:1, :] += gained

    for index in range(BLOCKS):
        collect.take(index, use)
        rings.tick(1)
    while total.steps:
        total.tick()
        rings.tick(1)
    rings.finish()
    total.finish(stats_total)
    collect.finish()


def exchange_last(first, tokens, gain, middle_grad, stats, pairs):
    size = tokens.shape[0]
    count = lax.axis_size("w")
    work = RingWork(pairs)

    def body(*refs):
        last_kernel(work, *refs)

    return pl.pallas_call(
        body,
        out_shape=[
            jax.ShapeDtypeStruct((size, MODEL_WIDTH), wide),
            jax.ShapeDtypeStruct(stats.shape, wide),
            *work.outputs(),
        ],
        in_specs=[ANY] + [VMEM] * (4 + len(work.operands)),
        out_specs=[VMEM] * 2 + [ANY] * len(work.columns),
        scratch_shapes=collect_shapes(size)
        + [
            pltpu.VMEM((2, *stats.shape), wide),
            pltpu.VMEM((2, *stats.shape), wide),
            pltpu.VMEM((count, *stats.shape), wide),
        ]
        + work.scratch()
        + [semaphores_for(16 * BLOCKS + 2 * count + 4 + work.semaphores())],
        compiler_params=settings(4),
        cost_estimate=pl.CostEstimate(flops=0, bytes_accessed=128 * 2**20, transcendentals=0),
        name="exchange_last",
    )(first, tokens, gain, middle_grad, stats, *work.operands)


FEEDFORWARD_ROWS = 256
FEEDFORWARD_COLUMNS = 512


def feedforward_kernel(
    sizes, core, rows, upstream, large, small, gate_out, up_out, hidden_out, back_out, down_out
):
    weights = [(large.at[0], 0, sizes[0]), (small, sizes[0], sizes[1])]
    for weight, base, size in weights:
        for start in range(0, size, FEEDFORWARD_COLUMNS):
            width = min(FEEDFORWARD_COLUMNS, size - start)
            columns = slice(base + start, base + start + width)
            gate_part = dot(rows[...], weight[:, start : start + width], 1, 0)
            up_part = dot(rows[...], weight[:, size + start : size + start + width], 1, 0)
            hidden_grad = dot(
                upstream[...], weight[:, 2 * size + start : 2 * size + start + width], 1, 0
            )
            sigmoid_gate = jax.nn.sigmoid(gate_part)
            silu_gate = gate_part * sigmoid_gate
            hidden_out[:, columns] = (silu_gate * up_part).astype(low)
            gate_out[:, columns] = (
                hidden_grad * up_part * sigmoid_gate * (1.0 + gate_part * (1.0 - sigmoid_gate))
            ).astype(low)
            up_out[:, columns] = (hidden_grad * silu_gate).astype(low)
    for start in range(0, MODEL_WIDTH, FEEDFORWARD_COLUMNS):
        across = slice(start, start + FEEDFORWARD_COLUMNS)
        back = 0.0
        down = 0.0
        for weight, base, size in weights:
            columns = slice(base, base + size)
            back = back + dot(gate_out[:, columns], weight[across, :size], 1, 1)
            back = back + dot(up_out[:, columns], weight[across, size : 2 * size], 1, 1)
            down = down + dot(hidden_out[:, columns], weight[across, 2 * size :], 1, 1)
        back_out[:, across] = back.astype(low)
        down_out[:, across] = down.astype(low)


def feedforward(core, rows, upstream, large, small):
    sizes = (large.shape[2] // 3, small.shape[1] // 3)
    count = rows.shape[0]
    hidden = sum(sizes)

    def body(*refs):
        feedforward_kernel(sizes, *refs)

    def block(columns):
        return pl.BlockSpec((FEEDFORWARD_ROWS, columns), lambda index, core: (index, 0))

    once = pl.Buffered(1)
    return pl.pallas_call(
        body,
        grid_spec=pltpu.PrefetchScalarGridSpec(
            num_scalar_prefetch=1,
            grid=(count // FEEDFORWARD_ROWS,),
            in_specs=[
                block(MODEL_WIDTH),
                block(MODEL_WIDTH),
                pl.BlockSpec(
                    (1, *large.shape[1:]),
                    lambda index, core: (core[0], 0, 0),
                    pipeline_mode=once,
                ),
                pl.BlockSpec(small.shape, lambda index, core: (0, 0), pipeline_mode=once),
            ],
            out_specs=[block(hidden)] * 3 + [block(MODEL_WIDTH)] * 2,
        ),
        out_shape=[jax.ShapeDtypeStruct((count, hidden), low)] * 3
        + [jax.ShapeDtypeStruct((count, MODEL_WIDTH), low)] * 2,
        compiler_params=pltpu.CompilerParams(vmem_limit_bytes=52 * 2**20),
        cost_estimate=pl.CostEstimate(
            flops=12 * count * MODEL_WIDTH * hidden,
            bytes_accessed=48 * 2**20,
            transcendentals=count * hidden,
        ),
        name="feedforward",
    )(core, rows, upstream, large, small)


def head_rows(values, gain, cosine, sine):
    factor = lax.rsqrt(jnp.mean(values * values, axis=-1, keepdims=True) + norm_epsilon)
    normed = values * factor * gain
    return (normed * cosine + pltpu.roll(normed, HEAD_WIDTH // 2, 1) * sine).astype(low)


def head_back(values, gain, cosine, sine, upstream):
    turned = upstream * cosine - pltpu.roll(upstream, HEAD_WIDTH // 2, 1) * sine
    return norm_back_rows(values, gain, turned)


def head_at(index):
    return slice(index * HEAD_WIDTH, (index + 1) * HEAD_WIDTH)


def gate_column(logits, head):
    lanes = lax.broadcasted_iota(jnp.int32, logits.shape, 1)
    logit = jnp.sum(jnp.where(lanes == head, logits, 0.0), axis=-1, keepdims=True)
    return jax.nn.sigmoid(logit)


def probabilities(queries, keys, start, valid_count, piece_start):
    raw = dot(queries, keys, 1, 1) * HEAD_WIDTH ** (-0.5)
    row = start + lax.broadcasted_iota(jnp.int32, raw.shape, 0)
    column = lax.broadcasted_iota(jnp.int32, raw.shape, 1)
    last = piece_start + PIC
    inside = (row >= piece_start) & (row < last) & (column >= piece_start) & (column < last)
    allowed = (column < valid_count) & ((column <= row) | inside)
    scores = jnp.where(allowed, raw, masked_score)
    expos = jnp.exp(scores - jnp.max(scores, axis=-1, keepdims=True))
    return expos * (1.0 / jnp.sum(expos, axis=-1, keepdims=True))


QUERY_ROWS = 256


def attention_forward_kernel(groups, share, valid, start, pre, gains, cosine, sine, gated):
    sequence = pl.program_id(0)
    heads = groups * share
    length = pre.shape[0]
    for group in range(groups):
        keys = head_rows(pre[:, head_at(heads + group)], gains[1:2, :], cosine[...], sine[...])
        values = pre[:, head_at(heads + groups + group)].astype(low)
        for head in range(group * share, (group + 1) * share):
            for at in range(0, length, QUERY_ROWS):
                rows = slice(at, at + QUERY_ROWS)
                queries = head_rows(
                    pre[rows, head_at(head)], gains[0:1, :], cosine[rows, :], sine[rows, :]
                )
                probs = probabilities(queries, keys, at, valid[sequence], start[sequence])
                mixed = dot(probs.astype(low), values, 1, 0)
                gate = gate_column(pre[rows, head_at(heads + 2 * groups)], head)
                gated[rows, head_at(head)] = (mixed * gate).astype(low)


def attention_backward_kernel(
    groups, share, valid, start, pre, upstream, gains, cosine, sine, grads, gain_grads
):
    sequence = pl.program_id(0)
    heads = groups * share
    length = pre.shape[0]
    scale = HEAD_WIDTH ** (-0.5)

    @pl.when(sequence == 0)
    def _():
        gain_grads[...] = jnp.zeros_like(gain_grads)

    logit_grads = [jnp.zeros((QUERY_ROWS, HEAD_WIDTH), wide)] * (length // QUERY_ROWS)
    for group in range(groups):
        key_pre = pre[:, head_at(heads + group)]
        keys = head_rows(key_pre, gains[1:2, :], cosine[...], sine[...])
        values = pre[:, head_at(heads + groups + group)].astype(low)
        value_grad = jnp.zeros((length, HEAD_WIDTH), wide)
        key_grad = jnp.zeros((length, HEAD_WIDTH), wide)
        for head in range(group * share, (group + 1) * share):
            for block, at in enumerate(range(0, length, QUERY_ROWS)):
                rows = slice(at, at + QUERY_ROWS)
                query_pre = pre[rows, head_at(head)]
                queries = head_rows(query_pre, gains[0:1, :], cosine[rows, :], sine[rows, :])
                probs = probabilities(queries, keys, at, valid[sequence], start[sequence])
                probs_low = probs.astype(low)
                mixed = dot(probs_low, values, 1, 0)
                gate = gate_column(pre[rows, head_at(heads + 2 * groups)], head)
                gated_grad = upstream[rows, head_at(head)]
                mixed_grad = (gated_grad * gate).astype(low)
                logit_grad = (
                    jnp.sum(gated_grad * mixed, axis=-1, keepdims=True) * gate * (1.0 - gate)
                )
                lanes = lax.broadcasted_iota(jnp.int32, (QUERY_ROWS, HEAD_WIDTH), 1)
                logit_grads[block] = logit_grads[block] + jnp.where(lanes == head, logit_grad, 0.0)
                value_grad = value_grad + dot(probs_low, mixed_grad, 0, 0)
                prob_grad = dot(mixed_grad, values, 1, 1)
                score_grad = (
                    probs * (prob_grad - jnp.sum(prob_grad * probs, axis=-1, keepdims=True))
                ).astype(low)
                key_grad = key_grad + dot(score_grad, queries, 0, 0)
                query_grad, gained = head_back(
                    query_pre,
                    gains[0:1, :],
                    cosine[rows, :],
                    sine[rows, :],
                    dot(score_grad, keys, 1, 0) * scale,
                )
                grads[rows, head_at(head)] = query_grad.astype(low)
                gain_grads[0:1, :] += gained
        key_grad, gained = head_back(
            key_pre, gains[1:2, :], cosine[...], sine[...], key_grad * scale
        )
        gain_grads[1:2, :] += gained
        grads[:, head_at(heads + group)] = key_grad.astype(low)
        grads[:, head_at(heads + groups + group)] = value_grad.astype(low)
    for block, at in enumerate(range(0, length, QUERY_ROWS)):
        grads[slice(at, at + QUERY_ROWS), head_at(heads + 2 * groups)] = logit_grads[block].astype(
            low
        )


def sequence_block(columns, length):
    return pl.BlockSpec((length, columns), lambda sequence: (sequence, 0))


def fixed_block(*shape):
    return pl.BlockSpec(shape, lambda sequence: (0, 0))


SCALARS = pl.BlockSpec(memory_space=pltpu.SMEM)


def attention_forward(groups, share, valid, start, pre, gains, cosine, sine):
    length, columns = cosine.shape[0], groups * share * HEAD_WIDTH

    def body(*refs):
        attention_forward_kernel(groups, share, *refs)

    return pl.pallas_call(
        body,
        grid=(pre.shape[0] // length,),
        out_shape=jax.ShapeDtypeStruct((pre.shape[0], columns), low),
        in_specs=[
            SCALARS,
            SCALARS,
            sequence_block(pre.shape[1], length),
            fixed_block(2, HEAD_WIDTH),
            fixed_block(length, HEAD_WIDTH),
            fixed_block(length, HEAD_WIDTH),
        ],
        out_specs=sequence_block(columns, length),
        compiler_params=pltpu.CompilerParams(vmem_limit_bytes=48 * 2**20),
        cost_estimate=pl.CostEstimate(
            flops=2**30, bytes_accessed=8 * 2**20, transcendentals=2**21
        ),
        name="attention_forward",
    )(valid, start, pre, gains, cosine, sine)


def attention_backward(groups, share, valid, start, pre, upstream, gains, cosine, sine):
    length = cosine.shape[0]

    def body(*refs):
        attention_backward_kernel(groups, share, *refs)

    return pl.pallas_call(
        body,
        grid=(pre.shape[0] // length,),
        out_shape=[
            jax.ShapeDtypeStruct(pre.shape, low),
            jax.ShapeDtypeStruct((2, HEAD_WIDTH), wide),
        ],
        in_specs=[
            SCALARS,
            SCALARS,
            sequence_block(pre.shape[1], length),
            sequence_block(upstream.shape[1], length),
            fixed_block(2, HEAD_WIDTH),
            fixed_block(length, HEAD_WIDTH),
            fixed_block(length, HEAD_WIDTH),
        ],
        out_specs=[sequence_block(pre.shape[1], length), fixed_block(2, HEAD_WIDTH)],
        compiler_params=pltpu.CompilerParams(vmem_limit_bytes=48 * 2**20),
        cost_estimate=pl.CostEstimate(
            flops=2**32, bytes_accessed=12 * 2**20, transcendentals=2**21
        ),
        name="attention_backward",
    )(valid, start, pre, upstream, gains, cosine, sine)


def take_columns(sums, start, size):
    part = sums[:, :, start : start + size].astype(wide)
    return jnp.concatenate([part[0], part[1]], axis=1)


def adam_kernel(layouts, names, *refs):
    sources, refs = dict(zip(names, refs)), refs[len(names) :]
    count = len(layouts)
    states, refs = refs[: 3 * count], refs[3 * count :]
    targets, refs = refs[: 3 * count], refs[3 * count :]
    buffers, semaphores = refs[: 3 * count], refs[3 * count]
    loads = [
        pltpu.make_async_copy(states[i], buffers[i], semaphores.at[0, i]) for i in range(3 * count)
    ]
    stores = [
        pltpu.make_async_copy(buffers[i], targets[i], semaphores.at[1, i])
        for i in range(3 * count)
    ]
    for load in loads:
        load.start()
    for number, (transposed, rate, leads) in enumerate(layouts):
        matrix = buffers[3 * number : 3 * number + 3]
        for load in loads[3 * number : 3 * number + 3]:
            load.wait()
        for lead, pieces in enumerate(leads):
            quarter = sum(size for _, _, size in pieces)
            for core in range(2):
                start = core * quarter
                for name, column, size in pieces:
                    step = min(size, 256)

                    @pl.loop(0, size // step)
                    def _(block):
                        columns = pl.ds(pl.multiple_of(column + block * step, 128), step)
                        gradient = sources[name][core, :, columns].astype(wide)
                        place = pl.ds(pl.multiple_of(start + block * step, 128), step)
                        if transposed:
                            gradient = gradient.T
                            at = (place, slice(None))
                        elif len(leads) > 1:
                            at = (lead, slice(None), place)
                        else:
                            at = (slice(None), place)
                        weight, moment, square = (part[at] for part in matrix)
                        for part, value in zip(
                            matrix,
                            adam_update(weight, moment, square, gradient, rate, weight_decay),
                        ):
                            part[at] = value

                    start += size
        for store in stores[3 * number : 3 * number + 3]:
            store.start()
    for store in stores:
        store.wait()


def adam_matrices(layouts, sums, states):
    def body(*refs):
        adam_kernel(layouts, list(sums), *refs)

    shapes = [jax.ShapeDtypeStruct(value.shape, value.dtype) for value in states]
    return pl.pallas_call(
        body,
        out_shape=shapes,
        in_specs=[VMEM] * len(sums) + [ANY] * len(states),
        out_specs=[ANY] * len(states),
        scratch_shapes=[pltpu.VMEM(value.shape, value.dtype) for value in states]
        + [pltpu.SemaphoreType.DMA((2, len(states)))],
        compiler_params=pltpu.CompilerParams(vmem_limit_bytes=48 * 2**20),
        cost_estimate=pl.CostEstimate(
            flops=2**25, bytes_accessed=40 * 2**20, transcendentals=2**21
        ),
        name="adam_matrices",
    )(*sums.values(), *states)


def local(
    tokens,
    cotangent,
    valid_len,
    pic_start,
    norm_gains,
    norm_moment,
    norm_square,
    head_gains,
    head_moment,
    head_square,
    query_weight,
    query_moment,
    query_square,
    keyvalue_matrix,
    keyvalue_first_moment,
    keyvalue_second_moment,
    headgate_weight,
    headgate_moment,
    headgate_square,
    output_weight,
    output_moment,
    output_square,
    gateup_weight,
    gateup_moment,
    gateup_square,
    down_weight,
    down_moment,
    down_square,
):
    local_rows = tokens.shape[0]
    length_value = local_rows * 2
    rows = length_value * 2
    group = lax.axis_index("w")
    core = lax.axis_index("c")
    place = lax.axis_index("t")
    heads_here = query_weight.shape[1] // HEAD_WIDTH // 2
    groups_here = keyvalue_matrix.shape[2] // HEAD_WIDTH // 2
    share = heads_here // groups_here
    head_cols = heads_here * HEAD_WIDTH
    group_cols = groups_here * HEAD_WIDTH
    hidden_here = gateup_weight.shape[2] // 2

    bounds = [0, head_cols, group_cols, group_cols, 128, head_cols]
    edges = [sum(bounds[: i + 1]) for i in range(6)]
    quarters = []
    for index in range(2):
        pieces = []
        for matrix in (
            query_weight, keyvalue_matrix[0], keyvalue_matrix[1], headgate_weight, output_weight.T
        ):
            size = matrix.shape[1] // 2
            piece = matrix[:, index * size : (index + 1) * size].astype(low)
            pieces.append(jnp.pad(piece, ((0, 0), (0, -size % 128))))
        quarters.append(jnp.concatenate(pieces, axis=1))
    residual = tokens.astype(wide)
    attention_full, first_full, output_grad_full = gather_attention(
        jnp.where(core == 0, quarters[0], quarters[1]),
        jnp.where(core == 0, quarters[1], quarters[0]),
        normalize(residual, norm_gains[0]).astype(low),
        cotangent,
    )
    matrices = (gateup_weight[0], gateup_weight[1], down_weight.T)
    late_size = hidden_here // 3
    early_size = hidden_here - late_size

    def quarter_columns(index, start, size):
        return jnp.concatenate(
            [
                matrix[:, index * hidden_here + start : index * hidden_here + start + size].astype(
                    low
                )
                for matrix in matrices
            ],
            axis=1,
        )

    large_block = jnp.stack([quarter_columns(index, 0, early_size) for index in range(2)])
    attention_full, large_block = lax.optimization_barrier((attention_full, large_block))
    large_both = lax.all_gather(large_block, ("w", "c"), axis=1, tiled=True)
    small_quarters = [quarter_columns(index, early_size, late_size) for index in range(2)]
    projection_full, output_full = attention_full[:, : edges[4]], attention_full[:, edges[4] :]
    valid_pair = lax.dynamic_slice_in_dim(valid_len, 2 * group, 2)
    start_pair = lax.dynamic_slice_in_dim(pic_start, 2 * group, 2)
    cosine, sine = rotary_tables(length_value)
    projected = dot(first_full, projection_full, 1, 0)
    gated_low = attention_forward(
        groups_here, share, valid_pair, start_pair, projected, head_gains, cosine, sine
    )
    attention_local, second_full, small_full = exchange_forward(
        dot(gated_low, output_full, 1, 1).astype(low),
        tokens,
        norm_gains[1:2],
        jnp.where(core == 0, small_quarters[0], small_quarters[1]),
        jnp.where(core == 0, small_quarters[1], small_quarters[0]),
    )
    middle = residual + attention_local

    gate_grad, up_grad, hidden_low, second_partial, feedforward_partial = feedforward(
        core[None], second_full, output_grad_full, large_both, small_full
    )
    own_places = place * local_rows + jnp.arange(local_rows, dtype=jnp.int32)
    counted = (own_places < valid_pair[core]).astype(wide)[:, None]
    split = hidden_here // 2
    pieces = [(0, split), (split, hidden_here - split)]
    middle_grad, second_gain_grad, feedforward_local, output_squares, attention_grad, *sums = (
        exchange_backward(
            second_partial,
            feedforward_partial,
            middle,
            cotangent,
            norm_gains[1:2],
            counted,
            [(second_full, gate_grad, *piece) for piece in pieces]
            + [(second_full, up_grad, *piece) for piece in pieces],
        )
    )
    block_output = (middle + feedforward_local).astype(low)
    projected_grad, head_gain_grads = attention_backward(
        groups_here,
        share,
        valid_pair,
        start_pair,
        projected,
        dot(attention_grad, output_full, 1, 0),
        head_gains,
        cosine,
        sine,
    )
    first_partial = dot(projected_grad, projection_full, 1, 1)
    squares = jnp.stack(
        [
            jnp.sum(counted * residual * residual),
            jnp.sum(counted * attention_local * attention_local),
        ]
    )
    small = jnp.concatenate([head_gain_grads.reshape(-1), squares])
    nothing = jnp.zeros((1, MODEL_WIDTH), wide)
    stats = jnp.concatenate(
        [
            nothing,
            second_gain_grad,
            jnp.pad(small, (0, MODEL_WIDTH - small.shape[0]))[None],
            output_squares,
            jnp.tile(nothing, (4, 1)),
        ]
    )
    tokens_grad, stats, projected_sums, output_sums, *more = exchange_last(
        first_partial.astype(low),
        tokens,
        norm_gains[0:1],
        middle_grad,
        stats,
        [
            (first_full, projected_grad, 0, edges[4]),
            (attention_grad, gated_low, 0, head_cols),
        ]
        + [(output_grad_full, hidden_low, *piece) for piece in pieces],
    )
    norms_total = stats[:2]
    heads_total = stats[2, : 2 * HEAD_WIDTH].reshape(2, HEAD_WIDTH)
    squares_total = jnp.concatenate(
        [stats[2, 2 * HEAD_WIDTH : 2 * HEAD_WIDTH + 2], jnp.sum(stats[3], keepdims=True)]
    )
    denominator = jnp.sum(valid_len).astype(wide) * MODEL_WIDTH
    branch_scales = jnp.sqrt(squares_total / denominator)
    input_rate = MODEL_WIDTH ** (-0.5)
    down_rate = FF ** (-0.5)
    output_rate = max(QUERY_HEADS * HEAD_WIDTH // 128, 4) ** (-0.5)
    gain_rate = 0.5
    norms_new = adam_update(norm_gains, norm_moment, norm_square, norms_total, gain_rate, 0.0)
    heads_new = adam_update(head_gains, head_moment, head_square, heads_total, gain_rate, 0.0)
    headgate_new = adam_update(
        headgate_weight,
        headgate_moment,
        headgate_square,
        take_columns(projected_sums, edges[3], heads_here),
        input_rate,
        weight_decay,
    )
    first_size, second_size = split, hidden_here - split
    layouts = [
        (
            False,
            input_rate,
            [
                [("gate 0", 0, first_size), ("gate 1", 0, second_size)],
                [("up 0", 0, first_size), ("up 1", 0, second_size)],
            ],
        ),
        (True, down_rate, [[("down 0", 0, first_size), ("down 1", 0, second_size)]]),
        (False, input_rate, [[("projected", edges[0], head_cols)]]),
        (
            False,
            input_rate,
            [[("projected", edges[1], group_cols)], [("projected", edges[2], group_cols)]],
        ),
        (True, output_rate, [[("output", 0, head_cols)]]),
    ]
    names = ["gate 0", "gate 1", "up 0", "up 1", "down 0", "down 1"]
    sums = dict(zip(names, [*sums, *more]))
    sums["projected"], sums["output"] = projected_sums, output_sums
    updated = adam_matrices(
        layouts,
        sums,
        [
            gateup_weight,
            gateup_moment,
            gateup_square,
            down_weight,
            down_moment,
            down_square,
            query_weight,
            query_moment,
            query_square,
            keyvalue_matrix,
            keyvalue_first_moment,
            keyvalue_second_moment,
            output_weight,
            output_moment,
            output_square,
        ],
    )
    gateup_new, down_new, query_new, keyvalue_new, output_new = (
        updated[3 * i : 3 * i + 3] for i in range(5)
    )
    return (
        block_output,
        tokens_grad,
        branch_scales,
        *norms_new,
        *heads_new,
        *query_new,
        *keyvalue_new,
        *headgate_new,
        *output_new,
        *gateup_new,
        *down_new,
    )


def solution(mesh):
    fsdp, tp = mesh.devices.shape
    fine = Mesh(mesh.devices.reshape(fsdp // 2, 2, tp), ("w", "c", "t"))
    whole = ("w", "c")
    rows = P(("w", "c", "t"), None)
    first = P(whole, "t")
    second = P(None, whole, "t")
    last = P("t", whole)
    matrices = (first,) * 3 + (second,) * 3 + (first,) * 3 + (last,) * 3 + (second,) * 3 + (last,) * 3
    return jax.shard_map(
        local,
        mesh=fine,
        in_specs=(rows, rows, P(), P()) + (P(),) * 6 + matrices,
        out_specs=(rows, rows, P()) + (P(),) * 6 + matrices,
        check_vma=False,
    )
```

```python
import jax
import jax.numpy as jnp
from jax import lax
from jax.experimental import pallas as pl
from jax.experimental.pallas import tpu as pltpu
from jax.sharding import Mesh
from jax.sharding import PartitionSpec as P

MODEL_WIDTH = 2048
QUERY_HEADS = 16
HEAD_WIDTH = 128
FF = 6144
PIC = 256
STEP = 10

norm_epsilon = 1e-06
rope_base = 1000000.0
beta_first = 0.9
beta_second = 0.999
adam_epsilon = 1e-08
weight_decay = 0.1
masked_score = -1e30
low = jnp.bfloat16
wide = jnp.float32


def normalize(values, scaling):
    return (
        values
        * lax.rsqrt(jnp.mean(values * values, axis=-1, keepdims=True) + norm_epsilon)
        * scaling
    )


def norm_back(values, scaling, upstream):
    factor = lax.rsqrt(jnp.mean(values * values, axis=-1, keepdims=True) + norm_epsilon)
    weighted = upstream * scaling
    projected = jnp.mean(weighted * values, axis=-1, keepdims=True)
    result = factor * weighted - values * (factor * factor * factor) * projected
    return (result, jnp.sum(upstream * values * factor, axis=tuple(range(values.ndim - 1))))


def rotary_tables(length_value):
    halves = HEAD_WIDTH // 2
    frequency = rope_base ** (-(jnp.arange(halves, dtype=wide) * 2.0 / HEAD_WIDTH))
    angles = jnp.arange(length_value, dtype=wide)[:, None] * frequency[None, :]
    cosine, sine = jnp.cos(angles), jnp.sin(angles)
    return (
        jnp.concatenate([cosine, cosine], axis=1),
        jnp.concatenate([-sine, sine], axis=1),
    )


def adam_update(weight, moment, square, gradient, step_rate, decay_rate):
    moment_new = beta_first * moment + (1.0 - beta_first) * gradient
    square_new = beta_second * square + (1.0 - beta_second) * gradient * gradient
    bias_first = 1.0 - beta_first**STEP
    bias_second = 1.0 - beta_second**STEP
    update = moment_new / bias_first / (jnp.sqrt(square_new / bias_second) + adam_epsilon)
    return (weight - step_rate * (update + decay_rate * weight), moment_new, square_new)


def dot(left, right, left_dim, right_dim):
    return lax.dot_general(
        left, right, (((left_dim,), (right_dim,)), ((), ())), preferred_element_type=wide
    )


def fetch(parts):
    pieces = []
    for core in range(2):
        for part in parts:
            size = part.shape[1] // 2
            pieces.append(part[:, core * size : (core + 1) * size].astype(low))
    count = len(parts)
    local_block = jnp.stack(
        [jnp.concatenate(pieces[core * count : (core + 1) * count], axis=1) for core in range(2)]
    )
    return lax.all_gather(local_block, ("w", "c"), axis=1, tiled=True)


def columns_of(both, start, size):
    return lax.dynamic_slice(
        both, (lax.axis_index("c"), 0, start), (1, both.shape[1], size)
    ).reshape(both.shape[1], size)


MESH = pl.DeviceIdType.MESH
BLOCKS = 4
STRIP = 16
ANY = pl.BlockSpec(memory_space=pl.ANY)
VMEM = pl.BlockSpec(memory_space=pltpu.VMEM)


def ring_place(index, count):
    odd = lax.rem(index, 2)
    pair = lax.div(index, 2)
    return (1 - odd) * pair + odd * (count - 1 - pair)


def ring_index(place, count):
    late = lax.div(place, count // 2)
    return (1 - late) * 2 * place + late * (2 * (count - 1 - place) + 1)


class Device:
    def __init__(self, semaphores):
        self.w, self.c, self.t = (lax.axis_index(axis) for axis in ("w", "c", "t"))
        self.count = lax.axis_size("w")
        self.place = ring_place(self.w, self.count)
        self.semaphores = semaphores
        self.used = 0
        self.other_core = {"c": 1 - self.c}
        self.other_row = {"t": 1 - self.t}

    def owner(self, distance):
        return ring_index(lax.rem(self.place + distance + self.count, self.count), self.count)

    def meet(self, partners):
        barrier = pltpu.get_barrier_semaphore()
        for partner in partners:
            pl.semaphore_signal(barrier, inc=1, device_id=partner, device_id_type=MESH)
        pl.semaphore_wait(barrier, len(partners))

    def remote(self, source, target, device):
        slot = self.used
        self.used += 1
        return pltpu.make_async_remote_copy(
            src_ref=source,
            dst_ref=target,
            send_sem=self.semaphores.at[0, slot],
            recv_sem=self.semaphores.at[1, slot],
            device_id=device,
            device_id_type=MESH,
        )

    def inside(self, source, target):
        slot = self.used
        self.used += 1
        return pltpu.make_async_copy(source, target, self.semaphores.at[0, slot])


def rows_at(start, size):
    return pl.ds(pl.multiple_of(start, STRIP), size)


class Spread:
    def __init__(self, device, full):
        self.device, self.full = device, full
        self.size = full.shape[0] // 4
        self.block = self.size // BLOCKS
        self.rows, self.core, self.passed, self.kept = {}, {}, {}, {}

    def where(self, core, row, index):
        return self.full.at[
            rows_at((core * 2 + row) * self.size + index * self.block, self.block)
        ]

    def put(self, index, source):
        device = self.device
        target = self.where(device.c, device.t, index)
        self.rows[index] = device.remote(source, target, device.other_row)
        self.core[index] = device.remote(source, target, device.other_core)
        self.kept[index] = device.inside(source, target)
        for copy in (self.rows[index], self.core[index], self.kept[index]):
            copy.start()

    def forward(self, index):
        device = self.device
        self.rows[index].wait_recv()
        place = self.where(device.c, 1 - device.t, index)
        self.passed[index] = device.remote(place, place, device.other_core)
        self.passed[index].start()

    def finish(self):
        for index in range(BLOCKS):
            self.rows[index].wait_send()
            self.core[index].wait()
            self.passed[index].wait()
            self.kept[index].wait()


class Collect:
    def __init__(self, device, partial, near, far, sent, came):
        self.device = device
        self.partial, self.near, self.far, self.sent, self.came = partial, near, far, sent, came
        self.size = partial.shape[0] // 4
        self.block = self.size // BLOCKS
        self.core, self.rows = {}, {}

    def start(self):
        device = self.device
        self.load = device.inside(
            self.partial.at[rows_at(device.c * 2 * self.size, 2 * self.size)], self.near
        )
        for part, row in enumerate((1 - device.t, device.t)):
            for index in range(BLOCKS):
                start = row * self.size + index * self.block
                copy = device.remote(
                    self.partial.at[rows_at((1 - device.c) * 2 * self.size + start, self.block)],
                    self.far.at[rows_at(start, self.block)],
                    device.other_core,
                )
                copy.start()
                self.core[part, index] = copy
        self.load.start()

    def pass_on(self, index):
        device = self.device
        if index == 0:
            self.load.wait()
        self.core[0, index].wait_recv()

        @pl.loop(0, self.block // STRIP)
        def _(strip):
            at = index * self.block + strip * STRIP
            rows = rows_at((1 - device.t) * self.size + at, STRIP)
            total = self.near[rows, :].astype(wide) + self.far[rows, :].astype(wide)
            self.sent[rows_at(at, STRIP), :] = total.astype(low)

        place = rows_at(index * self.block, self.block)
        self.rows[index] = device.remote(
            self.sent.at[place], self.came.at[place], device.other_row
        )
        self.rows[index].start()

    def take(self, index, use):
        device = self.device
        self.core[1, index].wait_recv()
        self.rows[index].wait_recv()

        @pl.loop(0, self.block // STRIP)
        def _(strip):
            at = index * self.block + strip * STRIP
            rows = rows_at(device.t * self.size + at, STRIP)
            mine = rows_at(at, STRIP)
            total = (
                self.near[rows, :].astype(wide)
                + self.far[rows, :].astype(wide)
                + self.came[mine, :].astype(wide)
            )
            use(mine, total)

    def finish(self):
        for index in range(BLOCKS):
            self.core[0, index].wait_send()
            self.core[1, index].wait_send()
            self.rows[index].wait_send()


class Given:
    parts = 2

    def __init__(self, grads):
        self.rows, self.columns = grads.shape
        self.grads = grads

    def take(self, starts, size):
        return [self.grads[rows_at(start, size), :].astype(wide) for start in starts]

    def sources(self, starts, size, keep):
        return [self.grads.at[rows_at(start, size)] for start in starts]


class Product:
    parts = 1

    def __init__(self, left, right, start, columns):
        self.rows, self.columns = left.shape[1], columns
        self.left, self.right, self.start = left, right, start

    def take(self, starts, size):
        left = jnp.concatenate(
            [self.left[:, pl.ds(pl.multiple_of(start, 128), size)] for start in starts], axis=1
        )
        both = dot(left, self.right[:, self.start : self.start + self.columns], 0, 0)
        return [both[:size], both[size:]]

    def sources(self, starts, size, keep):
        for way, value in enumerate(self.take(starts, size)):
            keep[way] = value.astype(low)
        return [keep.at[way] for way in range(2)]


class RingSum:
    def __init__(self, device, grads, scratch, sums):
        self.device, self.grads, self.sums = device, grads, sums
        self.slots, self.totals, self.first = scratch
        self.half = grads.rows // device.count // 2
        self.parts = grads.parts
        self.part = self.half // self.parts
        self.copies = {}
        self.ticks = [
            (step, part) for step in range(device.count) for part in range(self.parts)
        ]

    def own(self, way, distance, part):
        owner = self.device.owner(-(1 - 2 * way) * distance)
        return (owner * 2 + way) * self.half + part * self.part

    def slot(self, way, step, part):
        return self.slots.at[
            way * (self.device.count - 1) + step, pl.ds(part * self.part, self.part)
        ]

    def send(self, way, step, part, source):
        device = self.device
        copy = device.remote(
            source, self.slot(way, step, part), {"w": device.owner(1 - 2 * way)}
        )
        copy.start()
        self.copies[way, step, part] = copy

    def tick(self, count=1):
        device = self.device
        for _ in range(count):
            if not self.ticks:
                return
            step, part = self.ticks.pop(0)
            starts = [self.own(way, step + 1, part) for way in range(2)]
            if step == 0:
                sources = self.grads.sources(starts, self.part, self.first)
                for way in range(2):
                    self.send(way, step, part, sources[way])
                continue
            own = self.grads.take(starts, self.part)
            for way in range(2):
                self.copies[way, step - 1, part].wait_recv()
                slot = self.slot(way, step - 1, part)
                total = (slot[...].astype(wide) + own[way]).astype(low)
                if step < device.count - 1:
                    slot[...] = total
                    self.send(way, step, part, slot)
                else:
                    self.totals[way, pl.ds(part * self.part, self.part), :] = total

    def close(self):
        device = self.device
        self.tick(len(self.ticks))
        self.away = device.remote(
            self.totals.at[1 - device.c], self.sums.at[device.c], device.other_core
        )
        self.kept = device.inside(self.totals.at[device.c], self.sums.at[device.c])
        self.away.start()
        self.kept.start()

    def finish(self):
        for copy in self.copies.values():
            copy.wait_send()
        self.away.wait()
        self.kept.wait()


def ring_shapes(columns, count):
    half = MODEL_WIDTH // count // 2
    return [
        pltpu.VMEM((2 * (count - 1), half, columns), low),
        pltpu.VMEM((2, half, columns), low),
        pltpu.VMEM((2, half, columns), low),
    ]


class RingWork:
    def __init__(self, pairs):
        self.pairs = pairs
        self.columns = [columns for _, _, _, columns in pairs]
        self.fit = (MODEL_WIDTH // lax.axis_size("w") // 2) % 128 == 0
        self.operands, self.places = [], []
        for left, right, start, columns in pairs:
            if self.fit:
                self.places.append((self.add(left), self.add(right), start, columns))
            else:
                part = right[:, start : start + columns]
                self.places.append((self.add(dot(left, part, 0, 0).astype(low)),))

    def add(self, value):
        for index, other in enumerate(self.operands):
            if other is value:
                return index
        self.operands.append(value)
        return len(self.operands) - 1

    def sources(self, refs):
        sources = [
            Product(refs[place[0]], refs[place[1]], *place[2:]) if self.fit else Given(refs[place[0]])
            for place in self.places
        ]
        return sources, refs[len(self.operands) :]

    def outputs(self):
        half = MODEL_WIDTH // lax.axis_size("w") // 2
        return [jax.ShapeDtypeStruct((2, half, size), low) for size in self.columns]

    def scratch(self):
        count = lax.axis_size("w")
        return [shape for size in self.columns for shape in ring_shapes(size, count)]

    def semaphores(self):
        return 4 * (lax.axis_size("w") + 1) * len(self.columns)


def collect_shapes(size):
    return [
        pltpu.VMEM((2 * size, MODEL_WIDTH), low),
        pltpu.VMEM((2 * size, MODEL_WIDTH), low),
        pltpu.VMEM((size, MODEL_WIDTH), low),
        pltpu.VMEM((size, MODEL_WIDTH), low),
    ]


def semaphores_for(count):
    return pltpu.SemaphoreType.DMA((2, count))


def settings(collective):
    return pltpu.CompilerParams(
        collective_id=collective, has_side_effects=True, vmem_limit_bytes=56 * 2**20
    )


def neighbours(device):
    return [
        device.other_core,
        device.other_row,
        {"w": device.owner(1)},
        {"w": device.owner(-1)},
    ]


class RingGather:
    def __init__(self, device, mine, other, full):
        self.device, self.full = device, full
        self.size = mine.shape[0]
        self.parts = min(4, self.size // STRIP)
        self.part = self.size // self.parts
        here = rows_at((device.w * 2 + device.c) * self.size, self.size)
        self.kept = device.inside(mine, full.at[here])
        self.crossed = device.remote(other, full.at[here], device.other_core)
        self.copies = {}
        self.ticks = [
            (step, part) for step in range(device.count - 1) for part in range(self.parts)
        ]

    def start(self):
        self.kept.start()
        self.crossed.start()

    def ready(self):
        self.kept.wait()
        self.crossed.wait()

    def tick(self, count=1):
        device = self.device
        for _ in range(count):
            if not self.ticks:
                return
            step, part = self.ticks.pop(0)
            for way in range(2):
                if step > 0:
                    self.copies[way, step - 1, part].wait_recv()
                owner = device.owner(-(1 - 2 * way) * step)
                block = self.full.at[
                    rows_at((owner * 2 + way) * self.size + part * self.part, self.part)
                ]
                copy = device.remote(block, block, {"w": device.owner(1 - 2 * way)})
                copy.start()
                self.copies[way, step, part] = copy

    def finish(self):
        self.tick(len(self.ticks))
        for part in range(self.parts):
            for way in range(2):
                self.copies[way, self.device.count - 2, part].wait_recv()
        for copy in self.copies.values():
            copy.wait_send()


def gather_kernel(mine, other, first, second, full, first_full, second_full, semaphores):
    device = Device(semaphores)
    device.meet(neighbours(device))
    gather = RingGather(device, mine, other, full)
    gather.start()
    spreads = []
    for rows, target in ((first, first_full), (second, second_full)):
        spread = Spread(device, target)
        block = spread.block
        for index in range(BLOCKS):
            spread.put(index, rows.at[pl.ds(index * block, block)])
        spreads.append(spread)
    gather.ready()
    for spread in spreads:
        for index in range(BLOCKS):
            gather.tick(gather.parts)
            spread.forward(index)
    gather.finish()
    for spread in spreads:
        spread.finish()


def gather_attention(mine, other, first, second):
    count = lax.axis_size("w")
    rows = first.shape[0] * 4
    return pl.pallas_call(
        gather_kernel,
        out_shape=[
            jax.ShapeDtypeStruct((MODEL_WIDTH, mine.shape[1]), low),
            jax.ShapeDtypeStruct((rows, MODEL_WIDTH), low),
            jax.ShapeDtypeStruct((rows, MODEL_WIDTH), low),
        ],
        in_specs=[ANY] * 4,
        out_specs=[ANY] * 3,
        scratch_shapes=[semaphores_for(8 * count + 8 * BLOCKS + 2)],
        compiler_params=settings(1),
        cost_estimate=pl.CostEstimate(flops=0, bytes_accessed=64 * 2**20, transcendentals=0),
        name="gather_attention",
    )(mine, other, first, second)


def forward_kernel(
    partial, rows, gain, mine, other, total, full, gathered,
    near, far, sent, came, normed, semaphores,
):
    device = Device(semaphores)
    device.meet(neighbours(device))
    collect = Collect(device, partial, near, far, sent, came)
    spread = Spread(device, full)
    gather = RingGather(device, mine, other, gathered)
    collect.start()
    gather.start()
    collect.pass_on(0)
    gather.ready()
    gather.tick(gather.parts)
    for index in range(1, BLOCKS):
        collect.pass_on(index)
    gather.tick(2)

    def use(at, value):
        total[at, :] = value
        middle = rows[at, :].astype(wide) + value
        normed[at, :] = normalize(middle, gain[...]).astype(low)

    for index in range(BLOCKS):
        collect.take(index, use)
        spread.put(index, normed.at[pl.ds(index * spread.block, spread.block)])
        gather.tick(2)
    gather.tick(2)
    for index in range(BLOCKS):
        spread.forward(index)
        gather.tick(2)
    gather.finish()
    spread.finish()
    collect.finish()


def exchange_forward(partial, rows, gain, mine, other):
    size = rows.shape[0]
    count = lax.axis_size("w")
    return pl.pallas_call(
        forward_kernel,
        out_shape=[
            jax.ShapeDtypeStruct((size, MODEL_WIDTH), wide),
            jax.ShapeDtypeStruct((4 * size, MODEL_WIDTH), low),
            jax.ShapeDtypeStruct((MODEL_WIDTH, mine.shape[1]), low),
        ],
        in_specs=[ANY, VMEM, VMEM, ANY, ANY],
        out_specs=[VMEM, ANY, ANY],
        scratch_shapes=collect_shapes(size)
        + [
            pltpu.VMEM((size, MODEL_WIDTH), low),
            semaphores_for(16 * BLOCKS + 8 * count + 2),
        ],
        compiler_params=settings(2),
        cost_estimate=pl.CostEstimate(flops=0, bytes_accessed=64 * 2**20, transcendentals=0),
        name="exchange_forward",
    )(partial, rows, gain, mine, other)


class Rings:
    def __init__(self, rings):
        self.rings = rings
        self.next = 0

    def tick(self, count=1):
        for _ in range(count):
            ring = self.rings[self.next]
            self.next = (self.next + 1) % len(self.rings)
            ring.tick()

    def finish(self):
        while any(ring.ticks for ring in self.rings):
            self.tick()
        for ring in self.rings:
            ring.close()
        for ring in self.rings:
            ring.finish()


def norm_back_rows(values, gain, upstream):
    factor = lax.rsqrt(jnp.mean(values * values, axis=-1, keepdims=True) + norm_epsilon)
    weighted = upstream * gain
    projected = jnp.mean(weighted * values, axis=-1, keepdims=True)
    result = factor * weighted - values * (factor * factor * factor) * projected
    return result, jnp.sum(upstream * values * factor, axis=0, keepdims=True)


def backward_kernel(work, partial, output, middle, rows, gain, counted, *refs):
    count = len(work.columns)
    grads, refs = work.sources(refs)
    grad, gain_grad, output_total, squares, full, refs = *refs[:5], refs[5:]
    sums, refs = refs[:count], refs[count:]
    rounded = refs[8]
    device = Device(refs[-1])
    device.meet(neighbours(device))
    collect = Collect(device, partial, *refs[:4])
    output_collect = Collect(device, output, *refs[4:8])
    spread = Spread(device, full)
    rings = Rings(
        [RingSum(device, grads[i], refs[9 + 3 * i : 12 + 3 * i], sums[i]) for i in range(count)]
    )
    collect.start()
    rings.tick(2)
    gain_grad[...] = jnp.zeros_like(gain_grad)
    squares[...] = jnp.zeros_like(squares)
    for index in range(BLOCKS):
        collect.pass_on(index)
    rings.tick(count - 2)
    output_collect.start()

    def use(at, upstream):
        result, gained = norm_back_rows(middle[at, :], gain[...], upstream)
        result = result + rows[at, :].astype(wide)
        grad[at, :] = result
        rounded[at, :] = result.astype(low)
        gain_grad[...] += gained

    def use_output(at, value):
        output_total[at, :] = value
        squares[...] += jnp.sum(counted[at, :] * value * value, axis=0, keepdims=True)

    for index in range(BLOCKS):
        collect.take(index, use)
        spread.put(index, rounded.at[pl.ds(index * spread.block, spread.block)])
        rings.tick(1)
    for index in range(BLOCKS):
        output_collect.pass_on(index)
    rings.tick(2)
    for index in range(BLOCKS):
        spread.forward(index)
        rings.tick(1)
    for index in range(BLOCKS):
        output_collect.take(index, use_output)
        rings.tick(1)
    rings.finish()
    spread.finish()
    collect.finish()
    output_collect.finish()


def exchange_backward(partial, output, middle, rows, gain, counted, pairs):
    size = rows.shape[0]
    work = RingWork(pairs)

    def body(*refs):
        backward_kernel(work, *refs)

    return pl.pallas_call(
        body,
        out_shape=[
            jax.ShapeDtypeStruct((size, MODEL_WIDTH), wide),
            jax.ShapeDtypeStruct((1, MODEL_WIDTH), wide),
            jax.ShapeDtypeStruct((size, MODEL_WIDTH), wide),
            jax.ShapeDtypeStruct((1, MODEL_WIDTH), wide),
            jax.ShapeDtypeStruct((4 * size, MODEL_WIDTH), low),
            *work.outputs(),
        ],
        in_specs=[ANY, ANY] + [VMEM] * (4 + len(work.operands)),
        out_specs=[VMEM] * 4 + [ANY] * (1 + len(work.columns)),
        scratch_shapes=collect_shapes(size) * 2
        + [pltpu.VMEM((size, MODEL_WIDTH), low)]
        + work.scratch()
        + [semaphores_for(32 * BLOCKS + work.semaphores())],
        compiler_params=settings(3),
        cost_estimate=pl.CostEstimate(flops=0, bytes_accessed=128 * 2**20, transcendentals=0),
        name="exchange_backward",
    )(partial, output, middle, rows, gain, counted, *work.operands)


class Total:
    def __init__(self, device, mine, crossed, gathered):
        self.device, self.mine = device, mine
        self.crossed, self.gathered = crossed, gathered
        self.copies = {}
        self.steps = [("c", 0), ("t", 0)] + [("w", step) for step in range(device.count // 2)]

    def tick(self):
        device = self.device
        if not self.steps:
            return
        axis, step = self.steps.pop(0)
        if axis != "w":
            slot = 0 if axis == "c" else 1
            partner = device.other_core if axis == "c" else device.other_row
            copy = device.remote(self.mine.at[slot], self.crossed.at[slot], partner)
            copy.start()
            copy.wait()
            total = self.mine[slot] + self.crossed[slot]
            if slot == 0:
                self.mine[1] = total
            else:
                self.gathered[device.w] = total
            return
        for way in range(2):
            if way == 1 and step == device.count // 2 - 1:
                continue
            if step > 0:
                self.copies[way, step - 1].wait_recv()
            block = self.gathered.at[device.owner(-(1 - 2 * way) * step)]
            copy = device.remote(block, block, {"w": device.owner(1 - 2 * way)})
            copy.start()
            self.copies[way, step] = copy

    def finish(self, target):
        while self.steps:
            self.tick()
        half = self.device.count // 2
        self.copies[0, half - 1].wait_recv()
        self.copies[1, half - 2].wait_recv()
        for copy in self.copies.values():
            copy.wait_send()
        target[...] = self.gathered[0]
        for index in range(1, self.device.count):
            target[...] += self.gathered[index]


def last_kernel(work, first, tokens, gain, middle_grad, stats, *refs):
    count = len(work.columns)
    grads, refs = work.sources(refs)
    first_total, stats_total, refs = refs[0], refs[1], refs[2:]
    sums, scratch = refs[:count], refs[count:]
    device = Device(scratch[-1])
    device.meet(neighbours(device))
    collect = Collect(device, first, *scratch[:4])
    mine, crossed, gathered = scratch[4:7]
    rings = Rings(
        [
            RingSum(device, grads[i], scratch[7 + 3 * i : 10 + 3 * i], sums[i])
            for i in range(count)
        ]
    )
    total = Total(device, mine, crossed, gathered)
    mine[0] = stats[...]
    collect.start()
    rings.tick(2)
    for index in range(BLOCKS):
        collect.pass_on(index)
    rings.tick(count - 2)

    def use(at, upstream):
        result, gained = norm_back_rows(tokens[at, :].astype(wide), gain[...], upstream)
        first_total[at, :] = result + middle_grad[at, :]
        mine[0, 0:1, :] += gained

    for index in range(BLOCKS):
        collect.take(index, use)
        rings.tick(1)
    while total.steps:
        total.tick()
        rings.tick(1)
    rings.finish()
    total.finish(stats_total)
    collect.finish()


def exchange_last(first, tokens, gain, middle_grad, stats, pairs):
    size = tokens.shape[0]
    count = lax.axis_size("w")
    work = RingWork(pairs)

    def body(*refs):
        last_kernel(work, *refs)

    return pl.pallas_call(
        body,
        out_shape=[
            jax.ShapeDtypeStruct((size, MODEL_WIDTH), wide),
            jax.ShapeDtypeStruct(stats.shape, wide),
            *work.outputs(),
        ],
        in_specs=[ANY] + [VMEM] * (4 + len(work.operands)),
        out_specs=[VMEM] * 2 + [ANY] * len(work.columns),
        scratch_shapes=collect_shapes(size)
        + [
            pltpu.VMEM((2, *stats.shape), wide),
            pltpu.VMEM((2, *stats.shape), wide),
            pltpu.VMEM((count, *stats.shape), wide),
        ]
        + work.scratch()
        + [semaphores_for(16 * BLOCKS + 2 * count + 4 + work.semaphores())],
        compiler_params=settings(4),
        cost_estimate=pl.CostEstimate(flops=0, bytes_accessed=128 * 2**20, transcendentals=0),
        name="exchange_last",
    )(first, tokens, gain, middle_grad, stats, *work.operands)


FEEDFORWARD_ROWS = 256
FEEDFORWARD_COLUMNS = 512


def feedforward_kernel(
    sizes, core, rows, upstream, large, small, gate_out, up_out, hidden_out, back_out, down_out
):
    weights = [(large.at[0], 0, sizes[0]), (small, sizes[0], sizes[1])]
    for weight, base, size in weights:
        for start in range(0, size, FEEDFORWARD_COLUMNS):
            width = min(FEEDFORWARD_COLUMNS, size - start)
            columns = slice(base + start, base + start + width)
            gate_part = dot(rows[...], weight[:, start : start + width], 1, 0)
            up_part = dot(rows[...], weight[:, size + start : size + start + width], 1, 0)
            hidden_grad = dot(
                upstream[...], weight[:, 2 * size + start : 2 * size + start + width], 1, 0
            )
            sigmoid_gate = jax.nn.sigmoid(gate_part)
            silu_gate = gate_part * sigmoid_gate
            hidden_out[:, columns] = (silu_gate * up_part).astype(low)
            gate_out[:, columns] = (
                hidden_grad * up_part * sigmoid_gate * (1.0 + gate_part * (1.0 - sigmoid_gate))
            ).astype(low)
            up_out[:, columns] = (hidden_grad * silu_gate).astype(low)
    for start in range(0, MODEL_WIDTH, FEEDFORWARD_COLUMNS):
        across = slice(start, start + FEEDFORWARD_COLUMNS)
        back = 0.0
        down = 0.0
        for weight, base, size in weights:
            columns = slice(base, base + size)
            back = back + dot(gate_out[:, columns], weight[across, :size], 1, 1)
            back = back + dot(up_out[:, columns], weight[across, size : 2 * size], 1, 1)
            down = down + dot(hidden_out[:, columns], weight[across, 2 * size :], 1, 1)
        back_out[:, across] = back.astype(low)
        down_out[:, across] = down.astype(low)


def feedforward(core, rows, upstream, large, small):
    sizes = (large.shape[2] // 3, small.shape[1] // 3)
    count = rows.shape[0]
    hidden = sum(sizes)

    def body(*refs):
        feedforward_kernel(sizes, *refs)

    def block(columns):
        return pl.BlockSpec((FEEDFORWARD_ROWS, columns), lambda index, core: (index, 0))

    once = pl.Buffered(1)
    return pl.pallas_call(
        body,
        grid_spec=pltpu.PrefetchScalarGridSpec(
            num_scalar_prefetch=1,
            grid=(count // FEEDFORWARD_ROWS,),
            in_specs=[
                block(MODEL_WIDTH),
                block(MODEL_WIDTH),
                pl.BlockSpec(
                    (1, *large.shape[1:]),
                    lambda index, core: (core[0], 0, 0),
                    pipeline_mode=once,
                ),
                pl.BlockSpec(small.shape, lambda index, core: (0, 0), pipeline_mode=once),
            ],
            out_specs=[block(hidden)] * 3 + [block(MODEL_WIDTH)] * 2,
        ),
        out_shape=[jax.ShapeDtypeStruct((count, hidden), low)] * 3
        + [jax.ShapeDtypeStruct((count, MODEL_WIDTH), low)] * 2,
        compiler_params=pltpu.CompilerParams(vmem_limit_bytes=52 * 2**20),
        cost_estimate=pl.CostEstimate(
            flops=12 * count * MODEL_WIDTH * hidden,
            bytes_accessed=48 * 2**20,
            transcendentals=count * hidden,
        ),
        name="feedforward",
    )(core, rows, upstream, large, small)


def head_rows(values, gain, cosine, sine):
    factor = lax.rsqrt(jnp.mean(values * values, axis=-1, keepdims=True) + norm_epsilon)
    normed = values * factor * gain
    return (normed * cosine + pltpu.roll(normed, HEAD_WIDTH // 2, 1) * sine).astype(low)


def head_back(values, gain, cosine, sine, upstream):
    turned = upstream * cosine - pltpu.roll(upstream, HEAD_WIDTH // 2, 1) * sine
    return norm_back_rows(values, gain, turned)


def head_at(index):
    return slice(index * HEAD_WIDTH, (index + 1) * HEAD_WIDTH)


def gate_column(logits, head):
    lanes = lax.broadcasted_iota(jnp.int32, logits.shape, 1)
    logit = jnp.sum(jnp.where(lanes == head, logits, 0.0), axis=-1, keepdims=True)
    return jax.nn.sigmoid(logit)


def probabilities(queries, keys, start, valid_count, piece_start):
    raw = dot(queries, keys, 1, 1) * HEAD_WIDTH ** (-0.5)
    row = start + lax.broadcasted_iota(jnp.int32, raw.shape, 0)
    column = lax.broadcasted_iota(jnp.int32, raw.shape, 1)
    last = piece_start + PIC
    inside = (row >= piece_start) & (row < last) & (column >= piece_start) & (column < last)
    allowed = (column < valid_count) & ((column <= row) | inside)
    scores = jnp.where(allowed, raw, masked_score)
    expos = jnp.exp(scores - jnp.max(scores, axis=-1, keepdims=True))
    return expos * (1.0 / jnp.sum(expos, axis=-1, keepdims=True))


QUERY_ROWS = 256


def attention_forward_kernel(groups, share, valid, start, pre, gains, cosine, sine, gated):
    sequence = pl.program_id(0)
    heads = groups * share
    length = pre.shape[0]
    for group in range(groups):
        keys = head_rows(pre[:, head_at(heads + group)], gains[1:2, :], cosine[...], sine[...])
        values = pre[:, head_at(heads + groups + group)].astype(low)
        for head in range(group * share, (group + 1) * share):
            for at in range(0, length, QUERY_ROWS):
                rows = slice(at, at + QUERY_ROWS)
                queries = head_rows(
                    pre[rows, head_at(head)], gains[0:1, :], cosine[rows, :], sine[rows, :]
                )
                probs = probabilities(queries, keys, at, valid[sequence], start[sequence])
                mixed = dot(probs.astype(low), values, 1, 0)
                gate = gate_column(pre[rows, head_at(heads + 2 * groups)], head)
                gated[rows, head_at(head)] = (mixed * gate).astype(low)


def attention_backward_kernel(
    groups, share, valid, start, pre, upstream, gains, cosine, sine, grads, gain_grads
):
    sequence = pl.program_id(0)
    heads = groups * share
    length = pre.shape[0]
    scale = HEAD_WIDTH ** (-0.5)

    @pl.when(sequence == 0)
    def _():
        gain_grads[...] = jnp.zeros_like(gain_grads)

    logit_grads = [jnp.zeros((QUERY_ROWS, HEAD_WIDTH), wide)] * (length // QUERY_ROWS)
    for group in range(groups):
        key_pre = pre[:, head_at(heads + group)]
        keys = head_rows(key_pre, gains[1:2, :], cosine[...], sine[...])
        values = pre[:, head_at(heads + groups + group)].astype(low)
        value_grad = jnp.zeros((length, HEAD_WIDTH), wide)
        key_grad = jnp.zeros((length, HEAD_WIDTH), wide)
        for head in range(group * share, (group + 1) * share):
            for block, at in enumerate(range(0, length, QUERY_ROWS)):
                rows = slice(at, at + QUERY_ROWS)
                query_pre = pre[rows, head_at(head)]
                queries = head_rows(query_pre, gains[0:1, :], cosine[rows, :], sine[rows, :])
                probs = probabilities(queries, keys, at, valid[sequence], start[sequence])
                probs_low = probs.astype(low)
                mixed = dot(probs_low, values, 1, 0)
                gate = gate_column(pre[rows, head_at(heads + 2 * groups)], head)
                gated_grad = upstream[rows, head_at(head)]
                mixed_grad = (gated_grad * gate).astype(low)
                logit_grad = (
                    jnp.sum(gated_grad * mixed, axis=-1, keepdims=True) * gate * (1.0 - gate)
                )
                lanes = lax.broadcasted_iota(jnp.int32, (QUERY_ROWS, HEAD_WIDTH), 1)
                logit_grads[block] = logit_grads[block] + jnp.where(lanes == head, logit_grad, 0.0)
                value_grad = value_grad + dot(probs_low, mixed_grad, 0, 0)
                prob_grad = dot(mixed_grad, values, 1, 1)
                score_grad = (
                    probs * (prob_grad - jnp.sum(prob_grad * probs, axis=-1, keepdims=True))
                ).astype(low)
                key_grad = key_grad + dot(score_grad, queries, 0, 0)
                query_grad, gained = head_back(
                    query_pre,
                    gains[0:1, :],
                    cosine[rows, :],
                    sine[rows, :],
                    dot(score_grad, keys, 1, 0) * scale,
                )
                grads[rows, head_at(head)] = query_grad.astype(low)
                gain_grads[0:1, :] += gained
        key_grad, gained = head_back(
            key_pre, gains[1:2, :], cosine[...], sine[...], key_grad * scale
        )
        gain_grads[1:2, :] += gained
        grads[:, head_at(heads + group)] = key_grad.astype(low)
        grads[:, head_at(heads + groups + group)] = value_grad.astype(low)
    for block, at in enumerate(range(0, length, QUERY_ROWS)):
        grads[slice(at, at + QUERY_ROWS), head_at(heads + 2 * groups)] = logit_grads[block].astype(
            low
        )


def sequence_block(columns, length):
    return pl.BlockSpec((length, columns), lambda sequence: (sequence, 0))


def fixed_block(*shape):
    return pl.BlockSpec(shape, lambda sequence: (0, 0))


SCALARS = pl.BlockSpec(memory_space=pltpu.SMEM)


def attention_forward(groups, share, valid, start, pre, gains, cosine, sine):
    length, columns = cosine.shape[0], groups * share * HEAD_WIDTH

    def body(*refs):
        attention_forward_kernel(groups, share, *refs)

    return pl.pallas_call(
        body,
        grid=(pre.shape[0] // length,),
        out_shape=jax.ShapeDtypeStruct((pre.shape[0], columns), low),
        in_specs=[
            SCALARS,
            SCALARS,
            sequence_block(pre.shape[1], length),
            fixed_block(2, HEAD_WIDTH),
            fixed_block(length, HEAD_WIDTH),
            fixed_block(length, HEAD_WIDTH),
        ],
        out_specs=sequence_block(columns, length),
        compiler_params=pltpu.CompilerParams(vmem_limit_bytes=48 * 2**20),
        cost_estimate=pl.CostEstimate(
            flops=2**30, bytes_accessed=8 * 2**20, transcendentals=2**21
        ),
        name="attention_forward",
    )(valid, start, pre, gains, cosine, sine)


def attention_backward(groups, share, valid, start, pre, upstream, gains, cosine, sine):
    length = cosine.shape[0]

    def body(*refs):
        attention_backward_kernel(groups, share, *refs)

    return pl.pallas_call(
        body,
        grid=(pre.shape[0] // length,),
        out_shape=[
            jax.ShapeDtypeStruct(pre.shape, low),
            jax.ShapeDtypeStruct((2, HEAD_WIDTH), wide),
        ],
        in_specs=[
            SCALARS,
            SCALARS,
            sequence_block(pre.shape[1], length),
            sequence_block(upstream.shape[1], length),
            fixed_block(2, HEAD_WIDTH),
            fixed_block(length, HEAD_WIDTH),
            fixed_block(length, HEAD_WIDTH),
        ],
        out_specs=[sequence_block(pre.shape[1], length), fixed_block(2, HEAD_WIDTH)],
        compiler_params=pltpu.CompilerParams(vmem_limit_bytes=48 * 2**20),
        cost_estimate=pl.CostEstimate(
            flops=2**32, bytes_accessed=12 * 2**20, transcendentals=2**21
        ),
        name="attention_backward",
    )(valid, start, pre, upstream, gains, cosine, sine)


def adam_kernel(layouts, names, heads, *refs):
    sources, refs = dict(zip(names, refs)), refs[len(names) :]
    count = len(layouts)
    stats, inverse, refs = refs[0], refs[1], refs[2:]
    small, refs = refs[:9], refs[9:]
    states, refs = refs[: 3 * count], refs[3 * count :]
    scales, small_targets, refs = refs[0], refs[1:10], refs[10:]
    targets, refs = refs[: 3 * count], refs[3 * count :]
    buffers, semaphores = refs[: 3 * count], refs[3 * count]
    loads = [
        pltpu.make_async_copy(states[i], buffers[i], semaphores.at[0, i]) for i in range(3 * count)
    ]
    stores = [
        pltpu.make_async_copy(buffers[i], targets[i], semaphores.at[1, i])
        for i in range(3 * count)
    ]
    for load in loads:
        load.start()

    def update(part, at, gradient, rate, decay_rate):
        old = (small[3 * part + i][at] for i in range(3))
        for i, value in enumerate(adam_update(*old, gradient, rate, decay_rate)):
            small_targets[3 * part + i][at] = value

    everything = (slice(None), slice(None))
    update(0, everything, stats[0:2, :], 0.5, 0.0)
    for row in range(2):
        update(1, (slice(row, row + 1), slice(None)), stats[2:3, head_at(row)], 0.5, 0.0)
    column, size = heads
    projected = sources["projected"]
    gradient = jnp.concatenate(
        [projected[core, :, column : column + 128][:, :size].astype(wide) for core in range(2)],
        axis=1,
    )
    update(2, everything, gradient, layouts[0][1], weight_decay)
    lanes = lax.broadcasted_iota(jnp.int32, scales.shape, 1)
    squares = stats[2:3, head_at(2)]
    squares = jnp.where(lanes == 2, jnp.sum(stats[3:4, :], axis=-1, keepdims=True), squares)
    scales[...] = jnp.sqrt(squares * inverse[...])
    for number, (transposed, rate, leads) in enumerate(layouts):
        matrix = buffers[3 * number : 3 * number + 3]
        for load in loads[3 * number : 3 * number + 3]:
            load.wait()
        for lead, pieces in enumerate(leads):
            quarter = sum(size for _, _, size in pieces)
            for core in range(2):
                start = core * quarter
                for name, column, size in pieces:
                    step = min(size, 256)

                    @pl.loop(0, size // step)
                    def _(block):
                        columns = pl.ds(pl.multiple_of(column + block * step, 128), step)
                        gradient = sources[name][core, :, columns].astype(wide)
                        place = pl.ds(pl.multiple_of(start + block * step, 128), step)
                        if transposed:
                            gradient = gradient.T
                            at = (place, slice(None))
                        elif len(leads) > 1:
                            at = (lead, slice(None), place)
                        else:
                            at = (slice(None), place)
                        weight, moment, square = (part[at] for part in matrix)
                        for part, value in zip(
                            matrix,
                            adam_update(weight, moment, square, gradient, rate, weight_decay),
                        ):
                            part[at] = value

                    start += size
        for store in stores[3 * number : 3 * number + 3]:
            store.start()
    for store in stores:
        store.wait()


def adam_matrices(layouts, heads, sums, stats, inverse, small, states):
    def body(*refs):
        adam_kernel(layouts, list(sums), heads, *refs)

    def like(values):
        return [jax.ShapeDtypeStruct(value.shape, value.dtype) for value in values]

    return pl.pallas_call(
        body,
        out_shape=like([inverse, *small, *states]),
        in_specs=[VMEM] * (len(sums) + 2 + len(small)) + [ANY] * len(states),
        out_specs=[VMEM] * (1 + len(small)) + [ANY] * len(states),
        scratch_shapes=[pltpu.VMEM(value.shape, value.dtype) for value in states]
        + [pltpu.SemaphoreType.DMA((2, len(states)))],
        compiler_params=pltpu.CompilerParams(vmem_limit_bytes=48 * 2**20),
        cost_estimate=pl.CostEstimate(
            flops=2**25, bytes_accessed=40 * 2**20, transcendentals=2**21
        ),
        name="adam_matrices",
    )(*sums.values(), stats, inverse, *small, *states)


def local(
    tokens,
    cotangent,
    valid_len,
    pic_start,
    norm_gains,
    norm_moment,
    norm_square,
    head_gains,
    head_moment,
    head_square,
    query_weight,
    query_moment,
    query_square,
    keyvalue_matrix,
    keyvalue_first_moment,
    keyvalue_second_moment,
    headgate_weight,
    headgate_moment,
    headgate_square,
    output_weight,
    output_moment,
    output_square,
    gateup_weight,
    gateup_moment,
    gateup_square,
    down_weight,
    down_moment,
    down_square,
):
    local_rows = tokens.shape[0]
    length_value = local_rows * 2
    rows = length_value * 2
    group = lax.axis_index("w")
    core = lax.axis_index("c")
    place = lax.axis_index("t")
    heads_here = query_weight.shape[1] // HEAD_WIDTH // 2
    groups_here = keyvalue_matrix.shape[2] // HEAD_WIDTH // 2
    share = heads_here // groups_here
    head_cols = heads_here * HEAD_WIDTH
    group_cols = groups_here * HEAD_WIDTH
    hidden_here = gateup_weight.shape[2] // 2

    bounds = [0, head_cols, group_cols, group_cols, 128, head_cols]
    edges = [sum(bounds[: i + 1]) for i in range(6)]
    quarters = []
    for index in range(2):
        pieces = []
        for matrix in (
            query_weight, keyvalue_matrix[0], keyvalue_matrix[1], headgate_weight, output_weight.T
        ):
            size = matrix.shape[1] // 2
            piece = matrix[:, index * size : (index + 1) * size].astype(low)
            pieces.append(jnp.pad(piece, ((0, 0), (0, -size % 128))))
        quarters.append(jnp.concatenate(pieces, axis=1))
    residual = tokens.astype(wide)
    attention_full, first_full, output_grad_full = gather_attention(
        jnp.where(core == 0, quarters[0], quarters[1]),
        jnp.where(core == 0, quarters[1], quarters[0]),
        normalize(residual, norm_gains[0]).astype(low),
        cotangent,
    )
    matrices = (gateup_weight[0], gateup_weight[1], down_weight.T)
    late_size = hidden_here // 3
    early_size = hidden_here - late_size

    def quarter_columns(index, start, size):
        return jnp.concatenate(
            [
                matrix[:, index * hidden_here + start : index * hidden_here + start + size].astype(
                    low
                )
                for matrix in matrices
            ],
            axis=1,
        )

    large_block = jnp.stack([quarter_columns(index, 0, early_size) for index in range(2)])
    large_both = lax.all_gather(large_block, ("w", "c"), axis=1, tiled=True)
    small_quarters = [quarter_columns(index, early_size, late_size) for index in range(2)]
    projection_full, output_full = attention_full[:, : edges[4]], attention_full[:, edges[4] :]
    valid_pair = lax.dynamic_slice_in_dim(valid_len, 2 * group, 2)
    start_pair = lax.dynamic_slice_in_dim(pic_start, 2 * group, 2)
    cosine, sine = rotary_tables(length_value)
    projected = dot(first_full, projection_full, 1, 0)
    gated_low = attention_forward(
        groups_here, share, valid_pair, start_pair, projected, head_gains, cosine, sine
    )
    attention_local, second_full, small_full = exchange_forward(
        dot(gated_low, output_full, 1, 1).astype(low),
        tokens,
        norm_gains[1:2],
        jnp.where(core == 0, small_quarters[0], small_quarters[1]),
        jnp.where(core == 0, small_quarters[1], small_quarters[0]),
    )
    middle = residual + attention_local

    gate_grad, up_grad, hidden_low, second_partial, feedforward_partial = feedforward(
        core[None], second_full, output_grad_full, large_both, small_full
    )
    own_places = place * local_rows + jnp.arange(local_rows, dtype=jnp.int32)
    counted = (own_places < valid_pair[core]).astype(wide)[:, None]
    split = hidden_here // 2
    pieces = [(0, split), (split, hidden_here - split)]
    middle_grad, second_gain_grad, feedforward_local, output_squares, attention_grad, *sums = (
        exchange_backward(
            second_partial,
            feedforward_partial,
            middle,
            cotangent,
            norm_gains[1:2],
            counted,
            [(second_full, gate_grad, *piece) for piece in pieces]
            + [(second_full, up_grad, *piece) for piece in pieces],
        )
    )
    block_output = (middle + feedforward_local).astype(low)
    projected_grad, head_gain_grads = attention_backward(
        groups_here,
        share,
        valid_pair,
        start_pair,
        projected,
        dot(attention_grad, output_full, 1, 0),
        head_gains,
        cosine,
        sine,
    )
    first_partial = dot(projected_grad, projection_full, 1, 1)
    squares = jnp.stack(
        [
            jnp.sum(counted * residual * residual),
            jnp.sum(counted * attention_local * attention_local),
        ]
    )
    small = jnp.concatenate([head_gain_grads.reshape(-1), squares])
    nothing = jnp.zeros((1, MODEL_WIDTH), wide)
    stats = jnp.concatenate(
        [
            nothing,
            second_gain_grad,
            jnp.pad(small, (0, MODEL_WIDTH - small.shape[0]))[None],
            output_squares,
            jnp.tile(nothing, (4, 1)),
        ]
    )
    tokens_grad, stats, projected_sums, output_sums, *more = exchange_last(
        first_partial.astype(low),
        tokens,
        norm_gains[0:1],
        middle_grad,
        stats,
        [
            (first_full, projected_grad, 0, edges[4]),
            (attention_grad, gated_low, 0, head_cols),
        ]
        + [(output_grad_full, hidden_low, *piece) for piece in pieces],
    )
    denominator = jnp.sum(valid_len).astype(wide) * MODEL_WIDTH
    inverse = jnp.full((1, HEAD_WIDTH), 1.0 / denominator)
    input_rate = MODEL_WIDTH ** (-0.5)
    down_rate = FF ** (-0.5)
    output_rate = max(QUERY_HEADS * HEAD_WIDTH // 128, 4) ** (-0.5)
    first_size, second_size = split, hidden_here - split
    layouts = [
        (
            False,
            input_rate,
            [
                [("gate 0", 0, first_size), ("gate 1", 0, second_size)],
                [("up 0", 0, first_size), ("up 1", 0, second_size)],
            ],
        ),
        (True, down_rate, [[("down 0", 0, first_size), ("down 1", 0, second_size)]]),
        (False, input_rate, [[("projected", edges[0], head_cols)]]),
        (
            False,
            input_rate,
            [[("projected", edges[1], group_cols)], [("projected", edges[2], group_cols)]],
        ),
        (True, output_rate, [[("output", 0, head_cols)]]),
    ]
    names = ["gate 0", "gate 1", "up 0", "up 1", "down 0", "down 1"]
    sums = dict(zip(names, [*sums, *more]))
    sums["projected"], sums["output"] = projected_sums, output_sums
    scales, *updated = adam_matrices(
        layouts,
        (edges[3], heads_here),
        sums,
        stats,
        inverse,
        [
            norm_gains,
            norm_moment,
            norm_square,
            head_gains,
            head_moment,
            head_square,
            headgate_weight,
            headgate_moment,
            headgate_square,
        ],
        [
            gateup_weight,
            gateup_moment,
            gateup_square,
            down_weight,
            down_moment,
            down_square,
            query_weight,
            query_moment,
            query_square,
            keyvalue_matrix,
            keyvalue_first_moment,
            keyvalue_second_moment,
            output_weight,
            output_moment,
            output_square,
        ],
    )
    norms_new, heads_new, headgate_new, gateup_new, down_new, query_new, keyvalue_new, output_new = (
        updated[3 * i : 3 * i + 3] for i in range(8)
    )
    branch_scales = scales[0, :3]
    return (
        block_output,
        tokens_grad,
        branch_scales,
        *norms_new,
        *heads_new,
        *query_new,
        *keyvalue_new,
        *headgate_new,
        *output_new,
        *gateup_new,
        *down_new,
    )


def solution(mesh):
    fsdp, tp = mesh.devices.shape
    fine = Mesh(mesh.devices.reshape(fsdp // 2, 2, tp), ("w", "c", "t"))
    whole = ("w", "c")
    rows = P(("w", "c", "t"), None)
    first = P(whole, "t")
    second = P(None, whole, "t")
    last = P("t", whole)
    matrices = (first,) * 3 + (second,) * 3 + (first,) * 3 + (last,) * 3 + (second,) * 3 + (last,) * 3
    return jax.shard_map(
        local,
        mesh=fine,
        in_specs=(rows, rows, P(), P()) + (P(),) * 6 + matrices,
        out_specs=(rows, rows, P()) + (P(),) * 6 + matrices,
        check_vma=False,
    )
```

```python
import jax
import jax.numpy as jnp
from jax import lax
from jax.experimental import pallas as pl
from jax.experimental.pallas import tpu as pltpu
from jax.sharding import Mesh
from jax.sharding import PartitionSpec as P

MODEL_WIDTH = 2048
QUERY_HEADS = 16
HEAD_WIDTH = 128
FF = 6144
PIC = 256
STEP = 10

norm_epsilon = 1e-06
rope_base = 1000000.0
beta_first = 0.9
beta_second = 0.999
adam_epsilon = 1e-08
weight_decay = 0.1
masked_score = -1e30
low = jnp.bfloat16
wide = jnp.float32


def normalize(values, scaling):
    return (
        values
        * lax.rsqrt(jnp.mean(values * values, axis=-1, keepdims=True) + norm_epsilon)
        * scaling
    )


def norm_back(values, scaling, upstream):
    factor = lax.rsqrt(jnp.mean(values * values, axis=-1, keepdims=True) + norm_epsilon)
    weighted = upstream * scaling
    projected = jnp.mean(weighted * values, axis=-1, keepdims=True)
    result = factor * weighted - values * (factor * factor * factor) * projected
    return (result, jnp.sum(upstream * values * factor, axis=tuple(range(values.ndim - 1))))


def rotary_tables(length_value):
    halves = HEAD_WIDTH // 2
    frequency = rope_base ** (-(jnp.arange(halves, dtype=wide) * 2.0 / HEAD_WIDTH))
    angles = jnp.arange(length_value, dtype=wide)[:, None] * frequency[None, :]
    cosine, sine = jnp.cos(angles), jnp.sin(angles)
    return (
        jnp.concatenate([cosine, cosine], axis=1),
        jnp.concatenate([-sine, sine], axis=1),
    )


def adam_update(weight, moment, square, gradient, step_rate, decay_rate):
    moment_new = beta_first * moment + (1.0 - beta_first) * gradient
    square_new = beta_second * square + (1.0 - beta_second) * gradient * gradient
    bias_first = 1.0 - beta_first**STEP
    bias_second = 1.0 - beta_second**STEP
    update = moment_new / bias_first / (jnp.sqrt(square_new / bias_second) + adam_epsilon)
    return (weight - step_rate * (update + decay_rate * weight), moment_new, square_new)


def dot(left, right, left_dim, right_dim):
    return lax.dot_general(
        left, right, (((left_dim,), (right_dim,)), ((), ())), preferred_element_type=wide
    )


def fetch(parts):
    pieces = []
    for core in range(2):
        for part in parts:
            size = part.shape[1] // 2
            pieces.append(part[:, core * size : (core + 1) * size].astype(low))
    count = len(parts)
    local_block = jnp.stack(
        [jnp.concatenate(pieces[core * count : (core + 1) * count], axis=1) for core in range(2)]
    )
    return lax.all_gather(local_block, ("w", "c"), axis=1, tiled=True)


def columns_of(both, start, size):
    return lax.dynamic_slice(
        both, (lax.axis_index("c"), 0, start), (1, both.shape[1], size)
    ).reshape(both.shape[1], size)


MESH = pl.DeviceIdType.MESH
BLOCKS = 4
STRIP = 16
ANY = pl.BlockSpec(memory_space=pl.ANY)
VMEM = pl.BlockSpec(memory_space=pltpu.VMEM)


def ring_place(index, count):
    odd = lax.rem(index, 2)
    pair = lax.div(index, 2)
    return (1 - odd) * pair + odd * (count - 1 - pair)


def ring_index(place, count):
    late = lax.div(place, count // 2)
    return (1 - late) * 2 * place + late * (2 * (count - 1 - place) + 1)


class Device:
    def __init__(self, semaphores):
        self.w, self.c, self.t = (lax.axis_index(axis) for axis in ("w", "c", "t"))
        self.count = lax.axis_size("w")
        self.place = ring_place(self.w, self.count)
        self.semaphores = semaphores
        self.used = 0
        self.other_core = {"c": 1 - self.c}
        self.other_row = {"t": 1 - self.t}

    def owner(self, distance):
        return ring_index(lax.rem(self.place + distance + self.count, self.count), self.count)

    def meet(self, partners):
        barrier = pltpu.get_barrier_semaphore()
        for partner in partners:
            pl.semaphore_signal(barrier, inc=1, device_id=partner, device_id_type=MESH)
        pl.semaphore_wait(barrier, len(partners))

    def remote(self, source, target, device):
        slot = self.used
        self.used += 1
        return pltpu.make_async_remote_copy(
            src_ref=source,
            dst_ref=target,
            send_sem=self.semaphores.at[0, slot],
            recv_sem=self.semaphores.at[1, slot],
            device_id=device,
            device_id_type=MESH,
        )

    def inside(self, source, target):
        slot = self.used
        self.used += 1
        return pltpu.make_async_copy(source, target, self.semaphores.at[0, slot])


def rows_at(start, size):
    return pl.ds(pl.multiple_of(start, STRIP), size)


class Spread:
    def __init__(self, device, full):
        self.device, self.full = device, full
        self.size = full.shape[0] // 4
        self.block = self.size // BLOCKS
        self.rows, self.core, self.passed, self.kept = {}, {}, {}, {}

    def where(self, core, row, index):
        return self.full.at[
            rows_at((core * 2 + row) * self.size + index * self.block, self.block)
        ]

    def put(self, index, source):
        device = self.device
        target = self.where(device.c, device.t, index)
        self.rows[index] = device.remote(source, target, device.other_row)
        self.core[index] = device.remote(source, target, device.other_core)
        self.kept[index] = device.inside(source, target)
        for copy in (self.rows[index], self.core[index], self.kept[index]):
            copy.start()

    def forward(self, index):
        device = self.device
        self.rows[index].wait_recv()
        place = self.where(device.c, 1 - device.t, index)
        self.passed[index] = device.remote(place, place, device.other_core)
        self.passed[index].start()

    def finish(self):
        for index in range(BLOCKS):
            self.rows[index].wait_send()
            self.core[index].wait()
            self.passed[index].wait()
            self.kept[index].wait()


class Collect:
    def __init__(self, device, partial, near, far, sent, came):
        self.device = device
        self.partial, self.near, self.far, self.sent, self.came = partial, near, far, sent, came
        self.size = partial.shape[0] // 4
        self.block = self.size // BLOCKS
        self.core, self.rows = {}, {}

    def start(self):
        device = self.device
        self.load = device.inside(
            self.partial.at[rows_at(device.c * 2 * self.size, 2 * self.size)], self.near
        )
        for part, row in enumerate((1 - device.t, device.t)):
            for index in range(BLOCKS):
                start = row * self.size + index * self.block
                copy = device.remote(
                    self.partial.at[rows_at((1 - device.c) * 2 * self.size + start, self.block)],
                    self.far.at[rows_at(start, self.block)],
                    device.other_core,
                )
                copy.start()
                self.core[part, index] = copy
        self.load.start()

    def pass_on(self, index):
        device = self.device
        if index == 0:
            self.load.wait()
        self.core[0, index].wait_recv()

        @pl.loop(0, self.block // STRIP)
        def _(strip):
            at = index * self.block + strip * STRIP
            rows = rows_at((1 - device.t) * self.size + at, STRIP)
            total = self.near[rows, :].astype(wide) + self.far[rows, :].astype(wide)
            self.sent[rows_at(at, STRIP), :] = total.astype(low)

        place = rows_at(index * self.block, self.block)
        self.rows[index] = device.remote(
            self.sent.at[place], self.came.at[place], device.other_row
        )
        self.rows[index].start()

    def take(self, index, use):
        device = self.device
        self.core[1, index].wait_recv()
        self.rows[index].wait_recv()

        @pl.loop(0, self.block // STRIP)
        def _(strip):
            at = index * self.block + strip * STRIP
            rows = rows_at(device.t * self.size + at, STRIP)
            mine = rows_at(at, STRIP)
            total = (
                self.near[rows, :].astype(wide)
                + self.far[rows, :].astype(wide)
                + self.came[mine, :].astype(wide)
            )
            use(mine, total)

    def finish(self):
        for index in range(BLOCKS):
            self.core[0, index].wait_send()
            self.core[1, index].wait_send()
            self.rows[index].wait_send()


class Given:
    parts = 2

    def __init__(self, grads):
        self.rows, self.columns = grads.shape
        self.grads = grads

    def take(self, starts, size):
        return [self.grads[rows_at(start, size), :].astype(wide) for start in starts]

    def sources(self, starts, size, keep):
        return [self.grads.at[rows_at(start, size)] for start in starts]


class Product:
    parts = 1

    def __init__(self, left, right, start, columns):
        self.rows, self.columns = left.shape[1], columns
        self.left, self.right, self.start = left, right, start

    def take(self, starts, size):
        left = jnp.concatenate(
            [self.left[:, pl.ds(pl.multiple_of(start, 128), size)] for start in starts], axis=1
        )
        both = dot(left, self.right[:, self.start : self.start + self.columns], 0, 0)
        return [both[:size], both[size:]]

    def sources(self, starts, size, keep):
        for way, value in enumerate(self.take(starts, size)):
            keep[way] = value.astype(low)
        return [keep.at[way] for way in range(2)]


class RingSum:
    def __init__(self, device, grads, scratch, sums):
        self.device, self.grads, self.sums = device, grads, sums
        self.slots, self.totals, self.first = scratch
        self.half = grads.rows // device.count // 2
        self.parts = grads.parts
        self.part = self.half // self.parts
        self.copies = {}
        self.ticks = [
            (step, part) for step in range(device.count) for part in range(self.parts)
        ]

    def own(self, way, distance, part):
        owner = self.device.owner(-(1 - 2 * way) * distance)
        return (owner * 2 + way) * self.half + part * self.part

    def slot(self, way, step, part):
        return self.slots.at[
            way * (self.device.count - 1) + step, pl.ds(part * self.part, self.part)
        ]

    def send(self, way, step, part, source):
        device = self.device
        copy = device.remote(
            source, self.slot(way, step, part), {"w": device.owner(1 - 2 * way)}
        )
        copy.start()
        self.copies[way, step, part] = copy

    def tick(self, count=1):
        device = self.device
        for _ in range(count):
            if not self.ticks:
                return
            step, part = self.ticks.pop(0)
            starts = [self.own(way, step + 1, part) for way in range(2)]
            if step == 0:
                sources = self.grads.sources(starts, self.part, self.first)
                for way in range(2):
                    self.send(way, step, part, sources[way])
                continue
            own = self.grads.take(starts, self.part)
            for way in range(2):
                self.copies[way, step - 1, part].wait_recv()
                slot = self.slot(way, step - 1, part)
                total = (slot[...].astype(wide) + own[way]).astype(low)
                if step < device.count - 1:
                    slot[...] = total
                    self.send(way, step, part, slot)
                else:
                    self.totals[way, pl.ds(part * self.part, self.part), :] = total

    def close(self):
        device = self.device
        self.tick(len(self.ticks))
        self.away = device.remote(
            self.totals.at[1 - device.c], self.sums.at[device.c], device.other_core
        )
        self.kept = device.inside(self.totals.at[device.c], self.sums.at[device.c])
        self.away.start()
        self.kept.start()

    def finish(self):
        for copy in self.copies.values():
            copy.wait_send()
        self.away.wait()
        self.kept.wait()


def ring_shapes(columns, count):
    half = MODEL_WIDTH // count // 2
    return [
        pltpu.VMEM((2 * (count - 1), half, columns), low),
        pltpu.VMEM((2, half, columns), low),
        pltpu.VMEM((2, half, columns), low),
    ]


class RingWork:
    def __init__(self, pairs):
        self.pairs = pairs
        self.columns = [columns for _, _, _, columns in pairs]
        self.fit = (MODEL_WIDTH // lax.axis_size("w") // 2) % 128 == 0
        self.operands, self.places = [], []
        for left, right, start, columns in pairs:
            if self.fit:
                self.places.append((self.add(left), self.add(right), start, columns))
            else:
                part = right[:, start : start + columns]
                self.places.append((self.add(dot(left, part, 0, 0).astype(low)),))

    def add(self, value):
        for index, other in enumerate(self.operands):
            if other is value:
                return index
        self.operands.append(value)
        return len(self.operands) - 1

    def sources(self, refs):
        sources = [
            Product(refs[place[0]], refs[place[1]], *place[2:]) if self.fit else Given(refs[place[0]])
            for place in self.places
        ]
        return sources, refs[len(self.operands) :]

    def outputs(self):
        half = MODEL_WIDTH // lax.axis_size("w") // 2
        return [jax.ShapeDtypeStruct((2, half, size), low) for size in self.columns]

    def scratch(self):
        count = lax.axis_size("w")
        return [shape for size in self.columns for shape in ring_shapes(size, count)]

    def semaphores(self):
        return 4 * (lax.axis_size("w") + 1) * len(self.columns)


def collect_shapes(size):
    return [
        pltpu.VMEM((2 * size, MODEL_WIDTH), low),
        pltpu.VMEM((2 * size, MODEL_WIDTH), low),
        pltpu.VMEM((size, MODEL_WIDTH), low),
        pltpu.VMEM((size, MODEL_WIDTH), low),
    ]


def semaphores_for(count):
    return pltpu.SemaphoreType.DMA((2, count))


def settings(collective):
    return pltpu.CompilerParams(
        collective_id=collective, has_side_effects=True, vmem_limit_bytes=56 * 2**20
    )


def neighbours(device):
    return [
        device.other_core,
        device.other_row,
        {"w": device.owner(1)},
        {"w": device.owner(-1)},
    ]


class RingGather:
    def __init__(self, device, mine, other, full):
        self.device, self.full = device, full
        self.size = mine.shape[0]
        self.parts = min(4, self.size // STRIP)
        self.part = self.size // self.parts
        here = rows_at((device.w * 2 + device.c) * self.size, self.size)
        self.kept = device.inside(mine, full.at[here])
        self.crossed = device.remote(other, full.at[here], device.other_core)
        self.copies = {}
        self.ticks = [
            (step, part) for step in range(device.count - 1) for part in range(self.parts)
        ]

    def start(self):
        self.kept.start()
        self.crossed.start()

    def ready(self):
        self.kept.wait()
        self.crossed.wait()

    def tick(self, count=1):
        device = self.device
        for _ in range(count):
            if not self.ticks:
                return
            step, part = self.ticks.pop(0)
            for way in range(2):
                if step > 0:
                    self.copies[way, step - 1, part].wait_recv()
                owner = device.owner(-(1 - 2 * way) * step)
                block = self.full.at[
                    rows_at((owner * 2 + way) * self.size + part * self.part, self.part)
                ]
                copy = device.remote(block, block, {"w": device.owner(1 - 2 * way)})
                copy.start()
                self.copies[way, step, part] = copy

    def finish(self):
        self.tick(len(self.ticks))
        for part in range(self.parts):
            for way in range(2):
                self.copies[way, self.device.count - 2, part].wait_recv()
        for copy in self.copies.values():
            copy.wait_send()


def gather_kernel(mine, other, first, second, full, first_full, second_full, semaphores):
    device = Device(semaphores)
    device.meet(neighbours(device))
    gather = RingGather(device, mine, other, full)
    gather.start()
    spreads = []
    for rows, target in ((first, first_full), (second, second_full)):
        spread = Spread(device, target)
        block = spread.block
        for index in range(BLOCKS):
            spread.put(index, rows.at[pl.ds(index * block, block)])
        spreads.append(spread)
    gather.ready()
    for spread in spreads:
        for index in range(BLOCKS):
            gather.tick(gather.parts)
            spread.forward(index)
    gather.finish()
    for spread in spreads:
        spread.finish()


def gather_attention(mine, other, first, second):
    count = lax.axis_size("w")
    rows = first.shape[0] * 4
    return pl.pallas_call(
        gather_kernel,
        out_shape=[
            jax.ShapeDtypeStruct((MODEL_WIDTH, mine.shape[1]), low),
            jax.ShapeDtypeStruct((rows, MODEL_WIDTH), low),
            jax.ShapeDtypeStruct((rows, MODEL_WIDTH), low),
        ],
        in_specs=[ANY] * 4,
        out_specs=[ANY] * 3,
        scratch_shapes=[semaphores_for(8 * count + 8 * BLOCKS + 2)],
        compiler_params=settings(1),
        cost_estimate=pl.CostEstimate(flops=0, bytes_accessed=64 * 2**20, transcendentals=0),
        name="gather_attention",
    )(mine, other, first, second)


def forward_kernel(
    partial, rows, gain, total, full, near, far, sent, came, normed, semaphores
):
    device = Device(semaphores)
    device.meet([device.other_core, device.other_row])
    collect = Collect(device, partial, near, far, sent, came)
    spread = Spread(device, full)
    collect.start()
    for index in range(BLOCKS):
        collect.pass_on(index)

    def use(at, value):
        total[at, :] = value
        middle = rows[at, :].astype(wide) + value
        normed[at, :] = normalize(middle, gain[...]).astype(low)

    for index in range(BLOCKS):
        collect.take(index, use)
        spread.put(index, normed.at[pl.ds(index * spread.block, spread.block)])
    for index in range(BLOCKS):
        spread.forward(index)
    spread.finish()
    collect.finish()


def exchange_forward(partial, rows, gain):
    size = rows.shape[0]
    return pl.pallas_call(
        forward_kernel,
        out_shape=[
            jax.ShapeDtypeStruct((size, MODEL_WIDTH), wide),
            jax.ShapeDtypeStruct((4 * size, MODEL_WIDTH), low),
        ],
        in_specs=[ANY, VMEM, VMEM],
        out_specs=[VMEM, ANY],
        scratch_shapes=collect_shapes(size)
        + [pltpu.VMEM((size, MODEL_WIDTH), low), semaphores_for(16 * BLOCKS)],
        compiler_params=settings(2),
        cost_estimate=pl.CostEstimate(flops=0, bytes_accessed=64 * 2**20, transcendentals=0),
        name="exchange_forward",
    )(partial, rows, gain)


class Rings:
    def __init__(self, rings):
        self.rings = rings
        self.next = 0

    def tick(self, count=1):
        for _ in range(count):
            ring = self.rings[self.next]
            self.next = (self.next + 1) % len(self.rings)
            ring.tick()

    def finish(self):
        while any(ring.ticks for ring in self.rings):
            self.tick()
        for ring in self.rings:
            ring.close()
        for ring in self.rings:
            ring.finish()


def norm_back_rows(values, gain, upstream):
    factor = lax.rsqrt(jnp.mean(values * values, axis=-1, keepdims=True) + norm_epsilon)
    weighted = upstream * gain
    projected = jnp.mean(weighted * values, axis=-1, keepdims=True)
    result = factor * weighted - values * (factor * factor * factor) * projected
    return result, jnp.sum(upstream * values * factor, axis=0, keepdims=True)


def backward_kernel(work, partial, output, middle, rows, gain, counted, *refs):
    count = len(work.columns)
    grads, refs = work.sources(refs)
    grad, gain_grad, output_total, squares, full, refs = *refs[:5], refs[5:]
    sums, refs = refs[:count], refs[count:]
    rounded = refs[8]
    device = Device(refs[-1])
    device.meet(neighbours(device))
    collect = Collect(device, partial, *refs[:4])
    output_collect = Collect(device, output, *refs[4:8])
    spread = Spread(device, full)
    rings = Rings(
        [RingSum(device, grads[i], refs[9 + 3 * i : 12 + 3 * i], sums[i]) for i in range(count)]
    )
    collect.start()
    rings.tick(2)
    gain_grad[...] = jnp.zeros_like(gain_grad)
    squares[...] = jnp.zeros_like(squares)
    for index in range(BLOCKS):
        collect.pass_on(index)
    rings.tick(count - 2)
    output_collect.start()

    def use(at, upstream):
        result, gained = norm_back_rows(middle[at, :], gain[...], upstream)
        result = result + rows[at, :].astype(wide)
        grad[at, :] = result
        rounded[at, :] = result.astype(low)
        gain_grad[...] += gained

    def use_output(at, value):
        output_total[at, :] = value
        squares[...] += jnp.sum(counted[at, :] * value * value, axis=0, keepdims=True)

    for index in range(BLOCKS):
        collect.take(index, use)
        spread.put(index, rounded.at[pl.ds(index * spread.block, spread.block)])
        rings.tick(1)
    for index in range(BLOCKS):
        output_collect.pass_on(index)
    rings.tick(2)
    for index in range(BLOCKS):
        spread.forward(index)
        rings.tick(1)
    for index in range(BLOCKS):
        output_collect.take(index, use_output)
        rings.tick(1)
    rings.finish()
    spread.finish()
    collect.finish()
    output_collect.finish()


def exchange_backward(partial, output, middle, rows, gain, counted, pairs):
    size = rows.shape[0]
    work = RingWork(pairs)

    def body(*refs):
        backward_kernel(work, *refs)

    return pl.pallas_call(
        body,
        out_shape=[
            jax.ShapeDtypeStruct((size, MODEL_WIDTH), wide),
            jax.ShapeDtypeStruct((1, MODEL_WIDTH), wide),
            jax.ShapeDtypeStruct((size, MODEL_WIDTH), wide),
            jax.ShapeDtypeStruct((1, MODEL_WIDTH), wide),
            jax.ShapeDtypeStruct((4 * size, MODEL_WIDTH), low),
            *work.outputs(),
        ],
        in_specs=[ANY, ANY] + [VMEM] * (4 + len(work.operands)),
        out_specs=[VMEM] * 4 + [ANY] * (1 + len(work.columns)),
        scratch_shapes=collect_shapes(size) * 2
        + [pltpu.VMEM((size, MODEL_WIDTH), low)]
        + work.scratch()
        + [semaphores_for(32 * BLOCKS + work.semaphores())],
        compiler_params=settings(3),
        cost_estimate=pl.CostEstimate(flops=0, bytes_accessed=128 * 2**20, transcendentals=0),
        name="exchange_backward",
    )(partial, output, middle, rows, gain, counted, *work.operands)


class Total:
    def __init__(self, device, mine, crossed, gathered):
        self.device, self.mine = device, mine
        self.crossed, self.gathered = crossed, gathered
        self.copies = {}
        self.steps = [("c", 0), ("t", 0)] + [("w", step) for step in range(device.count // 2)]

    def tick(self):
        device = self.device
        if not self.steps:
            return
        axis, step = self.steps.pop(0)
        if axis != "w":
            slot = 0 if axis == "c" else 1
            partner = device.other_core if axis == "c" else device.other_row
            copy = device.remote(self.mine.at[slot], self.crossed.at[slot], partner)
            copy.start()
            copy.wait()
            total = self.mine[slot] + self.crossed[slot]
            if slot == 0:
                self.mine[1] = total
            else:
                self.gathered[device.w] = total
            return
        for way in range(2):
            if way == 1 and step == device.count // 2 - 1:
                continue
            if step > 0:
                self.copies[way, step - 1].wait_recv()
            block = self.gathered.at[device.owner(-(1 - 2 * way) * step)]
            copy = device.remote(block, block, {"w": device.owner(1 - 2 * way)})
            copy.start()
            self.copies[way, step] = copy

    def finish(self, target):
        while self.steps:
            self.tick()
        half = self.device.count // 2
        self.copies[0, half - 1].wait_recv()
        self.copies[1, half - 2].wait_recv()
        for copy in self.copies.values():
            copy.wait_send()
        target[...] = self.gathered[0]
        for index in range(1, self.device.count):
            target[...] += self.gathered[index]


def last_kernel(work, first, tokens, gain, middle_grad, stats, *refs):
    count = len(work.columns)
    grads, refs = work.sources(refs)
    first_total, stats_total, refs = refs[0], refs[1], refs[2:]
    sums, scratch = refs[:count], refs[count:]
    device = Device(scratch[-1])
    device.meet(neighbours(device))
    collect = Collect(device, first, *scratch[:4])
    mine, crossed, gathered = scratch[4:7]
    rings = Rings(
        [
            RingSum(device, grads[i], scratch[7 + 3 * i : 10 + 3 * i], sums[i])
            for i in range(count)
        ]
    )
    total = Total(device, mine, crossed, gathered)
    mine[0] = stats[...]
    collect.start()
    rings.tick(2)
    for index in range(BLOCKS):
        collect.pass_on(index)
    rings.tick(count - 2)

    def use(at, upstream):
        result, gained = norm_back_rows(tokens[at, :].astype(wide), gain[...], upstream)
        first_total[at, :] = result + middle_grad[at, :]
        mine[0, 0:1, :] += gained

    for index in range(BLOCKS):
        collect.take(index, use)
        rings.tick(1)
    while total.steps:
        total.tick()
        rings.tick(1)
    rings.finish()
    total.finish(stats_total)
    collect.finish()


def exchange_last(first, tokens, gain, middle_grad, stats, pairs):
    size = tokens.shape[0]
    count = lax.axis_size("w")
    work = RingWork(pairs)

    def body(*refs):
        last_kernel(work, *refs)

    return pl.pallas_call(
        body,
        out_shape=[
            jax.ShapeDtypeStruct((size, MODEL_WIDTH), wide),
            jax.ShapeDtypeStruct(stats.shape, wide),
            *work.outputs(),
        ],
        in_specs=[ANY] + [VMEM] * (4 + len(work.operands)),
        out_specs=[VMEM] * 2 + [ANY] * len(work.columns),
        scratch_shapes=collect_shapes(size)
        + [
            pltpu.VMEM((2, *stats.shape), wide),
            pltpu.VMEM((2, *stats.shape), wide),
            pltpu.VMEM((count, *stats.shape), wide),
        ]
        + work.scratch()
        + [semaphores_for(16 * BLOCKS + 2 * count + 4 + work.semaphores())],
        compiler_params=settings(4),
        cost_estimate=pl.CostEstimate(flops=0, bytes_accessed=128 * 2**20, transcendentals=0),
        name="exchange_last",
    )(first, tokens, gain, middle_grad, stats, *work.operands)


FEEDFORWARD_ROWS = 256
FEEDFORWARD_COLUMNS = 512


def feedforward_kernel(core, rows, upstream, weights, *refs):
    before, refs = refs[:-5], refs[-5:]
    gate_out, up_out, hidden_out, back_out, down_out = refs
    weight = weights.at[0]
    size = gate_out.shape[1]
    for start in range(0, size, FEEDFORWARD_COLUMNS):
        width = min(FEEDFORWARD_COLUMNS, size - start)
        columns = slice(start, start + width)
        gate_part = dot(rows[...], weight[:, start : start + width], 1, 0)
        up_part = dot(rows[...], weight[:, size + start : size + start + width], 1, 0)
        hidden_grad = dot(
            upstream[...], weight[:, 2 * size + start : 2 * size + start + width], 1, 0
        )
        sigmoid_gate = jax.nn.sigmoid(gate_part)
        silu_gate = gate_part * sigmoid_gate
        hidden_out[:, columns] = (silu_gate * up_part).astype(low)
        gate_out[:, columns] = (
            hidden_grad * up_part * sigmoid_gate * (1.0 + gate_part * (1.0 - sigmoid_gate))
        ).astype(low)
        up_out[:, columns] = (hidden_grad * silu_gate).astype(low)
    for start in range(0, MODEL_WIDTH, FEEDFORWARD_COLUMNS):
        across = slice(start, start + FEEDFORWARD_COLUMNS)
        back = dot(gate_out[...], weight[across, :size], 1, 1)
        back = back + dot(up_out[...], weight[across, size : 2 * size], 1, 1)
        down = dot(hidden_out[...], weight[across, 2 * size :], 1, 1)
        if before:
            back = back + before[0][:, across].astype(wide)
            down = down + before[1][:, across].astype(wide)
        back_out[:, across] = back.astype(low)
        down_out[:, across] = down.astype(low)


def feedforward(core, rows, upstream, weights, before=()):
    count = rows.shape[0]
    hidden = weights.shape[2] // 3

    def block(columns):
        return pl.BlockSpec((FEEDFORWARD_ROWS, columns), lambda index, core: (index, 0))

    return pl.pallas_call(
        feedforward_kernel,
        grid_spec=pltpu.PrefetchScalarGridSpec(
            num_scalar_prefetch=1,
            grid=(count // FEEDFORWARD_ROWS,),
            in_specs=[
                block(MODEL_WIDTH),
                block(MODEL_WIDTH),
                pl.BlockSpec(
                    (1, *weights.shape[1:]),
                    lambda index, core: (core[0], 0, 0),
                    pipeline_mode=pl.Buffered(1),
                ),
            ]
            + [block(MODEL_WIDTH)] * len(before),
            out_specs=[block(hidden)] * 3 + [block(MODEL_WIDTH)] * 2,
        ),
        out_shape=[jax.ShapeDtypeStruct((count, hidden), low)] * 3
        + [jax.ShapeDtypeStruct((count, MODEL_WIDTH), low)] * 2,
        compiler_params=pltpu.CompilerParams(vmem_limit_bytes=52 * 2**20),
        cost_estimate=pl.CostEstimate(
            flops=12 * count * MODEL_WIDTH * hidden,
            bytes_accessed=48 * 2**20,
            transcendentals=count * hidden,
        ),
        name="feedforward_more" if before else "feedforward",
    )(core, rows, upstream, weights, *before)


def head_rows(values, gain, cosine, sine):
    factor = lax.rsqrt(jnp.mean(values * values, axis=-1, keepdims=True) + norm_epsilon)
    normed = values * factor * gain
    return (normed * cosine + pltpu.roll(normed, HEAD_WIDTH // 2, 1) * sine).astype(low)


def head_back(values, gain, cosine, sine, upstream):
    turned = upstream * cosine - pltpu.roll(upstream, HEAD_WIDTH // 2, 1) * sine
    return norm_back_rows(values, gain, turned)


def head_at(index):
    return slice(index * HEAD_WIDTH, (index + 1) * HEAD_WIDTH)


def gate_column(logits, head):
    lanes = lax.broadcasted_iota(jnp.int32, logits.shape, 1)
    logit = jnp.sum(jnp.where(lanes == head, logits, 0.0), axis=-1, keepdims=True)
    return jax.nn.sigmoid(logit)


def probabilities(queries, keys, start, valid_count, piece_start):
    raw = dot(queries, keys, 1, 1) * HEAD_WIDTH ** (-0.5)
    row = start + lax.broadcasted_iota(jnp.int32, raw.shape, 0)
    column = lax.broadcasted_iota(jnp.int32, raw.shape, 1)
    last = piece_start + PIC
    inside = (row >= piece_start) & (row < last) & (column >= piece_start) & (column < last)
    allowed = (column < valid_count) & ((column <= row) | inside)
    scores = jnp.where(allowed, raw, masked_score)
    expos = jnp.exp(scores - jnp.max(scores, axis=-1, keepdims=True))
    return expos * (1.0 / jnp.sum(expos, axis=-1, keepdims=True))


QUERY_ROWS = 256


def attention_forward_kernel(groups, share, valid, start, pre, gains, cosine, sine, gated):
    sequence = pl.program_id(0)
    heads = groups * share
    length = pre.shape[0]
    for group in range(groups):
        keys = head_rows(pre[:, head_at(heads + group)], gains[1:2, :], cosine[...], sine[...])
        values = pre[:, head_at(heads + groups + group)].astype(low)
        for head in range(group * share, (group + 1) * share):
            for at in range(0, length, QUERY_ROWS):
                rows = slice(at, at + QUERY_ROWS)
                queries = head_rows(
                    pre[rows, head_at(head)], gains[0:1, :], cosine[rows, :], sine[rows, :]
                )
                probs = probabilities(queries, keys, at, valid[sequence], start[sequence])
                mixed = dot(probs.astype(low), values, 1, 0)
                gate = gate_column(pre[rows, head_at(heads + 2 * groups)], head)
                gated[rows, head_at(head)] = (mixed * gate).astype(low)


def attention_backward_kernel(
    groups, share, valid, start, pre, upstream, gains, cosine, sine, grads, gain_grads
):
    sequence = pl.program_id(0)
    heads = groups * share
    length = pre.shape[0]
    scale = HEAD_WIDTH ** (-0.5)

    @pl.when(sequence == 0)
    def _():
        gain_grads[...] = jnp.zeros_like(gain_grads)

    logit_grads = [jnp.zeros((QUERY_ROWS, HEAD_WIDTH), wide)] * (length // QUERY_ROWS)
    for group in range(groups):
        key_pre = pre[:, head_at(heads + group)]
        keys = head_rows(key_pre, gains[1:2, :], cosine[...], sine[...])
        values = pre[:, head_at(heads + groups + group)].astype(low)
        value_grad = jnp.zeros((length, HEAD_WIDTH), wide)
        key_grad = jnp.zeros((length, HEAD_WIDTH), wide)
        for head in range(group * share, (group + 1) * share):
            for block, at in enumerate(range(0, length, QUERY_ROWS)):
                rows = slice(at, at + QUERY_ROWS)
                query_pre = pre[rows, head_at(head)]
                queries = head_rows(query_pre, gains[0:1, :], cosine[rows, :], sine[rows, :])
                probs = probabilities(queries, keys, at, valid[sequence], start[sequence])
                probs_low = probs.astype(low)
                mixed = dot(probs_low, values, 1, 0)
                gate = gate_column(pre[rows, head_at(heads + 2 * groups)], head)
                gated_grad = upstream[rows, head_at(head)]
                mixed_grad = (gated_grad * gate).astype(low)
                logit_grad = (
                    jnp.sum(gated_grad * mixed, axis=-1, keepdims=True) * gate * (1.0 - gate)
                )
                lanes = lax.broadcasted_iota(jnp.int32, (QUERY_ROWS, HEAD_WIDTH), 1)
                logit_grads[block] = logit_grads[block] + jnp.where(lanes == head, logit_grad, 0.0)
                value_grad = value_grad + dot(probs_low, mixed_grad, 0, 0)
                prob_grad = dot(mixed_grad, values, 1, 1)
                score_grad = (
                    probs * (prob_grad - jnp.sum(prob_grad * probs, axis=-1, keepdims=True))
                ).astype(low)
                key_grad = key_grad + dot(score_grad, queries, 0, 0)
                query_grad, gained = head_back(
                    query_pre,
                    gains[0:1, :],
                    cosine[rows, :],
                    sine[rows, :],
                    dot(score_grad, keys, 1, 0) * scale,
                )
                grads[rows, head_at(head)] = query_grad.astype(low)
                gain_grads[0:1, :] += gained
        key_grad, gained = head_back(
            key_pre, gains[1:2, :], cosine[...], sine[...], key_grad * scale
        )
        gain_grads[1:2, :] += gained
        grads[:, head_at(heads + group)] = key_grad.astype(low)
        grads[:, head_at(heads + groups + group)] = value_grad.astype(low)
    for block, at in enumerate(range(0, length, QUERY_ROWS)):
        grads[slice(at, at + QUERY_ROWS), head_at(heads + 2 * groups)] = logit_grads[block].astype(
            low
        )


def sequence_block(columns, length):
    return pl.BlockSpec((length, columns), lambda sequence: (sequence, 0))


def fixed_block(*shape):
    return pl.BlockSpec(shape, lambda sequence: (0, 0))


SCALARS = pl.BlockSpec(memory_space=pltpu.SMEM)


def attention_forward(groups, share, valid, start, pre, gains, cosine, sine):
    length, columns = cosine.shape[0], groups * share * HEAD_WIDTH

    def body(*refs):
        attention_forward_kernel(groups, share, *refs)

    return pl.pallas_call(
        body,
        grid=(pre.shape[0] // length,),
        out_shape=jax.ShapeDtypeStruct((pre.shape[0], columns), low),
        in_specs=[
            SCALARS,
            SCALARS,
            sequence_block(pre.shape[1], length),
            fixed_block(2, HEAD_WIDTH),
            fixed_block(length, HEAD_WIDTH),
            fixed_block(length, HEAD_WIDTH),
        ],
        out_specs=sequence_block(columns, length),
        compiler_params=pltpu.CompilerParams(vmem_limit_bytes=48 * 2**20),
        cost_estimate=pl.CostEstimate(
            flops=2**30, bytes_accessed=8 * 2**20, transcendentals=2**21
        ),
        name="attention_forward",
    )(valid, start, pre, gains, cosine, sine)


def attention_backward(groups, share, valid, start, pre, upstream, gains, cosine, sine):
    length = cosine.shape[0]

    def body(*refs):
        attention_backward_kernel(groups, share, *refs)

    return pl.pallas_call(
        body,
        grid=(pre.shape[0] // length,),
        out_shape=[
            jax.ShapeDtypeStruct(pre.shape, low),
            jax.ShapeDtypeStruct((2, HEAD_WIDTH), wide),
        ],
        in_specs=[
            SCALARS,
            SCALARS,
            sequence_block(pre.shape[1], length),
            sequence_block(upstream.shape[1], length),
            fixed_block(2, HEAD_WIDTH),
            fixed_block(length, HEAD_WIDTH),
            fixed_block(length, HEAD_WIDTH),
        ],
        out_specs=[sequence_block(pre.shape[1], length), fixed_block(2, HEAD_WIDTH)],
        compiler_params=pltpu.CompilerParams(vmem_limit_bytes=48 * 2**20),
        cost_estimate=pl.CostEstimate(
            flops=2**32, bytes_accessed=12 * 2**20, transcendentals=2**21
        ),
        name="attention_backward",
    )(valid, start, pre, upstream, gains, cosine, sine)


def adam_kernel(layouts, names, heads, *refs):
    sources, refs = dict(zip(names, refs)), refs[len(names) :]
    count = len(layouts)
    stats, inverse, refs = refs[0], refs[1], refs[2:]
    small, refs = refs[:9], refs[9:]
    states, refs = refs[: 3 * count], refs[3 * count :]
    scales, small_targets, refs = refs[0], refs[1:10], refs[10:]
    targets, refs = refs[: 3 * count], refs[3 * count :]
    buffers, semaphores = refs[: 3 * count], refs[3 * count]
    loads = [
        pltpu.make_async_copy(states[i], buffers[i], semaphores.at[0, i]) for i in range(3 * count)
    ]
    stores = [
        pltpu.make_async_copy(buffers[i], targets[i], semaphores.at[1, i])
        for i in range(3 * count)
    ]
    for load in loads:
        load.start()

    def update(part, at, gradient, rate, decay_rate):
        old = (small[3 * part + i][at] for i in range(3))
        for i, value in enumerate(adam_update(*old, gradient, rate, decay_rate)):
            small_targets[3 * part + i][at] = value

    everything = (slice(None), slice(None))
    update(0, everything, stats[0:2, :], 0.5, 0.0)
    for row in range(2):
        update(1, (slice(row, row + 1), slice(None)), stats[2:3, head_at(row)], 0.5, 0.0)
    column, size = heads
    projected = sources["projected"]
    gradient = jnp.concatenate(
        [projected[core, :, column : column + 128][:, :size].astype(wide) for core in range(2)],
        axis=1,
    )
    update(2, everything, gradient, layouts[0][1], weight_decay)
    lanes = lax.broadcasted_iota(jnp.int32, scales.shape, 1)
    squares = stats[2:3, head_at(2)]
    squares = jnp.where(lanes == 2, jnp.sum(stats[3:4, :], axis=-1, keepdims=True), squares)
    scales[...] = jnp.sqrt(squares * inverse[...])
    for number, (transposed, rate, leads) in enumerate(layouts):
        matrix = buffers[3 * number : 3 * number + 3]
        for load in loads[3 * number : 3 * number + 3]:
            load.wait()
        for lead, pieces in enumerate(leads):
            quarter = sum(size for _, _, size in pieces)
            for core in range(2):
                start = core * quarter
                for name, column, size in pieces:
                    step = 256 if size % 256 == 0 else 128

                    @pl.loop(0, size // step)
                    def _(block):
                        columns = pl.ds(pl.multiple_of(column + block * step, 128), step)
                        gradient = sources[name][core, :, columns].astype(wide)
                        place = pl.ds(pl.multiple_of(start + block * step, 128), step)
                        if transposed:
                            gradient = gradient.T
                            at = (place, slice(None))
                        elif len(leads) > 1:
                            at = (lead, slice(None), place)
                        else:
                            at = (slice(None), place)
                        weight, moment, square = (part[at] for part in matrix)
                        for part, value in zip(
                            matrix,
                            adam_update(weight, moment, square, gradient, rate, weight_decay),
                        ):
                            part[at] = value

                    start += size
        for store in stores[3 * number : 3 * number + 3]:
            store.start()
    for store in stores:
        store.wait()


def adam_matrices(layouts, heads, sums, stats, inverse, small, states):
    def body(*refs):
        adam_kernel(layouts, list(sums), heads, *refs)

    def like(values):
        return [jax.ShapeDtypeStruct(value.shape, value.dtype) for value in values]

    return pl.pallas_call(
        body,
        out_shape=like([inverse, *small, *states]),
        in_specs=[VMEM] * (len(sums) + 2 + len(small)) + [ANY] * len(states),
        out_specs=[VMEM] * (1 + len(small)) + [ANY] * len(states),
        scratch_shapes=[pltpu.VMEM(value.shape, value.dtype) for value in states]
        + [pltpu.SemaphoreType.DMA((2, len(states)))],
        compiler_params=pltpu.CompilerParams(vmem_limit_bytes=48 * 2**20),
        cost_estimate=pl.CostEstimate(
            flops=2**25, bytes_accessed=40 * 2**20, transcendentals=2**21
        ),
        name="adam_matrices",
    )(*sums.values(), stats, inverse, *small, *states)


def local(
    tokens,
    cotangent,
    valid_len,
    pic_start,
    norm_gains,
    norm_moment,
    norm_square,
    head_gains,
    head_moment,
    head_square,
    query_weight,
    query_moment,
    query_square,
    keyvalue_matrix,
    keyvalue_first_moment,
    keyvalue_second_moment,
    headgate_weight,
    headgate_moment,
    headgate_square,
    output_weight,
    output_moment,
    output_square,
    gateup_weight,
    gateup_moment,
    gateup_square,
    down_weight,
    down_moment,
    down_square,
):
    local_rows = tokens.shape[0]
    length_value = local_rows * 2
    rows = length_value * 2
    group = lax.axis_index("w")
    core = lax.axis_index("c")
    place = lax.axis_index("t")
    heads_here = query_weight.shape[1] // HEAD_WIDTH // 2
    groups_here = keyvalue_matrix.shape[2] // HEAD_WIDTH // 2
    share = heads_here // groups_here
    head_cols = heads_here * HEAD_WIDTH
    group_cols = groups_here * HEAD_WIDTH
    hidden_here = gateup_weight.shape[2] // 2

    bounds = [0, head_cols, group_cols, group_cols, 128, head_cols]
    edges = [sum(bounds[: i + 1]) for i in range(6)]
    quarters = []
    for index in range(2):
        pieces = []
        for matrix in (
            query_weight, keyvalue_matrix[0], keyvalue_matrix[1], headgate_weight, output_weight.T
        ):
            size = matrix.shape[1] // 2
            piece = matrix[:, index * size : (index + 1) * size].astype(low)
            pieces.append(jnp.pad(piece, ((0, 0), (0, -size % 128))))
        quarters.append(jnp.concatenate(pieces, axis=1))
    matrices = (gateup_weight[0], gateup_weight[1], down_weight.T)
    sizes = (hidden_here - hidden_here // 6, hidden_here // 6)

    def quarter_columns(index, start, size):
        return jnp.concatenate(
            [
                matrix[:, index * hidden_here + start : index * hidden_here + start + size].astype(
                    low
                )
                for matrix in matrices
            ],
            axis=1,
        )

    large_block, small_block = (
        jnp.stack([quarter_columns(index, start, size) for index in range(2)])
        for start, size in zip((0, sizes[0]), sizes)
    )
    residual = tokens.astype(wide)
    mine, other, normed, large_block, small_block = lax.optimization_barrier(
        (
            jnp.where(core == 0, quarters[0], quarters[1]),
            jnp.where(core == 0, quarters[1], quarters[0]),
            normalize(residual, norm_gains[0]).astype(low),
            large_block,
            small_block,
        )
    )
    large_both = lax.all_gather(large_block, ("w", "c"), axis=1, tiled=True)
    small_both = lax.all_gather(small_block, ("w", "c"), axis=1, tiled=True)
    attention_full, first_full, output_grad_full = gather_attention(mine, other, normed, cotangent)
    projection_full, output_full = attention_full[:, : edges[4]], attention_full[:, edges[4] :]
    valid_pair = lax.dynamic_slice_in_dim(valid_len, 2 * group, 2)
    start_pair = lax.dynamic_slice_in_dim(pic_start, 2 * group, 2)
    cosine, sine = rotary_tables(length_value)
    projected = dot(first_full, projection_full, 1, 0)
    gated_low = attention_forward(
        groups_here, share, valid_pair, start_pair, projected, head_gains, cosine, sine
    )
    attention_local, second_full = exchange_forward(
        dot(gated_low, output_full, 1, 1).astype(low), tokens, norm_gains[1:2]
    )
    middle = residual + attention_local
    gate_large, up_large, hidden_large, *before = feedforward(
        core[None], second_full, output_grad_full, large_both
    )
    gate_small, up_small, hidden_small, second_partial, feedforward_partial = feedforward(
        core[None], second_full, output_grad_full, small_both, before
    )
    own_places = place * local_rows + jnp.arange(local_rows, dtype=jnp.int32)
    counted = (own_places < valid_pair[core]).astype(wide)[:, None]
    half = sizes[0] // 2
    pieces = [(0, half), (half, sizes[0] - half)]
    middle_grad, second_gain_grad, feedforward_local, output_squares, attention_grad, *sums = (
        exchange_backward(
            second_partial,
            feedforward_partial,
            middle,
            cotangent,
            norm_gains[1:2],
            counted,
            [
                (second_full, grad, *piece) for grad in (gate_large, up_large) for piece in pieces
            ]
            + [(second_full, grad, 0, sizes[1]) for grad in (gate_small, up_small)],
        )
    )
    block_output = (middle + feedforward_local).astype(low)
    projected_grad, head_gain_grads = attention_backward(
        groups_here,
        share,
        valid_pair,
        start_pair,
        projected,
        dot(attention_grad, output_full, 1, 0),
        head_gains,
        cosine,
        sine,
    )
    first_partial = dot(projected_grad, projection_full, 1, 1)
    squares = jnp.stack(
        [
            jnp.sum(counted * residual * residual),
            jnp.sum(counted * attention_local * attention_local),
        ]
    )
    small = jnp.concatenate([head_gain_grads.reshape(-1), squares])
    nothing = jnp.zeros((1, MODEL_WIDTH), wide)
    stats = jnp.concatenate(
        [
            nothing,
            second_gain_grad,
            jnp.pad(small, (0, MODEL_WIDTH - small.shape[0]))[None],
            output_squares,
            jnp.tile(nothing, (4, 1)),
        ]
    )
    tokens_grad, stats, projected_sums, output_sums, *more = exchange_last(
        first_partial.astype(low),
        tokens,
        norm_gains[0:1],
        middle_grad,
        stats,
        [
            (first_full, projected_grad, 0, edges[4]),
            (attention_grad, gated_low, 0, head_cols),
        ]
        + [(output_grad_full, hidden_large, *piece) for piece in pieces]
        + [(output_grad_full, hidden_small, 0, sizes[1])],
    )
    denominator = jnp.sum(valid_len).astype(wide) * MODEL_WIDTH
    inverse = jnp.full((1, HEAD_WIDTH), 1.0 / denominator)
    input_rate = MODEL_WIDTH ** (-0.5)
    down_rate = FF ** (-0.5)
    output_rate = max(QUERY_HEADS * HEAD_WIDTH // 128, 4) ** (-0.5)
    widths = [half, sizes[0] - half, sizes[1]]

    def parts_of(name):
        return [(f"{name} {index}", 0, width) for index, width in enumerate(widths)]

    layouts = [
        (
            False,
            input_rate,
            [parts_of("gate"), parts_of("up")],
        ),
        (True, down_rate, [parts_of("down")]),
        (False, input_rate, [[("projected", edges[0], head_cols)]]),
        (
            False,
            input_rate,
            [[("projected", edges[1], group_cols)], [("projected", edges[2], group_cols)]],
        ),
        (True, output_rate, [[("output", 0, head_cols)]]),
    ]
    names = ["gate 0", "gate 1", "up 0", "up 1", "gate 2", "up 2", "down 0", "down 1", "down 2"]
    sums = dict(zip(names, [*sums, *more]))
    sums["projected"], sums["output"] = projected_sums, output_sums
    scales, *updated = adam_matrices(
        layouts,
        (edges[3], heads_here),
        sums,
        stats,
        inverse,
        [
            norm_gains,
            norm_moment,
            norm_square,
            head_gains,
            head_moment,
            head_square,
            headgate_weight,
            headgate_moment,
            headgate_square,
        ],
        [
            gateup_weight,
            gateup_moment,
            gateup_square,
            down_weight,
            down_moment,
            down_square,
            query_weight,
            query_moment,
            query_square,
            keyvalue_matrix,
            keyvalue_first_moment,
            keyvalue_second_moment,
            output_weight,
            output_moment,
            output_square,
        ],
    )
    norms_new, heads_new, headgate_new, gateup_new, down_new, query_new, keyvalue_new, output_new = (
        updated[3 * i : 3 * i + 3] for i in range(8)
    )
    branch_scales = scales[0, :3]
    return (
        block_output,
        tokens_grad,
        branch_scales,
        *norms_new,
        *heads_new,
        *query_new,
        *keyvalue_new,
        *headgate_new,
        *output_new,
        *gateup_new,
        *down_new,
    )


def solution(mesh):
    fsdp, tp = mesh.devices.shape
    fine = Mesh(mesh.devices.reshape(fsdp // 2, 2, tp), ("w", "c", "t"))
    whole = ("w", "c")
    rows = P(("w", "c", "t"), None)
    first = P(whole, "t")
    second = P(None, whole, "t")
    last = P("t", whole)
    matrices = (first,) * 3 + (second,) * 3 + (first,) * 3 + (last,) * 3 + (second,) * 3 + (last,) * 3
    return jax.shard_map(
        local,
        mesh=fine,
        in_specs=(rows, rows, P(), P()) + (P(),) * 6 + matrices,
        out_specs=(rows, rows, P()) + (P(),) * 6 + matrices,
        check_vma=False,
    )
```

```python
import jax
import jax.numpy as jnp
from jax import lax
from jax.experimental import pallas as pl
from jax.experimental.pallas import tpu as pltpu
from jax.sharding import Mesh
from jax.sharding import PartitionSpec as P

MODEL_WIDTH = 2048
QUERY_HEADS = 16
HEAD_WIDTH = 128
FF = 6144
PIC = 256
STEP = 10

norm_epsilon = 1e-06
rope_base = 1000000.0
beta_first = 0.9
beta_second = 0.999
adam_epsilon = 1e-08
weight_decay = 0.1
masked_score = -1e30
low = jnp.bfloat16
wide = jnp.float32


def normalize(values, scaling):
    return (
        values
        * lax.rsqrt(jnp.mean(values * values, axis=-1, keepdims=True) + norm_epsilon)
        * scaling
    )


def norm_back(values, scaling, upstream):
    factor = lax.rsqrt(jnp.mean(values * values, axis=-1, keepdims=True) + norm_epsilon)
    weighted = upstream * scaling
    projected = jnp.mean(weighted * values, axis=-1, keepdims=True)
    result = factor * weighted - values * (factor * factor * factor) * projected
    return (result, jnp.sum(upstream * values * factor, axis=tuple(range(values.ndim - 1))))


def rotary_tables(length_value):
    halves = HEAD_WIDTH // 2
    frequency = rope_base ** (-(jnp.arange(halves, dtype=wide) * 2.0 / HEAD_WIDTH))
    angles = jnp.arange(length_value, dtype=wide)[:, None] * frequency[None, :]
    cosine, sine = jnp.cos(angles), jnp.sin(angles)
    return (
        jnp.concatenate([cosine, cosine], axis=1),
        jnp.concatenate([-sine, sine], axis=1),
    )


def adam_update(weight, moment, square, gradient, step_rate, decay_rate):
    moment_new = beta_first * moment + (1.0 - beta_first) * gradient
    square_new = beta_second * square + (1.0 - beta_second) * gradient * gradient
    bias_first = 1.0 - beta_first**STEP
    bias_second = 1.0 - beta_second**STEP
    update = moment_new / bias_first / (jnp.sqrt(square_new / bias_second) + adam_epsilon)
    return (weight - step_rate * (update + decay_rate * weight), moment_new, square_new)


def dot(left, right, left_dim, right_dim):
    return lax.dot_general(
        left, right, (((left_dim,), (right_dim,)), ((), ())), preferred_element_type=wide
    )


def fetch(parts):
    pieces = []
    for core in range(2):
        for part in parts:
            size = part.shape[1] // 2
            pieces.append(part[:, core * size : (core + 1) * size].astype(low))
    count = len(parts)
    local_block = jnp.stack(
        [jnp.concatenate(pieces[core * count : (core + 1) * count], axis=1) for core in range(2)]
    )
    return lax.all_gather(local_block, ("w", "c"), axis=1, tiled=True)


def columns_of(both, start, size):
    return lax.dynamic_slice(
        both, (lax.axis_index("c"), 0, start), (1, both.shape[1], size)
    ).reshape(both.shape[1], size)


MESH = pl.DeviceIdType.MESH
BLOCKS = 4
STRIP = 16
ANY = pl.BlockSpec(memory_space=pl.ANY)
VMEM = pl.BlockSpec(memory_space=pltpu.VMEM)


def ring_place(index, count):
    odd = lax.rem(index, 2)
    pair = lax.div(index, 2)
    return (1 - odd) * pair + odd * (count - 1 - pair)


def ring_index(place, count):
    late = lax.div(place, count // 2)
    return (1 - late) * 2 * place + late * (2 * (count - 1 - place) + 1)


class Device:
    def __init__(self, semaphores):
        self.w, self.c, self.t = (lax.axis_index(axis) for axis in ("w", "c", "t"))
        self.count = lax.axis_size("w")
        self.place = ring_place(self.w, self.count)
        self.semaphores = semaphores
        self.used = 0
        self.other_core = {"c": 1 - self.c}
        self.other_row = {"t": 1 - self.t}

    def owner(self, distance):
        return ring_index(lax.rem(self.place + distance + self.count, self.count), self.count)

    def meet(self, partners):
        barrier = pltpu.get_barrier_semaphore()
        for partner in partners:
            pl.semaphore_signal(barrier, inc=1, device_id=partner, device_id_type=MESH)
        pl.semaphore_wait(barrier, len(partners))

    def remote(self, source, target, device):
        slot = self.used
        self.used += 1
        return pltpu.make_async_remote_copy(
            src_ref=source,
            dst_ref=target,
            send_sem=self.semaphores.at[0, slot],
            recv_sem=self.semaphores.at[1, slot],
            device_id=device,
            device_id_type=MESH,
        )

    def inside(self, source, target):
        slot = self.used
        self.used += 1
        return pltpu.make_async_copy(source, target, self.semaphores.at[0, slot])


def rows_at(start, size):
    return pl.ds(pl.multiple_of(start, STRIP), size)


class Spread:
    def __init__(self, device, full):
        self.device, self.full = device, full
        self.size = full.shape[0] // 4
        self.block = self.size // BLOCKS
        self.rows, self.core, self.passed, self.kept = {}, {}, {}, {}

    def where(self, core, row, index):
        return self.full.at[
            rows_at((core * 2 + row) * self.size + index * self.block, self.block)
        ]

    def put(self, index, source):
        device = self.device
        target = self.where(device.c, device.t, index)
        self.rows[index] = device.remote(source, target, device.other_row)
        self.core[index] = device.remote(source, target, device.other_core)
        self.kept[index] = device.inside(source, target)
        for copy in (self.rows[index], self.core[index], self.kept[index]):
            copy.start()

    def forward(self, index):
        device = self.device
        self.rows[index].wait_recv()
        place = self.where(device.c, 1 - device.t, index)
        self.passed[index] = device.remote(place, place, device.other_core)
        self.passed[index].start()

    def finish(self):
        for index in range(BLOCKS):
            self.rows[index].wait_send()
            self.core[index].wait()
            self.passed[index].wait()
            self.kept[index].wait()


class Collect:
    def __init__(self, device, partial, near, far, sent, came):
        self.device = device
        self.partial, self.near, self.far, self.sent, self.came = partial, near, far, sent, came
        self.size = partial.shape[0] // 4
        self.block = self.size // BLOCKS
        self.core, self.rows = {}, {}

    def start(self):
        device = self.device
        self.load = device.inside(
            self.partial.at[rows_at(device.c * 2 * self.size, 2 * self.size)], self.near
        )
        for part, row in enumerate((1 - device.t, device.t)):
            for index in range(BLOCKS):
                start = row * self.size + index * self.block
                copy = device.remote(
                    self.partial.at[rows_at((1 - device.c) * 2 * self.size + start, self.block)],
                    self.far.at[rows_at(start, self.block)],
                    device.other_core,
                )
                copy.start()
                self.core[part, index] = copy
        self.load.start()

    def pass_on(self, index):
        device = self.device
        if index == 0:
            self.load.wait()
        self.core[0, index].wait_recv()

        @pl.loop(0, self.block // STRIP)
        def _(strip):
            at = index * self.block + strip * STRIP
            rows = rows_at((1 - device.t) * self.size + at, STRIP)
            total = self.near[rows, :].astype(wide) + self.far[rows, :].astype(wide)
            self.sent[rows_at(at, STRIP), :] = total.astype(low)

        place = rows_at(index * self.block, self.block)
        self.rows[index] = device.remote(
            self.sent.at[place], self.came.at[place], device.other_row
        )
        self.rows[index].start()

    def take(self, index, use):
        device = self.device
        self.core[1, index].wait_recv()
        self.rows[index].wait_recv()

        @pl.loop(0, self.block // STRIP)
        def _(strip):
            at = index * self.block + strip * STRIP
            rows = rows_at(device.t * self.size + at, STRIP)
            mine = rows_at(at, STRIP)
            total = (
                self.near[rows, :].astype(wide)
                + self.far[rows, :].astype(wide)
                + self.came[mine, :].astype(wide)
            )
            use(mine, total)

    def finish(self):
        for index in range(BLOCKS):
            self.core[0, index].wait_send()
            self.core[1, index].wait_send()
            self.rows[index].wait_send()


class Given:
    parts = 2

    def __init__(self, grads):
        self.rows, self.columns = grads.shape
        self.grads = grads

    def take(self, starts, size):
        return [self.grads[rows_at(start, size), :].astype(wide) for start in starts]

    def sources(self, starts, size, keep):
        return [self.grads.at[rows_at(start, size)] for start in starts]


class Product:
    parts = 1

    def __init__(self, left, right, start, columns):
        self.rows, self.columns = left.shape[1], columns
        self.left, self.right, self.start = left, right, start

    def take(self, starts, size):
        left = jnp.concatenate(
            [self.left[:, pl.ds(pl.multiple_of(start, 128), size)] for start in starts], axis=1
        )
        both = dot(left, self.right[:, self.start : self.start + self.columns], 0, 0)
        return [both[:size], both[size:]]

    def sources(self, starts, size, keep):
        for way, value in enumerate(self.take(starts, size)):
            keep[way] = value.astype(low)
        return [keep.at[way] for way in range(2)]


class RingSum:
    def __init__(self, device, grads, ready, scratch, sums):
        self.device, self.grads, self.sums = device, grads, sums
        self.ready = ready
        self.slots, self.totals, self.first = scratch
        self.half = grads.rows // device.count // 2
        self.parts = grads.parts
        self.part = self.half // self.parts
        self.copies = {}
        self.ticks = [
            (step, part) for step in range(device.count) for part in range(self.parts)
        ]

    def own(self, way, distance, part):
        owner = self.device.owner(-(1 - 2 * way) * distance)
        return (owner * 2 + way) * self.half + part * self.part

    def slot(self, way, step, part):
        return self.slots.at[
            way * (self.device.count - 1) + step, pl.ds(part * self.part, self.part)
        ]

    def send(self, way, step, part, source):
        device = self.device
        copy = device.remote(
            source, self.slot(way, step, part), {"w": device.owner(1 - 2 * way)}
        )
        copy.start()
        self.copies[way, step, part] = copy

    def tick(self, count=1):
        device = self.device
        for _ in range(count):
            if not self.ticks:
                return
            step, part = self.ticks.pop(0)
            starts = [self.own(way, step + 1, part) for way in range(2)]
            if step == 0:
                self.ready()
                sources = self.grads.sources(starts, self.part, self.first)
                for way in range(2):
                    self.send(way, step, part, sources[way])
                continue
            own = self.grads.take(starts, self.part)
            for way in range(2):
                self.copies[way, step - 1, part].wait_recv()
                slot = self.slot(way, step - 1, part)
                total = (slot[...].astype(wide) + own[way]).astype(low)
                if step < device.count - 1:
                    slot[...] = total
                    self.send(way, step, part, slot)
                else:
                    self.totals[way, pl.ds(part * self.part, self.part), :] = total

    def close(self):
        device = self.device
        self.tick(len(self.ticks))
        self.away = device.remote(
            self.totals.at[1 - device.c], self.sums.at[device.c], device.other_core
        )
        self.kept = device.inside(self.totals.at[device.c], self.sums.at[device.c])
        self.away.start()
        self.kept.start()

    def finish(self):
        for copy in self.copies.values():
            copy.wait_send()
        self.away.wait()
        self.kept.wait()


def ring_shapes(columns, count):
    half = MODEL_WIDTH // count // 2
    return [
        pltpu.VMEM((2 * (count - 1), half, columns), low),
        pltpu.VMEM((2, half, columns), low),
        pltpu.VMEM((2, half, columns), low),
    ]


class RingWork:
    def __init__(self, pairs):
        self.columns = [columns for _, _, _, columns in pairs]
        self.fit = (MODEL_WIDTH // lax.axis_size("w") // 2) % 128 == 0
        self.operands, self.places = [], []
        for left, right, start, columns in pairs:
            if self.fit:
                self.places.append((self.add(left), self.add(right), start, columns))
            else:
                part = right[:, start : start + columns]
                self.places.append((self.add(dot(left, part, 0, 0).astype(low)),))

    def add(self, value):
        for index, other in enumerate(self.operands):
            if other is value:
                return index
        self.operands.append(value)
        return len(self.operands) - 1

    def begin(self, device, operands, scratch, sums):
        count = len(self.operands)
        buffers, scratch = scratch[:count], scratch[count:]
        loads = [device.inside(value, buffer) for value, buffer in zip(operands, buffers)]
        for load in loads:
            load.start()
        waiting = set(range(count))
        rings = []
        for index, place in enumerate(self.places):
            used = place[:2] if self.fit else place[:1]

            def ready(used=used):
                for number in used:
                    if number in waiting:
                        waiting.remove(number)
                        loads[number].wait()

            refs = [buffers[number] for number in used]
            grads = Product(*refs, *place[2:]) if self.fit else Given(*refs)
            rings.append(
                RingSum(device, grads, ready, scratch[3 * index : 3 * index + 3], sums[index])
            )
        return Rings(rings)

    def outputs(self):
        half = MODEL_WIDTH // lax.axis_size("w") // 2
        return [jax.ShapeDtypeStruct((2, half, size), low) for size in self.columns]

    def scratch(self):
        count = lax.axis_size("w")
        return [pltpu.VMEM(value.shape, value.dtype) for value in self.operands] + [
            shape for size in self.columns for shape in ring_shapes(size, count)
        ]

    def semaphores(self):
        return 4 * (lax.axis_size("w") + 1) * len(self.columns) + len(self.operands)


def collect_shapes(size):
    return [
        pltpu.VMEM((2 * size, MODEL_WIDTH), low),
        pltpu.VMEM((2 * size, MODEL_WIDTH), low),
        pltpu.VMEM((size, MODEL_WIDTH), low),
        pltpu.VMEM((size, MODEL_WIDTH), low),
    ]


def semaphores_for(count):
    return pltpu.SemaphoreType.DMA((2, count))


def settings(collective):
    return pltpu.CompilerParams(
        collective_id=collective, has_side_effects=True, vmem_limit_bytes=56 * 2**20
    )


def neighbours(device):
    return [
        device.other_core,
        device.other_row,
        {"w": device.owner(1)},
        {"w": device.owner(-1)},
    ]


class RingGather:
    def __init__(self, device, mine, other, full):
        self.device, self.full = device, full
        self.size = mine.shape[0]
        self.parts = min(4, self.size // STRIP)
        self.part = self.size // self.parts
        here = rows_at((device.w * 2 + device.c) * self.size, self.size)
        self.kept = device.inside(mine, full.at[here])
        self.crossed = device.remote(other, full.at[here], device.other_core)
        self.copies = {}
        self.ticks = [
            (step, part) for step in range(device.count - 1) for part in range(self.parts)
        ]

    def start(self):
        self.kept.start()
        self.crossed.start()

    def ready(self):
        self.kept.wait()
        self.crossed.wait()

    def tick(self, count=1):
        device = self.device
        for _ in range(count):
            if not self.ticks:
                return
            step, part = self.ticks.pop(0)
            for way in range(2):
                if step > 0:
                    self.copies[way, step - 1, part].wait_recv()
                owner = device.owner(-(1 - 2 * way) * step)
                block = self.full.at[
                    rows_at((owner * 2 + way) * self.size + part * self.part, self.part)
                ]
                copy = device.remote(block, block, {"w": device.owner(1 - 2 * way)})
                copy.start()
                self.copies[way, step, part] = copy

    def finish(self):
        self.tick(len(self.ticks))
        for part in range(self.parts):
            for way in range(2):
                self.copies[way, self.device.count - 2, part].wait_recv()
        for copy in self.copies.values():
            copy.wait_send()


def gather_kernel(mine, other, first, second, full, first_full, second_full, semaphores):
    device = Device(semaphores)
    device.meet(neighbours(device))
    gather = RingGather(device, mine, other, full)
    gather.start()
    spreads = []
    for rows, target in ((first, first_full), (second, second_full)):
        spread = Spread(device, target)
        block = spread.block
        for index in range(BLOCKS):
            spread.put(index, rows.at[pl.ds(index * block, block)])
        spreads.append(spread)
    gather.ready()
    for spread in spreads:
        for index in range(BLOCKS):
            gather.tick(gather.parts)
            spread.forward(index)
    gather.finish()
    for spread in spreads:
        spread.finish()


def gather_attention(mine, other, first, second):
    count = lax.axis_size("w")
    rows = first.shape[0] * 4
    return pl.pallas_call(
        gather_kernel,
        out_shape=[
            jax.ShapeDtypeStruct((MODEL_WIDTH, mine.shape[1]), low),
            jax.ShapeDtypeStruct((rows, MODEL_WIDTH), low),
            jax.ShapeDtypeStruct((rows, MODEL_WIDTH), low),
        ],
        in_specs=[ANY] * 4,
        out_specs=[ANY] * 3,
        scratch_shapes=[semaphores_for(8 * count + 8 * BLOCKS + 2)],
        compiler_params=settings(1),
        cost_estimate=pl.CostEstimate(flops=0, bytes_accessed=64 * 2**20, transcendentals=0),
        name="gather_attention",
    )(mine, other, first, second)


def forward_kernel(
    partial, rows, gain, total, full, near, far, sent, came, normed, semaphores
):
    device = Device(semaphores)
    device.meet([device.other_core, device.other_row])
    collect = Collect(device, partial, near, far, sent, came)
    spread = Spread(device, full)
    collect.start()
    for index in range(BLOCKS):
        collect.pass_on(index)

    def use(at, value):
        total[at, :] = value
        middle = rows[at, :].astype(wide) + value
        normed[at, :] = normalize(middle, gain[...]).astype(low)

    for index in range(BLOCKS):
        collect.take(index, use)
        spread.put(index, normed.at[pl.ds(index * spread.block, spread.block)])
    for index in range(BLOCKS):
        spread.forward(index)
    spread.finish()
    collect.finish()


def exchange_forward(partial, rows, gain):
    size = rows.shape[0]
    return pl.pallas_call(
        forward_kernel,
        out_shape=[
            jax.ShapeDtypeStruct((size, MODEL_WIDTH), wide),
            jax.ShapeDtypeStruct((4 * size, MODEL_WIDTH), low),
        ],
        in_specs=[ANY, VMEM, VMEM],
        out_specs=[VMEM, ANY],
        scratch_shapes=collect_shapes(size)
        + [pltpu.VMEM((size, MODEL_WIDTH), low), semaphores_for(16 * BLOCKS)],
        compiler_params=settings(2),
        cost_estimate=pl.CostEstimate(flops=0, bytes_accessed=64 * 2**20, transcendentals=0),
        name="exchange_forward",
    )(partial, rows, gain)


class Rings:
    def __init__(self, rings):
        self.rings = rings
        self.next = 0

    def tick(self, count=1):
        for _ in range(count):
            ring = self.rings[self.next]
            self.next = (self.next + 1) % len(self.rings)
            ring.tick()

    def finish(self):
        while any(ring.ticks for ring in self.rings):
            self.tick()
        for ring in self.rings:
            ring.close()
        for ring in self.rings:
            ring.finish()


def norm_back_rows(values, gain, upstream):
    factor = lax.rsqrt(jnp.mean(values * values, axis=-1, keepdims=True) + norm_epsilon)
    weighted = upstream * gain
    projected = jnp.mean(weighted * values, axis=-1, keepdims=True)
    result = factor * weighted - values * (factor * factor * factor) * projected
    return result, jnp.sum(upstream * values * factor, axis=0, keepdims=True)


def backward_kernel(work, partial, output, middle, rows, gain, counted, *refs):
    count = len(work.columns)
    operands, refs = refs[: len(work.operands)], refs[len(work.operands) :]
    grad, gain_grad, block, squares, full, refs = *refs[:5], refs[5:]
    sums, refs = refs[:count], refs[count:]
    rounded = refs[8]
    device = Device(refs[-1])
    rings = work.begin(device, operands, refs[9:-1], sums)
    device.meet(neighbours(device))
    collect = Collect(device, partial, *refs[:4])
    output_collect = Collect(device, output, *refs[4:8])
    spread = Spread(device, full)
    collect.start()
    rings.tick(2)
    gain_grad[...] = jnp.zeros_like(gain_grad)
    squares[...] = jnp.zeros_like(squares)
    for index in range(BLOCKS):
        collect.pass_on(index)
    rings.tick(count - 2)
    output_collect.start()

    def use(at, upstream):
        result, gained = norm_back_rows(middle[at, :], gain[...], upstream)
        result = result + rows[at, :].astype(wide)
        grad[at, :] = result
        rounded[at, :] = result.astype(low)
        gain_grad[...] += gained

    def use_output(at, value):
        block[at, :] = (middle[at, :] + value).astype(low)
        squares[...] += jnp.sum(counted[at, :] * value * value, axis=0, keepdims=True)

    for index in range(BLOCKS):
        collect.take(index, use)
        spread.put(index, rounded.at[pl.ds(index * spread.block, spread.block)])
        rings.tick(1)
    for index in range(BLOCKS):
        output_collect.pass_on(index)
    rings.tick(2)
    for index in range(BLOCKS):
        spread.forward(index)
        rings.tick(1)
    for index in range(BLOCKS):
        output_collect.take(index, use_output)
        rings.tick(1)
    rings.finish()
    spread.finish()
    collect.finish()
    output_collect.finish()


def exchange_backward(partial, output, middle, rows, gain, counted, pairs):
    size = rows.shape[0]
    work = RingWork(pairs)

    def body(*refs):
        backward_kernel(work, *refs)

    return pl.pallas_call(
        body,
        out_shape=[
            jax.ShapeDtypeStruct((size, MODEL_WIDTH), wide),
            jax.ShapeDtypeStruct((1, MODEL_WIDTH), wide),
            jax.ShapeDtypeStruct((size, MODEL_WIDTH), low),
            jax.ShapeDtypeStruct((1, MODEL_WIDTH), wide),
            jax.ShapeDtypeStruct((4 * size, MODEL_WIDTH), low),
            *work.outputs(),
        ],
        in_specs=[ANY, ANY] + [VMEM] * 4 + [ANY] * len(work.operands),
        out_specs=[VMEM] * 4 + [ANY] * (1 + len(work.columns)),
        scratch_shapes=collect_shapes(size) * 2
        + [pltpu.VMEM((size, MODEL_WIDTH), low)]
        + work.scratch()
        + [semaphores_for(32 * BLOCKS + work.semaphores())],
        compiler_params=settings(3),
        cost_estimate=pl.CostEstimate(flops=0, bytes_accessed=128 * 2**20, transcendentals=0),
        name="exchange_backward",
    )(partial, output, middle, rows, gain, counted, *work.operands)


class Total:
    def __init__(self, device, mine, crossed, gathered):
        self.device, self.mine = device, mine
        self.crossed, self.gathered = crossed, gathered
        self.copies = {}
        self.steps = [("c", 0), ("t", 0)] + [("w", step) for step in range(device.count // 2)]

    def tick(self):
        device = self.device
        if not self.steps:
            return
        axis, step = self.steps.pop(0)
        if axis != "w":
            slot = 0 if axis == "c" else 1
            partner = device.other_core if axis == "c" else device.other_row
            copy = device.remote(self.mine.at[slot], self.crossed.at[slot], partner)
            copy.start()
            copy.wait()
            total = self.mine[slot] + self.crossed[slot]
            if slot == 0:
                self.mine[1] = total
            else:
                self.gathered[device.w] = total
            return
        for way in range(2):
            if way == 1 and step == device.count // 2 - 1:
                continue
            if step > 0:
                self.copies[way, step - 1].wait_recv()
            block = self.gathered.at[device.owner(-(1 - 2 * way) * step)]
            copy = device.remote(block, block, {"w": device.owner(1 - 2 * way)})
            copy.start()
            self.copies[way, step] = copy

    def finish(self, target):
        while self.steps:
            self.tick()
        half = self.device.count // 2
        self.copies[0, half - 1].wait_recv()
        self.copies[1, half - 2].wait_recv()
        for copy in self.copies.values():
            copy.wait_send()
        target[...] = self.gathered[0]
        for index in range(1, self.device.count):
            target[...] += self.gathered[index]


def last_kernel(work, first, tokens, gain, middle_grad, stats, *refs):
    count = len(work.columns)
    operands, refs = refs[: len(work.operands)], refs[len(work.operands) :]
    first_total, stats_total, refs = refs[0], refs[1], refs[2:]
    sums, scratch = refs[:count], refs[count:]
    device = Device(scratch[-1])
    rings = work.begin(device, operands, scratch[7:-1], sums)
    device.meet(neighbours(device))
    collect = Collect(device, first, *scratch[:4])
    mine, crossed, gathered = scratch[4:7]
    total = Total(device, mine, crossed, gathered)
    mine[0] = stats[...]
    collect.start()
    rings.tick(2)
    for index in range(BLOCKS):
        collect.pass_on(index)
    rings.tick(count - 2)

    def use(at, upstream):
        result, gained = norm_back_rows(tokens[at, :].astype(wide), gain[...], upstream)
        first_total[at, :] = result + middle_grad[at, :]
        mine[0, 0:1, :] += gained

    for index in range(BLOCKS):
        collect.take(index, use)
        rings.tick(1)
    while total.steps:
        total.tick()
        rings.tick(1)
    rings.finish()
    total.finish(stats_total)
    collect.finish()


def exchange_last(first, tokens, gain, middle_grad, stats, pairs):
    size = tokens.shape[0]
    count = lax.axis_size("w")
    work = RingWork(pairs)

    def body(*refs):
        last_kernel(work, *refs)

    return pl.pallas_call(
        body,
        out_shape=[
            jax.ShapeDtypeStruct((size, MODEL_WIDTH), wide),
            jax.ShapeDtypeStruct(stats.shape, wide),
            *work.outputs(),
        ],
        in_specs=[ANY] + [VMEM] * 4 + [ANY] * len(work.operands),
        out_specs=[VMEM] * 2 + [ANY] * len(work.columns),
        scratch_shapes=collect_shapes(size)
        + [
            pltpu.VMEM((2, *stats.shape), wide),
            pltpu.VMEM((2, *stats.shape), wide),
            pltpu.VMEM((count, *stats.shape), wide),
        ]
        + work.scratch()
        + [semaphores_for(16 * BLOCKS + 2 * count + 4 + work.semaphores())],
        compiler_params=settings(4),
        cost_estimate=pl.CostEstimate(flops=0, bytes_accessed=128 * 2**20, transcendentals=0),
        name="exchange_last",
    )(first, tokens, gain, middle_grad, stats, *work.operands)


FEEDFORWARD_ROWS = 256
FEEDFORWARD_COLUMNS = 512


def feedforward_kernel(core, rows, upstream, weights, *refs):
    before, refs = refs[:-5][:2], refs[-5:]
    gate_out, up_out, hidden_out, back_out, down_out = refs
    weight = weights.at[0]
    size = gate_out.shape[1]
    for start in range(0, size, FEEDFORWARD_COLUMNS):
        width = min(FEEDFORWARD_COLUMNS, size - start)
        columns = slice(start, start + width)
        gate_part = dot(rows[...], weight[:, start : start + width], 1, 0)
        up_part = dot(rows[...], weight[:, size + start : size + start + width], 1, 0)
        hidden_grad = dot(
            upstream[...], weight[:, 2 * size + start : 2 * size + start + width], 1, 0
        )
        sigmoid_gate = jax.nn.sigmoid(gate_part)
        silu_gate = gate_part * sigmoid_gate
        hidden_out[:, columns] = (silu_gate * up_part).astype(low)
        gate_out[:, columns] = (
            hidden_grad * up_part * sigmoid_gate * (1.0 + gate_part * (1.0 - sigmoid_gate))
        ).astype(low)
        up_out[:, columns] = (hidden_grad * silu_gate).astype(low)
    for start in range(0, MODEL_WIDTH, FEEDFORWARD_COLUMNS):
        across = slice(start, start + FEEDFORWARD_COLUMNS)
        back = dot(gate_out[...], weight[across, :size], 1, 1)
        back = back + dot(up_out[...], weight[across, size : 2 * size], 1, 1)
        down = dot(hidden_out[...], weight[across, 2 * size :], 1, 1)
        if before:
            back = back + before[0][:, across].astype(wide)
            down = down + before[1][:, across].astype(wide)
        back_out[:, across] = back.astype(low)
        down_out[:, across] = down.astype(low)


def feedforward(core, rows, upstream, weights, start, hidden, before=()):
    count = rows.shape[0]
    size = weights.shape[2] // 3

    def block(columns, place=0):
        return pl.BlockSpec((FEEDFORWARD_ROWS, columns), lambda index, core: (index, place))

    return pl.pallas_call(
        feedforward_kernel,
        grid_spec=pltpu.PrefetchScalarGridSpec(
            num_scalar_prefetch=1,
            grid=(count // FEEDFORWARD_ROWS,),
            in_specs=[
                block(MODEL_WIDTH),
                block(MODEL_WIDTH),
                pl.BlockSpec(
                    (1, *weights.shape[1:]),
                    lambda index, core: (core[0], 0, 0),
                    pipeline_mode=pl.Buffered(1),
                ),
            ]
            + [block(MODEL_WIDTH)] * len(before[:2])
            + [ANY] * len(before[2:]),
            out_specs=[block(size, start // size)] * 3 + [block(MODEL_WIDTH)] * 2,
        ),
        out_shape=[jax.ShapeDtypeStruct((count, hidden), low)] * 3
        + [jax.ShapeDtypeStruct((count, MODEL_WIDTH), low)] * 2,
        input_output_aliases={6 + i: i for i in range(len(before[2:]))},
        compiler_params=pltpu.CompilerParams(vmem_limit_bytes=52 * 2**20),
        cost_estimate=pl.CostEstimate(
            flops=12 * count * MODEL_WIDTH * size,
            bytes_accessed=48 * 2**20,
            transcendentals=count * size,
        ),
        name="feedforward_more" if before else "feedforward",
    )(core, rows, upstream, weights, *before)


def head_rows(values, gain, cosine, sine):
    factor = lax.rsqrt(jnp.mean(values * values, axis=-1, keepdims=True) + norm_epsilon)
    normed = values * factor * gain
    return (normed * cosine + pltpu.roll(normed, HEAD_WIDTH // 2, 1) * sine).astype(low)


def head_back(values, gain, cosine, sine, upstream):
    turned = upstream * cosine - pltpu.roll(upstream, HEAD_WIDTH // 2, 1) * sine
    return norm_back_rows(values, gain, turned)


def head_at(index):
    return slice(index * HEAD_WIDTH, (index + 1) * HEAD_WIDTH)


def gate_column(logits, head):
    lanes = lax.broadcasted_iota(jnp.int32, logits.shape, 1)
    logit = jnp.sum(jnp.where(lanes == head, logits, 0.0), axis=-1, keepdims=True)
    return jax.nn.sigmoid(logit)


def probabilities(queries, keys, start, valid_count, piece_start):
    raw = dot(queries, keys, 1, 1) * HEAD_WIDTH ** (-0.5)
    row = start + lax.broadcasted_iota(jnp.int32, raw.shape, 0)
    column = lax.broadcasted_iota(jnp.int32, raw.shape, 1)
    last = piece_start + PIC
    inside = (row >= piece_start) & (row < last) & (column >= piece_start) & (column < last)
    allowed = (column < valid_count) & ((column <= row) | inside)
    scores = jnp.where(allowed, raw, masked_score)
    expos = jnp.exp(scores - jnp.max(scores, axis=-1, keepdims=True))
    return expos * (1.0 / jnp.sum(expos, axis=-1, keepdims=True))


QUERY_ROWS = 256


def attention_forward_kernel(
    groups, share, valid, start, rows_in, weights, gains, cosine, sine, pre, gated, partial
):
    sequence = pl.program_id(0)
    heads = groups * share
    length, projected = pre.shape
    for column in range(0, projected, 3 * HEAD_WIDTH):
        columns = slice(column, min(column + 3 * HEAD_WIDTH, projected))
        pre[:, columns] = dot(rows_in[...], weights[:, columns], 1, 0)
    for group in range(groups):
        keys = head_rows(pre[:, head_at(heads + group)], gains[1:2, :], cosine[...], sine[...])
        values = pre[:, head_at(heads + groups + group)].astype(low)
        for head in range(group * share, (group + 1) * share):
            for at in range(0, length, QUERY_ROWS):
                rows = slice(at, at + QUERY_ROWS)
                queries = head_rows(
                    pre[rows, head_at(head)], gains[0:1, :], cosine[rows, :], sine[rows, :]
                )
                probs = probabilities(queries, keys, at, valid[sequence], start[sequence])
                mixed = dot(probs.astype(low), values, 1, 0)
                gate = gate_column(pre[rows, head_at(heads + 2 * groups)], head)
                gated[rows, head_at(head)] = (mixed * gate).astype(low)
    for column in range(0, MODEL_WIDTH, 512):
        partial[:, column : column + 512] = dot(
            gated[...], weights[column : column + 512, projected:], 1, 1
        ).astype(low)


def attention_backward_kernel(
    groups, share, valid, start, pre, rows_in, weights, gains, cosine, sine,
    grads, gain_grads, partial, upstream,
):
    sequence = pl.program_id(0)
    heads = groups * share
    length, projected = pre.shape
    upstream[...] = dot(rows_in[...], weights[:, projected:], 1, 0)
    scale = HEAD_WIDTH ** (-0.5)

    @pl.when(sequence == 0)
    def _():
        gain_grads[...] = jnp.zeros_like(gain_grads)

    logit_grads = [jnp.zeros((QUERY_ROWS, HEAD_WIDTH), wide)] * (length // QUERY_ROWS)
    for group in range(groups):
        key_pre = pre[:, head_at(heads + group)]
        keys = head_rows(key_pre, gains[1:2, :], cosine[...], sine[...])
        values = pre[:, head_at(heads + groups + group)].astype(low)
        value_grad = jnp.zeros((length, HEAD_WIDTH), wide)
        key_grad = jnp.zeros((length, HEAD_WIDTH), wide)
        for head in range(group * share, (group + 1) * share):
            for block, at in enumerate(range(0, length, QUERY_ROWS)):
                rows = slice(at, at + QUERY_ROWS)
                query_pre = pre[rows, head_at(head)]
                queries = head_rows(query_pre, gains[0:1, :], cosine[rows, :], sine[rows, :])
                probs = probabilities(queries, keys, at, valid[sequence], start[sequence])
                probs_low = probs.astype(low)
                mixed = dot(probs_low, values, 1, 0)
                gate = gate_column(pre[rows, head_at(heads + 2 * groups)], head)
                gated_grad = upstream[rows, head_at(head)]
                mixed_grad = (gated_grad * gate).astype(low)
                logit_grad = (
                    jnp.sum(gated_grad * mixed, axis=-1, keepdims=True) * gate * (1.0 - gate)
                )
                lanes = lax.broadcasted_iota(jnp.int32, (QUERY_ROWS, HEAD_WIDTH), 1)
                logit_grads[block] = logit_grads[block] + jnp.where(lanes == head, logit_grad, 0.0)
                value_grad = value_grad + dot(probs_low, mixed_grad, 0, 0)
                prob_grad = dot(mixed_grad, values, 1, 1)
                score_grad = (
                    probs * (prob_grad - jnp.sum(prob_grad * probs, axis=-1, keepdims=True))
                ).astype(low)
                key_grad = key_grad + dot(score_grad, queries, 0, 0)
                query_grad, gained = head_back(
                    query_pre,
                    gains[0:1, :],
                    cosine[rows, :],
                    sine[rows, :],
                    dot(score_grad, keys, 1, 0) * scale,
                )
                grads[rows, head_at(head)] = query_grad.astype(low)
                gain_grads[0:1, :] += gained
        key_grad, gained = head_back(
            key_pre, gains[1:2, :], cosine[...], sine[...], key_grad * scale
        )
        gain_grads[1:2, :] += gained
        grads[:, head_at(heads + group)] = key_grad.astype(low)
        grads[:, head_at(heads + groups + group)] = value_grad.astype(low)
    for block, at in enumerate(range(0, length, QUERY_ROWS)):
        grads[slice(at, at + QUERY_ROWS), head_at(heads + 2 * groups)] = logit_grads[block].astype(
            low
        )
    for column in range(0, MODEL_WIDTH, 512):
        partial[:, column : column + 512] = dot(
            grads[...], weights[column : column + 512, :projected], 1, 1
        ).astype(low)


def sequence_block(columns, length):
    return pl.BlockSpec((length, columns), lambda sequence: (sequence, 0))


def fixed_block(*shape):
    return pl.BlockSpec(shape, lambda sequence: (0, 0))


SCALARS = pl.BlockSpec(memory_space=pltpu.SMEM)


def attention_call(body, name, specs, sequences, outputs, out_specs, scratch, operands):
    return pl.pallas_call(
        body,
        grid=(sequences,),
        out_shape=outputs,
        in_specs=[SCALARS, SCALARS, *specs],
        out_specs=out_specs,
        scratch_shapes=scratch,
        compiler_params=pltpu.CompilerParams(vmem_limit_bytes=52 * 2**20),
        cost_estimate=pl.CostEstimate(
            flops=2**33, bytes_accessed=24 * 2**20, transcendentals=2**21
        ),
        name=name,
    )(*operands)


def attention_specs(weights, length):
    return [
        pl.BlockSpec(weights.shape, lambda sequence: (0, 0), pipeline_mode=pl.Buffered(1)),
        fixed_block(2, HEAD_WIDTH),
        fixed_block(length, HEAD_WIDTH),
        fixed_block(length, HEAD_WIDTH),
    ]


def attention_forward(groups, share, valid, start, rows, weights, gains, cosine, sine):
    length, columns = cosine.shape[0], groups * share * HEAD_WIDTH
    projected, count = weights.shape[1] - columns, rows.shape[0]

    def body(*refs):
        attention_forward_kernel(groups, share, *refs)

    return attention_call(
        body,
        "attention_forward",
        [sequence_block(MODEL_WIDTH, length), *attention_specs(weights, length)],
        count // length,
        [
            jax.ShapeDtypeStruct((count, projected), wide),
            jax.ShapeDtypeStruct((count, columns), low),
            jax.ShapeDtypeStruct((count, MODEL_WIDTH), low),
        ],
        [sequence_block(size, length) for size in (projected, columns, MODEL_WIDTH)],
        [],
        (valid, start, rows, weights, gains, cosine, sine),
    )


def attention_backward(groups, share, valid, start, pre, rows, weights, gains, cosine, sine):
    length, columns = cosine.shape[0], groups * share * HEAD_WIDTH
    count, projected = pre.shape

    def body(*refs):
        attention_backward_kernel(groups, share, *refs)

    return attention_call(
        body,
        "attention_backward",
        [
            sequence_block(projected, length),
            sequence_block(MODEL_WIDTH, length),
            *attention_specs(weights, length),
        ],
        count // length,
        [
            jax.ShapeDtypeStruct((count, projected), low),
            jax.ShapeDtypeStruct((2, HEAD_WIDTH), wide),
            jax.ShapeDtypeStruct((count, MODEL_WIDTH), low),
        ],
        [
            sequence_block(projected, length),
            fixed_block(2, HEAD_WIDTH),
            sequence_block(MODEL_WIDTH, length),
        ],
        [pltpu.VMEM((length, columns), wide)],
        (valid, start, pre, rows, weights, gains, cosine, sine),
    )


def adam_kernel(layouts, names, heads, *refs):
    sources, refs = dict(zip(names, refs)), refs[len(names) :]
    count = len(layouts)
    stats, inverse, refs = refs[0], refs[1], refs[2:]
    small, refs = refs[:9], refs[9:]
    states, refs = refs[: 3 * count], refs[3 * count :]
    scales, small_targets, refs = refs[0], refs[1:10], refs[10:]
    targets, refs = refs[: 3 * count], refs[3 * count :]
    buffers, semaphores = refs[: 3 * count], refs[3 * count]
    loads = [
        pltpu.make_async_copy(states[i], buffers[i], semaphores.at[0, i]) for i in range(3 * count)
    ]
    stores = [
        pltpu.make_async_copy(buffers[i], targets[i], semaphores.at[1, i])
        for i in range(3 * count)
    ]
    for load in loads:
        load.start()

    def update(part, at, gradient, rate, decay_rate):
        old = (small[3 * part + i][at] for i in range(3))
        for i, value in enumerate(adam_update(*old, gradient, rate, decay_rate)):
            small_targets[3 * part + i][at] = value

    everything = (slice(None), slice(None))
    update(0, everything, stats[0:2, :], 0.5, 0.0)
    for row in range(2):
        update(1, (slice(row, row + 1), slice(None)), stats[2:3, head_at(row)], 0.5, 0.0)
    column, size = heads
    projected = sources["projected"]
    gradient = jnp.concatenate(
        [projected[core, :, column : column + 128][:, :size].astype(wide) for core in range(2)],
        axis=1,
    )
    update(2, everything, gradient, layouts[0][1], weight_decay)
    lanes = lax.broadcasted_iota(jnp.int32, scales.shape, 1)
    squares = stats[2:3, head_at(2)]
    squares = jnp.where(lanes == 2, jnp.sum(stats[3:4, :], axis=-1, keepdims=True), squares)
    scales[...] = jnp.sqrt(squares * inverse[...])
    for number, (transposed, rate, leads) in enumerate(layouts):
        matrix = buffers[3 * number : 3 * number + 3]
        for load in loads[3 * number : 3 * number + 3]:
            load.wait()
        for lead, pieces in enumerate(leads):
            quarter = sum(size for _, _, size in pieces)
            for core in range(2):
                start = core * quarter
                for name, column, size in pieces:
                    step = 256 if size % 256 == 0 else 128

                    @pl.loop(0, size // step)
                    def _(block):
                        columns = pl.ds(pl.multiple_of(column + block * step, 128), step)
                        gradient = sources[name][core, :, columns].astype(wide)
                        place = pl.ds(pl.multiple_of(start + block * step, 128), step)
                        if transposed:
                            gradient = gradient.T
                            at = (place, slice(None))
                        elif len(leads) > 1:
                            at = (lead, slice(None), place)
                        else:
                            at = (slice(None), place)
                        weight, moment, square = (part[at] for part in matrix)
                        for part, value in zip(
                            matrix,
                            adam_update(weight, moment, square, gradient, rate, weight_decay),
                        ):
                            part[at] = value

                    start += size
        for store in stores[3 * number : 3 * number + 3]:
            store.start()
    for store in stores:
        store.wait()


def adam_matrices(layouts, heads, sums, stats, inverse, small, states):
    def body(*refs):
        adam_kernel(layouts, list(sums), heads, *refs)

    def like(values):
        return [jax.ShapeDtypeStruct(value.shape, value.dtype) for value in values]

    return pl.pallas_call(
        body,
        out_shape=like([inverse, *small, *states]),
        in_specs=[VMEM] * (len(sums) + 2 + len(small)) + [ANY] * len(states),
        out_specs=[VMEM] * (1 + len(small)) + [ANY] * len(states),
        scratch_shapes=[pltpu.VMEM(value.shape, value.dtype) for value in states]
        + [pltpu.SemaphoreType.DMA((2, len(states)))],
        compiler_params=pltpu.CompilerParams(vmem_limit_bytes=48 * 2**20),
        cost_estimate=pl.CostEstimate(
            flops=2**25, bytes_accessed=40 * 2**20, transcendentals=2**21
        ),
        name="adam_matrices",
    )(*sums.values(), stats, inverse, *small, *states)


def local(
    tokens,
    cotangent,
    valid_len,
    pic_start,
    norm_gains,
    norm_moment,
    norm_square,
    head_gains,
    head_moment,
    head_square,
    query_weight,
    query_moment,
    query_square,
    keyvalue_matrix,
    keyvalue_first_moment,
    keyvalue_second_moment,
    headgate_weight,
    headgate_moment,
    headgate_square,
    output_weight,
    output_moment,
    output_square,
    gateup_weight,
    gateup_moment,
    gateup_square,
    down_weight,
    down_moment,
    down_square,
):
    local_rows = tokens.shape[0]
    length_value = local_rows * 2
    rows = length_value * 2
    group = lax.axis_index("w")
    core = lax.axis_index("c")
    place = lax.axis_index("t")
    heads_here = query_weight.shape[1] // HEAD_WIDTH // 2
    groups_here = keyvalue_matrix.shape[2] // HEAD_WIDTH // 2
    share = heads_here // groups_here
    head_cols = heads_here * HEAD_WIDTH
    group_cols = groups_here * HEAD_WIDTH
    hidden_here = gateup_weight.shape[2] // 2

    bounds = [0, head_cols, group_cols, group_cols, 128, head_cols]
    edges = [sum(bounds[: i + 1]) for i in range(6)]
    quarters = []
    for index in range(2):
        pieces = []
        for matrix in (
            query_weight, keyvalue_matrix[0], keyvalue_matrix[1], headgate_weight, output_weight.T
        ):
            size = matrix.shape[1] // 2
            piece = matrix[:, index * size : (index + 1) * size].astype(low)
            pieces.append(jnp.pad(piece, ((0, 0), (0, -size % 128))))
        quarters.append(jnp.concatenate(pieces, axis=1))
    matrices = (gateup_weight[0], gateup_weight[1], down_weight.T)
    sizes = (hidden_here - hidden_here // 6, hidden_here // 6)

    def quarter_columns(index, start, size):
        return jnp.concatenate(
            [
                matrix[:, index * hidden_here + start : index * hidden_here + start + size].astype(
                    low
                )
                for matrix in matrices
            ],
            axis=1,
        )

    large_block, small_block = (
        jnp.stack([quarter_columns(index, start, size) for index in range(2)])
        for start, size in zip((0, sizes[0]), sizes)
    )
    residual = tokens.astype(wide)
    mine, other, normed, large_block, small_block = lax.optimization_barrier(
        (
            jnp.where(core == 0, quarters[0], quarters[1]),
            jnp.where(core == 0, quarters[1], quarters[0]),
            normalize(residual, norm_gains[0]).astype(low),
            large_block,
            small_block,
        )
    )
    large_both = lax.all_gather(large_block, ("w", "c"), axis=1, tiled=True)
    small_both = lax.all_gather(small_block, ("w", "c"), axis=1, tiled=True)
    attention_full, first_full, output_grad_full = gather_attention(mine, other, normed, cotangent)
    valid_pair = lax.dynamic_slice_in_dim(valid_len, 2 * group, 2)
    start_pair = lax.dynamic_slice_in_dim(pic_start, 2 * group, 2)
    cosine, sine = rotary_tables(length_value)
    projected, gated_low, attention_partial = attention_forward(
        groups_here,
        share,
        valid_pair,
        start_pair,
        first_full,
        attention_full,
        head_gains,
        cosine,
        sine,
    )
    attention_local, second_full = exchange_forward(attention_partial, tokens, norm_gains[1:2])
    middle = residual + attention_local
    *held, back_partial, down_partial = feedforward(
        core[None], second_full, output_grad_full, large_both, 0, hidden_here
    )
    gate_grad, up_grad, hidden_low, second_partial, feedforward_partial = feedforward(
        core[None],
        second_full,
        output_grad_full,
        small_both,
        sizes[0],
        hidden_here,
        (back_partial, down_partial, *held),
    )
    own_places = place * local_rows + jnp.arange(local_rows, dtype=jnp.int32)
    counted = (own_places < valid_pair[core]).astype(wide)[:, None]
    half = hidden_here // 2
    pieces = [(0, half), (half, hidden_here - half)]
    middle_grad, second_gain_grad, block_output, output_squares, attention_grad, *sums = (
        exchange_backward(
            second_partial,
            feedforward_partial,
            middle,
            cotangent,
            norm_gains[1:2],
            counted,
            [(second_full, grad, *piece) for grad in (gate_grad, up_grad) for piece in pieces],
        )
    )
    projected_grad, head_gain_grads, first_partial = attention_backward(
        groups_here,
        share,
        valid_pair,
        start_pair,
        projected,
        attention_grad,
        attention_full,
        head_gains,
        cosine,
        sine,
    )
    squares = jnp.stack(
        [
            jnp.sum(counted * residual * residual),
            jnp.sum(counted * attention_local * attention_local),
        ]
    )
    small = jnp.concatenate([head_gain_grads.reshape(-1), squares])
    nothing = jnp.zeros((1, MODEL_WIDTH), wide)
    stats = jnp.concatenate(
        [
            nothing,
            second_gain_grad,
            jnp.pad(small, (0, MODEL_WIDTH - small.shape[0]))[None],
            output_squares,
            jnp.tile(nothing, (4, 1)),
        ]
    )
    tokens_grad, stats, *more = exchange_last(
        first_partial,
        tokens,
        norm_gains[0:1],
        middle_grad,
        stats,
        [
            *((output_grad_full, hidden_low, *piece) for piece in pieces),
            (first_full, projected_grad, 0, edges[4]),
            (attention_grad, gated_low, 0, head_cols),
        ],
    )
    denominator = jnp.sum(valid_len).astype(wide) * MODEL_WIDTH
    inverse = jnp.full((1, HEAD_WIDTH), 1.0 / denominator)
    input_rate = MODEL_WIDTH ** (-0.5)
    down_rate = FF ** (-0.5)
    output_rate = max(QUERY_HEADS * HEAD_WIDTH // 128, 4) ** (-0.5)
    widths = [half, hidden_here - half]

    def parts_of(name):
        return [(f"{name} {index}", 0, width) for index, width in enumerate(widths)]

    layouts = [
        (
            False,
            input_rate,
            [parts_of("gate"), parts_of("up")],
        ),
        (True, down_rate, [parts_of("down")]),
        (False, input_rate, [[("projected", edges[0], head_cols)]]),
        (
            False,
            input_rate,
            [[("projected", edges[1], group_cols)], [("projected", edges[2], group_cols)]],
        ),
        (True, output_rate, [[("output", 0, head_cols)]]),
    ]
    names = ["gate 0", "gate 1", "up 0", "up 1", "down 0", "down 1", "projected", "output"]
    sums = dict(zip(names, [*sums, *more]))
    scales, *updated = adam_matrices(
        layouts,
        (edges[3], heads_here),
        sums,
        stats,
        inverse,
        [
            norm_gains,
            norm_moment,
            norm_square,
            head_gains,
            head_moment,
            head_square,
            headgate_weight,
            headgate_moment,
            headgate_square,
        ],
        [
            gateup_weight,
            gateup_moment,
            gateup_square,
            down_weight,
            down_moment,
            down_square,
            query_weight,
            query_moment,
            query_square,
            keyvalue_matrix,
            keyvalue_first_moment,
            keyvalue_second_moment,
            output_weight,
            output_moment,
            output_square,
        ],
    )
    norms_new, heads_new, headgate_new, gateup_new, down_new, query_new, keyvalue_new, output_new = (
        updated[3 * i : 3 * i + 3] for i in range(8)
    )
    branch_scales = scales[0, :3]
    return (
        block_output,
        tokens_grad,
        branch_scales,
        *norms_new,
        *heads_new,
        *query_new,
        *keyvalue_new,
        *headgate_new,
        *output_new,
        *gateup_new,
        *down_new,
    )


def solution(mesh):
    fsdp, tp = mesh.devices.shape
    fine = Mesh(mesh.devices.reshape(fsdp // 2, 2, tp), ("w", "c", "t"))
    whole = ("w", "c")
    rows = P(("w", "c", "t"), None)
    first = P(whole, "t")
    second = P(None, whole, "t")
    last = P("t", whole)
    matrices = (first,) * 3 + (second,) * 3 + (first,) * 3 + (last,) * 3 + (second,) * 3 + (last,) * 3
    return jax.shard_map(
        local,
        mesh=fine,
        in_specs=(rows, rows, P(), P()) + (P(),) * 6 + matrices,
        out_specs=(rows, rows, P()) + (P(),) * 6 + matrices,
        check_vma=False,
    )
```

```python
import jax
import jax.numpy as jnp
from jax import lax
from jax.experimental import pallas as pl
from jax.experimental.pallas import tpu as pltpu
from jax.sharding import Mesh
from jax.sharding import PartitionSpec as P

MODEL_WIDTH = 2048
QUERY_HEADS = 16
HEAD_WIDTH = 128
FF = 6144
PIC = 256
STEP = 10

norm_epsilon = 1e-06
rope_base = 1000000.0
beta_first = 0.9
beta_second = 0.999
adam_epsilon = 1e-08
weight_decay = 0.1
masked_score = -1e30
low = jnp.bfloat16
wide = jnp.float32


def normalize(values, scaling):
    return (
        values
        * lax.rsqrt(jnp.mean(values * values, axis=-1, keepdims=True) + norm_epsilon)
        * scaling
    )


def norm_back(values, scaling, upstream):
    factor = lax.rsqrt(jnp.mean(values * values, axis=-1, keepdims=True) + norm_epsilon)
    weighted = upstream * scaling
    projected = jnp.mean(weighted * values, axis=-1, keepdims=True)
    result = factor * weighted - values * (factor * factor * factor) * projected
    return (result, jnp.sum(upstream * values * factor, axis=tuple(range(values.ndim - 1))))


def rotary_tables(length_value):
    halves = HEAD_WIDTH // 2
    frequency = rope_base ** (-(jnp.arange(halves, dtype=wide) * 2.0 / HEAD_WIDTH))
    angles = jnp.arange(length_value, dtype=wide)[:, None] * frequency[None, :]
    cosine, sine = jnp.cos(angles), jnp.sin(angles)
    return (
        jnp.concatenate([cosine, cosine], axis=1),
        jnp.concatenate([-sine, sine], axis=1),
    )


def adam_update(weight, moment, square, gradient, step_rate, decay_rate):
    moment_new = beta_first * moment + (1.0 - beta_first) * gradient
    square_new = beta_second * square + (1.0 - beta_second) * gradient * gradient
    bias_first = 1.0 - beta_first**STEP
    bias_second = 1.0 - beta_second**STEP
    update = moment_new / bias_first / (jnp.sqrt(square_new / bias_second) + adam_epsilon)
    return (weight - step_rate * (update + decay_rate * weight), moment_new, square_new)


def dot(left, right, left_dim, right_dim):
    return lax.dot_general(
        left, right, (((left_dim,), (right_dim,)), ((), ())), preferred_element_type=wide
    )


def fetch(parts):
    pieces = []
    for core in range(2):
        for part in parts:
            size = part.shape[1] // 2
            pieces.append(part[:, core * size : (core + 1) * size].astype(low))
    count = len(parts)
    local_block = jnp.stack(
        [jnp.concatenate(pieces[core * count : (core + 1) * count], axis=1) for core in range(2)]
    )
    return lax.all_gather(local_block, ("w", "c"), axis=1, tiled=True)


def columns_of(both, start, size):
    return lax.dynamic_slice(
        both, (lax.axis_index("c"), 0, start), (1, both.shape[1], size)
    ).reshape(both.shape[1], size)


MESH = pl.DeviceIdType.MESH
BLOCKS = 4
STRIP = 16
ANY = pl.BlockSpec(memory_space=pl.ANY)
VMEM = pl.BlockSpec(memory_space=pltpu.VMEM)


def ring_place(index, count):
    odd = lax.rem(index, 2)
    pair = lax.div(index, 2)
    return (1 - odd) * pair + odd * (count - 1 - pair)


def ring_index(place, count):
    late = lax.div(place, count // 2)
    return (1 - late) * 2 * place + late * (2 * (count - 1 - place) + 1)


class Device:
    def __init__(self, semaphores):
        self.w, self.c, self.t = (lax.axis_index(axis) for axis in ("w", "c", "t"))
        self.count = lax.axis_size("w")
        self.place = ring_place(self.w, self.count)
        self.semaphores = semaphores
        self.used = 0
        self.other_core = {"c": 1 - self.c}
        self.other_row = {"t": 1 - self.t}

    def owner(self, distance):
        return ring_index(lax.rem(self.place + distance + self.count, self.count), self.count)

    def meet(self, partners):
        barrier = pltpu.get_barrier_semaphore()
        for partner in partners:
            pl.semaphore_signal(barrier, inc=1, device_id=partner, device_id_type=MESH)
        pl.semaphore_wait(barrier, len(partners))

    def remote(self, source, target, device):
        slot = self.used
        self.used += 1
        return pltpu.make_async_remote_copy(
            src_ref=source,
            dst_ref=target,
            send_sem=self.semaphores.at[0, slot],
            recv_sem=self.semaphores.at[1, slot],
            device_id=device,
            device_id_type=MESH,
        )

    def inside(self, source, target):
        slot = self.used
        self.used += 1
        return pltpu.make_async_copy(source, target, self.semaphores.at[0, slot])


def rows_at(start, size):
    return pl.ds(pl.multiple_of(start, STRIP), size)


class Spread:
    def __init__(self, device, full):
        self.device, self.full = device, full
        self.size = full.shape[0] // 4
        self.block = self.size // BLOCKS
        self.rows, self.core, self.passed, self.kept = {}, {}, {}, {}

    def where(self, core, row, index):
        return self.full.at[
            rows_at((core * 2 + row) * self.size + index * self.block, self.block)
        ]

    def put(self, index, source):
        device = self.device
        target = self.where(device.c, device.t, index)
        self.rows[index] = device.remote(source, target, device.other_row)
        self.core[index] = device.remote(source, target, device.other_core)
        self.kept[index] = device.inside(source, target)
        for copy in (self.rows[index], self.core[index], self.kept[index]):
            copy.start()

    def forward(self, index):
        device = self.device
        self.rows[index].wait_recv()
        place = self.where(device.c, 1 - device.t, index)
        self.passed[index] = device.remote(place, place, device.other_core)
        self.passed[index].start()

    def finish(self):
        for index in range(BLOCKS):
            self.rows[index].wait_send()
            self.core[index].wait()
            self.passed[index].wait()
            self.kept[index].wait()


class Collect:
    def __init__(self, device, partial, near, far, sent, came):
        self.device = device
        self.partial, self.near, self.far, self.sent, self.came = partial, near, far, sent, came
        self.size = partial.shape[0] // 4
        self.block = self.size // BLOCKS
        self.core, self.rows = {}, {}

    def start(self):
        device = self.device
        self.load = device.inside(
            self.partial.at[rows_at(device.c * 2 * self.size, 2 * self.size)], self.near
        )
        for part, row in enumerate((1 - device.t, device.t)):
            for index in range(BLOCKS):
                start = row * self.size + index * self.block
                copy = device.remote(
                    self.partial.at[rows_at((1 - device.c) * 2 * self.size + start, self.block)],
                    self.far.at[rows_at(start, self.block)],
                    device.other_core,
                )
                copy.start()
                self.core[part, index] = copy
        self.load.start()

    def pass_on(self, index):
        device = self.device
        if index == 0:
            self.load.wait()
        self.core[0, index].wait_recv()

        @pl.loop(0, self.block // STRIP)
        def _(strip):
            at = index * self.block + strip * STRIP
            rows = rows_at((1 - device.t) * self.size + at, STRIP)
            total = self.near[rows, :].astype(wide) + self.far[rows, :].astype(wide)
            self.sent[rows_at(at, STRIP), :] = total.astype(low)

        place = rows_at(index * self.block, self.block)
        self.rows[index] = device.remote(
            self.sent.at[place], self.came.at[place], device.other_row
        )
        self.rows[index].start()

    def take(self, index, use):
        device = self.device
        self.core[1, index].wait_recv()
        self.rows[index].wait_recv()

        @pl.loop(0, self.block // STRIP)
        def _(strip):
            at = index * self.block + strip * STRIP
            rows = rows_at(device.t * self.size + at, STRIP)
            mine = rows_at(at, STRIP)
            total = (
                self.near[rows, :].astype(wide)
                + self.far[rows, :].astype(wide)
                + self.came[mine, :].astype(wide)
            )
            use(mine, total)

    def finish(self):
        for index in range(BLOCKS):
            self.core[0, index].wait_send()
            self.core[1, index].wait_send()
            self.rows[index].wait_send()


class Given:
    parts = 2

    def __init__(self, grads):
        self.rows, self.columns = grads.shape
        self.grads = grads

    def take(self, starts, size):
        return [self.grads[rows_at(start, size), :].astype(wide) for start in starts]

    def sources(self, starts, size, keep):
        return [self.grads.at[rows_at(start, size)] for start in starts]


class Product:
    parts = 1

    def __init__(self, left, right, start, columns):
        self.rows, self.columns = left.shape[1], columns
        self.left, self.right, self.start = left, right, start

    def take(self, starts, size):
        left = jnp.concatenate(
            [self.left[:, pl.ds(pl.multiple_of(start, 128), size)] for start in starts], axis=1
        )
        both = dot(left, self.right[:, self.start : self.start + self.columns], 0, 0)
        return [both[:size], both[size:]]

    def sources(self, starts, size, keep):
        for way, value in enumerate(self.take(starts, size)):
            keep[way] = value.astype(low)
        return [keep.at[way] for way in range(2)]


class RingSum:
    def __init__(self, device, grads, ready, scratch, sums):
        self.device, self.grads, self.sums = device, grads, sums
        self.ready = ready
        self.slots, self.totals, self.first = scratch
        self.half = grads.rows // device.count // 2
        self.parts = grads.parts
        self.part = self.half // self.parts
        self.copies = {}
        self.ticks = [
            (step, part) for step in range(device.count) for part in range(self.parts)
        ]

    def own(self, way, distance, part):
        owner = self.device.owner(-(1 - 2 * way) * distance)
        return (owner * 2 + way) * self.half + part * self.part

    def slot(self, way, step, part):
        return self.slots.at[
            way * (self.device.count - 1) + step, pl.ds(part * self.part, self.part)
        ]

    def send(self, way, step, part, source):
        device = self.device
        copy = device.remote(
            source, self.slot(way, step, part), {"w": device.owner(1 - 2 * way)}
        )
        copy.start()
        self.copies[way, step, part] = copy

    def tick(self, count=1):
        device = self.device
        for _ in range(count):
            if not self.ticks:
                return
            step, part = self.ticks.pop(0)
            starts = [self.own(way, step + 1, part) for way in range(2)]
            if step == 0:
                self.ready()
                sources = self.grads.sources(starts, self.part, self.first)
                for way in range(2):
                    self.send(way, step, part, sources[way])
                continue
            own = self.grads.take(starts, self.part)
            for way in range(2):
                self.copies[way, step - 1, part].wait_recv()
                slot = self.slot(way, step - 1, part)
                total = (slot[...].astype(wide) + own[way]).astype(low)
                if step < device.count - 1:
                    slot[...] = total
                    self.send(way, step, part, slot)
                else:
                    self.totals[way, pl.ds(part * self.part, self.part), :] = total

    def close(self):
        device = self.device
        self.tick(len(self.ticks))
        self.away = device.remote(
            self.totals.at[1 - device.c], self.sums.at[device.c], device.other_core
        )
        self.kept = device.inside(self.totals.at[device.c], self.sums.at[device.c])
        self.away.start()
        self.kept.start()

    def finish(self):
        for copy in self.copies.values():
            copy.wait_send()
        self.away.wait()
        self.kept.wait()


def ring_shapes(columns, count):
    half = MODEL_WIDTH // count // 2
    return [
        pltpu.VMEM((2 * (count - 1), half, columns), low),
        pltpu.VMEM((2, half, columns), low),
        pltpu.VMEM((2, half, columns), low),
    ]


class RingWork:
    def __init__(self, pairs):
        self.columns = [columns for _, _, _, columns in pairs]
        self.fit = (MODEL_WIDTH // lax.axis_size("w") // 2) % 128 == 0
        self.operands, self.places = [], []
        for left, right, start, columns in pairs:
            if self.fit:
                self.places.append((self.add(left), self.add(right), start, columns))
            else:
                part = right[:, start : start + columns]
                self.places.append((self.add(dot(left, part, 0, 0).astype(low)),))

    def add(self, value):
        for index, other in enumerate(self.operands):
            if other is value:
                return index
        self.operands.append(value)
        return len(self.operands) - 1

    def begin(self, device, operands, scratch, sums):
        count = len(self.operands)
        buffers, scratch = scratch[:count], scratch[count:]
        loads = [device.inside(value, buffer) for value, buffer in zip(operands, buffers)]
        for load in loads:
            load.start()
        waiting = set(range(count))
        rings = []
        for index, place in enumerate(self.places):
            used = place[:2] if self.fit else place[:1]

            def ready(used=used):
                for number in used:
                    if number in waiting:
                        waiting.remove(number)
                        loads[number].wait()

            refs = [buffers[number] for number in used]
            grads = Product(*refs, *place[2:]) if self.fit else Given(*refs)
            rings.append(
                RingSum(device, grads, ready, scratch[3 * index : 3 * index + 3], sums[index])
            )
        return Rings(rings)

    def outputs(self):
        half = MODEL_WIDTH // lax.axis_size("w") // 2
        return [jax.ShapeDtypeStruct((2, half, size), low) for size in self.columns]

    def scratch(self):
        count = lax.axis_size("w")
        return [pltpu.VMEM(value.shape, value.dtype) for value in self.operands] + [
            shape for size in self.columns for shape in ring_shapes(size, count)
        ]

    def semaphores(self):
        return 4 * (lax.axis_size("w") + 1) * len(self.columns) + len(self.operands)


def collect_shapes(size):
    return [
        pltpu.VMEM((2 * size, MODEL_WIDTH), low),
        pltpu.VMEM((2 * size, MODEL_WIDTH), low),
        pltpu.VMEM((size, MODEL_WIDTH), low),
        pltpu.VMEM((size, MODEL_WIDTH), low),
    ]


def semaphores_for(count):
    return pltpu.SemaphoreType.DMA((2, count))


def settings(collective):
    return pltpu.CompilerParams(
        collective_id=collective, has_side_effects=True, vmem_limit_bytes=56 * 2**20
    )


def neighbours(device):
    return [
        device.other_core,
        device.other_row,
        {"w": device.owner(1)},
        {"w": device.owner(-1)},
    ]


class RingGather:
    def __init__(self, device, mine, other, full):
        self.device, self.full = device, full
        self.size = mine.shape[0]
        self.parts = min(4, self.size // STRIP)
        self.part = self.size // self.parts
        here = rows_at((device.w * 2 + device.c) * self.size, self.size)
        self.kept = device.inside(mine, full.at[here])
        self.crossed = device.remote(other, full.at[here], device.other_core)
        self.copies = {}
        self.ticks = [
            (step, part) for step in range(device.count - 1) for part in range(self.parts)
        ]

    def start(self):
        self.kept.start()
        self.crossed.start()

    def ready(self):
        self.kept.wait()
        self.crossed.wait()

    def tick(self, count=1):
        device = self.device
        for _ in range(count):
            if not self.ticks:
                return
            step, part = self.ticks.pop(0)
            for way in range(2):
                if step > 0:
                    self.copies[way, step - 1, part].wait_recv()
                owner = device.owner(-(1 - 2 * way) * step)
                block = self.full.at[
                    rows_at((owner * 2 + way) * self.size + part * self.part, self.part)
                ]
                copy = device.remote(block, block, {"w": device.owner(1 - 2 * way)})
                copy.start()
                self.copies[way, step, part] = copy

    def finish(self):
        self.tick(len(self.ticks))
        for part in range(self.parts):
            for way in range(2):
                self.copies[way, self.device.count - 2, part].wait_recv()
        for copy in self.copies.values():
            copy.wait_send()


def gather_kernel(pieces, first, second, full, first_full, second_full, semaphores):
    device = Device(semaphores)
    device.meet(neighbours(device))
    gather = RingGather(device, pieces.at[0], pieces.at[1], full)
    gather.start()
    spreads = []
    for rows, target in ((first, first_full), (second, second_full)):
        spread = Spread(device, target)
        block = spread.block
        for index in range(BLOCKS):
            spread.put(index, rows.at[pl.ds(index * block, block)])
        spreads.append(spread)
    gather.ready()
    for spread in spreads:
        for index in range(BLOCKS):
            gather.tick(gather.parts)
            spread.forward(index)
    gather.finish()
    for spread in spreads:
        spread.finish()


def gather_attention(pieces, first, second):
    count = lax.axis_size("w")
    rows = first.shape[0] * 4
    return pl.pallas_call(
        gather_kernel,
        out_shape=[
            jax.ShapeDtypeStruct((MODEL_WIDTH, pieces.shape[2]), low),
            jax.ShapeDtypeStruct((rows, MODEL_WIDTH), low),
            jax.ShapeDtypeStruct((rows, MODEL_WIDTH), low),
        ],
        in_specs=[ANY] * 3,
        out_specs=[ANY] * 3,
        scratch_shapes=[semaphores_for(8 * count + 8 * BLOCKS + 2)],
        compiler_params=settings(1),
        cost_estimate=pl.CostEstimate(flops=0, bytes_accessed=64 * 2**20, transcendentals=0),
        name="gather_attention",
    )(pieces, first, second)


def counted_rows(device, valid, at, size):
    place = device.t * size + at.start + lax.broadcasted_iota(jnp.int32, (at.size, 1), 0)
    return jnp.where(place < valid[device.w * 2 + device.c], 1.0, 0.0)


def forward_kernel(
    valid, partial, rows, gain, pieces, middle, squares, full, gathered,
    near, far, sent, came, normed, semaphores,
):
    device = Device(semaphores)
    device.meet(neighbours(device))
    collect = Collect(device, partial, near, far, sent, came)
    spread = Spread(device, full)
    gather = RingGather(device, pieces.at[0], pieces.at[1], gathered)
    collect.start()
    gather.start()
    squares[...] = jnp.zeros_like(squares)
    collect.pass_on(0)
    gather.ready()
    gather.tick(gather.parts)
    for index in range(1, BLOCKS):
        collect.pass_on(index)

    def use(at, value):
        row = rows[at, :].astype(wide)
        counted = counted_rows(device, valid, at, rows.shape[0])
        squares[0:1, :] += jnp.sum(counted * row * row, axis=0, keepdims=True)
        squares[1:2, :] += jnp.sum(counted * value * value, axis=0, keepdims=True)
        total = row + value
        middle[at, :] = total
        normed[at, :] = normalize(total, gain[...]).astype(low)

    for index in range(BLOCKS):
        collect.take(index, use)
        spread.put(index, normed.at[pl.ds(index * spread.block, spread.block)])
        gather.tick(2)
    gather.tick(4)
    for index in range(BLOCKS):
        spread.forward(index)
        gather.tick(2)
    gather.finish()
    spread.finish()
    collect.finish()


SCALARS = pl.BlockSpec(memory_space=pltpu.SMEM)


def exchange_forward(valid, partial, rows, gain, pieces):
    size = rows.shape[0]
    count = lax.axis_size("w")
    return pl.pallas_call(
        forward_kernel,
        out_shape=[
            jax.ShapeDtypeStruct((size, MODEL_WIDTH), wide),
            jax.ShapeDtypeStruct((2, MODEL_WIDTH), wide),
            jax.ShapeDtypeStruct((4 * size, MODEL_WIDTH), low),
            jax.ShapeDtypeStruct((MODEL_WIDTH, pieces.shape[2]), low),
        ],
        in_specs=[SCALARS, ANY, VMEM, VMEM, ANY],
        out_specs=[VMEM, VMEM, ANY, ANY],
        scratch_shapes=collect_shapes(size)
        + [pltpu.VMEM((size, MODEL_WIDTH), low), semaphores_for(16 * BLOCKS + 8 * count + 2)],
        compiler_params=settings(2),
        cost_estimate=pl.CostEstimate(flops=0, bytes_accessed=64 * 2**20, transcendentals=0),
        name="exchange_forward",
    )(valid, partial, rows, gain, pieces)


class Rings:
    def __init__(self, rings):
        self.rings = rings
        self.next = 0

    def tick(self, count=1):
        for _ in range(count):
            ring = self.rings[self.next]
            self.next = (self.next + 1) % len(self.rings)
            ring.tick()

    def finish(self):
        while any(ring.ticks for ring in self.rings):
            self.tick()
        for ring in self.rings:
            ring.close()
        for ring in self.rings:
            ring.finish()


def norm_back_rows(values, gain, upstream):
    factor = lax.rsqrt(jnp.mean(values * values, axis=-1, keepdims=True) + norm_epsilon)
    weighted = upstream * gain
    projected = jnp.mean(weighted * values, axis=-1, keepdims=True)
    result = factor * weighted - values * (factor * factor * factor) * projected
    return result, jnp.sum(upstream * values * factor, axis=0, keepdims=True)


def backward_kernel(work, valid, partial, output, middle, rows, gain, *refs):
    count = len(work.columns)
    operands, refs = refs[: len(work.operands)], refs[len(work.operands) :]
    grad, gain_grad, block, squares, full, refs = *refs[:5], refs[5:]
    sums, refs = refs[:count], refs[count:]
    rounded = refs[8]
    device = Device(refs[-1])
    rings = work.begin(device, operands, refs[9:-1], sums)
    device.meet(neighbours(device))
    collect = Collect(device, partial, *refs[:4])
    output_collect = Collect(device, output, *refs[4:8])
    spread = Spread(device, full)
    collect.start()
    rings.tick(2)
    gain_grad[...] = jnp.zeros_like(gain_grad)
    squares[...] = jnp.zeros_like(squares)
    for index in range(BLOCKS):
        collect.pass_on(index)
    rings.tick(count - 2)
    output_collect.start()

    def use(at, upstream):
        result, gained = norm_back_rows(middle[at, :], gain[...], upstream)
        result = result + rows[at, :].astype(wide)
        grad[at, :] = result
        rounded[at, :] = result.astype(low)
        gain_grad[...] += gained

    def use_output(at, value):
        block[at, :] = (middle[at, :] + value).astype(low)
        counted = counted_rows(device, valid, at, middle.shape[0])
        squares[...] += jnp.sum(counted * value * value, axis=0, keepdims=True)

    for index in range(BLOCKS):
        collect.take(index, use)
        spread.put(index, rounded.at[pl.ds(index * spread.block, spread.block)])
        rings.tick(1)
    for index in range(BLOCKS):
        output_collect.pass_on(index)
    rings.tick(2)
    for index in range(BLOCKS):
        spread.forward(index)
        rings.tick(1)
    for index in range(BLOCKS):
        output_collect.take(index, use_output)
        rings.tick(1)
    rings.finish()
    spread.finish()
    collect.finish()
    output_collect.finish()


def exchange_backward(valid, partial, output, middle, rows, gain, pairs):
    size = rows.shape[0]
    work = RingWork(pairs)

    def body(*refs):
        backward_kernel(work, *refs)

    return pl.pallas_call(
        body,
        out_shape=[
            jax.ShapeDtypeStruct((size, MODEL_WIDTH), wide),
            jax.ShapeDtypeStruct((1, MODEL_WIDTH), wide),
            jax.ShapeDtypeStruct((size, MODEL_WIDTH), low),
            jax.ShapeDtypeStruct((1, MODEL_WIDTH), wide),
            jax.ShapeDtypeStruct((4 * size, MODEL_WIDTH), low),
            *work.outputs(),
        ],
        in_specs=[SCALARS, ANY, ANY] + [VMEM] * 3 + [ANY] * len(work.operands),
        out_specs=[VMEM] * 4 + [ANY] * (1 + len(work.columns)),
        scratch_shapes=collect_shapes(size) * 2
        + [pltpu.VMEM((size, MODEL_WIDTH), low)]
        + work.scratch()
        + [semaphores_for(32 * BLOCKS + work.semaphores())],
        compiler_params=settings(3),
        cost_estimate=pl.CostEstimate(flops=0, bytes_accessed=128 * 2**20, transcendentals=0),
        name="exchange_backward",
    )(valid, partial, output, middle, rows, gain, *work.operands)


class Total:
    def __init__(self, device, mine, crossed, gathered):
        self.device, self.mine = device, mine
        self.crossed, self.gathered = crossed, gathered
        self.copies = {}
        self.steps = [("c", 0), ("t", 0)] + [("w", step) for step in range(device.count // 2)]

    def tick(self):
        device = self.device
        if not self.steps:
            return
        axis, step = self.steps.pop(0)
        if axis != "w":
            slot = 0 if axis == "c" else 1
            partner = device.other_core if axis == "c" else device.other_row
            copy = device.remote(self.mine.at[slot], self.crossed.at[slot], partner)
            copy.start()
            copy.wait()
            total = self.mine[slot] + self.crossed[slot]
            if slot == 0:
                self.mine[1] = total
            else:
                self.gathered[device.w] = total
            return
        for way in range(2):
            if way == 1 and step == device.count // 2 - 1:
                continue
            if step > 0:
                self.copies[way, step - 1].wait_recv()
            block = self.gathered.at[device.owner(-(1 - 2 * way) * step)]
            copy = device.remote(block, block, {"w": device.owner(1 - 2 * way)})
            copy.start()
            self.copies[way, step] = copy

    def finish(self, target):
        while self.steps:
            self.tick()
        half = self.device.count // 2
        self.copies[0, half - 1].wait_recv()
        self.copies[1, half - 2].wait_recv()
        for copy in self.copies.values():
            copy.wait_send()
        target[...] = self.gathered[0]
        for index in range(1, self.device.count):
            target[...] += self.gathered[index]


def last_kernel(
    work, first, tokens, gain, middle_grad, gain_grad, head_grads, output_squares, squares, *refs
):
    count = len(work.columns)
    operands, refs = refs[: len(work.operands)], refs[len(work.operands) :]
    first_total, stats_total, refs = refs[0], refs[1], refs[2:]
    sums, scratch = refs[:count], refs[count:]
    device = Device(scratch[-1])
    rings = work.begin(device, operands, scratch[7:-1], sums)
    device.meet(neighbours(device))
    collect = Collect(device, first, *scratch[:4])
    mine, crossed, gathered = scratch[4:7]
    total = Total(device, mine, crossed, gathered)
    mine[0] = jnp.zeros(mine.shape[1:], wide)
    mine[0, 1:2, :] = gain_grad[...]
    for row in range(2):
        mine[0, 2:3, head_at(row)] = head_grads[row : row + 1, :]
    mine[0, 3:4, :] = output_squares[...]
    mine[0, 4:6, :] = squares[...]
    collect.start()
    rings.tick(2)
    for index in range(BLOCKS):
        collect.pass_on(index)
    rings.tick(count - 2)

    def use(at, upstream):
        result, gained = norm_back_rows(tokens[at, :].astype(wide), gain[...], upstream)
        first_total[at, :] = result + middle_grad[at, :]
        mine[0, 0:1, :] += gained

    for index in range(BLOCKS):
        collect.take(index, use)
        rings.tick(1)
    while total.steps:
        total.tick()
        rings.tick(1)
    rings.finish()
    total.finish(stats_total)
    collect.finish()


def exchange_last(first, tokens, gain, middle_grad, sums, pairs):
    size = tokens.shape[0]
    count = lax.axis_size("w")
    stats = (8, MODEL_WIDTH)
    work = RingWork(pairs)

    def body(*refs):
        last_kernel(work, *refs)

    return pl.pallas_call(
        body,
        out_shape=[
            jax.ShapeDtypeStruct((size, MODEL_WIDTH), wide),
            jax.ShapeDtypeStruct(stats, wide),
            *work.outputs(),
        ],
        in_specs=[ANY] + [VMEM] * (3 + len(sums)) + [ANY] * len(work.operands),
        out_specs=[VMEM] * 2 + [ANY] * len(work.columns),
        scratch_shapes=collect_shapes(size)
        + [
            pltpu.VMEM((2, *stats), wide),
            pltpu.VMEM((2, *stats), wide),
            pltpu.VMEM((count, *stats), wide),
        ]
        + work.scratch()
        + [semaphores_for(16 * BLOCKS + 2 * count + 4 + work.semaphores())],
        compiler_params=settings(4),
        cost_estimate=pl.CostEstimate(flops=0, bytes_accessed=128 * 2**20, transcendentals=0),
        name="exchange_last",
    )(first, tokens, gain, middle_grad, *sums, *work.operands)


FEEDFORWARD_ROWS = 256
FEEDFORWARD_COLUMNS = 512


def feedforward_kernel(
    sizes, core, rows, upstream, large, small, gate_out, up_out, hidden_out, back_out, down_out
):
    weights = [(large.at[0], 0, sizes[0]), (small, sizes[0], sizes[1])]
    for weight, base, size in weights:
        for start in range(0, size, FEEDFORWARD_COLUMNS):
            width = min(FEEDFORWARD_COLUMNS, size - start)
            columns = slice(base + start, base + start + width)
            gate_part = dot(rows[...], weight[:, start : start + width], 1, 0)
            up_part = dot(rows[...], weight[:, size + start : size + start + width], 1, 0)
            hidden_grad = dot(
                upstream[...], weight[:, 2 * size + start : 2 * size + start + width], 1, 0
            )
            sigmoid_gate = jax.nn.sigmoid(gate_part)
            silu_gate = gate_part * sigmoid_gate
            hidden_out[:, columns] = (silu_gate * up_part).astype(low)
            gate_out[:, columns] = (
                hidden_grad * up_part * sigmoid_gate * (1.0 + gate_part * (1.0 - sigmoid_gate))
            ).astype(low)
            up_out[:, columns] = (hidden_grad * silu_gate).astype(low)
    for start in range(0, MODEL_WIDTH, FEEDFORWARD_COLUMNS):
        across = slice(start, start + FEEDFORWARD_COLUMNS)
        back = 0.0
        down = 0.0
        for weight, base, size in weights:
            columns = slice(base, base + size)
            back = back + dot(gate_out[:, columns], weight[across, :size], 1, 1)
            back = back + dot(up_out[:, columns], weight[across, size : 2 * size], 1, 1)
            down = down + dot(hidden_out[:, columns], weight[across, 2 * size :], 1, 1)
        back_out[:, across] = back.astype(low)
        down_out[:, across] = down.astype(low)


def feedforward(core, rows, upstream, large, small):
    sizes = (large.shape[2] // 3, small.shape[1] // 3)
    count = rows.shape[0]
    hidden = sum(sizes)

    def body(*refs):
        feedforward_kernel(sizes, *refs)

    def block(columns):
        return pl.BlockSpec((FEEDFORWARD_ROWS, columns), lambda index, core: (index, 0))

    once = pl.Buffered(1)
    return pl.pallas_call(
        body,
        grid_spec=pltpu.PrefetchScalarGridSpec(
            num_scalar_prefetch=1,
            grid=(count // FEEDFORWARD_ROWS,),
            in_specs=[
                block(MODEL_WIDTH),
                block(MODEL_WIDTH),
                pl.BlockSpec(
                    (1, *large.shape[1:]),
                    lambda index, core: (core[0], 0, 0),
                    pipeline_mode=once,
                ),
                pl.BlockSpec(small.shape, lambda index, core: (0, 0), pipeline_mode=once),
            ],
            out_specs=[block(hidden)] * 3 + [block(MODEL_WIDTH)] * 2,
        ),
        out_shape=[jax.ShapeDtypeStruct((count, hidden), low)] * 3
        + [jax.ShapeDtypeStruct((count, MODEL_WIDTH), low)] * 2,
        compiler_params=pltpu.CompilerParams(vmem_limit_bytes=52 * 2**20),
        cost_estimate=pl.CostEstimate(
            flops=12 * count * MODEL_WIDTH * hidden,
            bytes_accessed=48 * 2**20,
            transcendentals=count * hidden,
        ),
        name="feedforward",
    )(core, rows, upstream, large, small)


def head_rows(values, gain, cosine, sine):
    factor = lax.rsqrt(jnp.mean(values * values, axis=-1, keepdims=True) + norm_epsilon)
    normed = values * factor * gain
    return (normed * cosine + pltpu.roll(normed, HEAD_WIDTH // 2, 1) * sine).astype(low)


def head_back(values, gain, cosine, sine, upstream):
    turned = upstream * cosine - pltpu.roll(upstream, HEAD_WIDTH // 2, 1) * sine
    return norm_back_rows(values, gain, turned)


def head_at(index):
    return slice(index * HEAD_WIDTH, (index + 1) * HEAD_WIDTH)


def gate_column(logits, head):
    lanes = lax.broadcasted_iota(jnp.int32, logits.shape, 1)
    logit = jnp.sum(jnp.where(lanes == head, logits, 0.0), axis=-1, keepdims=True)
    return jax.nn.sigmoid(logit)


def probabilities(queries, keys, start, valid_count, piece_start):
    raw = dot(queries, keys, 1, 1) * HEAD_WIDTH ** (-0.5)
    row = start + lax.broadcasted_iota(jnp.int32, raw.shape, 0)
    column = lax.broadcasted_iota(jnp.int32, raw.shape, 1)
    last = piece_start + PIC
    inside = (row >= piece_start) & (row < last) & (column >= piece_start) & (column < last)
    allowed = (column < valid_count) & ((column <= row) | inside)
    scores = jnp.where(allowed, raw, masked_score)
    expos = jnp.exp(scores - jnp.max(scores, axis=-1, keepdims=True))
    return expos * (1.0 / jnp.sum(expos, axis=-1, keepdims=True))


QUERY_ROWS = 256


def attention_forward_kernel(
    groups, share, valid, start, rows_in, weights, gains, cosine, sine, pre, gated, partial
):
    sequence = pl.program_id(0)
    heads = groups * share
    length, projected = pre.shape
    for column in range(0, projected, 3 * HEAD_WIDTH):
        columns = slice(column, min(column + 3 * HEAD_WIDTH, projected))
        pre[:, columns] = dot(rows_in[...], weights[:, columns], 1, 0)
    for group in range(groups):
        keys = head_rows(pre[:, head_at(heads + group)], gains[1:2, :], cosine[...], sine[...])
        values = pre[:, head_at(heads + groups + group)].astype(low)
        for head in range(group * share, (group + 1) * share):
            for at in range(0, length, QUERY_ROWS):
                rows = slice(at, at + QUERY_ROWS)
                queries = head_rows(
                    pre[rows, head_at(head)], gains[0:1, :], cosine[rows, :], sine[rows, :]
                )
                probs = probabilities(queries, keys, at, valid[sequence], start[sequence])
                mixed = dot(probs.astype(low), values, 1, 0)
                gate = gate_column(pre[rows, head_at(heads + 2 * groups)], head)
                gated[rows, head_at(head)] = (mixed * gate).astype(low)
    for column in range(0, MODEL_WIDTH, 512):
        partial[:, column : column + 512] = dot(
            gated[...], weights[column : column + 512, projected:], 1, 1
        ).astype(low)


def attention_backward_kernel(
    groups, share, valid, start, pre, rows_in, weights, gains, cosine, sine,
    grads, gain_grads, partial, upstream,
):
    sequence = pl.program_id(0)
    heads = groups * share
    length, projected = pre.shape
    upstream[...] = dot(rows_in[...], weights[:, projected:], 1, 0)
    scale = HEAD_WIDTH ** (-0.5)

    @pl.when(sequence == 0)
    def _():
        gain_grads[...] = jnp.zeros_like(gain_grads)

    logit_grads = [jnp.zeros((QUERY_ROWS, HEAD_WIDTH), wide)] * (length // QUERY_ROWS)
    for group in range(groups):
        key_pre = pre[:, head_at(heads + group)]
        keys = head_rows(key_pre, gains[1:2, :], cosine[...], sine[...])
        values = pre[:, head_at(heads + groups + group)].astype(low)
        value_grad = jnp.zeros((length, HEAD_WIDTH), wide)
        key_grad = jnp.zeros((length, HEAD_WIDTH), wide)
        for head in range(group * share, (group + 1) * share):
            for block, at in enumerate(range(0, length, QUERY_ROWS)):
                rows = slice(at, at + QUERY_ROWS)
                query_pre = pre[rows, head_at(head)]
                queries = head_rows(query_pre, gains[0:1, :], cosine[rows, :], sine[rows, :])
                probs = probabilities(queries, keys, at, valid[sequence], start[sequence])
                probs_low = probs.astype(low)
                mixed = dot(probs_low, values, 1, 0)
                gate = gate_column(pre[rows, head_at(heads + 2 * groups)], head)
                gated_grad = upstream[rows, head_at(head)]
                mixed_grad = (gated_grad * gate).astype(low)
                logit_grad = (
                    jnp.sum(gated_grad * mixed, axis=-1, keepdims=True) * gate * (1.0 - gate)
                )
                lanes = lax.broadcasted_iota(jnp.int32, (QUERY_ROWS, HEAD_WIDTH), 1)
                logit_grads[block] = logit_grads[block] + jnp.where(lanes == head, logit_grad, 0.0)
                value_grad = value_grad + dot(probs_low, mixed_grad, 0, 0)
                prob_grad = dot(mixed_grad, values, 1, 1)
                score_grad = (
                    probs * (prob_grad - jnp.sum(prob_grad * probs, axis=-1, keepdims=True))
                ).astype(low)
                key_grad = key_grad + dot(score_grad, queries, 0, 0)
                query_grad, gained = head_back(
                    query_pre,
                    gains[0:1, :],
                    cosine[rows, :],
                    sine[rows, :],
                    dot(score_grad, keys, 1, 0) * scale,
                )
                grads[rows, head_at(head)] = query_grad.astype(low)
                gain_grads[0:1, :] += gained
        key_grad, gained = head_back(
            key_pre, gains[1:2, :], cosine[...], sine[...], key_grad * scale
        )
        gain_grads[1:2, :] += gained
        grads[:, head_at(heads + group)] = key_grad.astype(low)
        grads[:, head_at(heads + groups + group)] = value_grad.astype(low)
    for block, at in enumerate(range(0, length, QUERY_ROWS)):
        grads[slice(at, at + QUERY_ROWS), head_at(heads + 2 * groups)] = logit_grads[block].astype(
            low
        )
    for column in range(0, MODEL_WIDTH, 512):
        partial[:, column : column + 512] = dot(
            grads[...], weights[column : column + 512, :projected], 1, 1
        ).astype(low)


def sequence_block(columns, length):
    return pl.BlockSpec((length, columns), lambda sequence: (sequence, 0))


def fixed_block(*shape):
    return pl.BlockSpec(shape, lambda sequence: (0, 0))


def attention_call(body, name, specs, sequences, outputs, out_specs, scratch, operands):
    return pl.pallas_call(
        body,
        grid=(sequences,),
        out_shape=outputs,
        in_specs=[SCALARS, SCALARS, *specs],
        out_specs=out_specs,
        scratch_shapes=scratch,
        compiler_params=pltpu.CompilerParams(vmem_limit_bytes=52 * 2**20),
        cost_estimate=pl.CostEstimate(
            flops=2**33, bytes_accessed=24 * 2**20, transcendentals=2**21
        ),
        name=name,
    )(*operands)


def attention_specs(weights, length):
    return [
        pl.BlockSpec(weights.shape, lambda sequence: (0, 0), pipeline_mode=pl.Buffered(1)),
        fixed_block(2, HEAD_WIDTH),
        fixed_block(length, HEAD_WIDTH),
        fixed_block(length, HEAD_WIDTH),
    ]


def attention_forward(groups, share, valid, start, rows, weights, gains, cosine, sine):
    length, columns = cosine.shape[0], groups * share * HEAD_WIDTH
    projected, count = weights.shape[1] - columns, rows.shape[0]

    def body(*refs):
        attention_forward_kernel(groups, share, *refs)

    return attention_call(
        body,
        "attention_forward",
        [sequence_block(MODEL_WIDTH, length), *attention_specs(weights, length)],
        count // length,
        [
            jax.ShapeDtypeStruct((count, projected), wide),
            jax.ShapeDtypeStruct((count, columns), low),
            jax.ShapeDtypeStruct((count, MODEL_WIDTH), low),
        ],
        [sequence_block(size, length) for size in (projected, columns, MODEL_WIDTH)],
        [],
        (valid, start, rows, weights, gains, cosine, sine),
    )


def attention_backward(groups, share, valid, start, pre, rows, weights, gains, cosine, sine):
    length, columns = cosine.shape[0], groups * share * HEAD_WIDTH
    count, projected = pre.shape

    def body(*refs):
        attention_backward_kernel(groups, share, *refs)

    return attention_call(
        body,
        "attention_backward",
        [
            sequence_block(projected, length),
            sequence_block(MODEL_WIDTH, length),
            *attention_specs(weights, length),
        ],
        count // length,
        [
            jax.ShapeDtypeStruct((count, projected), low),
            jax.ShapeDtypeStruct((2, HEAD_WIDTH), wide),
            jax.ShapeDtypeStruct((count, MODEL_WIDTH), low),
        ],
        [
            sequence_block(projected, length),
            fixed_block(2, HEAD_WIDTH),
            sequence_block(MODEL_WIDTH, length),
        ],
        [pltpu.VMEM((length, columns), wide)],
        (valid, start, pre, rows, weights, gains, cosine, sine),
    )


def adam_kernel(layouts, names, heads, *refs):
    given, refs = refs[: len(names)], refs[len(names) :]
    count = len(layouts)
    stats, inverse, refs = refs[0], refs[1], refs[2:]
    passed, refs = refs[:2], refs[2:]
    small, refs = refs[:9], refs[9:]
    states, refs = refs[: 3 * count], refs[3 * count :]
    scales, passed_targets, small_targets, refs = refs[0], refs[1:3], refs[3:12], refs[12:]
    targets, refs = refs[: 3 * count], refs[3 * count :]
    buffers, refs = refs[: 3 * count], refs[3 * count :]
    sources, semaphores, sum_semaphores = dict(zip(names, refs)), refs[-2], refs[-1]
    fetches = {
        name: pltpu.make_async_copy(value, sources[name], sum_semaphores.at[i])
        for i, (name, value) in enumerate(zip(names, given))
    }
    moves = [
        pltpu.make_async_copy(value, target, sum_semaphores.at[len(names) + i])
        for i, (value, target) in enumerate(zip(passed, passed_targets))
    ]
    loads = [
        pltpu.make_async_copy(states[i], buffers[i], semaphores.at[0, i]) for i in range(3 * count)
    ]
    stores = [
        pltpu.make_async_copy(buffers[i], targets[i], semaphores.at[1, i])
        for i in range(3 * count)
    ]
    for copy in (*fetches.values(), *moves):
        copy.start()
    for load in loads:
        load.start()
    for copy in fetches.values():
        copy.wait()

    def update(part, at, gradient, rate, decay_rate):
        old = (small[3 * part + i][at] for i in range(3))
        for i, value in enumerate(adam_update(*old, gradient, rate, decay_rate)):
            small_targets[3 * part + i][at] = value

    everything = (slice(None), slice(None))
    update(0, everything, stats[0:2, :], 0.5, 0.0)
    for row in range(2):
        update(1, (slice(row, row + 1), slice(None)), stats[2:3, head_at(row)], 0.5, 0.0)
    column, size = heads
    gradient = jnp.concatenate(
        [
            sources["projected"][core, :, column : column + HEAD_WIDTH].astype(wide).T[:size]
            for core in range(2)
        ],
        axis=0,
    )
    update(2, everything, gradient, layouts[0][1], weight_decay)
    lanes = lax.broadcasted_iota(jnp.int32, scales.shape, 1)
    squares = jnp.zeros(scales.shape, wide)
    for lane, row in enumerate((4, 5, 3)):
        squares = jnp.where(
            lanes == lane, jnp.sum(stats[row : row + 1, :], axis=-1, keepdims=True), squares
        )
    scales[...] = jnp.sqrt(squares * inverse[...])
    for number, (transposed, rate, leads) in enumerate(layouts):
        matrix = buffers[3 * number : 3 * number + 3]
        for load in loads[3 * number : 3 * number + 3]:
            load.wait()
        for lead, pieces in enumerate(leads):
            quarter = sum(size for _, _, size in pieces)
            for core in range(2):
                start = core * quarter
                for name, column, size in pieces:
                    step = 256 if size % 256 == 0 else 128

                    @pl.loop(0, size // step)
                    def _(block):
                        columns = pl.ds(pl.multiple_of(column + block * step, 128), step)
                        gradient = sources[name][core, :, columns].astype(wide)
                        place = pl.ds(pl.multiple_of(start + block * step, 128), step)
                        if transposed:
                            gradient = gradient.T
                            at = (place, slice(None))
                        elif len(leads) > 1:
                            at = (lead, slice(None), place)
                        else:
                            at = (slice(None), place)
                        weight, moment, square = (part[at] for part in matrix)
                        for part, value in zip(
                            matrix,
                            adam_update(weight, moment, square, gradient, rate, weight_decay),
                        ):
                            part[at] = value

                    start += size
        for store in stores[3 * number : 3 * number + 3]:
            store.start()
    for copy in (*stores, *moves):
        copy.wait()


def adam_matrices(layouts, heads, sums, stats, inverse, passed, small, states):
    def body(*refs):
        adam_kernel(layouts, list(sums), heads, *refs)

    def like(values):
        return [jax.ShapeDtypeStruct(value.shape, value.dtype) for value in values]

    return pl.pallas_call(
        body,
        out_shape=like([inverse, *passed, *small, *states]),
        in_specs=[ANY] * len(sums)
        + [VMEM] * 2
        + [ANY] * len(passed)
        + [VMEM] * len(small)
        + [ANY] * len(states),
        out_specs=[VMEM] + [ANY] * len(passed) + [VMEM] * len(small) + [ANY] * len(states),
        scratch_shapes=[
            pltpu.VMEM(value.shape, value.dtype) for value in (*states, *sums.values())
        ]
        + [
            pltpu.SemaphoreType.DMA((2, len(states))),
            pltpu.SemaphoreType.DMA((len(sums) + len(passed),)),
        ],
        compiler_params=pltpu.CompilerParams(vmem_limit_bytes=48 * 2**20),
        cost_estimate=pl.CostEstimate(
            flops=2**25, bytes_accessed=40 * 2**20, transcendentals=2**21
        ),
        name="adam_matrices",
    )(*sums.values(), stats, inverse, *passed, *small, *states)


def prepare_kernel(
    sizes, query, keyvalue, headgate, output, gateup, down, tokens, gain,
    attention, normed, large, small,
):
    core = lax.axis_index("c")
    head_cols, group_cols = query.shape[1] // 2, keyvalue.shape[2] // 2
    edges = [head_cols, head_cols + group_cols, head_cols + 2 * group_cols]
    heads = head_cols // HEAD_WIDTH
    rows = query.shape[0]
    hidden = sum(sizes)
    logits = jnp.concatenate(
        [headgate[...], jnp.zeros((HEAD_WIDTH - headgate.shape[0], rows), wide)], axis=0
    ).T
    lanes = lax.broadcasted_iota(jnp.int32, logits.shape, 1)
    for quarter in range(2):
        slot = lax.rem(quarter + core, 2)
        columns = slice(quarter * head_cols, (quarter + 1) * head_cols)
        attention[slot, :, :head_cols] = query[:, columns].astype(low)
        for part in range(2):
            attention[slot, :, edges[part] : edges[part + 1]] = keyvalue[
                part, :, quarter * group_cols : (quarter + 1) * group_cols
            ].astype(low)
        turned = pltpu.roll(logits, HEAD_WIDTH - heads, 1) if quarter else logits
        attention[slot, :, edges[2] : edges[2] + HEAD_WIDTH] = jnp.where(
            lanes < heads, turned, 0.0
        ).astype(low)
        attention[slot, :, edges[2] + HEAD_WIDTH :] = output[columns, :].T.astype(low)
        base = quarter * hidden
        for part in range(3):
            start = 0
            for target, size in ((large.at[quarter], sizes[0]), (small.at[slot], sizes[1])):
                here = slice(base + start, base + start + size)
                value = gateup[part, :, here] if part < 2 else down[here, :].T
                target[:, part * size : (part + 1) * size] = value.astype(low)
                start += size

    @pl.loop(0, tokens.shape[0] // STRIP)
    def _(strip):
        at = rows_at(strip * STRIP, STRIP)
        normed[at, :] = normalize(tokens[at, :].astype(wide), gain[...]).astype(low)


def prepare(sizes, query, keyvalue, headgate, output, gateup, down, tokens, gain):
    rows = query.shape[0]
    columns = query.shape[1] // 2 * 2 + keyvalue.shape[2] + HEAD_WIDTH

    def body(*refs):
        prepare_kernel(sizes, *refs)

    return pl.pallas_call(
        body,
        out_shape=[
            jax.ShapeDtypeStruct((2, rows, columns), low),
            jax.ShapeDtypeStruct(tokens.shape, low),
            jax.ShapeDtypeStruct((2, rows, 3 * sizes[0]), low),
            jax.ShapeDtypeStruct((2, rows, 3 * sizes[1]), low),
        ],
        in_specs=[VMEM] * 8,
        out_specs=[VMEM] * 4,
        compiler_params=pltpu.CompilerParams(vmem_limit_bytes=48 * 2**20),
        cost_estimate=pl.CostEstimate(
            flops=2**22, bytes_accessed=12 * 2**20, transcendentals=0
        ),
        name="prepare",
    )(query, keyvalue, headgate, output, gateup, down, tokens, gain)


def local(
    tokens,
    cotangent,
    valid_len,
    pic_start,
    norm_gains,
    norm_moment,
    norm_square,
    head_gains,
    head_moment,
    head_square,
    query_weight,
    query_moment,
    query_square,
    keyvalue_matrix,
    keyvalue_first_moment,
    keyvalue_second_moment,
    headgate_weight,
    headgate_moment,
    headgate_square,
    output_weight,
    output_moment,
    output_square,
    gateup_weight,
    gateup_moment,
    gateup_square,
    down_weight,
    down_moment,
    down_square,
):
    local_rows = tokens.shape[0]
    length_value = local_rows * 2
    rows = length_value * 2
    group = lax.axis_index("w")
    core = lax.axis_index("c")
    place = lax.axis_index("t")
    heads_here = query_weight.shape[1] // HEAD_WIDTH // 2
    groups_here = keyvalue_matrix.shape[2] // HEAD_WIDTH // 2
    share = heads_here // groups_here
    head_cols = heads_here * HEAD_WIDTH
    group_cols = groups_here * HEAD_WIDTH
    hidden_here = gateup_weight.shape[2] // 2

    bounds = [0, head_cols, group_cols, group_cols, 128, head_cols]
    edges = [sum(bounds[: i + 1]) for i in range(6)]
    sizes = (hidden_here - hidden_here // 6, hidden_here // 6)
    attention_pieces, normed, large_block, small_pieces = prepare(
        sizes,
        query_weight,
        keyvalue_matrix,
        headgate_weight.T,
        output_weight,
        gateup_weight,
        down_weight,
        tokens,
        norm_gains[0:1],
    )
    large_both = lax.all_gather(large_block, ("w", "c"), axis=1, tiled=True)
    attention_full, first_full, output_grad_full = gather_attention(
        attention_pieces, normed, cotangent
    )
    valid_pair = lax.dynamic_slice_in_dim(valid_len, 2 * group, 2)
    start_pair = lax.dynamic_slice_in_dim(pic_start, 2 * group, 2)
    cosine, sine = rotary_tables(length_value)
    projected, gated_low, attention_partial = attention_forward(
        groups_here,
        share,
        valid_pair,
        start_pair,
        first_full,
        attention_full,
        head_gains,
        cosine,
        sine,
    )
    middle, squares, second_full, small_full = exchange_forward(
        valid_len, attention_partial, tokens, norm_gains[1:2], small_pieces
    )
    gate_grad, up_grad, hidden_low, second_partial, feedforward_partial = feedforward(
        core[None], second_full, output_grad_full, large_both, small_full
    )
    half = hidden_here // 2
    pieces = [(0, half), (half, hidden_here - half)]
    middle_grad, second_gain_grad, block_output, output_squares, attention_grad, *sums = (
        exchange_backward(
            valid_len,
            second_partial,
            feedforward_partial,
            middle,
            cotangent,
            norm_gains[1:2],
            [(second_full, grad, *piece) for grad in (gate_grad, up_grad) for piece in pieces],
        )
    )
    projected_grad, head_gain_grads, first_partial = attention_backward(
        groups_here,
        share,
        valid_pair,
        start_pair,
        projected,
        attention_grad,
        attention_full,
        head_gains,
        cosine,
        sine,
    )
    tokens_grad, stats, *more = exchange_last(
        first_partial,
        tokens,
        norm_gains[0:1],
        middle_grad,
        [second_gain_grad, head_gain_grads, output_squares, squares],
        [
            *((output_grad_full, hidden_low, *piece) for piece in pieces),
            (first_full, projected_grad, 0, edges[4]),
            (attention_grad, gated_low, 0, head_cols),
        ],
    )
    denominator = jnp.sum(valid_len).astype(wide) * MODEL_WIDTH
    inverse = jnp.full((1, HEAD_WIDTH), 1.0 / denominator)
    input_rate = MODEL_WIDTH ** (-0.5)
    down_rate = FF ** (-0.5)
    output_rate = max(QUERY_HEADS * HEAD_WIDTH // 128, 4) ** (-0.5)
    widths = [half, hidden_here - half]

    def parts_of(name):
        return [(f"{name} {index}", 0, width) for index, width in enumerate(widths)]

    layouts = [
        (
            False,
            input_rate,
            [parts_of("gate"), parts_of("up")],
        ),
        (True, down_rate, [parts_of("down")]),
        (False, input_rate, [[("projected", edges[0], head_cols)]]),
        (
            False,
            input_rate,
            [[("projected", edges[1], group_cols)], [("projected", edges[2], group_cols)]],
        ),
        (True, output_rate, [[("output", 0, head_cols)]]),
    ]
    names = ["gate 0", "gate 1", "up 0", "up 1", "down 0", "down 1", "projected", "output"]
    sums = dict(zip(names, [*sums, *more]))
    scales, block_output, tokens_grad, *updated = adam_matrices(
        layouts,
        (edges[3], heads_here),
        sums,
        stats,
        inverse,
        [block_output, tokens_grad],
        [
            norm_gains,
            norm_moment,
            norm_square,
            head_gains,
            head_moment,
            head_square,
            headgate_weight.T,
            headgate_moment.T,
            headgate_square.T,
        ],
        [
            gateup_weight,
            gateup_moment,
            gateup_square,
            down_weight,
            down_moment,
            down_square,
            query_weight,
            query_moment,
            query_square,
            keyvalue_matrix,
            keyvalue_first_moment,
            keyvalue_second_moment,
            output_weight,
            output_moment,
            output_square,
        ],
    )
    norms_new, heads_new, headgate_new, gateup_new, down_new, query_new, keyvalue_new, output_new = (
        updated[3 * i : 3 * i + 3] for i in range(8)
    )
    branch_scales = scales[0, :3]
    return (
        block_output,
        tokens_grad,
        branch_scales,
        *norms_new,
        *heads_new,
        *query_new,
        *keyvalue_new,
        *(value.T for value in headgate_new),
        *output_new,
        *gateup_new,
        *down_new,
    )


def solution(mesh):
    fsdp, tp = mesh.devices.shape
    fine = Mesh(mesh.devices.reshape(fsdp // 2, 2, tp), ("w", "c", "t"))
    whole = ("w", "c")
    rows = P(("w", "c", "t"), None)
    first = P(whole, "t")
    second = P(None, whole, "t")
    last = P("t", whole)
    matrices = (first,) * 3 + (second,) * 3 + (first,) * 3 + (last,) * 3 + (second,) * 3 + (last,) * 3
    return jax.shard_map(
        local,
        mesh=fine,
        in_specs=(rows, rows, P(), P()) + (P(),) * 6 + matrices,
        out_specs=(rows, rows, P()) + (P(),) * 6 + matrices,
        check_vma=False,
    )
```

```python
import jax
import jax.numpy as jnp
from jax import lax
from jax.experimental import pallas as pl
from jax.experimental.pallas import tpu as pltpu
from jax.sharding import Mesh
from jax.sharding import PartitionSpec as P

MODEL_WIDTH = 2048
QUERY_HEADS = 16
HEAD_WIDTH = 128
FF = 6144
PIC = 256
STEP = 10

norm_epsilon = 1e-06
rope_base = 1000000.0
beta_first = 0.9
beta_second = 0.999
adam_epsilon = 1e-08
weight_decay = 0.1
masked_score = -1e30
low = jnp.bfloat16
wide = jnp.float32


def normalize(values, scaling):
    return (
        values
        * lax.rsqrt(jnp.mean(values * values, axis=-1, keepdims=True) + norm_epsilon)
        * scaling
    )


def norm_back(values, scaling, upstream):
    factor = lax.rsqrt(jnp.mean(values * values, axis=-1, keepdims=True) + norm_epsilon)
    weighted = upstream * scaling
    projected = jnp.mean(weighted * values, axis=-1, keepdims=True)
    result = factor * weighted - values * (factor * factor * factor) * projected
    return (result, jnp.sum(upstream * values * factor, axis=tuple(range(values.ndim - 1))))


def rotary_tables(length_value):
    halves = HEAD_WIDTH // 2
    frequency = rope_base ** (-(jnp.arange(halves, dtype=wide) * 2.0 / HEAD_WIDTH))
    angles = jnp.arange(length_value, dtype=wide)[:, None] * frequency[None, :]
    cosine, sine = jnp.cos(angles), jnp.sin(angles)
    return (
        jnp.concatenate([cosine, cosine], axis=1),
        jnp.concatenate([-sine, sine], axis=1),
    )


def adam_update(weight, moment, square, gradient, step_rate, decay_rate):
    moment_new = beta_first * moment + (1.0 - beta_first) * gradient
    square_new = beta_second * square + (1.0 - beta_second) * gradient * gradient
    bias_first = 1.0 - beta_first**STEP
    bias_second = 1.0 - beta_second**STEP
    update = moment_new / bias_first / (jnp.sqrt(square_new / bias_second) + adam_epsilon)
    return (weight - step_rate * (update + decay_rate * weight), moment_new, square_new)


def dot(left, right, left_dim, right_dim):
    return lax.dot_general(
        left, right, (((left_dim,), (right_dim,)), ((), ())), preferred_element_type=wide
    )


def fetch(parts):
    pieces = []
    for core in range(2):
        for part in parts:
            size = part.shape[1] // 2
            pieces.append(part[:, core * size : (core + 1) * size].astype(low))
    count = len(parts)
    local_block = jnp.stack(
        [jnp.concatenate(pieces[core * count : (core + 1) * count], axis=1) for core in range(2)]
    )
    return lax.all_gather(local_block, ("w", "c"), axis=1, tiled=True)


def columns_of(both, start, size):
    return lax.dynamic_slice(
        both, (lax.axis_index("c"), 0, start), (1, both.shape[1], size)
    ).reshape(both.shape[1], size)


MESH = pl.DeviceIdType.MESH
BLOCKS = 4
STRIP = 16
ANY = pl.BlockSpec(memory_space=pl.ANY)
VMEM = pl.BlockSpec(memory_space=pltpu.VMEM)


def ring_place(index, count):
    odd = lax.rem(index, 2)
    pair = lax.div(index, 2)
    return (1 - odd) * pair + odd * (count - 1 - pair)


def ring_index(place, count):
    late = lax.div(place, count // 2)
    return (1 - late) * 2 * place + late * (2 * (count - 1 - place) + 1)


class Device:
    def __init__(self, semaphores):
        self.w, self.c, self.t = (lax.axis_index(axis) for axis in ("w", "c", "t"))
        self.count = lax.axis_size("w")
        self.place = ring_place(self.w, self.count)
        self.semaphores = semaphores
        self.used = 0
        self.other_core = {"c": 1 - self.c}
        self.other_row = {"t": 1 - self.t}

    def owner(self, distance):
        return ring_index(lax.rem(self.place + distance + self.count, self.count), self.count)

    def meet(self, partners):
        barrier = pltpu.get_barrier_semaphore()
        for partner in partners:
            pl.semaphore_signal(barrier, inc=1, device_id=partner, device_id_type=MESH)
        pl.semaphore_wait(barrier, len(partners))

    def remote(self, source, target, device):
        slot = self.used
        self.used += 1
        return pltpu.make_async_remote_copy(
            src_ref=source,
            dst_ref=target,
            send_sem=self.semaphores.at[0, slot],
            recv_sem=self.semaphores.at[1, slot],
            device_id=device,
            device_id_type=MESH,
        )

    def inside(self, source, target):
        slot = self.used
        self.used += 1
        return pltpu.make_async_copy(source, target, self.semaphores.at[0, slot])


def rows_at(start, size):
    return pl.ds(pl.multiple_of(start, STRIP), size)


class Spread:
    def __init__(self, device, full):
        self.device, self.full = device, full
        self.size = full.shape[0] // 4
        self.block = self.size // BLOCKS
        self.rows, self.core, self.passed, self.kept = {}, {}, {}, {}

    def where(self, core, row, index):
        return self.full.at[
            rows_at((core * 2 + row) * self.size + index * self.block, self.block)
        ]

    def put(self, index, source):
        device = self.device
        target = self.where(device.c, device.t, index)
        self.rows[index] = device.remote(source, target, device.other_row)
        self.core[index] = device.remote(source, target, device.other_core)
        self.kept[index] = device.inside(source, target)
        for copy in (self.rows[index], self.core[index], self.kept[index]):
            copy.start()

    def forward(self, index):
        device = self.device
        self.rows[index].wait_recv()
        place = self.where(device.c, 1 - device.t, index)
        self.passed[index] = device.remote(place, place, device.other_core)
        self.passed[index].start()

    def finish(self):
        for index in range(BLOCKS):
            self.rows[index].wait_send()
            self.core[index].wait()
            self.passed[index].wait()
            self.kept[index].wait()


class Collect:
    def __init__(self, device, partial, near, far, sent, came):
        self.device = device
        self.partial, self.near, self.far, self.sent, self.came = partial, near, far, sent, came
        self.size = partial.shape[0] // 4
        self.block = self.size // BLOCKS
        self.core, self.rows = {}, {}

    def start(self):
        device = self.device
        self.load = device.inside(
            self.partial.at[rows_at(device.c * 2 * self.size, 2 * self.size)], self.near
        )
        for part, row in enumerate((1 - device.t, device.t)):
            for index in range(BLOCKS):
                start = row * self.size + index * self.block
                copy = device.remote(
                    self.partial.at[rows_at((1 - device.c) * 2 * self.size + start, self.block)],
                    self.far.at[rows_at(start, self.block)],
                    device.other_core,
                )
                copy.start()
                self.core[part, index] = copy
        self.load.start()

    def pass_on(self, index):
        device = self.device
        if index == 0:
            self.load.wait()
        self.core[0, index].wait_recv()

        @pl.loop(0, self.block // STRIP)
        def _(strip):
            at = index * self.block + strip * STRIP
            rows = rows_at((1 - device.t) * self.size + at, STRIP)
            total = self.near[rows, :].astype(wide) + self.far[rows, :].astype(wide)
            self.sent[rows_at(at, STRIP), :] = total.astype(low)

        place = rows_at(index * self.block, self.block)
        self.rows[index] = device.remote(
            self.sent.at[place], self.came.at[place], device.other_row
        )
        self.rows[index].start()

    def take(self, index, use):
        device = self.device
        self.core[1, index].wait_recv()
        self.rows[index].wait_recv()

        @pl.loop(0, self.block // STRIP)
        def _(strip):
            at = index * self.block + strip * STRIP
            rows = rows_at(device.t * self.size + at, STRIP)
            mine = rows_at(at, STRIP)
            total = (
                self.near[rows, :].astype(wide)
                + self.far[rows, :].astype(wide)
                + self.came[mine, :].astype(wide)
            )
            use(mine, total)

    def finish(self):
        for index in range(BLOCKS):
            self.core[0, index].wait_send()
            self.core[1, index].wait_send()
            self.rows[index].wait_send()


class Given:
    parts = 2

    def __init__(self, grads):
        self.rows, self.columns = grads.shape
        self.grads = grads

    def take(self, starts, size):
        return [self.grads[rows_at(start, size), :].astype(wide) for start in starts]

    def sources(self, starts, size, keep):
        return [self.grads.at[rows_at(start, size)] for start in starts]


class Product:
    parts = 1

    def __init__(self, left, right, start, columns):
        self.rows, self.columns = left.shape[1], columns
        self.left, self.right, self.start = left, right, start

    def take(self, starts, size):
        left = jnp.concatenate(
            [self.left[:, pl.ds(pl.multiple_of(start, 128), size)] for start in starts], axis=1
        )
        both = dot(left, self.right[:, self.start : self.start + self.columns], 0, 0)
        return [both[:size], both[size:]]

    def sources(self, starts, size, keep):
        for way, value in enumerate(self.take(starts, size)):
            keep[way] = value.astype(low)
        return [keep.at[way] for way in range(2)]


class RingSum:
    def __init__(self, device, grads, ready, scratch, sums):
        self.device, self.grads, self.sums = device, grads, sums
        self.ready = ready
        self.slots, self.totals, self.first = scratch
        self.half = grads.rows // device.count // 2
        self.parts = grads.parts
        self.part = self.half // self.parts
        self.copies = {}
        self.ticks = [
            (step, part) for step in range(device.count) for part in range(self.parts)
        ]

    def own(self, way, distance, part):
        owner = self.device.owner(-(1 - 2 * way) * distance)
        return (owner * 2 + way) * self.half + part * self.part

    def slot(self, way, step, part):
        return self.slots.at[
            way * (self.device.count - 1) + step, pl.ds(part * self.part, self.part)
        ]

    def send(self, way, step, part, source):
        device = self.device
        copy = device.remote(
            source, self.slot(way, step, part), {"w": device.owner(1 - 2 * way)}
        )
        copy.start()
        self.copies[way, step, part] = copy

    def tick(self, count=1):
        device = self.device
        for _ in range(count):
            if not self.ticks:
                return
            step, part = self.ticks.pop(0)
            starts = [self.own(way, step + 1, part) for way in range(2)]
            if step == 0:
                self.ready()
                sources = self.grads.sources(starts, self.part, self.first)
                for way in range(2):
                    self.send(way, step, part, sources[way])
                continue
            own = self.grads.take(starts, self.part)
            for way in range(2):
                self.copies[way, step - 1, part].wait_recv()
                slot = self.slot(way, step - 1, part)
                total = (slot[...].astype(wide) + own[way]).astype(low)
                if step < device.count - 1:
                    slot[...] = total
                    self.send(way, step, part, slot)
                else:
                    self.totals[way, pl.ds(part * self.part, self.part), :] = total

    def close(self):
        device = self.device
        self.tick(len(self.ticks))
        self.away = device.remote(
            self.totals.at[1 - device.c], self.sums.at[device.c], device.other_core
        )
        self.kept = device.inside(self.totals.at[device.c], self.sums.at[device.c])
        self.away.start()
        self.kept.start()

    def finish(self):
        for copy in self.copies.values():
            copy.wait_send()
        self.away.wait()
        self.kept.wait()


def ring_shapes(columns, count):
    half = MODEL_WIDTH // count // 2
    return [
        pltpu.VMEM((2 * (count - 1), half, columns), low),
        pltpu.VMEM((2, half, columns), low),
        pltpu.VMEM((2, half, columns), low),
    ]


class RingWork:
    def __init__(self, pairs):
        self.columns = [columns for _, _, _, columns in pairs]
        self.fit = (MODEL_WIDTH // lax.axis_size("w") // 2) % 128 == 0
        self.operands, self.places = [], []
        for left, right, start, columns in pairs:
            if self.fit:
                self.places.append((self.add(left), self.add(right), start, columns))
            else:
                part = right[:, start : start + columns]
                self.places.append((self.add(dot(left, part, 0, 0).astype(low)),))

    def add(self, value):
        for index, other in enumerate(self.operands):
            if other is value:
                return index
        self.operands.append(value)
        return len(self.operands) - 1

    def begin(self, device, operands, scratch, sums):
        count = len(self.operands)
        buffers, scratch = scratch[:count], scratch[count:]
        loads = [device.inside(value, buffer) for value, buffer in zip(operands, buffers)]
        for load in loads:
            load.start()
        waiting = set(range(count))
        rings = []
        for index, place in enumerate(self.places):
            used = place[:2] if self.fit else place[:1]

            def ready(used=used):
                for number in used:
                    if number in waiting:
                        waiting.remove(number)
                        loads[number].wait()

            refs = [buffers[number] for number in used]
            grads = Product(*refs, *place[2:]) if self.fit else Given(*refs)
            rings.append(
                RingSum(device, grads, ready, scratch[3 * index : 3 * index + 3], sums[index])
            )
        return Rings(rings)

    def outputs(self):
        half = MODEL_WIDTH // lax.axis_size("w") // 2
        return [jax.ShapeDtypeStruct((2, half, size), low) for size in self.columns]

    def scratch(self):
        count = lax.axis_size("w")
        return [pltpu.VMEM(value.shape, value.dtype) for value in self.operands] + [
            shape for size in self.columns for shape in ring_shapes(size, count)
        ]

    def semaphores(self):
        return 4 * (lax.axis_size("w") + 1) * len(self.columns) + len(self.operands)


def collect_shapes(size):
    return [
        pltpu.VMEM((2 * size, MODEL_WIDTH), low),
        pltpu.VMEM((2 * size, MODEL_WIDTH), low),
        pltpu.VMEM((size, MODEL_WIDTH), low),
        pltpu.VMEM((size, MODEL_WIDTH), low),
    ]


def semaphores_for(count):
    return pltpu.SemaphoreType.DMA((2, count))


def settings(collective):
    return pltpu.CompilerParams(
        collective_id=collective, has_side_effects=True, vmem_limit_bytes=56 * 2**20
    )


def neighbours(device):
    return [
        device.other_core,
        device.other_row,
        {"w": device.owner(1)},
        {"w": device.owner(-1)},
    ]


class RingGather:
    def __init__(self, device, mine, other, full, target):
        self.device, self.full, self.target = device, full, target
        self.size = mine.shape[0]
        self.parts = min(4, self.size // STRIP)
        self.part = self.size // self.parts
        self.here = (device.w * 2 + device.c) * self.size
        here = rows_at(self.here, self.size)
        self.kept = device.inside(mine, full.at[here])
        self.crossed = device.remote(other, full.at[here], device.other_core)
        self.copies = {}
        self.stores = []
        self.ticks = [
            (step, part) for step in range(device.count - 1) for part in range(self.parts)
        ]

    def start(self):
        self.kept.start()
        self.crossed.start()

    def store(self, start, size):
        place = rows_at(start, size)
        copy = self.device.inside(self.full.at[place], self.target.at[place])
        copy.start()
        self.stores.append(copy)

    def ready(self):
        self.kept.wait()
        self.crossed.wait()
        self.store(self.device.w * 2 * self.size, 2 * self.size)

    def begin(self, way, step, part):
        owner = self.device.owner(-(1 - 2 * way) * step)
        return (owner * 2 + way) * self.size + part * self.part

    def tick(self, count=1):
        device = self.device
        for _ in range(count):
            if not self.ticks:
                return
            step, part = self.ticks.pop(0)
            for way in range(2):
                start = self.begin(way, step, part)
                block = self.full.at[rows_at(start, self.part)]
                if step > 0:
                    self.copies[way, step - 1, part].wait_recv()
                copy = device.remote(block, block, {"w": device.owner(1 - 2 * way)})
                copy.start()
                self.copies[way, step, part] = copy
                if step > 0:
                    self.store(start, self.part)

    def finish(self):
        self.tick(len(self.ticks))
        last = self.device.count - 1
        for part in range(self.parts):
            for way in range(2):
                self.copies[way, last - 1, part].wait_recv()
                self.store(self.begin(way, last, part), self.part)
        for copy in self.copies.values():
            copy.wait_send()
        for copy in self.stores:
            copy.wait()


def gather_kernel(pieces, first, second, target, first_full, second_full, full, semaphores):
    device = Device(semaphores)
    device.meet(neighbours(device))
    gather = RingGather(device, pieces.at[0], pieces.at[1], full, target)
    gather.start()
    spreads = []
    for rows, target in ((first, first_full), (second, second_full)):
        spread = Spread(device, target)
        block = spread.block
        for index in range(BLOCKS):
            spread.put(index, rows.at[pl.ds(index * block, block)])
        spreads.append(spread)
    gather.ready()
    for spread in spreads:
        for index in range(BLOCKS):
            gather.tick(gather.parts)
            spread.forward(index)
    gather.finish()
    for spread in spreads:
        spread.finish()


def gather_attention(pieces, first, second):
    count = lax.axis_size("w")
    rows = first.shape[0] * 4
    return pl.pallas_call(
        gather_kernel,
        out_shape=[
            jax.ShapeDtypeStruct((MODEL_WIDTH, pieces.shape[2]), low),
            jax.ShapeDtypeStruct((rows, MODEL_WIDTH), low),
            jax.ShapeDtypeStruct((rows, MODEL_WIDTH), low),
        ],
        in_specs=[VMEM] * 3,
        out_specs=[ANY] * 3,
        scratch_shapes=[
            pltpu.VMEM((MODEL_WIDTH, pieces.shape[2]), low),
            semaphores_for(16 * count + 8 * BLOCKS + 4),
        ],
        compiler_params=settings(1),
        cost_estimate=pl.CostEstimate(flops=0, bytes_accessed=64 * 2**20, transcendentals=0),
        name="gather_attention",
    )(pieces, first, second)


def counted_rows(device, valid, at, size):
    place = device.t * size + at.start + lax.broadcasted_iota(jnp.int32, (at.size, 1), 0)
    return jnp.where(place < valid[device.w * 2 + device.c], 1.0, 0.0)


def forward_kernel(
    valid, partial, rows, gain, pieces, middle, squares, full, target,
    near, far, sent, came, normed, gathered, semaphores,
):
    device = Device(semaphores)
    device.meet(neighbours(device))
    collect = Collect(device, partial, near, far, sent, came)
    spread = Spread(device, full)
    gather = RingGather(device, pieces.at[0], pieces.at[1], gathered, target)
    collect.start()
    gather.start()
    squares[...] = jnp.zeros_like(squares)
    collect.pass_on(0)
    gather.ready()
    gather.tick(gather.parts)
    for index in range(1, BLOCKS):
        collect.pass_on(index)

    def use(at, value):
        row = rows[at, :].astype(wide)
        counted = counted_rows(device, valid, at, rows.shape[0])
        squares[0:1, :] += jnp.sum(counted * row * row, axis=0, keepdims=True)
        squares[1:2, :] += jnp.sum(counted * value * value, axis=0, keepdims=True)
        total = row + value
        middle[at, :] = total
        normed[at, :] = normalize(total, gain[...]).astype(low)

    for index in range(BLOCKS):
        collect.take(index, use)
        spread.put(index, normed.at[pl.ds(index * spread.block, spread.block)])
        gather.tick(2)
    gather.tick(4)
    for index in range(BLOCKS):
        spread.forward(index)
        gather.tick(2)
    gather.finish()
    spread.finish()
    collect.finish()


SCALARS = pl.BlockSpec(memory_space=pltpu.SMEM)


def exchange_forward(valid, partial, rows, gain, pieces):
    size = rows.shape[0]
    count = lax.axis_size("w")
    return pl.pallas_call(
        forward_kernel,
        out_shape=[
            jax.ShapeDtypeStruct((size, MODEL_WIDTH), wide),
            jax.ShapeDtypeStruct((2, MODEL_WIDTH), wide),
            jax.ShapeDtypeStruct((4 * size, MODEL_WIDTH), low),
            jax.ShapeDtypeStruct((MODEL_WIDTH, pieces.shape[2]), low),
        ],
        in_specs=[SCALARS, ANY, VMEM, VMEM, VMEM],
        out_specs=[VMEM, VMEM, ANY, ANY],
        scratch_shapes=collect_shapes(size)
        + [
            pltpu.VMEM((size, MODEL_WIDTH), low),
            pltpu.VMEM((MODEL_WIDTH, pieces.shape[2]), low),
            semaphores_for(16 * BLOCKS + 16 * count + 4),
        ],
        compiler_params=settings(2),
        cost_estimate=pl.CostEstimate(flops=0, bytes_accessed=64 * 2**20, transcendentals=0),
        name="exchange_forward",
    )(valid, partial, rows, gain, pieces)


class Rings:
    def __init__(self, rings):
        self.rings = rings
        self.next = 0

    def tick(self, count=1):
        for _ in range(count):
            ring = self.rings[self.next]
            self.next = (self.next + 1) % len(self.rings)
            ring.tick()

    def finish(self):
        while any(ring.ticks for ring in self.rings):
            self.tick()
        for ring in self.rings:
            ring.close()
        for ring in self.rings:
            ring.finish()


def norm_back_rows(values, gain, upstream):
    factor = lax.rsqrt(jnp.mean(values * values, axis=-1, keepdims=True) + norm_epsilon)
    weighted = upstream * gain
    projected = jnp.mean(weighted * values, axis=-1, keepdims=True)
    result = factor * weighted - values * (factor * factor * factor) * projected
    return result, jnp.sum(upstream * values * factor, axis=0, keepdims=True)


def backward_kernel(work, valid, partial, output, middle, rows, gain, *refs):
    count = len(work.columns)
    operands, refs = refs[: len(work.operands)], refs[len(work.operands) :]
    grad, gain_grad, block, squares, full, refs = *refs[:5], refs[5:]
    sums, refs = refs[:count], refs[count:]
    rounded = refs[8]
    device = Device(refs[-1])
    rings = work.begin(device, operands, refs[9:-1], sums)
    device.meet(neighbours(device))
    collect = Collect(device, partial, *refs[:4])
    output_collect = Collect(device, output, *refs[4:8])
    spread = Spread(device, full)
    collect.start()
    rings.tick(2)
    gain_grad[...] = jnp.zeros_like(gain_grad)
    squares[...] = jnp.zeros_like(squares)
    for index in range(BLOCKS):
        collect.pass_on(index)
    rings.tick(count - 2)
    output_collect.start()

    def use(at, upstream):
        result, gained = norm_back_rows(middle[at, :], gain[...], upstream)
        result = result + rows[at, :].astype(wide)
        grad[at, :] = result
        rounded[at, :] = result.astype(low)
        gain_grad[...] += gained

    def use_output(at, value):
        block[at, :] = (middle[at, :] + value).astype(low)
        counted = counted_rows(device, valid, at, middle.shape[0])
        squares[...] += jnp.sum(counted * value * value, axis=0, keepdims=True)

    for index in range(BLOCKS):
        collect.take(index, use)
        spread.put(index, rounded.at[pl.ds(index * spread.block, spread.block)])
        rings.tick(1)
    for index in range(BLOCKS):
        output_collect.pass_on(index)
    rings.tick(2)
    for index in range(BLOCKS):
        spread.forward(index)
        rings.tick(1)
    for index in range(BLOCKS):
        output_collect.take(index, use_output)
        rings.tick(1)
    rings.finish()
    spread.finish()
    collect.finish()
    output_collect.finish()


def exchange_backward(valid, partial, output, middle, rows, gain, pairs):
    size = rows.shape[0]
    work = RingWork(pairs)

    def body(*refs):
        backward_kernel(work, *refs)

    return pl.pallas_call(
        body,
        out_shape=[
            jax.ShapeDtypeStruct((size, MODEL_WIDTH), wide),
            jax.ShapeDtypeStruct((1, MODEL_WIDTH), wide),
            jax.ShapeDtypeStruct((size, MODEL_WIDTH), low),
            jax.ShapeDtypeStruct((1, MODEL_WIDTH), wide),
            jax.ShapeDtypeStruct((4 * size, MODEL_WIDTH), low),
            *work.outputs(),
        ],
        in_specs=[SCALARS, ANY, ANY] + [VMEM] * 3 + [ANY] * len(work.operands),
        out_specs=[VMEM] * 4 + [ANY] * (1 + len(work.columns)),
        scratch_shapes=collect_shapes(size) * 2
        + [pltpu.VMEM((size, MODEL_WIDTH), low)]
        + work.scratch()
        + [semaphores_for(32 * BLOCKS + work.semaphores())],
        compiler_params=settings(3),
        cost_estimate=pl.CostEstimate(flops=0, bytes_accessed=128 * 2**20, transcendentals=0),
        name="exchange_backward",
    )(valid, partial, output, middle, rows, gain, *work.operands)


class Total:
    def __init__(self, device, mine, crossed, gathered):
        self.device, self.mine = device, mine
        self.crossed, self.gathered = crossed, gathered
        self.copies = {}
        self.steps = [("c", 0), ("t", 0)] + [("w", step) for step in range(device.count // 2)]

    def tick(self):
        device = self.device
        if not self.steps:
            return
        axis, step = self.steps.pop(0)
        if axis != "w":
            slot = 0 if axis == "c" else 1
            partner = device.other_core if axis == "c" else device.other_row
            copy = device.remote(self.mine.at[slot], self.crossed.at[slot], partner)
            copy.start()
            copy.wait()
            total = self.mine[slot] + self.crossed[slot]
            if slot == 0:
                self.mine[1] = total
            else:
                self.gathered[device.w] = total
            return
        for way in range(2):
            if way == 1 and step == device.count // 2 - 1:
                continue
            if step > 0:
                self.copies[way, step - 1].wait_recv()
            block = self.gathered.at[device.owner(-(1 - 2 * way) * step)]
            copy = device.remote(block, block, {"w": device.owner(1 - 2 * way)})
            copy.start()
            self.copies[way, step] = copy

    def finish(self, target):
        while self.steps:
            self.tick()
        half = self.device.count // 2
        self.copies[0, half - 1].wait_recv()
        self.copies[1, half - 2].wait_recv()
        for copy in self.copies.values():
            copy.wait_send()
        target[...] = self.gathered[0]
        for index in range(1, self.device.count):
            target[...] += self.gathered[index]


def last_kernel(
    work, first, tokens, gain, middle_grad, gain_grad, head_grads, output_squares, squares, *refs
):
    count = len(work.columns)
    operands, refs = refs[: len(work.operands)], refs[len(work.operands) :]
    first_total, stats_total, refs = refs[0], refs[1], refs[2:]
    sums, scratch = refs[:count], refs[count:]
    device = Device(scratch[-1])
    rings = work.begin(device, operands, scratch[7:-1], sums)
    device.meet(neighbours(device))
    collect = Collect(device, first, *scratch[:4])
    mine, crossed, gathered = scratch[4:7]
    total = Total(device, mine, crossed, gathered)
    mine[0] = jnp.zeros(mine.shape[1:], wide)
    mine[0, 1:2, :] = gain_grad[...]
    for row in range(2):
        mine[0, 2:3, head_at(row)] = head_grads[row : row + 1, :]
    mine[0, 3:4, :] = output_squares[...]
    mine[0, 4:6, :] = squares[...]
    collect.start()
    rings.tick(2)
    for index in range(BLOCKS):
        collect.pass_on(index)
    rings.tick(count - 2)

    def use(at, upstream):
        result, gained = norm_back_rows(tokens[at, :].astype(wide), gain[...], upstream)
        first_total[at, :] = result + middle_grad[at, :]
        mine[0, 0:1, :] += gained

    for index in range(BLOCKS):
        collect.take(index, use)
        rings.tick(1)
    while total.steps:
        total.tick()
        rings.tick(1)
    rings.finish()
    total.finish(stats_total)
    collect.finish()


def exchange_last(first, tokens, gain, middle_grad, sums, pairs):
    size = tokens.shape[0]
    count = lax.axis_size("w")
    stats = (8, MODEL_WIDTH)
    work = RingWork(pairs)

    def body(*refs):
        last_kernel(work, *refs)

    return pl.pallas_call(
        body,
        out_shape=[
            jax.ShapeDtypeStruct((size, MODEL_WIDTH), wide),
            jax.ShapeDtypeStruct(stats, wide),
            *work.outputs(),
        ],
        in_specs=[ANY] + [VMEM] * (3 + len(sums)) + [ANY] * len(work.operands),
        out_specs=[VMEM] * 2 + [ANY] * len(work.columns),
        scratch_shapes=collect_shapes(size)
        + [
            pltpu.VMEM((2, *stats), wide),
            pltpu.VMEM((2, *stats), wide),
            pltpu.VMEM((count, *stats), wide),
        ]
        + work.scratch()
        + [semaphores_for(16 * BLOCKS + 2 * count + 4 + work.semaphores())],
        compiler_params=settings(4),
        cost_estimate=pl.CostEstimate(flops=0, bytes_accessed=128 * 2**20, transcendentals=0),
        name="exchange_last",
    )(first, tokens, gain, middle_grad, *sums, *work.operands)


FEEDFORWARD_ROWS = 256
FEEDFORWARD_COLUMNS = 512


def feedforward_kernel(
    sizes, core, rows, upstream, large, small, gate_out, up_out, hidden_out, back_out, down_out
):
    weights = [(large.at[0], 0, sizes[0]), (small, sizes[0], sizes[1])]
    for weight, base, size in weights:
        for start in range(0, size, FEEDFORWARD_COLUMNS):
            width = min(FEEDFORWARD_COLUMNS, size - start)
            columns = slice(base + start, base + start + width)
            gate_part = dot(rows[...], weight[:, start : start + width], 1, 0)
            up_part = dot(rows[...], weight[:, size + start : size + start + width], 1, 0)
            hidden_grad = dot(
                upstream[...], weight[:, 2 * size + start : 2 * size + start + width], 1, 0
            )
            sigmoid_gate = jax.nn.sigmoid(gate_part)
            silu_gate = gate_part * sigmoid_gate
            hidden_out[:, columns] = (silu_gate * up_part).astype(low)
            gate_out[:, columns] = (
                hidden_grad * up_part * sigmoid_gate * (1.0 + gate_part * (1.0 - sigmoid_gate))
            ).astype(low)
            up_out[:, columns] = (hidden_grad * silu_gate).astype(low)
    for start in range(0, MODEL_WIDTH, FEEDFORWARD_COLUMNS):
        across = slice(start, start + FEEDFORWARD_COLUMNS)
        back = 0.0
        down = 0.0
        for weight, base, size in weights:
            columns = slice(base, base + size)
            back = back + dot(gate_out[:, columns], weight[across, :size], 1, 1)
            back = back + dot(up_out[:, columns], weight[across, size : 2 * size], 1, 1)
            down = down + dot(hidden_out[:, columns], weight[across, 2 * size :], 1, 1)
        back_out[:, across] = back.astype(low)
        down_out[:, across] = down.astype(low)


def feedforward(core, rows, upstream, large, small):
    sizes = (large.shape[2] // 3, small.shape[1] // 3)
    count = rows.shape[0]
    hidden = sum(sizes)

    def body(*refs):
        feedforward_kernel(sizes, *refs)

    def block(columns):
        return pl.BlockSpec((FEEDFORWARD_ROWS, columns), lambda index, core: (index, 0))

    once = pl.Buffered(1)
    return pl.pallas_call(
        body,
        grid_spec=pltpu.PrefetchScalarGridSpec(
            num_scalar_prefetch=1,
            grid=(count // FEEDFORWARD_ROWS,),
            in_specs=[
                block(MODEL_WIDTH),
                block(MODEL_WIDTH),
                pl.BlockSpec(
                    (1, *large.shape[1:]),
                    lambda index, core: (core[0], 0, 0),
                    pipeline_mode=once,
                ),
                pl.BlockSpec(small.shape, lambda index, core: (0, 0), pipeline_mode=once),
            ],
            out_specs=[block(hidden)] * 3 + [block(MODEL_WIDTH)] * 2,
        ),
        out_shape=[jax.ShapeDtypeStruct((count, hidden), low)] * 3
        + [jax.ShapeDtypeStruct((count, MODEL_WIDTH), low)] * 2,
        compiler_params=pltpu.CompilerParams(vmem_limit_bytes=52 * 2**20),
        cost_estimate=pl.CostEstimate(
            flops=12 * count * MODEL_WIDTH * hidden,
            bytes_accessed=48 * 2**20,
            transcendentals=count * hidden,
        ),
        name="feedforward",
    )(core, rows, upstream, large, small)


def head_rows(values, gain, cosine, sine):
    factor = lax.rsqrt(jnp.mean(values * values, axis=-1, keepdims=True) + norm_epsilon)
    normed = values * factor * gain
    return (normed * cosine + pltpu.roll(normed, HEAD_WIDTH // 2, 1) * sine).astype(low)


def head_back(values, gain, cosine, sine, upstream):
    turned = upstream * cosine - pltpu.roll(upstream, HEAD_WIDTH // 2, 1) * sine
    return norm_back_rows(values, gain, turned)


def head_at(index):
    return slice(index * HEAD_WIDTH, (index + 1) * HEAD_WIDTH)


def gate_column(logits, head):
    lanes = lax.broadcasted_iota(jnp.int32, logits.shape, 1)
    logit = jnp.sum(jnp.where(lanes == head, logits, 0.0), axis=-1, keepdims=True)
    return jax.nn.sigmoid(logit)


def probabilities(queries, keys, start, valid_count, piece_start):
    raw = dot(queries, keys, 1, 1) * HEAD_WIDTH ** (-0.5)
    row = start + lax.broadcasted_iota(jnp.int32, raw.shape, 0)
    column = lax.broadcasted_iota(jnp.int32, raw.shape, 1)
    last = piece_start + PIC
    inside = (row >= piece_start) & (row < last) & (column >= piece_start) & (column < last)
    allowed = (column < valid_count) & ((column <= row) | inside)
    scores = jnp.where(allowed, raw, masked_score)
    expos = jnp.exp(scores - jnp.max(scores, axis=-1, keepdims=True))
    return expos * (1.0 / jnp.sum(expos, axis=-1, keepdims=True))


QUERY_ROWS = 256


def attention_forward_kernel(
    groups, share, valid, start, rows_in, weights, gains, cosine, sine, pre, gated, partial
):
    sequence = pl.program_id(0)
    heads = groups * share
    length, projected = pre.shape
    for column in range(0, projected, 3 * HEAD_WIDTH):
        columns = slice(column, min(column + 3 * HEAD_WIDTH, projected))
        pre[:, columns] = dot(rows_in[...], weights[:, columns], 1, 0)
    for group in range(groups):
        keys = head_rows(pre[:, head_at(heads + group)], gains[1:2, :], cosine[...], sine[...])
        values = pre[:, head_at(heads + groups + group)].astype(low)
        for head in range(group * share, (group + 1) * share):
            for at in range(0, length, QUERY_ROWS):
                rows = slice(at, at + QUERY_ROWS)
                queries = head_rows(
                    pre[rows, head_at(head)], gains[0:1, :], cosine[rows, :], sine[rows, :]
                )
                probs = probabilities(queries, keys, at, valid[sequence], start[sequence])
                mixed = dot(probs.astype(low), values, 1, 0)
                gate = gate_column(pre[rows, head_at(heads + 2 * groups)], head)
                gated[rows, head_at(head)] = (mixed * gate).astype(low)
    for column in range(0, MODEL_WIDTH, 512):
        partial[:, column : column + 512] = dot(
            gated[...], weights[column : column + 512, projected:], 1, 1
        ).astype(low)


def attention_backward_kernel(
    groups, share, valid, start, pre, rows_in, weights, gains, cosine, sine,
    grads, gain_grads, partial, upstream,
):
    sequence = pl.program_id(0)
    heads = groups * share
    length, projected = pre.shape
    upstream[...] = dot(rows_in[...], weights[:, projected:], 1, 0)
    scale = HEAD_WIDTH ** (-0.5)

    @pl.when(sequence == 0)
    def _():
        gain_grads[...] = jnp.zeros_like(gain_grads)

    logit_grads = [jnp.zeros((QUERY_ROWS, HEAD_WIDTH), wide)] * (length // QUERY_ROWS)
    for group in range(groups):
        key_pre = pre[:, head_at(heads + group)]
        keys = head_rows(key_pre, gains[1:2, :], cosine[...], sine[...])
        values = pre[:, head_at(heads + groups + group)].astype(low)
        value_grad = jnp.zeros((length, HEAD_WIDTH), wide)
        key_grad = jnp.zeros((length, HEAD_WIDTH), wide)
        for head in range(group * share, (group + 1) * share):
            for block, at in enumerate(range(0, length, QUERY_ROWS)):
                rows = slice(at, at + QUERY_ROWS)
                query_pre = pre[rows, head_at(head)]
                queries = head_rows(query_pre, gains[0:1, :], cosine[rows, :], sine[rows, :])
                probs = probabilities(queries, keys, at, valid[sequence], start[sequence])
                probs_low = probs.astype(low)
                mixed = dot(probs_low, values, 1, 0)
                gate = gate_column(pre[rows, head_at(heads + 2 * groups)], head)
                gated_grad = upstream[rows, head_at(head)]
                mixed_grad = (gated_grad * gate).astype(low)
                logit_grad = (
                    jnp.sum(gated_grad * mixed, axis=-1, keepdims=True) * gate * (1.0 - gate)
                )
                lanes = lax.broadcasted_iota(jnp.int32, (QUERY_ROWS, HEAD_WIDTH), 1)
                logit_grads[block] = logit_grads[block] + jnp.where(lanes == head, logit_grad, 0.0)
                value_grad = value_grad + dot(probs_low, mixed_grad, 0, 0)
                prob_grad = dot(mixed_grad, values, 1, 1)
                score_grad = (
                    probs * (prob_grad - jnp.sum(prob_grad * probs, axis=-1, keepdims=True))
                ).astype(low)
                key_grad = key_grad + dot(score_grad, queries, 0, 0)
                query_grad, gained = head_back(
                    query_pre,
                    gains[0:1, :],
                    cosine[rows, :],
                    sine[rows, :],
                    dot(score_grad, keys, 1, 0) * scale,
                )
                grads[rows, head_at(head)] = query_grad.astype(low)
                gain_grads[0:1, :] += gained
        key_grad, gained = head_back(
            key_pre, gains[1:2, :], cosine[...], sine[...], key_grad * scale
        )
        gain_grads[1:2, :] += gained
        grads[:, head_at(heads + group)] = key_grad.astype(low)
        grads[:, head_at(heads + groups + group)] = value_grad.astype(low)
    for block, at in enumerate(range(0, length, QUERY_ROWS)):
        grads[slice(at, at + QUERY_ROWS), head_at(heads + 2 * groups)] = logit_grads[block].astype(
            low
        )
    for column in range(0, MODEL_WIDTH, 512):
        partial[:, column : column + 512] = dot(
            grads[...], weights[column : column + 512, :projected], 1, 1
        ).astype(low)


def sequence_block(columns, length):
    return pl.BlockSpec((length, columns), lambda sequence: (sequence, 0))


def fixed_block(*shape):
    return pl.BlockSpec(shape, lambda sequence: (0, 0))


def attention_call(body, name, specs, sequences, outputs, out_specs, scratch, operands):
    return pl.pallas_call(
        body,
        grid=(sequences,),
        out_shape=outputs,
        in_specs=[SCALARS, SCALARS, *specs],
        out_specs=out_specs,
        scratch_shapes=scratch,
        compiler_params=pltpu.CompilerParams(vmem_limit_bytes=52 * 2**20),
        cost_estimate=pl.CostEstimate(
            flops=2**33, bytes_accessed=24 * 2**20, transcendentals=2**21
        ),
        name=name,
    )(*operands)


def attention_specs(weights, length):
    return [
        pl.BlockSpec(weights.shape, lambda sequence: (0, 0), pipeline_mode=pl.Buffered(1)),
        fixed_block(2, HEAD_WIDTH),
        fixed_block(length, HEAD_WIDTH),
        fixed_block(length, HEAD_WIDTH),
    ]


def attention_forward(groups, share, valid, start, rows, weights, gains, cosine, sine):
    length, columns = cosine.shape[0], groups * share * HEAD_WIDTH
    projected, count = weights.shape[1] - columns, rows.shape[0]

    def body(*refs):
        attention_forward_kernel(groups, share, *refs)

    return attention_call(
        body,
        "attention_forward",
        [sequence_block(MODEL_WIDTH, length), *attention_specs(weights, length)],
        count // length,
        [
            jax.ShapeDtypeStruct((count, projected), wide),
            jax.ShapeDtypeStruct((count, columns), low),
            jax.ShapeDtypeStruct((count, MODEL_WIDTH), low),
        ],
        [sequence_block(size, length) for size in (projected, columns, MODEL_WIDTH)],
        [],
        (valid, start, rows, weights, gains, cosine, sine),
    )


def attention_backward(groups, share, valid, start, pre, rows, weights, gains, cosine, sine):
    length, columns = cosine.shape[0], groups * share * HEAD_WIDTH
    count, projected = pre.shape

    def body(*refs):
        attention_backward_kernel(groups, share, *refs)

    return attention_call(
        body,
        "attention_backward",
        [
            sequence_block(projected, length),
            sequence_block(MODEL_WIDTH, length),
            *attention_specs(weights, length),
        ],
        count // length,
        [
            jax.ShapeDtypeStruct((count, projected), low),
            jax.ShapeDtypeStruct((2, HEAD_WIDTH), wide),
            jax.ShapeDtypeStruct((count, MODEL_WIDTH), low),
        ],
        [
            sequence_block(projected, length),
            fixed_block(2, HEAD_WIDTH),
            sequence_block(MODEL_WIDTH, length),
        ],
        [pltpu.VMEM((length, columns), wide)],
        (valid, start, pre, rows, weights, gains, cosine, sine),
    )


def adam_kernel(layouts, names, heads, *refs):
    given, refs = refs[: len(names)], refs[len(names) :]
    count = len(layouts)
    stats, inverse, refs = refs[0], refs[1], refs[2:]
    extra, states, refs = refs[:11], refs[11 : 11 + 3 * count], refs[11 + 3 * count :]
    scales, refs = refs[0], refs[1:]
    extra_targets, targets, refs = refs[:11], refs[11 : 11 + 3 * count], refs[11 + 3 * count :]
    buffers, extra_buffers, refs = refs[: 3 * count], refs[3 * count :][:11], refs[3 * count + 11 :]
    small = extra_buffers[2:]
    sources, semaphores, sum_semaphores = dict(zip(names, refs)), refs[-2], refs[-1]
    fetches = [
        pltpu.make_async_copy(value, sources[name], sum_semaphores.at[0, i])
        for i, (name, value) in enumerate(zip(names, given))
    ]
    for i in range(11):
        slot = len(names) + i
        fetches.append(
            pltpu.make_async_copy(extra[i], extra_buffers[i], sum_semaphores.at[0, slot])
        )
    moves = [
        pltpu.make_async_copy(extra_buffers[i], extra_targets[i], sum_semaphores.at[1, i])
        for i in range(11)
    ]
    loads = [
        pltpu.make_async_copy(states[i], buffers[i], semaphores.at[0, i]) for i in range(3 * count)
    ]
    stores = [
        pltpu.make_async_copy(buffers[i], targets[i], semaphores.at[1, i])
        for i in range(3 * count)
    ]
    for copy in (*fetches, *loads):
        copy.start()
    for copy in fetches:
        copy.wait()
    for copy in moves[:2]:
        copy.start()

    def update(part, at, gradient, rate, decay_rate):
        old = [small[3 * part + i][at] for i in range(3)]
        for i, value in enumerate(adam_update(*old, gradient, rate, decay_rate)):
            small[3 * part + i][at] = value

    everything = (slice(None), slice(None))
    update(0, everything, stats[0:2, :], 0.5, 0.0)
    for row in range(2):
        update(1, (slice(row, row + 1), slice(None)), stats[2:3, head_at(row)], 0.5, 0.0)
    column, size = heads
    gradient = jnp.concatenate(
        [
            sources["projected"][core, :, column : column + HEAD_WIDTH].astype(wide).T[:size]
            for core in range(2)
        ],
        axis=0,
    )
    update(2, everything, gradient, layouts[0][1], weight_decay)
    for copy in moves[2:]:
        copy.start()
    lanes = lax.broadcasted_iota(jnp.int32, scales.shape, 1)
    squares = jnp.zeros(scales.shape, wide)
    for lane, row in enumerate((4, 5, 3)):
        squares = jnp.where(
            lanes == lane, jnp.sum(stats[row : row + 1, :], axis=-1, keepdims=True), squares
        )
    scales[...] = jnp.sqrt(squares * inverse[...])
    for number, (transposed, rate, leads) in enumerate(layouts):
        matrix = buffers[3 * number : 3 * number + 3]
        for load in loads[3 * number : 3 * number + 3]:
            load.wait()
        for lead, pieces in enumerate(leads):
            quarter = sum(size for _, _, size in pieces)
            for core in range(2):
                start = core * quarter
                for name, column, size in pieces:
                    step = 256 if size % 256 == 0 else 128

                    @pl.loop(0, size // step)
                    def _(block):
                        columns = pl.ds(pl.multiple_of(column + block * step, 128), step)
                        gradient = sources[name][core, :, columns].astype(wide)
                        place = pl.ds(pl.multiple_of(start + block * step, 128), step)
                        if transposed:
                            gradient = gradient.T
                            at = (place, slice(None))
                        elif len(leads) > 1:
                            at = (lead, slice(None), place)
                        else:
                            at = (slice(None), place)
                        weight, moment, square = (part[at] for part in matrix)
                        for part, value in zip(
                            matrix,
                            adam_update(weight, moment, square, gradient, rate, weight_decay),
                        ):
                            part[at] = value

                    start += size
        for store in stores[3 * number : 3 * number + 3]:
            store.start()
    for copy in (*stores, *moves):
        copy.wait()


def adam_matrices(layouts, heads, sums, stats, inverse, passed, small, states):
    def body(*refs):
        adam_kernel(layouts, list(sums), heads, *refs)

    extra = [*passed, *small]

    def like(values):
        return [jax.ShapeDtypeStruct(value.shape, value.dtype) for value in values]

    return pl.pallas_call(
        body,
        out_shape=like([inverse, *extra, *states]),
        in_specs=[ANY] * len(sums) + [VMEM] * 2 + [ANY] * (len(extra) + len(states)),
        out_specs=[VMEM] + [ANY] * (len(extra) + len(states)),
        scratch_shapes=[
            pltpu.VMEM(value.shape, value.dtype) for value in (*states, *extra, *sums.values())
        ]
        + [
            pltpu.SemaphoreType.DMA((2, len(states))),
            pltpu.SemaphoreType.DMA((2, len(sums) + len(extra))),
        ],
        compiler_params=pltpu.CompilerParams(vmem_limit_bytes=48 * 2**20),
        cost_estimate=pl.CostEstimate(
            flops=2**25, bytes_accessed=40 * 2**20, transcendentals=2**21
        ),
        name="adam_matrices",
    )(*sums.values(), stats, inverse, *extra, *states)


def prepare_kernel(
    sizes, query, keyvalue, headgate, output, gateup, down, tokens, gain,
    attention, normed, large, small,
):
    core = lax.axis_index("c")
    head_cols, group_cols = query.shape[1] // 2, keyvalue.shape[2] // 2
    edges = [head_cols, head_cols + group_cols, head_cols + 2 * group_cols]
    heads = head_cols // HEAD_WIDTH
    rows = query.shape[0]
    hidden = sum(sizes)
    logits = jnp.concatenate(
        [headgate[...], jnp.zeros((HEAD_WIDTH - headgate.shape[0], rows), wide)], axis=0
    ).T
    lanes = lax.broadcasted_iota(jnp.int32, logits.shape, 1)
    for quarter in range(2):
        slot = lax.rem(quarter + core, 2)
        columns = slice(quarter * head_cols, (quarter + 1) * head_cols)
        attention[slot, :, :head_cols] = query[:, columns].astype(low)
        for part in range(2):
            attention[slot, :, edges[part] : edges[part + 1]] = keyvalue[
                part, :, quarter * group_cols : (quarter + 1) * group_cols
            ].astype(low)
        turned = pltpu.roll(logits, HEAD_WIDTH - heads, 1) if quarter else logits
        attention[slot, :, edges[2] : edges[2] + HEAD_WIDTH] = jnp.where(
            lanes < heads, turned, 0.0
        ).astype(low)
        attention[slot, :, edges[2] + HEAD_WIDTH :] = output[columns, :].T.astype(low)
        base = quarter * hidden
        for part in range(3):
            start = 0
            for target, size in ((large.at[quarter], sizes[0]), (small.at[slot], sizes[1])):
                here = slice(base + start, base + start + size)
                value = gateup[part, :, here] if part < 2 else down[here, :].T
                target[:, part * size : (part + 1) * size] = value.astype(low)
                start += size

    @pl.loop(0, tokens.shape[0] // STRIP)
    def _(strip):
        at = rows_at(strip * STRIP, STRIP)
        normed[at, :] = normalize(tokens[at, :].astype(wide), gain[...]).astype(low)


def prepare(sizes, query, keyvalue, headgate, output, gateup, down, tokens, gain):
    rows = query.shape[0]
    columns = query.shape[1] // 2 * 2 + keyvalue.shape[2] + HEAD_WIDTH

    def body(*refs):
        prepare_kernel(sizes, *refs)

    return pl.pallas_call(
        body,
        out_shape=[
            jax.ShapeDtypeStruct((2, rows, columns), low),
            jax.ShapeDtypeStruct(tokens.shape, low),
            jax.ShapeDtypeStruct((2, rows, 3 * sizes[0]), low),
            jax.ShapeDtypeStruct((2, rows, 3 * sizes[1]), low),
        ],
        in_specs=[VMEM] * 8,
        out_specs=[VMEM] * 4,
        compiler_params=pltpu.CompilerParams(vmem_limit_bytes=48 * 2**20),
        cost_estimate=pl.CostEstimate(
            flops=2**22, bytes_accessed=12 * 2**20, transcendentals=0
        ),
        name="prepare",
    )(query, keyvalue, headgate, output, gateup, down, tokens, gain)


def local(
    tokens,
    cotangent,
    valid_len,
    pic_start,
    norm_gains,
    norm_moment,
    norm_square,
    head_gains,
    head_moment,
    head_square,
    query_weight,
    query_moment,
    query_square,
    keyvalue_matrix,
    keyvalue_first_moment,
    keyvalue_second_moment,
    headgate_weight,
    headgate_moment,
    headgate_square,
    output_weight,
    output_moment,
    output_square,
    gateup_weight,
    gateup_moment,
    gateup_square,
    down_weight,
    down_moment,
    down_square,
):
    local_rows = tokens.shape[0]
    length_value = local_rows * 2
    rows = length_value * 2
    group = lax.axis_index("w")
    core = lax.axis_index("c")
    place = lax.axis_index("t")
    heads_here = query_weight.shape[1] // HEAD_WIDTH // 2
    groups_here = keyvalue_matrix.shape[2] // HEAD_WIDTH // 2
    share = heads_here // groups_here
    head_cols = heads_here * HEAD_WIDTH
    group_cols = groups_here * HEAD_WIDTH
    hidden_here = gateup_weight.shape[2] // 2

    bounds = [0, head_cols, group_cols, group_cols, 128, head_cols]
    edges = [sum(bounds[: i + 1]) for i in range(6)]
    sizes = (hidden_here - hidden_here // 6, hidden_here // 6)
    attention_pieces, normed, large_block, small_pieces = prepare(
        sizes,
        query_weight,
        keyvalue_matrix,
        headgate_weight.T,
        output_weight,
        gateup_weight,
        down_weight,
        tokens,
        norm_gains[0:1],
    )
    large_both = lax.all_gather(large_block, ("w", "c"), axis=1, tiled=True)
    attention_full, first_full, output_grad_full = gather_attention(
        attention_pieces, normed, cotangent
    )
    valid_pair = lax.dynamic_slice_in_dim(valid_len, 2 * group, 2)
    start_pair = lax.dynamic_slice_in_dim(pic_start, 2 * group, 2)
    cosine, sine = rotary_tables(length_value)
    projected, gated_low, attention_partial = attention_forward(
        groups_here,
        share,
        valid_pair,
        start_pair,
        first_full,
        attention_full,
        head_gains,
        cosine,
        sine,
    )
    middle, squares, second_full, small_full = exchange_forward(
        valid_len, attention_partial, tokens, norm_gains[1:2], small_pieces
    )
    gate_grad, up_grad, hidden_low, second_partial, feedforward_partial = feedforward(
        core[None], second_full, output_grad_full, large_both, small_full
    )
    half = hidden_here // 2
    pieces = [(0, half), (half, hidden_here - half)]
    middle_grad, second_gain_grad, block_output, output_squares, attention_grad, *sums = (
        exchange_backward(
            valid_len,
            second_partial,
            feedforward_partial,
            middle,
            cotangent,
            norm_gains[1:2],
            [(second_full, grad, *piece) for grad in (gate_grad, up_grad) for piece in pieces],
        )
    )
    projected_grad, head_gain_grads, first_partial = attention_backward(
        groups_here,
        share,
        valid_pair,
        start_pair,
        projected,
        attention_grad,
        attention_full,
        head_gains,
        cosine,
        sine,
    )
    tokens_grad, stats, *more = exchange_last(
        first_partial,
        tokens,
        norm_gains[0:1],
        middle_grad,
        [second_gain_grad, head_gain_grads, output_squares, squares],
        [
            *((output_grad_full, hidden_low, *piece) for piece in pieces),
            (first_full, projected_grad, 0, edges[4]),
            (attention_grad, gated_low, 0, head_cols),
        ],
    )
    denominator = jnp.sum(valid_len).astype(wide) * MODEL_WIDTH
    inverse = jnp.full((1, HEAD_WIDTH), 1.0 / denominator)
    input_rate = MODEL_WIDTH ** (-0.5)
    down_rate = FF ** (-0.5)
    output_rate = max(QUERY_HEADS * HEAD_WIDTH // 128, 4) ** (-0.5)
    widths = [half, hidden_here - half]

    def parts_of(name):
        return [(f"{name} {index}", 0, width) for index, width in enumerate(widths)]

    layouts = [
        (
            False,
            input_rate,
            [parts_of("gate"), parts_of("up")],
        ),
        (True, down_rate, [parts_of("down")]),
        (False, input_rate, [[("projected", edges[0], head_cols)]]),
        (
            False,
            input_rate,
            [[("projected", edges[1], group_cols)], [("projected", edges[2], group_cols)]],
        ),
        (True, output_rate, [[("output", 0, head_cols)]]),
    ]
    names = ["gate 0", "gate 1", "up 0", "up 1", "down 0", "down 1", "projected", "output"]
    sums = dict(zip(names, [*sums, *more]))
    scales, block_output, tokens_grad, *updated = adam_matrices(
        layouts,
        (edges[3], heads_here),
        sums,
        stats,
        inverse,
        [block_output, tokens_grad],
        [
            norm_gains,
            norm_moment,
            norm_square,
            head_gains,
            head_moment,
            head_square,
            headgate_weight.T,
            headgate_moment.T,
            headgate_square.T,
        ],
        [
            gateup_weight,
            gateup_moment,
            gateup_square,
            down_weight,
            down_moment,
            down_square,
            query_weight,
            query_moment,
            query_square,
            keyvalue_matrix,
            keyvalue_first_moment,
            keyvalue_second_moment,
            output_weight,
            output_moment,
            output_square,
        ],
    )
    norms_new, heads_new, headgate_new, gateup_new, down_new, query_new, keyvalue_new, output_new = (
        updated[3 * i : 3 * i + 3] for i in range(8)
    )
    branch_scales = scales[0, :3]
    return (
        block_output,
        tokens_grad,
        branch_scales,
        *norms_new,
        *heads_new,
        *query_new,
        *keyvalue_new,
        *(value.T for value in headgate_new),
        *output_new,
        *gateup_new,
        *down_new,
    )


def solution(mesh):
    fsdp, tp = mesh.devices.shape
    fine = Mesh(mesh.devices.reshape(fsdp // 2, 2, tp), ("w", "c", "t"))
    whole = ("w", "c")
    rows = P(("w", "c", "t"), None)
    first = P(whole, "t")
    second = P(None, whole, "t")
    last = P("t", whole)
    matrices = (first,) * 3 + (second,) * 3 + (first,) * 3 + (last,) * 3 + (second,) * 3 + (last,) * 3
    return jax.shard_map(
        local,
        mesh=fine,
        in_specs=(rows, rows, P(), P()) + (P(),) * 6 + matrices,
        out_specs=(rows, rows, P()) + (P(),) * 6 + matrices,
        check_vma=False,
    )
```

```python
import jax
import jax.numpy as jnp
from jax import lax
from jax.experimental import pallas as pl
from jax.experimental.pallas import tpu as pltpu
from jax.sharding import Mesh
from jax.sharding import PartitionSpec as P

MODEL_WIDTH = 2048
QUERY_HEADS = 16
HEAD_WIDTH = 128
FF = 6144
PIC = 256
STEP = 10

norm_epsilon = 1e-06
rope_base = 1000000.0
beta_first = 0.9
beta_second = 0.999
adam_epsilon = 1e-08
weight_decay = 0.1
masked_score = -1e30
low = jnp.bfloat16
wide = jnp.float32


def normalize(values, scaling):
    return (
        values
        * lax.rsqrt(jnp.mean(values * values, axis=-1, keepdims=True) + norm_epsilon)
        * scaling
    )


def norm_back(values, scaling, upstream):
    factor = lax.rsqrt(jnp.mean(values * values, axis=-1, keepdims=True) + norm_epsilon)
    weighted = upstream * scaling
    projected = jnp.mean(weighted * values, axis=-1, keepdims=True)
    result = factor * weighted - values * (factor * factor * factor) * projected
    return (result, jnp.sum(upstream * values * factor, axis=tuple(range(values.ndim - 1))))


def rotary_tables(length_value):
    halves = HEAD_WIDTH // 2
    frequency = rope_base ** (-(jnp.arange(halves, dtype=wide) * 2.0 / HEAD_WIDTH))
    angles = jnp.arange(length_value, dtype=wide)[:, None] * frequency[None, :]
    cosine, sine = jnp.cos(angles), jnp.sin(angles)
    return (
        jnp.concatenate([cosine, cosine], axis=1),
        jnp.concatenate([-sine, sine], axis=1),
    )


def adam_update(weight, moment, square, gradient, step_rate, decay_rate):
    moment_new = beta_first * moment + (1.0 - beta_first) * gradient
    square_new = beta_second * square + (1.0 - beta_second) * gradient * gradient
    bias_first = 1.0 - beta_first**STEP
    bias_second = 1.0 - beta_second**STEP
    update = moment_new / bias_first / (jnp.sqrt(square_new / bias_second) + adam_epsilon)
    return (weight - step_rate * (update + decay_rate * weight), moment_new, square_new)


def dot(left, right, left_dim, right_dim):
    return lax.dot_general(
        left, right, (((left_dim,), (right_dim,)), ((), ())), preferred_element_type=wide
    )


def fetch(parts):
    pieces = []
    for core in range(2):
        for part in parts:
            size = part.shape[1] // 2
            pieces.append(part[:, core * size : (core + 1) * size].astype(low))
    count = len(parts)
    local_block = jnp.stack(
        [jnp.concatenate(pieces[core * count : (core + 1) * count], axis=1) for core in range(2)]
    )
    return lax.all_gather(local_block, ("w", "c"), axis=1, tiled=True)


def columns_of(both, start, size):
    return lax.dynamic_slice(
        both, (lax.axis_index("c"), 0, start), (1, both.shape[1], size)
    ).reshape(both.shape[1], size)


MESH = pl.DeviceIdType.MESH
BLOCKS = 4
STRIP = 16
ANY = pl.BlockSpec(memory_space=pl.ANY)
VMEM = pl.BlockSpec(memory_space=pltpu.VMEM)


def ring_place(index, count):
    odd = lax.rem(index, 2)
    pair = lax.div(index, 2)
    return (1 - odd) * pair + odd * (count - 1 - pair)


def ring_index(place, count):
    late = lax.div(place, count // 2)
    return (1 - late) * 2 * place + late * (2 * (count - 1 - place) + 1)


class Device:
    def __init__(self, semaphores):
        self.w, self.c, self.t = (lax.axis_index(axis) for axis in ("w", "c", "t"))
        self.count = lax.axis_size("w")
        self.place = ring_place(self.w, self.count)
        self.semaphores = semaphores
        self.used = 0
        self.other_core = {"c": 1 - self.c}
        self.other_row = {"t": 1 - self.t}

    def owner(self, distance):
        return ring_index(lax.rem(self.place + distance + self.count, self.count), self.count)

    def meet(self, partners):
        barrier = pltpu.get_barrier_semaphore()
        for partner in partners:
            pl.semaphore_signal(barrier, inc=1, device_id=partner, device_id_type=MESH)
        pl.semaphore_wait(barrier, len(partners))

    def remote(self, source, target, device):
        slot = self.used
        self.used += 1
        return pltpu.make_async_remote_copy(
            src_ref=source,
            dst_ref=target,
            send_sem=self.semaphores.at[0, slot],
            recv_sem=self.semaphores.at[1, slot],
            device_id=device,
            device_id_type=MESH,
        )

    def inside(self, source, target):
        slot = self.used
        self.used += 1
        return pltpu.make_async_copy(source, target, self.semaphores.at[0, slot])


def rows_at(start, size):
    return pl.ds(pl.multiple_of(start, STRIP), size)


class Spread:
    def __init__(self, device, full):
        self.device, self.full = device, full
        self.size = full.shape[0] // 4
        self.block = self.size // BLOCKS
        self.rows, self.core, self.passed, self.kept = {}, {}, {}, {}

    def where(self, core, row, index):
        return self.full.at[
            rows_at((core * 2 + row) * self.size + index * self.block, self.block)
        ]

    def put(self, index, source):
        device = self.device
        target = self.where(device.c, device.t, index)
        self.rows[index] = device.remote(source, target, device.other_row)
        self.core[index] = device.remote(source, target, device.other_core)
        self.kept[index] = device.inside(source, target)
        for copy in (self.rows[index], self.core[index], self.kept[index]):
            copy.start()

    def forward(self, index):
        device = self.device
        self.rows[index].wait_recv()
        place = self.where(device.c, 1 - device.t, index)
        self.passed[index] = device.remote(place, place, device.other_core)
        self.passed[index].start()

    def finish(self):
        for index in range(BLOCKS):
            self.rows[index].wait_send()
            self.core[index].wait()
            self.passed[index].wait()
            self.kept[index].wait()


class Collect:
    def __init__(self, device, partial, near, far, sent, came):
        self.device = device
        self.partial, self.near, self.far, self.sent, self.came = partial, near, far, sent, came
        self.size = partial.shape[0] // 4
        self.block = self.size // BLOCKS
        self.core, self.rows = {}, {}

    def start(self):
        device = self.device
        self.load = device.inside(
            self.partial.at[rows_at(device.c * 2 * self.size, 2 * self.size)], self.near
        )
        for part, row in enumerate((1 - device.t, device.t)):
            for index in range(BLOCKS):
                start = row * self.size + index * self.block
                copy = device.remote(
                    self.partial.at[rows_at((1 - device.c) * 2 * self.size + start, self.block)],
                    self.far.at[rows_at(start, self.block)],
                    device.other_core,
                )
                copy.start()
                self.core[part, index] = copy
        self.load.start()

    def pass_on(self, index):
        device = self.device
        if index == 0:
            self.load.wait()
        self.core[0, index].wait_recv()

        @pl.loop(0, self.block // STRIP)
        def _(strip):
            at = index * self.block + strip * STRIP
            rows = rows_at((1 - device.t) * self.size + at, STRIP)
            total = self.near[rows, :].astype(wide) + self.far[rows, :].astype(wide)
            self.sent[rows_at(at, STRIP), :] = total.astype(low)

        place = rows_at(index * self.block, self.block)
        self.rows[index] = device.remote(
            self.sent.at[place], self.came.at[place], device.other_row
        )
        self.rows[index].start()

    def take(self, index, use):
        device = self.device
        self.core[1, index].wait_recv()
        self.rows[index].wait_recv()

        @pl.loop(0, self.block // STRIP)
        def _(strip):
            at = index * self.block + strip * STRIP
            rows = rows_at(device.t * self.size + at, STRIP)
            mine = rows_at(at, STRIP)
            total = (
                self.near[rows, :].astype(wide)
                + self.far[rows, :].astype(wide)
                + self.came[mine, :].astype(wide)
            )
            use(mine, total)

    def finish(self):
        for index in range(BLOCKS):
            self.core[0, index].wait_send()
            self.core[1, index].wait_send()
            self.rows[index].wait_send()


class Given:
    parts = 2

    def __init__(self, grads):
        self.rows, self.columns = grads.shape
        self.grads = grads

    def take(self, starts, size):
        return [self.grads[rows_at(start, size), :].astype(wide) for start in starts]

    def sources(self, starts, size, keep):
        return [self.grads.at[rows_at(start, size)] for start in starts]


class Product:
    parts = 1

    def __init__(self, left, right, start, columns):
        self.rows, self.columns = left.shape[1], columns
        self.left, self.right, self.start = left, right, start

    def take(self, starts, size):
        left = jnp.concatenate(
            [self.left[:, pl.ds(pl.multiple_of(start, 128), size)] for start in starts], axis=1
        )
        both = dot(left, self.right[:, self.start : self.start + self.columns], 0, 0)
        return [both[:size], both[size:]]

    def sources(self, starts, size, keep):
        for way, value in enumerate(self.take(starts, size)):
            keep[way] = value.astype(low)
        return [keep.at[way] for way in range(2)]


class RingSum:
    def __init__(self, device, grads, ready, scratch, sums):
        self.device, self.grads, self.sums = device, grads, sums
        self.ready = ready
        self.slots, self.totals, self.first = scratch
        self.half = grads.rows // device.count // 2
        self.parts = grads.parts
        self.part = self.half // self.parts
        self.copies = {}
        self.ticks = [
            (step, part) for step in range(device.count) for part in range(self.parts)
        ]

    def own(self, way, distance, part):
        owner = self.device.owner(-(1 - 2 * way) * distance)
        return (owner * 2 + way) * self.half + part * self.part

    def slot(self, way, step, part):
        return self.slots.at[
            way * (self.device.count - 1) + step, pl.ds(part * self.part, self.part)
        ]

    def send(self, way, step, part, source):
        device = self.device
        copy = device.remote(
            source, self.slot(way, step, part), {"w": device.owner(1 - 2 * way)}
        )
        copy.start()
        self.copies[way, step, part] = copy

    def tick(self, count=1):
        device = self.device
        for _ in range(count):
            if not self.ticks:
                return
            step, part = self.ticks.pop(0)
            starts = [self.own(way, step + 1, part) for way in range(2)]
            if step == 0:
                self.ready()
                sources = self.grads.sources(starts, self.part, self.first)
                for way in range(2):
                    self.send(way, step, part, sources[way])
                continue
            own = self.grads.take(starts, self.part)
            for way in range(2):
                self.copies[way, step - 1, part].wait_recv()
                slot = self.slot(way, step - 1, part)
                total = (slot[...].astype(wide) + own[way]).astype(low)
                if step < device.count - 1:
                    slot[...] = total
                    self.send(way, step, part, slot)
                else:
                    self.totals[way, pl.ds(part * self.part, self.part), :] = total

    def close(self):
        device = self.device
        self.tick(len(self.ticks))
        self.away = device.remote(
            self.totals.at[1 - device.c], self.sums.at[device.c], device.other_core
        )
        self.kept = device.inside(self.totals.at[device.c], self.sums.at[device.c])
        self.away.start()
        self.kept.start()

    def finish(self):
        for copy in self.copies.values():
            copy.wait_send()
        self.away.wait()
        self.kept.wait()


def ring_shapes(columns, count):
    half = MODEL_WIDTH // count // 2
    return [
        pltpu.VMEM((2 * (count - 1), half, columns), low),
        pltpu.VMEM((2, half, columns), low),
        pltpu.VMEM((2, half, columns), low),
    ]


class RingWork:
    def __init__(self, pairs):
        self.columns = [columns for _, _, _, columns in pairs]
        self.fit = (MODEL_WIDTH // lax.axis_size("w") // 2) % 128 == 0
        self.operands, self.places = [], []
        for left, right, start, columns in pairs:
            if self.fit:
                self.places.append((self.add(left), self.add(right), start, columns))
            else:
                part = right[:, start : start + columns]
                self.places.append((self.add(dot(left, part, 0, 0).astype(low)),))

    def add(self, value):
        for index, other in enumerate(self.operands):
            if other is value:
                return index
        self.operands.append(value)
        return len(self.operands) - 1

    def begin(self, device, operands, scratch, sums):
        count = len(self.operands)
        buffers, scratch = scratch[:count], scratch[count:]
        loads = [device.inside(value, buffer) for value, buffer in zip(operands, buffers)]
        for load in loads:
            load.start()
        waiting = set(range(count))
        rings = []
        for index, place in enumerate(self.places):
            used = place[:2] if self.fit else place[:1]

            def ready(used=used):
                for number in used:
                    if number in waiting:
                        waiting.remove(number)
                        loads[number].wait()

            refs = [buffers[number] for number in used]
            grads = Product(*refs, *place[2:]) if self.fit else Given(*refs)
            rings.append(
                RingSum(device, grads, ready, scratch[3 * index : 3 * index + 3], sums[index])
            )
        return Rings(rings)

    def outputs(self):
        half = MODEL_WIDTH // lax.axis_size("w") // 2
        return [jax.ShapeDtypeStruct((2, half, size), low) for size in self.columns]

    def scratch(self):
        count = lax.axis_size("w")
        return [pltpu.VMEM(value.shape, value.dtype) for value in self.operands] + [
            shape for size in self.columns for shape in ring_shapes(size, count)
        ]

    def semaphores(self):
        return 4 * (lax.axis_size("w") + 1) * len(self.columns) + len(self.operands)


def collect_shapes(size):
    return [
        pltpu.VMEM((2 * size, MODEL_WIDTH), low),
        pltpu.VMEM((2 * size, MODEL_WIDTH), low),
        pltpu.VMEM((size, MODEL_WIDTH), low),
        pltpu.VMEM((size, MODEL_WIDTH), low),
    ]


def semaphores_for(count):
    return pltpu.SemaphoreType.DMA((2, count))


def settings(collective):
    return pltpu.CompilerParams(
        collective_id=collective, has_side_effects=True, vmem_limit_bytes=60 * 2**20
    )


def neighbours(device):
    return [
        device.other_core,
        device.other_row,
        {"w": device.owner(1)},
        {"w": device.owner(-1)},
    ]


class RingGather:
    def __init__(self, device, mine, other, full, target):
        self.device, self.full, self.target = device, full, target
        self.size = mine.shape[0]
        self.parts = min(4, self.size // STRIP)
        self.part = self.size // self.parts
        self.here = (device.w * 2 + device.c) * self.size
        here = rows_at(self.here, self.size)
        self.kept = device.inside(mine, full.at[here])
        self.crossed = device.remote(other, full.at[here], device.other_core)
        self.copies = {}
        self.stores = []
        self.ticks = [
            (step, part) for step in range(device.count - 1) for part in range(self.parts)
        ]

    def start(self):
        self.kept.start()
        self.crossed.start()

    def store(self, start, size):
        place = rows_at(start, size)
        copy = self.device.inside(self.full.at[place], self.target.at[place])
        copy.start()
        self.stores.append(copy)

    def ready(self):
        self.kept.wait()
        self.crossed.wait()
        self.store(self.device.w * 2 * self.size, 2 * self.size)

    def begin(self, way, step, part):
        owner = self.device.owner(-(1 - 2 * way) * step)
        return (owner * 2 + way) * self.size + part * self.part

    def tick(self, count=1):
        device = self.device
        for _ in range(count):
            if not self.ticks:
                return
            step, part = self.ticks.pop(0)
            for way in range(2):
                start = self.begin(way, step, part)
                block = self.full.at[rows_at(start, self.part)]
                if step > 0:
                    self.copies[way, step - 1, part].wait_recv()
                copy = device.remote(block, block, {"w": device.owner(1 - 2 * way)})
                copy.start()
                self.copies[way, step, part] = copy
                if step > 0:
                    self.store(start, self.part)

    def finish(self):
        self.tick(len(self.ticks))
        last = self.device.count - 1
        for part in range(self.parts):
            for way in range(2):
                self.copies[way, last - 1, part].wait_recv()
                self.store(self.begin(way, last, part), self.part)
        for copy in self.copies.values():
            copy.wait_send()
        for copy in self.stores:
            copy.wait()


def gather_kernel(pieces, first, second, target, first_full, second_full, full, semaphores):
    device = Device(semaphores)
    device.meet(neighbours(device))
    gather = RingGather(device, pieces.at[0], pieces.at[1], full, target)
    gather.start()
    spreads = []
    for rows, target in ((first, first_full), (second, second_full)):
        spread = Spread(device, target)
        block = spread.block
        for index in range(BLOCKS):
            spread.put(index, rows.at[pl.ds(index * block, block)])
        spreads.append(spread)
    gather.ready()
    for spread in spreads:
        for index in range(BLOCKS):
            gather.tick(gather.parts)
            spread.forward(index)
    gather.finish()
    for spread in spreads:
        spread.finish()


def gather_attention(pieces, first, second):
    count = lax.axis_size("w")
    rows = first.shape[0] * 4
    return pl.pallas_call(
        gather_kernel,
        out_shape=[
            jax.ShapeDtypeStruct((MODEL_WIDTH, pieces.shape[2]), low),
            jax.ShapeDtypeStruct((rows, MODEL_WIDTH), low),
            jax.ShapeDtypeStruct((rows, MODEL_WIDTH), low),
        ],
        in_specs=[VMEM] * 3,
        out_specs=[ANY] * 3,
        scratch_shapes=[
            pltpu.VMEM((MODEL_WIDTH, pieces.shape[2]), low),
            semaphores_for(16 * count + 8 * BLOCKS + 4),
        ],
        compiler_params=settings(1),
        cost_estimate=pl.CostEstimate(flops=0, bytes_accessed=64 * 2**20, transcendentals=0),
        name="gather_attention",
    )(pieces, first, second)


def counted_rows(device, valid, at, size):
    place = device.t * size + at.start + lax.broadcasted_iota(jnp.int32, (at.size, 1), 0)
    return jnp.where(place < valid[device.w * 2 + device.c], 1.0, 0.0)


def forward_kernel(
    valid, partial, rows, gain, pieces, middle, squares, full, target,
    near, far, sent, came, normed, gathered, semaphores,
):
    device = Device(semaphores)
    device.meet(neighbours(device))
    collect = Collect(device, partial, near, far, sent, came)
    spread = Spread(device, full)
    gather = RingGather(device, pieces.at[0], pieces.at[1], gathered, target)
    collect.start()
    gather.start()
    squares[...] = jnp.zeros_like(squares)
    collect.pass_on(0)
    gather.ready()
    gather.tick(gather.parts)
    for index in range(1, BLOCKS):
        collect.pass_on(index)

    def use(at, value):
        row = rows[at, :].astype(wide)
        counted = counted_rows(device, valid, at, rows.shape[0])
        squares[0:1, :] += jnp.sum(counted * row * row, axis=0, keepdims=True)
        squares[1:2, :] += jnp.sum(counted * value * value, axis=0, keepdims=True)
        total = row + value
        middle[at, :] = total
        normed[at, :] = normalize(total, gain[...]).astype(low)

    for index in range(BLOCKS):
        collect.take(index, use)
        spread.put(index, normed.at[pl.ds(index * spread.block, spread.block)])
        gather.tick(2)
    gather.tick(4)
    for index in range(BLOCKS):
        spread.forward(index)
        gather.tick(2)
    gather.finish()
    spread.finish()
    collect.finish()


SCALARS = pl.BlockSpec(memory_space=pltpu.SMEM)


def exchange_forward(valid, partial, rows, gain, pieces):
    size = rows.shape[0]
    count = lax.axis_size("w")
    return pl.pallas_call(
        forward_kernel,
        out_shape=[
            jax.ShapeDtypeStruct((size, MODEL_WIDTH), wide),
            jax.ShapeDtypeStruct((2, MODEL_WIDTH), wide),
            jax.ShapeDtypeStruct((4 * size, MODEL_WIDTH), low),
            jax.ShapeDtypeStruct((MODEL_WIDTH, pieces.shape[2]), low),
        ],
        in_specs=[SCALARS, ANY, VMEM, VMEM, VMEM],
        out_specs=[VMEM, VMEM, ANY, ANY],
        scratch_shapes=collect_shapes(size)
        + [
            pltpu.VMEM((size, MODEL_WIDTH), low),
            pltpu.VMEM((MODEL_WIDTH, pieces.shape[2]), low),
            semaphores_for(16 * BLOCKS + 16 * count + 4),
        ],
        compiler_params=settings(2),
        cost_estimate=pl.CostEstimate(flops=0, bytes_accessed=64 * 2**20, transcendentals=0),
        name="exchange_forward",
    )(valid, partial, rows, gain, pieces)


class Rings:
    def __init__(self, rings):
        self.rings = rings
        self.next = 0

    def tick(self, count=1):
        for _ in range(count):
            ring = self.rings[self.next]
            self.next = (self.next + 1) % len(self.rings)
            ring.tick()

    def finish(self):
        while any(ring.ticks for ring in self.rings):
            self.tick()
        for ring in self.rings:
            ring.close()
        for ring in self.rings:
            ring.finish()


def norm_back_rows(values, gain, upstream):
    factor = lax.rsqrt(jnp.mean(values * values, axis=-1, keepdims=True) + norm_epsilon)
    weighted = upstream * gain
    projected = jnp.mean(weighted * values, axis=-1, keepdims=True)
    result = factor * weighted - values * (factor * factor * factor) * projected
    return result, jnp.sum(upstream * values * factor, axis=0, keepdims=True)


def backward_kernel(work, valid, partial, output, middle, rows, gain, *refs):
    count = len(work.columns)
    operands, refs = refs[: len(work.operands)], refs[len(work.operands) :]
    grad, gain_grad, block, squares, full, refs = *refs[:5], refs[5:]
    sums, refs = refs[:count], refs[count:]
    rounded = refs[8]
    device = Device(refs[-1])
    rings = work.begin(device, operands, refs[9:-1], sums)
    device.meet(neighbours(device))
    collect = Collect(device, partial, *refs[:4])
    output_collect = Collect(device, output, *refs[4:8])
    spread = Spread(device, full)
    collect.start()
    rings.tick(2)
    gain_grad[...] = jnp.zeros_like(gain_grad)
    squares[...] = jnp.zeros_like(squares)
    for index in range(BLOCKS):
        collect.pass_on(index)
    rings.tick(count - 2)
    output_collect.start()

    def use(at, upstream):
        result, gained = norm_back_rows(middle[at, :], gain[...], upstream)
        result = result + rows[at, :].astype(wide)
        grad[at, :] = result
        rounded[at, :] = result.astype(low)
        gain_grad[...] += gained

    def use_output(at, value):
        block[at, :] = (middle[at, :] + value).astype(low)
        counted = counted_rows(device, valid, at, middle.shape[0])
        squares[...] += jnp.sum(counted * value * value, axis=0, keepdims=True)

    for index in range(BLOCKS):
        collect.take(index, use)
        spread.put(index, rounded.at[pl.ds(index * spread.block, spread.block)])
        rings.tick(1)
    for index in range(BLOCKS):
        output_collect.pass_on(index)
    rings.tick(2)
    for index in range(BLOCKS):
        spread.forward(index)
        rings.tick(1)
    for index in range(BLOCKS):
        output_collect.take(index, use_output)
        rings.tick(1)
    rings.finish()
    spread.finish()
    collect.finish()
    output_collect.finish()


def exchange_backward(valid, partial, output, middle, rows, gain, pairs):
    size = rows.shape[0]
    work = RingWork(pairs)

    def body(*refs):
        backward_kernel(work, *refs)

    return pl.pallas_call(
        body,
        out_shape=[
            jax.ShapeDtypeStruct((size, MODEL_WIDTH), wide),
            jax.ShapeDtypeStruct((1, MODEL_WIDTH), wide),
            jax.ShapeDtypeStruct((size, MODEL_WIDTH), low),
            jax.ShapeDtypeStruct((1, MODEL_WIDTH), wide),
            jax.ShapeDtypeStruct((4 * size, MODEL_WIDTH), low),
            *work.outputs(),
        ],
        in_specs=[SCALARS, ANY, ANY] + [VMEM] * 3 + [ANY] * len(work.operands),
        out_specs=[VMEM] * 4 + [ANY] * (1 + len(work.columns)),
        scratch_shapes=collect_shapes(size) * 2
        + [pltpu.VMEM((size, MODEL_WIDTH), low)]
        + work.scratch()
        + [semaphores_for(32 * BLOCKS + work.semaphores())],
        compiler_params=settings(3),
        cost_estimate=pl.CostEstimate(flops=0, bytes_accessed=128 * 2**20, transcendentals=0),
        name="exchange_backward",
    )(valid, partial, output, middle, rows, gain, *work.operands)


class Total:
    def __init__(self, device, mine, crossed, gathered):
        self.device, self.mine = device, mine
        self.crossed, self.gathered = crossed, gathered
        self.copies = {}
        self.steps = [("c", 0), ("t", 0)] + [("w", step) for step in range(device.count // 2)]

    def tick(self):
        device = self.device
        if not self.steps:
            return
        axis, step = self.steps.pop(0)
        if axis != "w":
            slot = 0 if axis == "c" else 1
            partner = device.other_core if axis == "c" else device.other_row
            copy = device.remote(self.mine.at[slot], self.crossed.at[slot], partner)
            copy.start()
            copy.wait()
            total = self.mine[slot] + self.crossed[slot]
            if slot == 0:
                self.mine[1] = total
            else:
                self.gathered[device.w] = total
            return
        for way in range(2):
            if way == 1 and step == device.count // 2 - 1:
                continue
            if step > 0:
                self.copies[way, step - 1].wait_recv()
            block = self.gathered.at[device.owner(-(1 - 2 * way) * step)]
            copy = device.remote(block, block, {"w": device.owner(1 - 2 * way)})
            copy.start()
            self.copies[way, step] = copy

    def finish(self, target):
        while self.steps:
            self.tick()
        half = self.device.count // 2
        self.copies[0, half - 1].wait_recv()
        self.copies[1, half - 2].wait_recv()
        for copy in self.copies.values():
            copy.wait_send()
        target[...] = self.gathered[0]
        for index in range(1, self.device.count):
            target[...] += self.gathered[index]


def last_kernel(
    work, first, tokens, gain, middle_grad, gain_grad, head_grads, output_squares, squares, *refs
):
    count = len(work.columns)
    operands, refs = refs[: len(work.operands)], refs[len(work.operands) :]
    first_total, stats_total, refs = refs[0], refs[1], refs[2:]
    sums, scratch = refs[:count], refs[count:]
    device = Device(scratch[-1])
    rings = work.begin(device, operands, scratch[7:-1], sums)
    device.meet(neighbours(device))
    collect = Collect(device, first, *scratch[:4])
    mine, crossed, gathered = scratch[4:7]
    total = Total(device, mine, crossed, gathered)
    mine[0] = jnp.zeros(mine.shape[1:], wide)
    mine[0, 1:2, :] = gain_grad[...]
    for row in range(2):
        mine[0, 2:3, head_at(row)] = head_grads[row : row + 1, :]
    mine[0, 3:4, :] = output_squares[...]
    mine[0, 4:6, :] = squares[...]
    collect.start()
    rings.tick(2)
    for index in range(BLOCKS):
        collect.pass_on(index)
    rings.tick(count - 2)

    def use(at, upstream):
        result, gained = norm_back_rows(tokens[at, :].astype(wide), gain[...], upstream)
        first_total[at, :] = result + middle_grad[at, :]
        mine[0, 0:1, :] += gained

    for index in range(BLOCKS):
        collect.take(index, use)
        rings.tick(1)
    while total.steps:
        total.tick()
        rings.tick(1)
    rings.finish()
    total.finish(stats_total)
    collect.finish()


def exchange_last(first, tokens, gain, middle_grad, sums, pairs):
    size = tokens.shape[0]
    count = lax.axis_size("w")
    stats = (8, MODEL_WIDTH)
    work = RingWork(pairs)

    def body(*refs):
        last_kernel(work, *refs)

    return pl.pallas_call(
        body,
        out_shape=[
            jax.ShapeDtypeStruct((size, MODEL_WIDTH), wide),
            jax.ShapeDtypeStruct(stats, wide),
            *work.outputs(),
        ],
        in_specs=[ANY] + [VMEM] * (3 + len(sums)) + [ANY] * len(work.operands),
        out_specs=[VMEM] * 2 + [ANY] * len(work.columns),
        scratch_shapes=collect_shapes(size)
        + [
            pltpu.VMEM((2, *stats), wide),
            pltpu.VMEM((2, *stats), wide),
            pltpu.VMEM((count, *stats), wide),
        ]
        + work.scratch()
        + [semaphores_for(16 * BLOCKS + 2 * count + 4 + work.semaphores())],
        compiler_params=settings(4),
        cost_estimate=pl.CostEstimate(flops=0, bytes_accessed=128 * 2**20, transcendentals=0),
        name="exchange_last",
    )(first, tokens, gain, middle_grad, *sums, *work.operands)


FEEDFORWARD_ROWS = 256
FEEDFORWARD_COLUMNS = 512


def feedforward_kernel(
    sizes, core, rows, upstream, large, small, gate_out, up_out, hidden_out, back_out, down_out
):
    weights = [(large.at[0], 0, sizes[0]), (small, sizes[0], sizes[1])]
    for weight, base, size in weights:
        for start in range(0, size, FEEDFORWARD_COLUMNS):
            width = min(FEEDFORWARD_COLUMNS, size - start)
            columns = slice(base + start, base + start + width)
            gate_part = dot(rows[...], weight[:, start : start + width], 1, 0)
            up_part = dot(rows[...], weight[:, size + start : size + start + width], 1, 0)
            hidden_grad = dot(
                upstream[...], weight[:, 2 * size + start : 2 * size + start + width], 1, 0
            )
            sigmoid_gate = jax.nn.sigmoid(gate_part)
            silu_gate = gate_part * sigmoid_gate
            hidden_out[:, columns] = (silu_gate * up_part).astype(low)
            gate_out[:, columns] = (
                hidden_grad * up_part * sigmoid_gate * (1.0 + gate_part * (1.0 - sigmoid_gate))
            ).astype(low)
            up_out[:, columns] = (hidden_grad * silu_gate).astype(low)
    for start in range(0, MODEL_WIDTH, FEEDFORWARD_COLUMNS):
        across = slice(start, start + FEEDFORWARD_COLUMNS)
        back = 0.0
        down = 0.0
        for weight, base, size in weights:
            columns = slice(base, base + size)
            back = back + dot(gate_out[:, columns], weight[across, :size], 1, 1)
            back = back + dot(up_out[:, columns], weight[across, size : 2 * size], 1, 1)
            down = down + dot(hidden_out[:, columns], weight[across, 2 * size :], 1, 1)
        back_out[:, across] = back.astype(low)
        down_out[:, across] = down.astype(low)


def feedforward(core, rows, upstream, large, small):
    sizes = (large.shape[2] // 3, small.shape[1] // 3)
    count = rows.shape[0]
    hidden = sum(sizes)

    def body(*refs):
        feedforward_kernel(sizes, *refs)

    def block(columns):
        return pl.BlockSpec((FEEDFORWARD_ROWS, columns), lambda index, core: (index, 0))

    once = pl.Buffered(1)
    return pl.pallas_call(
        body,
        grid_spec=pltpu.PrefetchScalarGridSpec(
            num_scalar_prefetch=1,
            grid=(count // FEEDFORWARD_ROWS,),
            in_specs=[
                block(MODEL_WIDTH),
                block(MODEL_WIDTH),
                pl.BlockSpec(
                    (1, *large.shape[1:]),
                    lambda index, core: (core[0], 0, 0),
                    pipeline_mode=once,
                ),
                pl.BlockSpec(small.shape, lambda index, core: (0, 0), pipeline_mode=once),
            ],
            out_specs=[block(hidden)] * 3 + [block(MODEL_WIDTH)] * 2,
        ),
        out_shape=[jax.ShapeDtypeStruct((count, hidden), low)] * 3
        + [jax.ShapeDtypeStruct((count, MODEL_WIDTH), low)] * 2,
        compiler_params=pltpu.CompilerParams(vmem_limit_bytes=60 * 2**20),
        cost_estimate=pl.CostEstimate(
            flops=12 * count * MODEL_WIDTH * hidden,
            bytes_accessed=48 * 2**20,
            transcendentals=count * hidden,
        ),
        name="feedforward",
    )(core, rows, upstream, large, small)


def head_rows(values, gain, cosine, sine):
    factor = lax.rsqrt(jnp.mean(values * values, axis=-1, keepdims=True) + norm_epsilon)
    normed = values * factor * gain
    return (normed * cosine + pltpu.roll(normed, HEAD_WIDTH // 2, 1) * sine).astype(low)


def head_back(values, gain, cosine, sine, upstream):
    turned = upstream * cosine - pltpu.roll(upstream, HEAD_WIDTH // 2, 1) * sine
    return norm_back_rows(values, gain, turned)


def head_at(index):
    return slice(index * HEAD_WIDTH, (index + 1) * HEAD_WIDTH)


def gate_column(logits, head):
    lanes = lax.broadcasted_iota(jnp.int32, logits.shape, 1)
    logit = jnp.sum(jnp.where(lanes == head, logits, 0.0), axis=-1, keepdims=True)
    return jax.nn.sigmoid(logit)


def mask_rows(mask, valid_count, piece_start):
    length = mask.shape[0]
    for start in range(0, length, QUERY_ROWS):
        shape = (QUERY_ROWS, length)
        row = start + lax.broadcasted_iota(jnp.int32, shape, 0)
        column = lax.broadcasted_iota(jnp.int32, shape, 1)
        last = piece_start + PIC
        inside = (row >= piece_start) & (row < last) & (column >= piece_start) & (column < last)
        allowed = (column < valid_count) & ((column <= row) | inside)
        mask[start : start + QUERY_ROWS, :] = jnp.where(allowed, 0.0, masked_score)


def probabilities(queries, keys, mask):
    scores = dot(queries, keys, 1, 1) * HEAD_WIDTH ** (-0.5) + mask
    expos = jnp.exp(scores - jnp.max(scores, axis=-1, keepdims=True))
    return expos * (1.0 / jnp.sum(expos, axis=-1, keepdims=True))


QUERY_ROWS = 256


def attention_forward_kernel(
    groups, share, valid, start, rows_in, weights, gains, cosine, sine, pre, gated, partial, mask
):
    sequence = pl.program_id(0)
    mask_rows(mask, valid[sequence], start[sequence])
    heads = groups * share
    length, projected = pre.shape
    for column in range(0, projected, 3 * HEAD_WIDTH):
        columns = slice(column, min(column + 3 * HEAD_WIDTH, projected))
        pre[:, columns] = dot(rows_in[...], weights[:, columns], 1, 0)
    for group in range(groups):
        keys = head_rows(pre[:, head_at(heads + group)], gains[1:2, :], cosine[...], sine[...])
        values = pre[:, head_at(heads + groups + group)].astype(low)
        for head in range(group * share, (group + 1) * share):
            for at in range(0, length, QUERY_ROWS):
                rows = slice(at, at + QUERY_ROWS)
                queries = head_rows(
                    pre[rows, head_at(head)], gains[0:1, :], cosine[rows, :], sine[rows, :]
                )
                probs = probabilities(queries, keys, mask[rows, :])
                mixed = dot(probs.astype(low), values, 1, 0)
                gate = gate_column(pre[rows, head_at(heads + 2 * groups)], head)
                gated[rows, head_at(head)] = (mixed * gate).astype(low)
    for column in range(0, MODEL_WIDTH, 512):
        partial[:, column : column + 512] = dot(
            gated[...], weights[column : column + 512, projected:], 1, 1
        ).astype(low)


def attention_backward_kernel(
    groups, share, valid, start, pre, rows_in, weights, gains, cosine, sine,
    grads, gain_grads, partial, upstream, mask,
):
    sequence = pl.program_id(0)
    mask_rows(mask, valid[sequence], start[sequence])
    heads = groups * share
    length, projected = pre.shape
    upstream[...] = dot(rows_in[...], weights[:, projected:], 1, 0)
    scale = HEAD_WIDTH ** (-0.5)

    @pl.when(sequence == 0)
    def _():
        gain_grads[...] = jnp.zeros_like(gain_grads)

    logit_grads = [jnp.zeros((QUERY_ROWS, HEAD_WIDTH), wide)] * (length // QUERY_ROWS)
    for group in range(groups):
        key_pre = pre[:, head_at(heads + group)]
        keys = head_rows(key_pre, gains[1:2, :], cosine[...], sine[...])
        values = pre[:, head_at(heads + groups + group)].astype(low)
        value_grad = jnp.zeros((length, HEAD_WIDTH), wide)
        key_grad = jnp.zeros((length, HEAD_WIDTH), wide)
        for head in range(group * share, (group + 1) * share):
            for block, at in enumerate(range(0, length, QUERY_ROWS)):
                rows = slice(at, at + QUERY_ROWS)
                query_pre = pre[rows, head_at(head)]
                queries = head_rows(query_pre, gains[0:1, :], cosine[rows, :], sine[rows, :])
                probs = probabilities(queries, keys, mask[rows, :])
                probs_low = probs.astype(low)
                mixed = dot(probs_low, values, 1, 0)
                gate = gate_column(pre[rows, head_at(heads + 2 * groups)], head)
                gated_grad = upstream[rows, head_at(head)]
                mixed_grad = (gated_grad * gate).astype(low)
                logit_grad = (
                    jnp.sum(gated_grad * mixed, axis=-1, keepdims=True) * gate * (1.0 - gate)
                )
                lanes = lax.broadcasted_iota(jnp.int32, (QUERY_ROWS, HEAD_WIDTH), 1)
                logit_grads[block] = logit_grads[block] + jnp.where(lanes == head, logit_grad, 0.0)
                value_grad = value_grad + dot(probs_low, mixed_grad, 0, 0)
                prob_grad = dot(mixed_grad, values, 1, 1)
                score_grad = (
                    probs * (prob_grad - jnp.sum(prob_grad * probs, axis=-1, keepdims=True))
                ).astype(low)
                key_grad = key_grad + dot(score_grad, queries, 0, 0)
                query_grad, gained = head_back(
                    query_pre,
                    gains[0:1, :],
                    cosine[rows, :],
                    sine[rows, :],
                    dot(score_grad, keys, 1, 0) * scale,
                )
                grads[rows, head_at(head)] = query_grad.astype(low)
                gain_grads[0:1, :] += gained
        key_grad, gained = head_back(
            key_pre, gains[1:2, :], cosine[...], sine[...], key_grad * scale
        )
        gain_grads[1:2, :] += gained
        grads[:, head_at(heads + group)] = key_grad.astype(low)
        grads[:, head_at(heads + groups + group)] = value_grad.astype(low)
    for block, at in enumerate(range(0, length, QUERY_ROWS)):
        grads[slice(at, at + QUERY_ROWS), head_at(heads + 2 * groups)] = logit_grads[block].astype(
            low
        )
    for column in range(0, MODEL_WIDTH, 512):
        partial[:, column : column + 512] = dot(
            grads[...], weights[column : column + 512, :projected], 1, 1
        ).astype(low)


def sequence_block(columns, length):
    return pl.BlockSpec((length, columns), lambda sequence: (sequence, 0))


def fixed_block(*shape):
    return pl.BlockSpec(shape, lambda sequence: (0, 0))


def attention_call(body, name, specs, sequences, outputs, out_specs, scratch, operands):
    return pl.pallas_call(
        body,
        grid=(sequences,),
        out_shape=outputs,
        in_specs=[SCALARS, SCALARS, *specs],
        out_specs=out_specs,
        scratch_shapes=scratch,
        compiler_params=pltpu.CompilerParams(vmem_limit_bytes=60 * 2**20),
        cost_estimate=pl.CostEstimate(
            flops=2**33, bytes_accessed=24 * 2**20, transcendentals=2**21
        ),
        name=name,
    )(*operands)


def attention_specs(weights, length):
    return [
        pl.BlockSpec(weights.shape, lambda sequence: (0, 0), pipeline_mode=pl.Buffered(1)),
        fixed_block(2, HEAD_WIDTH),
        fixed_block(length, HEAD_WIDTH),
        fixed_block(length, HEAD_WIDTH),
    ]


def attention_forward(groups, share, valid, start, rows, weights, gains, cosine, sine):
    length, columns = cosine.shape[0], groups * share * HEAD_WIDTH
    projected, count = weights.shape[1] - columns, rows.shape[0]

    def body(*refs):
        attention_forward_kernel(groups, share, *refs)

    return attention_call(
        body,
        "attention_forward",
        [sequence_block(MODEL_WIDTH, length), *attention_specs(weights, length)],
        count // length,
        [
            jax.ShapeDtypeStruct((count, projected), wide),
            jax.ShapeDtypeStruct((count, columns), low),
            jax.ShapeDtypeStruct((count, MODEL_WIDTH), low),
        ],
        [sequence_block(size, length) for size in (projected, columns, MODEL_WIDTH)],
        [pltpu.VMEM((length, length), wide)],
        (valid, start, rows, weights, gains, cosine, sine),
    )


def attention_backward(groups, share, valid, start, pre, rows, weights, gains, cosine, sine):
    length, columns = cosine.shape[0], groups * share * HEAD_WIDTH
    count, projected = pre.shape

    def body(*refs):
        attention_backward_kernel(groups, share, *refs)

    return attention_call(
        body,
        "attention_backward",
        [
            sequence_block(projected, length),
            sequence_block(MODEL_WIDTH, length),
            *attention_specs(weights, length),
        ],
        count // length,
        [
            jax.ShapeDtypeStruct((count, projected), low),
            jax.ShapeDtypeStruct((2, HEAD_WIDTH), wide),
            jax.ShapeDtypeStruct((count, MODEL_WIDTH), low),
        ],
        [
            sequence_block(projected, length),
            fixed_block(2, HEAD_WIDTH),
            sequence_block(MODEL_WIDTH, length),
        ],
        [pltpu.VMEM((length, columns), wide), pltpu.VMEM((length, length), wide)],
        (valid, start, pre, rows, weights, gains, cosine, sine),
    )


def adam_kernel(layouts, names, heads, *refs):
    given, refs = refs[: len(names)], refs[len(names) :]
    count = len(layouts)
    stats, inverse, refs = refs[0], refs[1], refs[2:]
    extra, states, refs = refs[:11], refs[11 : 11 + 3 * count], refs[11 + 3 * count :]
    scales, refs = refs[0], refs[1:]
    extra_targets, targets, refs = refs[:11], refs[11 : 11 + 3 * count], refs[11 + 3 * count :]
    buffers, extra_buffers, refs = refs[: 3 * count], refs[3 * count :][:11], refs[3 * count + 11 :]
    small = extra_buffers[2:]
    sources, semaphores, sum_semaphores = dict(zip(names, refs)), refs[-2], refs[-1]
    fetches = [
        pltpu.make_async_copy(value, sources[name], sum_semaphores.at[0, i])
        for i, (name, value) in enumerate(zip(names, given))
    ]
    for i in range(11):
        slot = len(names) + i
        fetches.append(
            pltpu.make_async_copy(extra[i], extra_buffers[i], sum_semaphores.at[0, slot])
        )
    moves = [
        pltpu.make_async_copy(extra_buffers[i], extra_targets[i], sum_semaphores.at[1, i])
        for i in range(11)
    ]
    loads = [
        pltpu.make_async_copy(states[i], buffers[i], semaphores.at[0, i]) for i in range(3 * count)
    ]
    stores = [
        pltpu.make_async_copy(buffers[i], targets[i], semaphores.at[1, i])
        for i in range(3 * count)
    ]
    for copy in (*fetches, *loads):
        copy.start()
    for copy in fetches:
        copy.wait()
    for copy in moves[:2]:
        copy.start()

    def update(part, at, gradient, rate, decay_rate):
        old = [small[3 * part + i][at] for i in range(3)]
        for i, value in enumerate(adam_update(*old, gradient, rate, decay_rate)):
            small[3 * part + i][at] = value

    everything = (slice(None), slice(None))
    update(0, everything, stats[0:2, :], 0.5, 0.0)
    for row in range(2):
        update(1, (slice(row, row + 1), slice(None)), stats[2:3, head_at(row)], 0.5, 0.0)
    column, size = heads
    gradient = jnp.concatenate(
        [
            sources["projected"][core, :, column : column + HEAD_WIDTH].astype(wide).T[:size]
            for core in range(2)
        ],
        axis=0,
    )
    update(2, everything, gradient, layouts[0][1], weight_decay)
    for copy in moves[2:]:
        copy.start()
    lanes = lax.broadcasted_iota(jnp.int32, scales.shape, 1)
    squares = jnp.zeros(scales.shape, wide)
    for lane, row in enumerate((4, 5, 3)):
        squares = jnp.where(
            lanes == lane, jnp.sum(stats[row : row + 1, :], axis=-1, keepdims=True), squares
        )
    scales[...] = jnp.sqrt(squares * inverse[...])
    for number, (transposed, rate, leads) in enumerate(layouts):
        matrix = buffers[3 * number : 3 * number + 3]
        for load in loads[3 * number : 3 * number + 3]:
            load.wait()
        for lead, pieces in enumerate(leads):
            quarter = sum(size for _, _, size in pieces)
            for core in range(2):
                start = core * quarter
                for name, column, size in pieces:
                    step = 256 if size % 256 == 0 else 128

                    @pl.loop(0, size // step)
                    def _(block):
                        columns = pl.ds(pl.multiple_of(column + block * step, 128), step)
                        gradient = sources[name][core, :, columns].astype(wide)
                        place = pl.ds(pl.multiple_of(start + block * step, 128), step)
                        if transposed:
                            gradient = gradient.T
                            at = (place, slice(None))
                        elif len(leads) > 1:
                            at = (lead, slice(None), place)
                        else:
                            at = (slice(None), place)
                        weight, moment, square = (part[at] for part in matrix)
                        for part, value in zip(
                            matrix,
                            adam_update(weight, moment, square, gradient, rate, weight_decay),
                        ):
                            part[at] = value

                    start += size
        for store in stores[3 * number : 3 * number + 3]:
            store.start()
    for copy in (*stores, *moves):
        copy.wait()


def adam_matrices(layouts, heads, sums, stats, inverse, passed, small, states):
    def body(*refs):
        adam_kernel(layouts, list(sums), heads, *refs)

    extra = [*passed, *small]

    def like(values):
        return [jax.ShapeDtypeStruct(value.shape, value.dtype) for value in values]

    return pl.pallas_call(
        body,
        out_shape=like([inverse, *extra, *states]),
        in_specs=[ANY] * len(sums) + [VMEM] * 2 + [ANY] * (len(extra) + len(states)),
        out_specs=[VMEM] + [ANY] * (len(extra) + len(states)),
        scratch_shapes=[
            pltpu.VMEM(value.shape, value.dtype) for value in (*states, *extra, *sums.values())
        ]
        + [
            pltpu.SemaphoreType.DMA((2, len(states))),
            pltpu.SemaphoreType.DMA((2, len(sums) + len(extra))),
        ],
        compiler_params=pltpu.CompilerParams(vmem_limit_bytes=60 * 2**20),
        cost_estimate=pl.CostEstimate(
            flops=2**25, bytes_accessed=40 * 2**20, transcendentals=2**21
        ),
        name="adam_matrices",
    )(*sums.values(), stats, inverse, *extra, *states)


def prepare_kernel(sizes, *refs):
    given, (attention, normed, large, small), refs = refs[:8], refs[8:12], refs[12:]
    loads = [
        pltpu.make_async_copy(value, refs[i], refs[8].at[i]) for i, value in enumerate(given)
    ]
    for load in loads:
        load.start()
    for load in loads:
        load.wait()
    query, keyvalue, headgate, output, gateup, down, tokens, gain = refs[:8]
    core = lax.axis_index("c")
    head_cols, group_cols = query.shape[1] // 2, keyvalue.shape[2] // 2
    edges = [head_cols, head_cols + group_cols, head_cols + 2 * group_cols]
    heads = head_cols // HEAD_WIDTH
    rows = query.shape[0]
    hidden = sum(sizes)
    logits = jnp.concatenate(
        [headgate[...], jnp.zeros((HEAD_WIDTH - headgate.shape[0], rows), wide)], axis=0
    ).T
    lanes = lax.broadcasted_iota(jnp.int32, logits.shape, 1)
    for quarter in range(2):
        slot = lax.rem(quarter + core, 2)
        columns = slice(quarter * head_cols, (quarter + 1) * head_cols)
        attention[slot, :, :head_cols] = query[:, columns].astype(low)
        for part in range(2):
            attention[slot, :, edges[part] : edges[part + 1]] = keyvalue[
                part, :, quarter * group_cols : (quarter + 1) * group_cols
            ].astype(low)
        turned = pltpu.roll(logits, HEAD_WIDTH - heads, 1) if quarter else logits
        attention[slot, :, edges[2] : edges[2] + HEAD_WIDTH] = jnp.where(
            lanes < heads, turned, 0.0
        ).astype(low)
        attention[slot, :, edges[2] + HEAD_WIDTH :] = output[columns, :].T.astype(low)
        base = quarter * hidden
        for part in range(3):
            start = 0
            for target, size in ((large.at[quarter], sizes[0]), (small.at[slot], sizes[1])):
                here = slice(base + start, base + start + size)
                value = gateup[part, :, here] if part < 2 else down[here, :].T
                target[:, part * size : (part + 1) * size] = value.astype(low)
                start += size

    @pl.loop(0, tokens.shape[0] // STRIP)
    def _(strip):
        at = rows_at(strip * STRIP, STRIP)
        normed[at, :] = normalize(tokens[at, :].astype(wide), gain[...]).astype(low)


def prepare(sizes, query, keyvalue, headgate, output, gateup, down, tokens, gain):
    rows = query.shape[0]
    columns = query.shape[1] // 2 * 2 + keyvalue.shape[2] + HEAD_WIDTH
    operands = (query, keyvalue, headgate, output, gateup, down, tokens, gain)

    def body(*refs):
        prepare_kernel(sizes, *refs)

    return pl.pallas_call(
        body,
        out_shape=[
            jax.ShapeDtypeStruct((2, rows, columns), low),
            jax.ShapeDtypeStruct(tokens.shape, low),
            jax.ShapeDtypeStruct((2, rows, 3 * sizes[0]), low),
            jax.ShapeDtypeStruct((2, rows, 3 * sizes[1]), low),
        ],
        in_specs=[ANY] * 8,
        out_specs=[VMEM] * 4,
        scratch_shapes=[pltpu.VMEM(value.shape, value.dtype) for value in operands]
        + [pltpu.SemaphoreType.DMA((8,))],
        compiler_params=pltpu.CompilerParams(vmem_limit_bytes=60 * 2**20),
        cost_estimate=pl.CostEstimate(
            flops=2**22, bytes_accessed=12 * 2**20, transcendentals=0
        ),
        name="prepare",
    )(*operands)


def local(
    tokens,
    cotangent,
    valid_len,
    pic_start,
    norm_gains,
    norm_moment,
    norm_square,
    head_gains,
    head_moment,
    head_square,
    query_weight,
    query_moment,
    query_square,
    keyvalue_matrix,
    keyvalue_first_moment,
    keyvalue_second_moment,
    headgate_weight,
    headgate_moment,
    headgate_square,
    output_weight,
    output_moment,
    output_square,
    gateup_weight,
    gateup_moment,
    gateup_square,
    down_weight,
    down_moment,
    down_square,
):
    local_rows = tokens.shape[0]
    length_value = local_rows * 2
    rows = length_value * 2
    group = lax.axis_index("w")
    core = lax.axis_index("c")
    place = lax.axis_index("t")
    heads_here = query_weight.shape[1] // HEAD_WIDTH // 2
    groups_here = keyvalue_matrix.shape[2] // HEAD_WIDTH // 2
    share = heads_here // groups_here
    head_cols = heads_here * HEAD_WIDTH
    group_cols = groups_here * HEAD_WIDTH
    hidden_here = gateup_weight.shape[2] // 2

    bounds = [0, head_cols, group_cols, group_cols, 128, head_cols]
    edges = [sum(bounds[: i + 1]) for i in range(6)]
    sizes = (hidden_here - hidden_here // 6, hidden_here // 6)
    attention_pieces, normed, large_block, small_pieces = prepare(
        sizes,
        query_weight,
        keyvalue_matrix,
        headgate_weight.T,
        output_weight,
        gateup_weight,
        down_weight,
        tokens,
        norm_gains[0:1],
    )
    large_both = lax.all_gather(large_block, ("w", "c"), axis=1, tiled=True)
    attention_full, first_full, output_grad_full = gather_attention(
        attention_pieces, normed, cotangent
    )
    valid_pair = lax.dynamic_slice_in_dim(valid_len, 2 * group, 2)
    start_pair = lax.dynamic_slice_in_dim(pic_start, 2 * group, 2)
    cosine, sine = rotary_tables(length_value)
    projected, gated_low, attention_partial = attention_forward(
        groups_here,
        share,
        valid_pair,
        start_pair,
        first_full,
        attention_full,
        head_gains,
        cosine,
        sine,
    )
    middle, squares, second_full, small_full = exchange_forward(
        valid_len, attention_partial, tokens, norm_gains[1:2], small_pieces
    )
    gate_grad, up_grad, hidden_low, second_partial, feedforward_partial = feedforward(
        core[None], second_full, output_grad_full, large_both, small_full
    )
    half = hidden_here // 2
    pieces = [(0, half), (half, hidden_here - half)]
    middle_grad, second_gain_grad, block_output, output_squares, attention_grad, *sums = (
        exchange_backward(
            valid_len,
            second_partial,
            feedforward_partial,
            middle,
            cotangent,
            norm_gains[1:2],
            [(second_full, grad, *piece) for grad in (gate_grad, up_grad) for piece in pieces],
        )
    )
    projected_grad, head_gain_grads, first_partial = attention_backward(
        groups_here,
        share,
        valid_pair,
        start_pair,
        projected,
        attention_grad,
        attention_full,
        head_gains,
        cosine,
        sine,
    )
    tokens_grad, stats, *more = exchange_last(
        first_partial,
        tokens,
        norm_gains[0:1],
        middle_grad,
        [second_gain_grad, head_gain_grads, output_squares, squares],
        [
            *((output_grad_full, hidden_low, *piece) for piece in pieces),
            (first_full, projected_grad, 0, edges[4]),
            (attention_grad, gated_low, 0, head_cols),
        ],
    )
    denominator = jnp.sum(valid_len).astype(wide) * MODEL_WIDTH
    inverse = jnp.full((1, HEAD_WIDTH), 1.0 / denominator)
    input_rate = MODEL_WIDTH ** (-0.5)
    down_rate = FF ** (-0.5)
    output_rate = max(QUERY_HEADS * HEAD_WIDTH // 128, 4) ** (-0.5)
    widths = [half, hidden_here - half]

    def parts_of(name):
        return [(f"{name} {index}", 0, width) for index, width in enumerate(widths)]

    layouts = [
        (
            False,
            input_rate,
            [parts_of("gate"), parts_of("up")],
        ),
        (True, down_rate, [parts_of("down")]),
        (False, input_rate, [[("projected", edges[0], head_cols)]]),
        (
            False,
            input_rate,
            [[("projected", edges[1], group_cols)], [("projected", edges[2], group_cols)]],
        ),
        (True, output_rate, [[("output", 0, head_cols)]]),
    ]
    names = ["gate 0", "gate 1", "up 0", "up 1", "down 0", "down 1", "projected", "output"]
    sums = dict(zip(names, [*sums, *more]))
    scales, block_output, tokens_grad, *updated = adam_matrices(
        layouts,
        (edges[3], heads_here),
        sums,
        stats,
        inverse,
        [block_output, tokens_grad],
        [
            norm_gains,
            norm_moment,
            norm_square,
            head_gains,
            head_moment,
            head_square,
            headgate_weight.T,
            headgate_moment.T,
            headgate_square.T,
        ],
        [
            gateup_weight,
            gateup_moment,
            gateup_square,
            down_weight,
            down_moment,
            down_square,
            query_weight,
            query_moment,
            query_square,
            keyvalue_matrix,
            keyvalue_first_moment,
            keyvalue_second_moment,
            output_weight,
            output_moment,
            output_square,
        ],
    )
    norms_new, heads_new, headgate_new, gateup_new, down_new, query_new, keyvalue_new, output_new = (
        updated[3 * i : 3 * i + 3] for i in range(8)
    )
    branch_scales = scales[0, :3]
    return (
        block_output,
        tokens_grad,
        branch_scales,
        *norms_new,
        *heads_new,
        *query_new,
        *keyvalue_new,
        *(value.T for value in headgate_new),
        *output_new,
        *gateup_new,
        *down_new,
    )


def solution(mesh):
    fsdp, tp = mesh.devices.shape
    fine = Mesh(mesh.devices.reshape(fsdp // 2, 2, tp), ("w", "c", "t"))
    whole = ("w", "c")
    rows = P(("w", "c", "t"), None)
    first = P(whole, "t")
    second = P(None, whole, "t")
    last = P("t", whole)
    matrices = (first,) * 3 + (second,) * 3 + (first,) * 3 + (last,) * 3 + (second,) * 3 + (last,) * 3
    return jax.shard_map(
        local,
        mesh=fine,
        in_specs=(rows, rows, P(), P()) + (P(),) * 6 + matrices,
        out_specs=(rows, rows, P()) + (P(),) * 6 + matrices,
        check_vma=False,
    )
```

```python
import jax
import jax.numpy as jnp
from jax import lax
from jax.experimental import pallas as pl
from jax.experimental.pallas import tpu as pltpu
from jax.sharding import Mesh
from jax.sharding import PartitionSpec as P

MODEL_WIDTH = 2048
QUERY_HEADS = 16
HEAD_WIDTH = 128
FF = 6144
PIC = 256
STEP = 10

norm_epsilon = 1e-06
rope_base = 1000000.0
beta_first = 0.9
beta_second = 0.999
adam_epsilon = 1e-08
weight_decay = 0.1
masked_score = -1e30
low = jnp.bfloat16
wide = jnp.float32


def normalize(values, scaling):
    return (
        values
        * lax.rsqrt(jnp.mean(values * values, axis=-1, keepdims=True) + norm_epsilon)
        * scaling
    )


def norm_back(values, scaling, upstream):
    factor = lax.rsqrt(jnp.mean(values * values, axis=-1, keepdims=True) + norm_epsilon)
    weighted = upstream * scaling
    projected = jnp.mean(weighted * values, axis=-1, keepdims=True)
    result = factor * weighted - values * (factor * factor * factor) * projected
    return (result, jnp.sum(upstream * values * factor, axis=tuple(range(values.ndim - 1))))


def rotary_tables(length_value):
    halves = HEAD_WIDTH // 2
    frequency = rope_base ** (-(jnp.arange(halves, dtype=wide) * 2.0 / HEAD_WIDTH))
    angles = jnp.arange(length_value, dtype=wide)[:, None] * frequency[None, :]
    cosine, sine = jnp.cos(angles), jnp.sin(angles)
    return (
        jnp.concatenate([cosine, cosine], axis=1),
        jnp.concatenate([-sine, sine], axis=1),
    )


def adam_update(weight, moment, square, gradient, step_rate, decay_rate):
    moment_new = beta_first * moment + (1.0 - beta_first) * gradient
    square_new = beta_second * square + (1.0 - beta_second) * gradient * gradient
    bias_first = 1.0 - beta_first**STEP
    bias_second = 1.0 - beta_second**STEP
    update = moment_new / bias_first / (jnp.sqrt(square_new / bias_second) + adam_epsilon)
    return (weight - step_rate * (update + decay_rate * weight), moment_new, square_new)


def dot(left, right, left_dim, right_dim):
    return lax.dot_general(
        left, right, (((left_dim,), (right_dim,)), ((), ())), preferred_element_type=wide
    )


def fetch(parts):
    pieces = []
    for core in range(2):
        for part in parts:
            size = part.shape[1] // 2
            pieces.append(part[:, core * size : (core + 1) * size].astype(low))
    count = len(parts)
    local_block = jnp.stack(
        [jnp.concatenate(pieces[core * count : (core + 1) * count], axis=1) for core in range(2)]
    )
    return lax.all_gather(local_block, ("w", "c"), axis=1, tiled=True)


def columns_of(both, start, size):
    return lax.dynamic_slice(
        both, (lax.axis_index("c"), 0, start), (1, both.shape[1], size)
    ).reshape(both.shape[1], size)


MESH = pl.DeviceIdType.MESH
BLOCKS = 4
STRIP = 16
ANY = pl.BlockSpec(memory_space=pl.ANY)
VMEM = pl.BlockSpec(memory_space=pltpu.VMEM)


def ring_place(index, count):
    odd = lax.rem(index, 2)
    pair = lax.div(index, 2)
    return (1 - odd) * pair + odd * (count - 1 - pair)


def ring_index(place, count):
    late = lax.div(place, count // 2)
    return (1 - late) * 2 * place + late * (2 * (count - 1 - place) + 1)


class Device:
    def __init__(self, semaphores):
        self.w, self.c, self.t = (lax.axis_index(axis) for axis in ("w", "c", "t"))
        self.count = lax.axis_size("w")
        self.place = ring_place(self.w, self.count)
        self.semaphores = semaphores
        self.used = 0
        self.other_core = {"c": 1 - self.c}
        self.other_row = {"t": 1 - self.t}

    def owner(self, distance):
        return ring_index(lax.rem(self.place + distance + self.count, self.count), self.count)

    def meet(self, partners):
        barrier = pltpu.get_barrier_semaphore()
        for partner in partners:
            pl.semaphore_signal(barrier, inc=1, device_id=partner, device_id_type=MESH)
        pl.semaphore_wait(barrier, len(partners))

    def remote(self, source, target, device):
        slot = self.used
        self.used += 1
        return pltpu.make_async_remote_copy(
            src_ref=source,
            dst_ref=target,
            send_sem=self.semaphores.at[0, slot],
            recv_sem=self.semaphores.at[1, slot],
            device_id=device,
            device_id_type=MESH,
        )

    def inside(self, source, target):
        slot = self.used
        self.used += 1
        return pltpu.make_async_copy(source, target, self.semaphores.at[0, slot])


def rows_at(start, size):
    return pl.ds(pl.multiple_of(start, STRIP), size)


class Spread:
    def __init__(self, device, full):
        self.device, self.full = device, full
        self.size = full.shape[0] // 4
        self.block = self.size // BLOCKS
        self.rows, self.core, self.passed, self.kept = {}, {}, {}, {}

    def where(self, core, row, index):
        return self.full.at[
            rows_at((core * 2 + row) * self.size + index * self.block, self.block)
        ]

    def put(self, index, source):
        device = self.device
        target = self.where(device.c, device.t, index)
        self.rows[index] = device.remote(source, target, device.other_row)
        self.core[index] = device.remote(source, target, device.other_core)
        self.kept[index] = device.inside(source, target)
        for copy in (self.rows[index], self.core[index], self.kept[index]):
            copy.start()

    def forward(self, index):
        device = self.device
        self.rows[index].wait_recv()
        place = self.where(device.c, 1 - device.t, index)
        self.passed[index] = device.remote(place, place, device.other_core)
        self.passed[index].start()

    def finish(self):
        for index in range(BLOCKS):
            self.rows[index].wait_send()
            self.core[index].wait()
            self.passed[index].wait()
            self.kept[index].wait()


class Collect:
    def __init__(self, device, partial, near, far, sent, came):
        self.device = device
        self.partial, self.near, self.far, self.sent, self.came = partial, near, far, sent, came
        self.size = partial.shape[0] // 4
        self.block = self.size // BLOCKS
        self.core, self.rows = {}, {}

    def start(self):
        device = self.device
        self.load = device.inside(
            self.partial.at[rows_at(device.c * 2 * self.size, 2 * self.size)], self.near
        )
        for part, row in enumerate((1 - device.t, device.t)):
            for index in range(BLOCKS):
                start = row * self.size + index * self.block
                copy = device.remote(
                    self.partial.at[rows_at((1 - device.c) * 2 * self.size + start, self.block)],
                    self.far.at[rows_at(start, self.block)],
                    device.other_core,
                )
                copy.start()
                self.core[part, index] = copy
        self.load.start()

    def pass_on(self, index):
        device = self.device
        if index == 0:
            self.load.wait()
        self.core[0, index].wait_recv()

        @pl.loop(0, self.block // STRIP)
        def _(strip):
            at = index * self.block + strip * STRIP
            rows = rows_at((1 - device.t) * self.size + at, STRIP)
            total = self.near[rows, :].astype(wide) + self.far[rows, :].astype(wide)
            self.sent[rows_at(at, STRIP), :] = total.astype(low)

        place = rows_at(index * self.block, self.block)
        self.rows[index] = device.remote(
            self.sent.at[place], self.came.at[place], device.other_row
        )
        self.rows[index].start()

    def take(self, index, use):
        device = self.device
        self.core[1, index].wait_recv()
        self.rows[index].wait_recv()

        @pl.loop(0, self.block // STRIP)
        def _(strip):
            at = index * self.block + strip * STRIP
            rows = rows_at(device.t * self.size + at, STRIP)
            mine = rows_at(at, STRIP)
            total = (
                self.near[rows, :].astype(wide)
                + self.far[rows, :].astype(wide)
                + self.came[mine, :].astype(wide)
            )
            use(mine, total)

    def finish(self):
        for index in range(BLOCKS):
            self.core[0, index].wait_send()
            self.core[1, index].wait_send()
            self.rows[index].wait_send()


class Given:
    parts = 2

    def __init__(self, grads):
        self.rows, self.columns = grads.shape
        self.grads = grads

    def take(self, starts, size):
        return [self.grads[rows_at(start, size), :].astype(wide) for start in starts]

    def sources(self, starts, size, keep):
        return [self.grads.at[rows_at(start, size)] for start in starts]


class Product:
    parts = 1

    def __init__(self, left, right, start, columns):
        self.rows, self.columns = left.shape[1], columns
        self.left, self.right, self.start = left, right, start

    def take(self, starts, size):
        left = jnp.concatenate(
            [self.left[:, pl.ds(pl.multiple_of(start, 128), size)] for start in starts], axis=1
        )
        both = dot(left, self.right[:, self.start : self.start + self.columns], 0, 0)
        return [both[:size], both[size:]]

    def sources(self, starts, size, keep):
        for way, value in enumerate(self.take(starts, size)):
            keep[way] = value.astype(low)
        return [keep.at[way] for way in range(2)]


class RingSum:
    def __init__(self, device, grads, ready, scratch, sums):
        self.device, self.grads, self.sums = device, grads, sums
        self.ready = ready
        self.slots, self.totals, self.first = scratch
        self.half = grads.rows // device.count // 2
        self.parts = grads.parts
        self.part = self.half // self.parts
        self.copies = {}
        self.ticks = [
            (step, part) for step in range(device.count) for part in range(self.parts)
        ]

    def own(self, way, distance, part):
        owner = self.device.owner(-(1 - 2 * way) * distance)
        return (owner * 2 + way) * self.half + part * self.part

    def slot(self, way, step, part):
        return self.slots.at[
            way * (self.device.count - 1) + step, pl.ds(part * self.part, self.part)
        ]

    def send(self, way, step, part, source):
        device = self.device
        copy = device.remote(
            source, self.slot(way, step, part), {"w": device.owner(1 - 2 * way)}
        )
        copy.start()
        self.copies[way, step, part] = copy

    def tick(self, count=1):
        device = self.device
        for _ in range(count):
            if not self.ticks:
                return
            step, part = self.ticks.pop(0)
            starts = [self.own(way, step + 1, part) for way in range(2)]
            if step == 0:
                self.ready()
                sources = self.grads.sources(starts, self.part, self.first)
                for way in range(2):
                    self.send(way, step, part, sources[way])
                continue
            own = self.grads.take(starts, self.part)
            for way in range(2):
                self.copies[way, step - 1, part].wait_recv()
                slot = self.slot(way, step - 1, part)
                total = (slot[...].astype(wide) + own[way]).astype(low)
                if step < device.count - 1:
                    slot[...] = total
                    self.send(way, step, part, slot)
                else:
                    self.totals[way, pl.ds(part * self.part, self.part), :] = total

    def close(self):
        device = self.device
        self.tick(len(self.ticks))
        self.away = device.remote(
            self.totals.at[1 - device.c], self.sums.at[device.c], device.other_core
        )
        self.kept = device.inside(self.totals.at[device.c], self.sums.at[device.c])
        self.away.start()
        self.kept.start()

    def finish(self):
        for copy in self.copies.values():
            copy.wait_send()
        self.away.wait()
        self.kept.wait()


def ring_shapes(columns, count):
    half = MODEL_WIDTH // count // 2
    return [
        pltpu.VMEM((2 * (count - 1), half, columns), low),
        pltpu.VMEM((2, half, columns), low),
        pltpu.VMEM((2, half, columns), low),
    ]


class RingWork:
    def __init__(self, pairs):
        self.columns = [columns for _, _, _, columns in pairs]
        self.fit = (MODEL_WIDTH // lax.axis_size("w") // 2) % 128 == 0
        self.operands, self.places = [], []
        for left, right, start, columns in pairs:
            if self.fit:
                self.places.append((self.add(left), self.add(right), start, columns))
            else:
                part = right[:, start : start + columns]
                self.places.append((self.add(dot(left, part, 0, 0).astype(low)),))

    def add(self, value):
        for index, other in enumerate(self.operands):
            if other is value:
                return index
        self.operands.append(value)
        return len(self.operands) - 1

    def begin(self, device, operands, scratch, sums):
        count = len(self.operands)
        buffers, scratch = scratch[:count], scratch[count:]
        loads = [device.inside(value, buffer) for value, buffer in zip(operands, buffers)]
        for load in loads:
            load.start()
        waiting = set(range(count))
        rings = []
        for index, place in enumerate(self.places):
            used = place[:2] if self.fit else place[:1]

            def ready(used=used):
                for number in used:
                    if number in waiting:
                        waiting.remove(number)
                        loads[number].wait()

            refs = [buffers[number] for number in used]
            grads = Product(*refs, *place[2:]) if self.fit else Given(*refs)
            rings.append(
                RingSum(device, grads, ready, scratch[3 * index : 3 * index + 3], sums[index])
            )
        return Rings(rings)

    def outputs(self):
        half = MODEL_WIDTH // lax.axis_size("w") // 2
        return [jax.ShapeDtypeStruct((2, half, size), low) for size in self.columns]

    def scratch(self):
        count = lax.axis_size("w")
        return [pltpu.VMEM(value.shape, value.dtype) for value in self.operands] + [
            shape for size in self.columns for shape in ring_shapes(size, count)
        ]

    def semaphores(self):
        return 4 * (lax.axis_size("w") + 1) * len(self.columns) + len(self.operands)


def collect_shapes(size):
    return [
        pltpu.VMEM((2 * size, MODEL_WIDTH), low),
        pltpu.VMEM((2 * size, MODEL_WIDTH), low),
        pltpu.VMEM((size, MODEL_WIDTH), low),
        pltpu.VMEM((size, MODEL_WIDTH), low),
    ]


def semaphores_for(count):
    return pltpu.SemaphoreType.DMA((2, count))


def settings(collective):
    return pltpu.CompilerParams(
        collective_id=collective, has_side_effects=True, vmem_limit_bytes=60 * 2**20
    )


def neighbours(device):
    return [
        device.other_core,
        device.other_row,
        {"w": device.owner(1)},
        {"w": device.owner(-1)},
    ]


class RingGather:
    def __init__(self, device, mine, other, full, target):
        self.device, self.full, self.target = device, full, target
        self.size = mine.shape[0]
        self.parts = min(4, self.size // STRIP)
        self.part = self.size // self.parts
        self.here = (device.w * 2 + device.c) * self.size
        here = rows_at(self.here, self.size)
        self.kept = device.inside(mine, full.at[here])
        self.crossed = device.remote(other, full.at[here], device.other_core)
        self.copies = {}
        self.stores = []
        self.ticks = [
            (step, part) for step in range(device.count - 1) for part in range(self.parts)
        ]

    def start(self):
        self.kept.start()
        self.crossed.start()

    def store(self, start, size):
        place = rows_at(start, size)
        copy = self.device.inside(self.full.at[place], self.target.at[place])
        copy.start()
        self.stores.append(copy)

    def ready(self):
        self.kept.wait()
        self.crossed.wait()
        self.store(self.device.w * 2 * self.size, 2 * self.size)

    def begin(self, way, step, part):
        owner = self.device.owner(-(1 - 2 * way) * step)
        return (owner * 2 + way) * self.size + part * self.part

    def tick(self, count=1):
        device = self.device
        for _ in range(count):
            if not self.ticks:
                return
            step, part = self.ticks.pop(0)
            for way in range(2):
                start = self.begin(way, step, part)
                block = self.full.at[rows_at(start, self.part)]
                if step > 0:
                    self.copies[way, step - 1, part].wait_recv()
                copy = device.remote(block, block, {"w": device.owner(1 - 2 * way)})
                copy.start()
                self.copies[way, step, part] = copy
                if step > 0:
                    self.store(start, self.part)

    def finish(self):
        self.tick(len(self.ticks))
        last = self.device.count - 1
        for part in range(self.parts):
            for way in range(2):
                self.copies[way, last - 1, part].wait_recv()
                self.store(self.begin(way, last, part), self.part)
        for copy in self.copies.values():
            copy.wait_send()
        for copy in self.stores:
            copy.wait()


def gather_kernel(pieces, first, second, target, first_full, second_full, full, semaphores):
    device = Device(semaphores)
    device.meet(neighbours(device))
    gather = RingGather(device, pieces.at[0], pieces.at[1], full, target)
    gather.start()
    spreads = []
    for rows, target in ((first, first_full), (second, second_full)):
        spread = Spread(device, target)
        block = spread.block
        for index in range(BLOCKS):
            spread.put(index, rows.at[pl.ds(index * block, block)])
        spreads.append(spread)
    gather.ready()
    for spread in spreads:
        for index in range(BLOCKS):
            gather.tick(gather.parts)
            spread.forward(index)
    gather.finish()
    for spread in spreads:
        spread.finish()


def gather_attention(pieces, first, second):
    count = lax.axis_size("w")
    rows = first.shape[0] * 4
    return pl.pallas_call(
        gather_kernel,
        out_shape=[
            jax.ShapeDtypeStruct((MODEL_WIDTH, pieces.shape[2]), low),
            jax.ShapeDtypeStruct((rows, MODEL_WIDTH), low),
            jax.ShapeDtypeStruct((rows, MODEL_WIDTH), low),
        ],
        in_specs=[VMEM] * 3,
        out_specs=[ANY] * 3,
        scratch_shapes=[
            pltpu.VMEM((MODEL_WIDTH, pieces.shape[2]), low),
            semaphores_for(16 * count + 8 * BLOCKS + 4),
        ],
        compiler_params=settings(1),
        cost_estimate=pl.CostEstimate(flops=0, bytes_accessed=64 * 2**20, transcendentals=0),
        name="gather_attention",
    )(pieces, first, second)


def counted_rows(device, valid, at, size):
    place = device.t * size + at.start + lax.broadcasted_iota(jnp.int32, (at.size, 1), 0)
    return jnp.where(place < valid[device.w * 2 + device.c], 1.0, 0.0)


def forward_kernel(
    valid, partial, rows, gain, pieces, middle, squares, full, target,
    near, far, sent, came, normed, gathered, semaphores,
):
    device = Device(semaphores)
    device.meet(neighbours(device))
    collect = Collect(device, partial, near, far, sent, came)
    spread = Spread(device, full)
    gather = RingGather(device, pieces.at[0], pieces.at[1], gathered, target)
    collect.start()
    gather.start()
    squares[...] = jnp.zeros_like(squares)
    collect.pass_on(0)
    gather.ready()
    gather.tick(gather.parts)
    for index in range(1, BLOCKS):
        collect.pass_on(index)

    def use(at, value):
        row = rows[at, :].astype(wide)
        counted = counted_rows(device, valid, at, rows.shape[0])
        squares[0:1, :] += jnp.sum(counted * row * row, axis=0, keepdims=True)
        squares[1:2, :] += jnp.sum(counted * value * value, axis=0, keepdims=True)
        total = row + value
        middle[at, :] = total
        normed[at, :] = normalize(total, gain[...]).astype(low)

    for index in range(BLOCKS):
        collect.take(index, use)
        spread.put(index, normed.at[pl.ds(index * spread.block, spread.block)])
        gather.tick(2)
    gather.tick(4)
    for index in range(BLOCKS):
        spread.forward(index)
        gather.tick(2)
    gather.finish()
    spread.finish()
    collect.finish()


SCALARS = pl.BlockSpec(memory_space=pltpu.SMEM)


def exchange_forward(valid, partial, rows, gain, pieces):
    size = rows.shape[0]
    count = lax.axis_size("w")
    return pl.pallas_call(
        forward_kernel,
        out_shape=[
            jax.ShapeDtypeStruct((size, MODEL_WIDTH), wide),
            jax.ShapeDtypeStruct((2, MODEL_WIDTH), wide),
            jax.ShapeDtypeStruct((4 * size, MODEL_WIDTH), low),
            jax.ShapeDtypeStruct((MODEL_WIDTH, pieces.shape[2]), low),
        ],
        in_specs=[SCALARS, ANY, VMEM, VMEM, VMEM],
        out_specs=[VMEM, VMEM, ANY, ANY],
        scratch_shapes=collect_shapes(size)
        + [
            pltpu.VMEM((size, MODEL_WIDTH), low),
            pltpu.VMEM((MODEL_WIDTH, pieces.shape[2]), low),
            semaphores_for(16 * BLOCKS + 16 * count + 4),
        ],
        compiler_params=settings(2),
        cost_estimate=pl.CostEstimate(flops=0, bytes_accessed=64 * 2**20, transcendentals=0),
        name="exchange_forward",
    )(valid, partial, rows, gain, pieces)


class Rings:
    def __init__(self, rings):
        self.rings = rings
        self.next = 0

    def tick(self, count=1):
        for _ in range(count):
            ring = self.rings[self.next]
            self.next = (self.next + 1) % len(self.rings)
            ring.tick()

    def finish(self):
        while any(ring.ticks for ring in self.rings):
            self.tick()
        for ring in self.rings:
            ring.close()
        for ring in self.rings:
            ring.finish()


def norm_back_rows(values, gain, upstream):
    factor = lax.rsqrt(jnp.mean(values * values, axis=-1, keepdims=True) + norm_epsilon)
    weighted = upstream * gain
    projected = jnp.mean(weighted * values, axis=-1, keepdims=True)
    result = factor * weighted - values * (factor * factor * factor) * projected
    return result, jnp.sum(upstream * values * factor, axis=0, keepdims=True)


def backward_kernel(work, valid, partial, output, middle, rows, gain, *refs):
    count = len(work.columns)
    operands, refs = refs[: len(work.operands)], refs[len(work.operands) :]
    grad, gain_grad, block, squares, full, refs = *refs[:5], refs[5:]
    sums, refs = refs[:count], refs[count:]
    rounded = refs[8]
    device = Device(refs[-1])
    rings = work.begin(device, operands, refs[9:-1], sums)
    device.meet(neighbours(device))
    collect = Collect(device, partial, *refs[:4])
    output_collect = Collect(device, output, *refs[4:8])
    spread = Spread(device, full)
    collect.start()
    rings.tick(2)
    gain_grad[...] = jnp.zeros_like(gain_grad)
    squares[...] = jnp.zeros_like(squares)
    for index in range(BLOCKS):
        collect.pass_on(index)
    rings.tick(count - 2)
    output_collect.start()

    def use(at, upstream):
        result, gained = norm_back_rows(middle[at, :], gain[...], upstream)
        result = result + rows[at, :].astype(wide)
        grad[at, :] = result
        rounded[at, :] = result.astype(low)
        gain_grad[...] += gained

    def use_output(at, value):
        block[at, :] = (middle[at, :] + value).astype(low)
        counted = counted_rows(device, valid, at, middle.shape[0])
        squares[...] += jnp.sum(counted * value * value, axis=0, keepdims=True)

    for index in range(BLOCKS):
        collect.take(index, use)
        spread.put(index, rounded.at[pl.ds(index * spread.block, spread.block)])
        rings.tick(1)
    for index in range(BLOCKS):
        output_collect.pass_on(index)
    rings.tick(2)
    for index in range(BLOCKS):
        spread.forward(index)
        rings.tick(1)
    for index in range(BLOCKS):
        output_collect.take(index, use_output)
        rings.tick(1)
    rings.finish()
    spread.finish()
    collect.finish()
    output_collect.finish()


def exchange_backward(valid, partial, output, middle, rows, gain, pairs):
    size = rows.shape[0]
    work = RingWork(pairs)

    def body(*refs):
        backward_kernel(work, *refs)

    return pl.pallas_call(
        body,
        out_shape=[
            jax.ShapeDtypeStruct((size, MODEL_WIDTH), wide),
            jax.ShapeDtypeStruct((1, MODEL_WIDTH), wide),
            jax.ShapeDtypeStruct((size, MODEL_WIDTH), low),
            jax.ShapeDtypeStruct((1, MODEL_WIDTH), wide),
            jax.ShapeDtypeStruct((4 * size, MODEL_WIDTH), low),
            *work.outputs(),
        ],
        in_specs=[SCALARS, ANY, ANY] + [VMEM] * 3 + [ANY] * len(work.operands),
        out_specs=[VMEM] * 4 + [ANY] * (1 + len(work.columns)),
        scratch_shapes=collect_shapes(size) * 2
        + [pltpu.VMEM((size, MODEL_WIDTH), low)]
        + work.scratch()
        + [semaphores_for(32 * BLOCKS + work.semaphores())],
        compiler_params=settings(3),
        cost_estimate=pl.CostEstimate(flops=0, bytes_accessed=128 * 2**20, transcendentals=0),
        name="exchange_backward",
    )(valid, partial, output, middle, rows, gain, *work.operands)


class Total:
    def __init__(self, device, mine, crossed, gathered):
        self.device, self.mine = device, mine
        self.crossed, self.gathered = crossed, gathered
        self.copies = {}
        self.steps = [("c", 0), ("t", 0)] + [("w", step) for step in range(device.count // 2)]

    def tick(self):
        device = self.device
        if not self.steps:
            return
        axis, step = self.steps.pop(0)
        if axis != "w":
            slot = 0 if axis == "c" else 1
            partner = device.other_core if axis == "c" else device.other_row
            copy = device.remote(self.mine.at[slot], self.crossed.at[slot], partner)
            copy.start()
            copy.wait()
            total = self.mine[slot] + self.crossed[slot]
            if slot == 0:
                self.mine[1] = total
            else:
                self.gathered[device.w] = total
            return
        for way in range(2):
            if way == 1 and step == device.count // 2 - 1:
                continue
            if step > 0:
                self.copies[way, step - 1].wait_recv()
            block = self.gathered.at[device.owner(-(1 - 2 * way) * step)]
            copy = device.remote(block, block, {"w": device.owner(1 - 2 * way)})
            copy.start()
            self.copies[way, step] = copy

    def finish(self, target):
        while self.steps:
            self.tick()
        half = self.device.count // 2
        self.copies[0, half - 1].wait_recv()
        self.copies[1, half - 2].wait_recv()
        for copy in self.copies.values():
            copy.wait_send()
        target[...] = self.gathered[0]
        for index in range(1, self.device.count):
            target[...] += self.gathered[index]


def last_kernel(
    work, first, tokens, gain, middle_grad, gain_grad, head_grads, output_squares, squares, *refs
):
    count = len(work.columns)
    operands, refs = refs[: len(work.operands)], refs[len(work.operands) :]
    first_total, stats_total, refs = refs[0], refs[1], refs[2:]
    sums, scratch = refs[:count], refs[count:]
    device = Device(scratch[-1])
    rings = work.begin(device, operands, scratch[7:-1], sums)
    device.meet(neighbours(device))
    collect = Collect(device, first, *scratch[:4])
    mine, crossed, gathered = scratch[4:7]
    total = Total(device, mine, crossed, gathered)
    mine[0] = jnp.zeros(mine.shape[1:], wide)
    mine[0, 1:2, :] = gain_grad[...]
    for row in range(2):
        mine[0, 2:3, head_at(row)] = head_grads[row : row + 1, :]
    mine[0, 3:4, :] = output_squares[...]
    mine[0, 4:6, :] = squares[...]
    collect.start()
    rings.tick(2)
    for index in range(BLOCKS):
        collect.pass_on(index)
    rings.tick(count - 2)

    def use(at, upstream):
        result, gained = norm_back_rows(tokens[at, :].astype(wide), gain[...], upstream)
        first_total[at, :] = result + middle_grad[at, :]
        mine[0, 0:1, :] += gained

    for index in range(BLOCKS):
        collect.take(index, use)
        rings.tick(1)
    while total.steps:
        total.tick()
        rings.tick(1)
    rings.finish()
    total.finish(stats_total)
    collect.finish()


def exchange_last(first, tokens, gain, middle_grad, sums, pairs):
    size = tokens.shape[0]
    count = lax.axis_size("w")
    stats = (8, MODEL_WIDTH)
    work = RingWork(pairs)

    def body(*refs):
        last_kernel(work, *refs)

    return pl.pallas_call(
        body,
        out_shape=[
            jax.ShapeDtypeStruct((size, MODEL_WIDTH), wide),
            jax.ShapeDtypeStruct(stats, wide),
            *work.outputs(),
        ],
        in_specs=[ANY] + [VMEM] * (3 + len(sums)) + [ANY] * len(work.operands),
        out_specs=[VMEM] * 2 + [ANY] * len(work.columns),
        scratch_shapes=collect_shapes(size)
        + [
            pltpu.VMEM((2, *stats), wide),
            pltpu.VMEM((2, *stats), wide),
            pltpu.VMEM((count, *stats), wide),
        ]
        + work.scratch()
        + [semaphores_for(16 * BLOCKS + 2 * count + 4 + work.semaphores())],
        compiler_params=settings(4),
        cost_estimate=pl.CostEstimate(flops=0, bytes_accessed=128 * 2**20, transcendentals=0),
        name="exchange_last",
    )(first, tokens, gain, middle_grad, *sums, *work.operands)


FEEDFORWARD_ROWS = 256
FEEDFORWARD_COLUMNS = 512


def feedforward_kernel(
    sizes, core, rows, upstream, large, small, gate_out, up_out, hidden_out, back_out, down_out
):
    weights = [(large.at[0], 0, sizes[0]), (small, sizes[0], sizes[1])]
    for weight, base, size in weights:
        for start in range(0, size, FEEDFORWARD_COLUMNS):
            width = min(FEEDFORWARD_COLUMNS, size - start)
            columns = slice(base + start, base + start + width)
            gate_part = dot(rows[...], weight[:, start : start + width], 1, 0)
            up_part = dot(rows[...], weight[:, size + start : size + start + width], 1, 0)
            hidden_grad = dot(
                upstream[...], weight[:, 2 * size + start : 2 * size + start + width], 1, 0
            )
            sigmoid_gate = jax.nn.sigmoid(gate_part)
            silu_gate = gate_part * sigmoid_gate
            hidden_out[:, columns] = (silu_gate * up_part).astype(low)
            gate_out[:, columns] = (
                hidden_grad * up_part * sigmoid_gate * (1.0 + gate_part * (1.0 - sigmoid_gate))
            ).astype(low)
            up_out[:, columns] = (hidden_grad * silu_gate).astype(low)
    for start in range(0, MODEL_WIDTH, FEEDFORWARD_COLUMNS):
        across = slice(start, start + FEEDFORWARD_COLUMNS)
        back = 0.0
        down = 0.0
        for weight, base, size in weights:
            columns = slice(base, base + size)
            back = back + dot(gate_out[:, columns], weight[across, :size], 1, 1)
            back = back + dot(up_out[:, columns], weight[across, size : 2 * size], 1, 1)
            down = down + dot(hidden_out[:, columns], weight[across, 2 * size :], 1, 1)
        back_out[:, across] = back.astype(low)
        down_out[:, across] = down.astype(low)


def feedforward(core, rows, upstream, large, small):
    sizes = (large.shape[2] // 3, small.shape[1] // 3)
    count = rows.shape[0]
    hidden = sum(sizes)

    def body(*refs):
        feedforward_kernel(sizes, *refs)

    def block(columns):
        return pl.BlockSpec((FEEDFORWARD_ROWS, columns), lambda index, core: (index, 0))

    once = pl.Buffered(1)
    return pl.pallas_call(
        body,
        grid_spec=pltpu.PrefetchScalarGridSpec(
            num_scalar_prefetch=1,
            grid=(count // FEEDFORWARD_ROWS,),
            in_specs=[
                block(MODEL_WIDTH),
                block(MODEL_WIDTH),
                pl.BlockSpec(
                    (1, *large.shape[1:]),
                    lambda index, core: (core[0], 0, 0),
                    pipeline_mode=once,
                ),
                pl.BlockSpec(small.shape, lambda index, core: (0, 0), pipeline_mode=once),
            ],
            out_specs=[block(hidden)] * 3 + [block(MODEL_WIDTH)] * 2,
        ),
        out_shape=[jax.ShapeDtypeStruct((count, hidden), low)] * 3
        + [jax.ShapeDtypeStruct((count, MODEL_WIDTH), low)] * 2,
        compiler_params=pltpu.CompilerParams(vmem_limit_bytes=60 * 2**20),
        cost_estimate=pl.CostEstimate(
            flops=12 * count * MODEL_WIDTH * hidden,
            bytes_accessed=48 * 2**20,
            transcendentals=count * hidden,
        ),
        name="feedforward",
    )(core, rows, upstream, large, small)


def head_rows(values, gain, cosine, sine):
    factor = lax.rsqrt(jnp.mean(values * values, axis=-1, keepdims=True) + norm_epsilon)
    normed = values * factor * gain
    return (normed * cosine + pltpu.roll(normed, HEAD_WIDTH // 2, 1) * sine).astype(low)


def head_back(values, gain, cosine, sine, upstream):
    turned = upstream * cosine - pltpu.roll(upstream, HEAD_WIDTH // 2, 1) * sine
    return norm_back_rows(values, gain, turned)


def head_at(index):
    return slice(index * HEAD_WIDTH, (index + 1) * HEAD_WIDTH)


def gate_column(logits, head):
    lanes = lax.broadcasted_iota(jnp.int32, logits.shape, 1)
    logit = jnp.sum(jnp.where(lanes == head, logits, 0.0), axis=-1, keepdims=True)
    return jax.nn.sigmoid(logit)


def mask_rows(mask, valid_count, piece_start):
    length = mask.shape[0]
    for start in range(0, length, QUERY_ROWS):
        shape = (QUERY_ROWS, length)
        row = start + lax.broadcasted_iota(jnp.int32, shape, 0)
        column = lax.broadcasted_iota(jnp.int32, shape, 1)
        last = piece_start + PIC
        inside = (row >= piece_start) & (row < last) & (column >= piece_start) & (column < last)
        allowed = (column < valid_count) & ((column <= row) | inside)
        mask[start : start + QUERY_ROWS, :] = jnp.where(allowed, 0.0, masked_score)


def probabilities(queries, keys, mask):
    scores = dot(queries, keys, 1, 1) * HEAD_WIDTH ** (-0.5) + mask
    expos = jnp.exp(scores - jnp.max(scores, axis=-1, keepdims=True))
    return expos * (1.0 / jnp.sum(expos, axis=-1, keepdims=True))


QUERY_ROWS = 256


def attention_forward_kernel(
    groups, share, valid, start, rows_in, weights, gains, cosine, sine, pre, gated, partial, mask
):
    sequence = pl.program_id(0)
    mask_rows(mask, valid[sequence], start[sequence])
    heads = groups * share
    length, projected = pre.shape
    for column in range(0, projected, 3 * HEAD_WIDTH):
        columns = slice(column, min(column + 3 * HEAD_WIDTH, projected))
        pre[:, columns] = dot(rows_in[...], weights[:, columns], 1, 0)
    for group in range(groups):
        keys = head_rows(pre[:, head_at(heads + group)], gains[1:2, :], cosine[...], sine[...])
        values = pre[:, head_at(heads + groups + group)].astype(low)
        for head in range(group * share, (group + 1) * share):
            for at in range(0, length, QUERY_ROWS):
                rows = slice(at, at + QUERY_ROWS)
                queries = head_rows(
                    pre[rows, head_at(head)], gains[0:1, :], cosine[rows, :], sine[rows, :]
                )
                probs = probabilities(queries, keys, mask[rows, :])
                mixed = dot(probs.astype(low), values, 1, 0)
                gate = gate_column(pre[rows, head_at(heads + 2 * groups)], head)
                gated[rows, head_at(head)] = (mixed * gate).astype(low)
    for column in range(0, MODEL_WIDTH, 512):
        partial[:, column : column + 512] = dot(
            gated[...], weights[column : column + 512, projected:], 1, 1
        ).astype(low)


def attention_backward_kernel(
    groups, share, valid, start, pre, rows_in, weights, gains, cosine, sine,
    grads, gain_grads, partial, upstream, mask,
):
    sequence = pl.program_id(0)
    mask_rows(mask, valid[sequence], start[sequence])
    heads = groups * share
    length, projected = pre.shape
    upstream[...] = dot(rows_in[...], weights[:, projected:], 1, 0)
    scale = HEAD_WIDTH ** (-0.5)

    @pl.when(sequence == 0)
    def _():
        gain_grads[...] = jnp.zeros_like(gain_grads)

    logit_grads = [jnp.zeros((QUERY_ROWS, HEAD_WIDTH), wide)] * (length // QUERY_ROWS)
    for group in range(groups):
        key_pre = pre[:, head_at(heads + group)]
        keys = head_rows(key_pre, gains[1:2, :], cosine[...], sine[...])
        values = pre[:, head_at(heads + groups + group)].astype(low)
        value_grad = jnp.zeros((length, HEAD_WIDTH), wide)
        key_grad = jnp.zeros((length, HEAD_WIDTH), wide)
        for head in range(group * share, (group + 1) * share):
            for block, at in enumerate(range(0, length, QUERY_ROWS)):
                rows = slice(at, at + QUERY_ROWS)
                query_pre = pre[rows, head_at(head)]
                queries = head_rows(query_pre, gains[0:1, :], cosine[rows, :], sine[rows, :])
                probs = probabilities(queries, keys, mask[rows, :])
                probs_low = probs.astype(low)
                mixed = dot(probs_low, values, 1, 0)
                gate = gate_column(pre[rows, head_at(heads + 2 * groups)], head)
                gated_grad = upstream[rows, head_at(head)]
                mixed_grad = (gated_grad * gate).astype(low)
                logit_grad = (
                    jnp.sum(gated_grad * mixed, axis=-1, keepdims=True) * gate * (1.0 - gate)
                )
                lanes = lax.broadcasted_iota(jnp.int32, (QUERY_ROWS, HEAD_WIDTH), 1)
                logit_grads[block] = logit_grads[block] + jnp.where(lanes == head, logit_grad, 0.0)
                value_grad = value_grad + dot(probs_low, mixed_grad, 0, 0)
                prob_grad = dot(mixed_grad, values, 1, 1)
                score_grad = (
                    probs * (prob_grad - jnp.sum(prob_grad * probs, axis=-1, keepdims=True))
                ).astype(low)
                key_grad = key_grad + dot(score_grad, queries, 0, 0)
                query_grad, gained = head_back(
                    query_pre,
                    gains[0:1, :],
                    cosine[rows, :],
                    sine[rows, :],
                    dot(score_grad, keys, 1, 0) * scale,
                )
                grads[rows, head_at(head)] = query_grad.astype(low)
                gain_grads[0:1, :] += gained
        key_grad, gained = head_back(
            key_pre, gains[1:2, :], cosine[...], sine[...], key_grad * scale
        )
        gain_grads[1:2, :] += gained
        grads[:, head_at(heads + group)] = key_grad.astype(low)
        grads[:, head_at(heads + groups + group)] = value_grad.astype(low)
    for block, at in enumerate(range(0, length, QUERY_ROWS)):
        grads[slice(at, at + QUERY_ROWS), head_at(heads + 2 * groups)] = logit_grads[block].astype(
            low
        )
    for column in range(0, MODEL_WIDTH, 512):
        partial[:, column : column + 512] = dot(
            grads[...], weights[column : column + 512, :projected], 1, 1
        ).astype(low)


def sequence_block(columns, length):
    return pl.BlockSpec((length, columns), lambda sequence: (sequence, 0))


def fixed_block(*shape):
    return pl.BlockSpec(shape, lambda sequence: (0, 0))


def attention_call(body, name, specs, sequences, outputs, out_specs, scratch, operands):
    return pl.pallas_call(
        body,
        grid=(sequences,),
        out_shape=outputs,
        in_specs=[SCALARS, SCALARS, *specs],
        out_specs=out_specs,
        scratch_shapes=scratch,
        compiler_params=pltpu.CompilerParams(vmem_limit_bytes=60 * 2**20),
        cost_estimate=pl.CostEstimate(
            flops=2**33, bytes_accessed=24 * 2**20, transcendentals=2**21
        ),
        name=name,
    )(*operands)


def attention_specs(weights, length):
    return [
        pl.BlockSpec(weights.shape, lambda sequence: (0, 0), pipeline_mode=pl.Buffered(1)),
        fixed_block(2, HEAD_WIDTH),
        fixed_block(length, HEAD_WIDTH),
        fixed_block(length, HEAD_WIDTH),
    ]


def attention_forward(groups, share, valid, start, rows, weights, gains, cosine, sine):
    length, columns = cosine.shape[0], groups * share * HEAD_WIDTH
    projected, count = weights.shape[1] - columns, rows.shape[0]

    def body(*refs):
        attention_forward_kernel(groups, share, *refs)

    return attention_call(
        body,
        "attention_forward",
        [sequence_block(MODEL_WIDTH, length), *attention_specs(weights, length)],
        count // length,
        [
            jax.ShapeDtypeStruct((count, projected), wide),
            jax.ShapeDtypeStruct((count, columns), low),
            jax.ShapeDtypeStruct((count, MODEL_WIDTH), low),
        ],
        [sequence_block(size, length) for size in (projected, columns, MODEL_WIDTH)],
        [pltpu.VMEM((length, length), wide)],
        (valid, start, rows, weights, gains, cosine, sine),
    )


def attention_backward(groups, share, valid, start, pre, rows, weights, gains, cosine, sine):
    length, columns = cosine.shape[0], groups * share * HEAD_WIDTH
    count, projected = pre.shape

    def body(*refs):
        attention_backward_kernel(groups, share, *refs)

    return attention_call(
        body,
        "attention_backward",
        [
            sequence_block(projected, length),
            sequence_block(MODEL_WIDTH, length),
            *attention_specs(weights, length),
        ],
        count // length,
        [
            jax.ShapeDtypeStruct((count, projected), low),
            jax.ShapeDtypeStruct((2, HEAD_WIDTH), wide),
            jax.ShapeDtypeStruct((count, MODEL_WIDTH), low),
        ],
        [
            sequence_block(projected, length),
            fixed_block(2, HEAD_WIDTH),
            sequence_block(MODEL_WIDTH, length),
        ],
        [pltpu.VMEM((length, columns), wide), pltpu.VMEM((length, length), wide)],
        (valid, start, pre, rows, weights, gains, cosine, sine),
    )


def adam_kernel(layouts, names, heads, *refs):
    given, refs = refs[: len(names)], refs[len(names) :]
    count = len(layouts)
    stats, inverse, refs = refs[0], refs[1], refs[2:]
    extra, states, refs = refs[:11], refs[11 : 11 + 3 * count], refs[11 + 3 * count :]
    scales, refs = refs[0], refs[1:]
    extra_targets, targets, refs = refs[:11], refs[11 : 11 + 3 * count], refs[11 + 3 * count :]
    buffers, extra_buffers, refs = refs[: 3 * count], refs[3 * count :][:11], refs[3 * count + 11 :]
    small = extra_buffers[2:]
    sources, semaphores, sum_semaphores = dict(zip(names, refs)), refs[-2], refs[-1]
    fetches = [
        pltpu.make_async_copy(value, sources[name], sum_semaphores.at[0, i])
        for i, (name, value) in enumerate(zip(names, given))
    ]
    for i in range(11):
        slot = len(names) + i
        fetches.append(
            pltpu.make_async_copy(extra[i], extra_buffers[i], sum_semaphores.at[0, slot])
        )
    moves = [
        pltpu.make_async_copy(extra_buffers[i], extra_targets[i], sum_semaphores.at[1, i])
        for i in range(11)
    ]
    loads = [
        pltpu.make_async_copy(states[i], buffers[i], semaphores.at[0, i]) for i in range(3 * count)
    ]
    stores = [
        pltpu.make_async_copy(buffers[i], targets[i], semaphores.at[1, i])
        for i in range(3 * count)
    ]
    for copy in (*fetches, *loads):
        copy.start()
    for copy in fetches:
        copy.wait()
    for copy in moves[:2]:
        copy.start()

    def update(part, at, gradient, rate, decay_rate):
        old = [small[3 * part + i][at] for i in range(3)]
        for i, value in enumerate(adam_update(*old, gradient, rate, decay_rate)):
            small[3 * part + i][at] = value

    everything = (slice(None), slice(None))
    update(0, everything, stats[0:2, :], 0.5, 0.0)
    for row in range(2):
        update(1, (slice(row, row + 1), slice(None)), stats[2:3, head_at(row)], 0.5, 0.0)
    column, size = heads
    gradient = jnp.concatenate(
        [
            sources["projected"][core, :, column : column + HEAD_WIDTH].astype(wide).T[:size]
            for core in range(2)
        ],
        axis=0,
    )
    update(2, everything, gradient, layouts[0][1], weight_decay)
    for copy in moves[2:]:
        copy.start()
    lanes = lax.broadcasted_iota(jnp.int32, scales.shape, 1)
    squares = jnp.zeros(scales.shape, wide)
    for lane, row in enumerate((4, 5, 3)):
        squares = jnp.where(
            lanes == lane, jnp.sum(stats[row : row + 1, :], axis=-1, keepdims=True), squares
        )
    scales[...] = jnp.sqrt(squares * inverse[...])
    for number, (transposed, rate, leads) in enumerate(layouts):
        matrix = buffers[3 * number : 3 * number + 3]
        for load in loads[3 * number : 3 * number + 3]:
            load.wait()
        for lead, pieces in enumerate(leads):
            quarter = sum(size for _, _, size in pieces)
            for core in range(2):
                start = core * quarter
                for name, column, size in pieces:
                    step = 256 if size % 256 == 0 else 128

                    @pl.loop(0, size // step)
                    def _(block):
                        columns = pl.ds(pl.multiple_of(column + block * step, 128), step)
                        gradient = sources[name][core, :, columns].astype(wide)
                        place = pl.ds(pl.multiple_of(start + block * step, 128), step)
                        if transposed:
                            gradient = gradient.T
                            at = (place, slice(None))
                        elif len(leads) > 1:
                            at = (lead, slice(None), place)
                        else:
                            at = (slice(None), place)
                        weight, moment, square = (part[at] for part in matrix)
                        for part, value in zip(
                            matrix,
                            adam_update(weight, moment, square, gradient, rate, weight_decay),
                        ):
                            part[at] = value

                    start += size
        for store in stores[3 * number : 3 * number + 3]:
            store.start()
    for copy in (*stores, *moves):
        copy.wait()


def adam_matrices(layouts, heads, sums, stats, inverse, passed, small, states):
    def body(*refs):
        adam_kernel(layouts, list(sums), heads, *refs)

    extra = [*passed, *small]

    def like(values):
        return [jax.ShapeDtypeStruct(value.shape, value.dtype) for value in values]

    return pl.pallas_call(
        body,
        out_shape=like([inverse, *extra, *states]),
        in_specs=[ANY] * len(sums) + [VMEM] * 2 + [ANY] * (len(extra) + len(states)),
        out_specs=[VMEM] + [ANY] * (len(extra) + len(states)),
        scratch_shapes=[
            pltpu.VMEM(value.shape, value.dtype) for value in (*states, *extra, *sums.values())
        ]
        + [
            pltpu.SemaphoreType.DMA((2, len(states))),
            pltpu.SemaphoreType.DMA((2, len(sums) + len(extra))),
        ],
        compiler_params=pltpu.CompilerParams(vmem_limit_bytes=60 * 2**20),
        cost_estimate=pl.CostEstimate(
            flops=2**25, bytes_accessed=40 * 2**20, transcendentals=2**21
        ),
        name="adam_matrices",
    )(*sums.values(), stats, inverse, *extra, *states)


def prepare_kernel(sizes, *refs):
    given, (attention, normed, large, small), refs = refs[:8], refs[8:12], refs[12:]
    loads = [
        pltpu.make_async_copy(value, refs[i], refs[8].at[i]) for i, value in enumerate(given)
    ]
    for load in loads:
        load.start()
    for load in loads:
        load.wait()
    query, keyvalue, headgate, output, gateup, down, tokens, gain = refs[:8]
    core = lax.axis_index("c")
    head_cols, group_cols = query.shape[1] // 2, keyvalue.shape[2] // 2
    edges = [head_cols, head_cols + group_cols, head_cols + 2 * group_cols]
    heads = head_cols // HEAD_WIDTH
    rows = query.shape[0]
    hidden = sum(sizes)
    logits = jnp.concatenate(
        [headgate[...], jnp.zeros((HEAD_WIDTH - headgate.shape[0], rows), wide)], axis=0
    ).T
    lanes = lax.broadcasted_iota(jnp.int32, logits.shape, 1)
    for quarter in range(2):
        slot = lax.rem(quarter + core, 2)
        columns = slice(quarter * head_cols, (quarter + 1) * head_cols)
        attention[slot, :, :head_cols] = query[:, columns].astype(low)
        for part in range(2):
            attention[slot, :, edges[part] : edges[part + 1]] = keyvalue[
                part, :, quarter * group_cols : (quarter + 1) * group_cols
            ].astype(low)
        turned = pltpu.roll(logits, HEAD_WIDTH - heads, 1) if quarter else logits
        attention[slot, :, edges[2] : edges[2] + HEAD_WIDTH] = jnp.where(
            lanes < heads, turned, 0.0
        ).astype(low)
        attention[slot, :, edges[2] + HEAD_WIDTH :] = output[columns, :].T.astype(low)
        base = quarter * hidden
        for part in range(3):
            start = 0
            for target, size in ((large.at[quarter], sizes[0]), (small.at[slot], sizes[1])):
                here = slice(base + start, base + start + size)
                value = gateup[part, :, here] if part < 2 else down[here, :].T
                target[:, part * size : (part + 1) * size] = value.astype(low)
                start += size

    @pl.loop(0, tokens.shape[0] // STRIP)
    def _(strip):
        at = rows_at(strip * STRIP, STRIP)
        normed[at, :] = normalize(tokens[at, :].astype(wide), gain[...]).astype(low)


def prepare(sizes, query, keyvalue, headgate, output, gateup, down, tokens, gain):
    rows = query.shape[0]
    columns = query.shape[1] // 2 * 2 + keyvalue.shape[2] + HEAD_WIDTH
    operands = (query, keyvalue, headgate, output, gateup, down, tokens, gain)

    def body(*refs):
        prepare_kernel(sizes, *refs)

    return pl.pallas_call(
        body,
        out_shape=[
            jax.ShapeDtypeStruct((2, rows, columns), low),
            jax.ShapeDtypeStruct(tokens.shape, low),
            jax.ShapeDtypeStruct((2, rows, 3 * sizes[0]), low),
            jax.ShapeDtypeStruct((2, rows, 3 * sizes[1]), low),
        ],
        in_specs=[ANY] * 8,
        out_specs=[VMEM] * 4,
        scratch_shapes=[pltpu.VMEM(value.shape, value.dtype) for value in operands]
        + [pltpu.SemaphoreType.DMA((8,))],
        compiler_params=pltpu.CompilerParams(vmem_limit_bytes=60 * 2**20),
        cost_estimate=pl.CostEstimate(
            flops=2**22, bytes_accessed=12 * 2**20, transcendentals=0
        ),
        name="prepare",
    )(*operands)


def local(
    tokens,
    cotangent,
    valid_len,
    pic_start,
    norm_gains,
    norm_moment,
    norm_square,
    head_gains,
    head_moment,
    head_square,
    query_weight,
    query_moment,
    query_square,
    keyvalue_matrix,
    keyvalue_first_moment,
    keyvalue_second_moment,
    headgate_weight,
    headgate_moment,
    headgate_square,
    output_weight,
    output_moment,
    output_square,
    gateup_weight,
    gateup_moment,
    gateup_square,
    down_weight,
    down_moment,
    down_square,
):
    local_rows = tokens.shape[0]
    length_value = local_rows * 2
    rows = length_value * 2
    group = lax.axis_index("w")
    core = lax.axis_index("c")
    place = lax.axis_index("t")
    heads_here = query_weight.shape[1] // HEAD_WIDTH // 2
    groups_here = keyvalue_matrix.shape[2] // HEAD_WIDTH // 2
    share = heads_here // groups_here
    head_cols = heads_here * HEAD_WIDTH
    group_cols = groups_here * HEAD_WIDTH
    hidden_here = gateup_weight.shape[2] // 2

    bounds = [0, head_cols, group_cols, group_cols, 128, head_cols]
    edges = [sum(bounds[: i + 1]) for i in range(6)]
    sizes = (hidden_here - hidden_here // 6, hidden_here // 6)
    attention_pieces, normed, large_block, small_pieces = prepare(
        sizes,
        query_weight,
        keyvalue_matrix,
        headgate_weight.T,
        output_weight,
        gateup_weight,
        down_weight,
        tokens,
        norm_gains[0:1],
    )
    large_both = lax.all_gather(large_block, ("w", "c"), axis=1, tiled=True)
    attention_full, first_full, output_grad_full = gather_attention(
        attention_pieces, normed, cotangent
    )
    valid_pair = lax.dynamic_slice_in_dim(valid_len, 2 * group, 2)
    start_pair = lax.dynamic_slice_in_dim(pic_start, 2 * group, 2)
    cosine, sine = rotary_tables(length_value)
    projected, gated_low, attention_partial = attention_forward(
        groups_here,
        share,
        valid_pair,
        start_pair,
        first_full,
        attention_full,
        head_gains,
        cosine,
        sine,
    )
    middle, squares, second_full, small_full = exchange_forward(
        valid_len, attention_partial, tokens, norm_gains[1:2], small_pieces
    )
    gate_grad, up_grad, hidden_low, second_partial, feedforward_partial = feedforward(
        core[None], second_full, output_grad_full, large_both, small_full
    )
    pieces = [(0, hidden_here)]
    middle_grad, second_gain_grad, block_output, output_squares, attention_grad, *sums = (
        exchange_backward(
            valid_len,
            second_partial,
            feedforward_partial,
            middle,
            cotangent,
            norm_gains[1:2],
            [(second_full, grad, *piece) for grad in (gate_grad, up_grad) for piece in pieces],
        )
    )
    projected_grad, head_gain_grads, first_partial = attention_backward(
        groups_here,
        share,
        valid_pair,
        start_pair,
        projected,
        attention_grad,
        attention_full,
        head_gains,
        cosine,
        sine,
    )
    tokens_grad, stats, *more = exchange_last(
        first_partial,
        tokens,
        norm_gains[0:1],
        middle_grad,
        [second_gain_grad, head_gain_grads, output_squares, squares],
        [
            *((output_grad_full, hidden_low, *piece) for piece in pieces),
            (first_full, projected_grad, 0, edges[4]),
            (attention_grad, gated_low, 0, head_cols),
        ],
    )
    denominator = jnp.sum(valid_len).astype(wide) * MODEL_WIDTH
    inverse = jnp.full((1, HEAD_WIDTH), 1.0 / denominator)
    input_rate = MODEL_WIDTH ** (-0.5)
    down_rate = FF ** (-0.5)
    output_rate = max(QUERY_HEADS * HEAD_WIDTH // 128, 4) ** (-0.5)
    widths = [hidden_here]

    def parts_of(name):
        return [(f"{name} {index}", 0, width) for index, width in enumerate(widths)]

    layouts = [
        (
            False,
            input_rate,
            [parts_of("gate"), parts_of("up")],
        ),
        (True, down_rate, [parts_of("down")]),
        (False, input_rate, [[("projected", edges[0], head_cols)]]),
        (
            False,
            input_rate,
            [[("projected", edges[1], group_cols)], [("projected", edges[2], group_cols)]],
        ),
        (True, output_rate, [[("output", 0, head_cols)]]),
    ]
    names = ["gate 0", "up 0", "down 0", "projected", "output"]
    sums = dict(zip(names, [*sums, *more]))
    scales, block_output, tokens_grad, *updated = adam_matrices(
        layouts,
        (edges[3], heads_here),
        sums,
        stats,
        inverse,
        [block_output, tokens_grad],
        [
            norm_gains,
            norm_moment,
            norm_square,
            head_gains,
            head_moment,
            head_square,
            headgate_weight.T,
            headgate_moment.T,
            headgate_square.T,
        ],
        [
            gateup_weight,
            gateup_moment,
            gateup_square,
            down_weight,
            down_moment,
            down_square,
            query_weight,
            query_moment,
            query_square,
            keyvalue_matrix,
            keyvalue_first_moment,
            keyvalue_second_moment,
            output_weight,
            output_moment,
            output_square,
        ],
    )
    norms_new, heads_new, headgate_new, gateup_new, down_new, query_new, keyvalue_new, output_new = (
        updated[3 * i : 3 * i + 3] for i in range(8)
    )
    branch_scales = scales[0, :3]
    return (
        block_output,
        tokens_grad,
        branch_scales,
        *norms_new,
        *heads_new,
        *query_new,
        *keyvalue_new,
        *(value.T for value in headgate_new),
        *output_new,
        *gateup_new,
        *down_new,
    )


def solution(mesh):
    fsdp, tp = mesh.devices.shape
    fine = Mesh(mesh.devices.reshape(fsdp // 2, 2, tp), ("w", "c", "t"))
    whole = ("w", "c")
    rows = P(("w", "c", "t"), None)
    first = P(whole, "t")
    second = P(None, whole, "t")
    last = P("t", whole)
    matrices = (first,) * 3 + (second,) * 3 + (first,) * 3 + (last,) * 3 + (second,) * 3 + (last,) * 3
    return jax.shard_map(
        local,
        mesh=fine,
        in_specs=(rows, rows, P(), P()) + (P(),) * 6 + matrices,
        out_specs=(rows, rows, P()) + (P(),) * 6 + matrices,
        check_vma=False,
    )
```
